32 devices in a mesh: qx: 4 (over y, core), qy: 8 (over z, x).
Axes of the slice: x: 2, y: 2, z: 4, core: 2. Of those that a mesh axis runs over, the one named last changes fastest.
Arguments:
- positions: float32 [16, 32, 2, 256], replicated, may hold values from 0 to 32, as said below
- samples: bfloat16 [16, 32, 256, 256], P('qx', 'qy'), may hold values from -6 to 6
- leaf_basis: bfloat16 [16, 32, 256, 256], P('qx', 'qy'), may hold values from -0.375 to 0.375
- transfer_one: bfloat16 [16, 32, 256, 256], P('qx', 'qy'), may hold values from -0.25 to 0.25
- transfer_two: bfloat16 [8, 16, 256, 256], P('qx', 'qy'), may hold values from -0.25 to 0.25
- couplings: bfloat16 [3, 20, 256, 256], replicated, may hold values from -0.078125 to 0.078125
- near_lists: int32 [16, 32, 9], P('qx', 'qy'), may hold values from -1 to 511, as said below
- far_zero: int32 [16, 32, 27], P('qx', 'qy'), may hold values from -1 to 511, as said below
- far_one: int32 [8, 16, 27], P('qx', 'qy'), may hold values from -1 to 127, as said below
- far_two: int32 [4, 8, 27], P('qx', 'qy'), may hold values from -1 to 31, as said below
Outputs:
- product: bfloat16 [16, 32, 256, 256], P('qx', 'qy')
The draws below stay inside these ranges and needn't reach their ends.
Inputs may be any that keep to these rules, and one draw needn't show every extreme that they name: Site p of leaf (i, j) lies at positions[i, j, 0, p] between i and i + 1 and positions[i, j, 1, p] between j and j + 1. `near_lists`: every entry of the list of leaf (i, j) is -1 or the id r * 32 + c of a leaf (r, c) with abs(r - i) <= 1 and abs(c - j) <= 1; the leaf's own id is always in its list, and no id stands twice. `far_zero`: every entry of the list of leaf (i, j) is -1 or the id r * 32 + c of a leaf (r, c) with max(abs(r - i), abs(c - j)) >= 2 whose parent (r // 2, c // 2) is within one step of (i // 2, j // 2) along each coordinate; no id stands twice. `far_one`: every entry of the list of level-1 cell (i, j) is -1 or the id r * 16 + c of a level-1 cell (r, c) with max(abs(r - i), abs(c - j)) >= 2 and (r // 2, c // 2) within one step of (i // 2, j // 2) along each coordinate; no id stands twice. `far_two`: every entry of the list of level-2 cell (i, j) is -1 or the id r * 8 + c of a level-2 cell (r, c) with max(abs(r - i), abs(c - j)) >= 2 and (r // 2, c // 2) within one step of (i // 2, j // 2) along each coordinate; no id stands twice.
All inputs are finite; a program needn't handle non-finite values.
Results may differ from the reference program's by a relative error of at most 0.0085.
Values may be sent and summed in bfloat16 or wider, within the bound.
No kernel may reach another device: no remote copies, remote signals or barrier semaphores. Data moves between devices by JAX's collectives and lax.ppermute only.
A program may use at most 256 MiB of HBM per device.

```python
import jax
import jax.numpy as jnp
import numpy as np
from jax import lax

LEAF = 256
RANK = 256
COLS = 256
SIDE = 4
NEAR = 9
FAR = 27
HALF = 20
LEVELS = 3
GX0 = 16
GY0 = 32
GX1 = 8
GY1 = 16
GX2 = 4
GY2 = 8


def crowded_cells(key, grid_rows, grid_cols, cell_leaves):
    centre_row = jax.random.randint(jax.random.fold_in(key, 7), (), 0, GX0)
    centre_col = jax.random.randint(jax.random.fold_in(key, 8), (), 0, GY0)
    mid_rows = jnp.arange(grid_rows, dtype=jnp.int32) * cell_leaves + cell_leaves // 2
    mid_cols = jnp.arange(grid_cols, dtype=jnp.int32) * cell_leaves + cell_leaves // 2
    reach_leaves = 3 * SIDE
    near_rows = jnp.abs(mid_rows - centre_row) <= reach_leaves
    near_cols = jnp.abs(mid_cols - centre_col) <= reach_leaves
    return near_rows[:, None] & near_cols[None, :]


def far_lists(key, grid_rows, grid_cols, cell_leaves, salt):
    crowded = crowded_cells(key, grid_rows, grid_cols, cell_leaves)
    row_ids = jnp.arange(grid_rows, dtype=jnp.int32)[:, None, None]
    col_ids = jnp.arange(grid_cols, dtype=jnp.int32)[None, :, None]
    slot_ids = jnp.arange(36, dtype=jnp.int32)[None, None, :]
    source_row = row_ids + slot_ids // 6 - 2 - row_ids % 2
    source_col = col_ids + slot_ids % 6 - 2 - col_ids % 2
    adjacent = (jnp.abs(source_row - row_ids) <= 1) & (jnp.abs(source_col - col_ids) <= 1)
    inside = (source_row >= 0) & (source_row < grid_rows) & (source_col >= 0) & (source_col < grid_cols)
    coin_flips = jax.random.randint(jax.random.fold_in(key, salt), (grid_rows, grid_cols, 36), 0, 2) == 0
    retained = inside & jnp.logical_not(adjacent) & (crowded[:, :, None] | coin_flips)
    source_ids = jnp.where(retained, source_row * grid_cols + source_col, -1)
    scores = jax.random.randint(jax.random.fold_in(key, salt + 1), (grid_rows, grid_cols, 36), 0, 1 << 20) * 64 + slot_ids
    scores = scores + jnp.where(adjacent, 1 << 27, 0)
    ordering = jnp.argsort(scores, axis=-1)[:, :, :FAR]
    return jnp.take_along_axis(source_ids, ordering, axis=-1).astype(jnp.int32)


def draw_positions(key, part):
    array_shape = (GX0, GY0, 2, LEAF)
    inside_cell = jax.random.uniform(key, array_shape, jnp.float32, 0.005, 0.995)
    row_base = jnp.arange(GX0, dtype=jnp.float32)[:, None, None]
    col_base = jnp.arange(GY0, dtype=jnp.float32)[None, :, None]
    return jnp.stack([inside_cell[:, :, 0] + row_base, inside_cell[:, :, 1] + col_base], axis=2)


def draw_near_lists(key, part):
    crowded = crowded_cells(key, GX0, GY0, 1)
    row_ids = jnp.arange(GX0, dtype=jnp.int32)[:, None, None]
    col_ids = jnp.arange(GY0, dtype=jnp.int32)[None, :, None]
    slot_ids = jnp.arange(NEAR, dtype=jnp.int32)[None, None, :]
    source_row = row_ids + slot_ids // 3 - 1
    source_col = col_ids + slot_ids % 3 - 1
    inside = (source_row >= 0) & (source_row < GX0) & (source_col >= 0) & (source_col < GY0)
    coin_flips = jax.random.randint(jax.random.fold_in(key, 11), (GX0, GY0, NEAR), 0, 3) == 0
    retained = inside & ((slot_ids == 4) | crowded[:, :, None] | coin_flips)
    source_ids = jnp.where(retained, source_row * GY0 + source_col, -1)
    scores = jax.random.randint(jax.random.fold_in(key, 13), (GX0, GY0, NEAR), 0, 1 << 20) * 16 + slot_ids
    ordering = jnp.argsort(scores, axis=-1)
    return jnp.take_along_axis(source_ids, ordering, axis=-1).astype(jnp.int32)


def draw_far_zero(key, part):
    return far_lists(key, GX0, GY0, 1, 21)


def draw_far_one(key, part):
    return far_lists(key, GX1, GY1, 2, 23)


def draw_far_two(key, part):
    return far_lists(key, GX2, GY2, 4, 25)


def block_levels(own_key, shape, shards, low, high):
    gain = 1.0
    for axis_at, blocks in shards:
        heights = jax.random.uniform(jax.random.fold_in(jax.random.fold_in(own_key, 6), axis_at), (blocks,), jnp.float32, low / len(shards), high / len(shards))
        gain = gain * jnp.repeat(jnp.exp(heights), shape[axis_at] // blocks).reshape((-1,) + (1,) * (len(shape) - 1 - axis_at))
    return gain


def gaussian(own_key, extent, scale, reach, split=(), kind=jnp.bfloat16):
    factor_of = block_levels(own_key, extent, split, -0.22, 0.18) if split else 1.0
    values = jax.random.normal(own_key, extent, jnp.float32) * scale * factor_of
    return jnp.minimum(jnp.maximum(values, -reach), reach).astype(kind)


def setup_inputs(seed: int = 0) -> dict:
    splits = jax.random.split(jax.random.key(seed), 11)
    positions = draw_positions(jax.random.fold_in(splits[10], 71), 0)
    samples = gaussian(splits[1], (GX0, GY0, LEAF, COLS), 1.0, 6.0, ((0, 4), (1, 8)))
    leaf_basis = gaussian(splits[2], (GX0, GY0, LEAF, RANK), LEAF ** -0.5, 0.375, ((0, 4), (1, 8)))
    transfer_one = gaussian(splits[3], (GX0, GY0, RANK, RANK), (2 * RANK) ** -0.5, 0.25, ((0, 4), (1, 8)))
    transfer_two = gaussian(splits[4], (GX1, GY1, RANK, RANK), (2 * RANK) ** -0.5, 0.25, ((0, 4), (1, 8)))
    couplings = gaussian(splits[5], (LEVELS, HALF, RANK, RANK), (FAR * RANK) ** -0.5, 0.078125)
    near_lists = draw_near_lists(jax.random.fold_in(splits[10], 71), 0)
    far_zero = draw_far_zero(jax.random.fold_in(splits[10], 71), 0)
    far_one = draw_far_one(jax.random.fold_in(splits[10], 71), 0)
    far_two = draw_far_two(jax.random.fold_in(splits[10], 71), 0)
    return dict(positions=positions, samples=samples, leaf_basis=leaf_basis, transfer_one=transfer_one, transfer_two=transfer_two, couplings=couplings, near_lists=near_lists, far_zero=far_zero, far_one=far_one, far_two=far_two)


root_three = 1.7320508075688772
length_scale = 1.0

def offset_plan():
    slot_of = np.zeros((49,), np.int32)
    flip_of = np.zeros((49,), np.int32)
    active = np.zeros((49,), np.int32)
    upper_half = []
    for number in range(49):
        row_step = number // 7 - 3
        col_step = number % 7 - 3
        if max(abs(row_step), abs(col_step)) >= 2 and (row_step > 0 or (row_step == 0 and col_step > 0)):
            upper_half.append(number)
    for number in range(49):
        row_step = number // 7 - 3
        col_step = number % 7 - 3
        if max(abs(row_step), abs(col_step)) >= 2:
            active[number] = 1
            if number in upper_half:
                slot_of[number] = upper_half.index(number)
            else:
                slot_of[number] = upper_half.index((3 - row_step) * 7 + 3 - col_step)
                flip_of[number] = 1
    return (slot_of, flip_of, active)

def coupling_table(level_couplings):
    slot_of, flip_of, active = offset_plan()
    pieces = []
    for number in range(49):
        matrix = level_couplings[int(slot_of[number])]
        if flip_of[number] == 1:
            matrix = matrix.T
        if active[number] == 0:
            matrix = jnp.zeros_like(matrix)
        pieces.append(matrix)
    return jnp.stack(pieces)

def matern_tiles(targets, sources, allowed):
    gap_rows = targets[:, 0][:, :, None] - sources[:, 0][:, None, :]
    gap_cols = targets[:, 1][:, :, None] - sources[:, 1][:, None, :]
    distance = jnp.sqrt(gap_rows * gap_rows + gap_cols * gap_cols)
    scaled = root_three * distance / length_scale
    variance = float(sources.shape[2]) ** (-0.5)
    kernel_value = (1.0 + scaled) * jnp.exp(-scaled) * variance
    return jnp.where(allowed[:, None, None], kernel_value, 0.0).astype(jnp.bfloat16)

def children_sum(transfer, coef):
    child_terms = jnp.einsum('xyrs,xyrc->xysc', transfer.astype(jnp.float32), coef.astype(jnp.float32))
    grid_rows, grid_cols = (coef.shape[0], coef.shape[1])
    shaped = child_terms.reshape(grid_rows // 2, 2, grid_cols // 2, 2, transfer.shape[3], coef.shape[3])
    return shaped.sum(axis=(1, 3))

def descend(transfer, parent):
    grid_rows, grid_cols = (parent.shape[0], parent.shape[1])
    shaped = transfer.reshape(grid_rows, 2, grid_cols, 2, transfer.shape[2], transfer.shape[3])
    spread = jnp.einsum('xaybrs,xysc->xaybrc', shaped.astype(jnp.float32), parent.astype(jnp.float32))
    return spread.reshape(2 * grid_rows, 2 * grid_cols, transfer.shape[2], parent.shape[3])

def far_level(coef, lists, couple_table):
    grid_rows, grid_cols = (lists.shape[0], lists.shape[1])
    padded = jnp.pad(coef, ((3, 3), (3, 3), (0, 0), (0, 0)))
    flattened = padded.reshape(-1, coef.shape[2], coef.shape[3])
    source_ids = lists.reshape(grid_rows * grid_cols, lists.shape[2])
    usable = source_ids >= 0
    clipped = jnp.maximum(source_ids, 0)
    source_row = clipped // grid_cols
    source_col = clipped % grid_cols
    cell_ids = jnp.arange(grid_rows * grid_cols, dtype=jnp.int32)
    target_row = (cell_ids // grid_cols)[:, None]
    target_col = (cell_ids % grid_cols)[:, None]
    offset_kind = jnp.clip((source_row - target_row + 3) * 7 + source_col - target_col + 3, 0, 48)
    located = (source_row + 3) * (grid_cols + 6) + source_col + 3

    def one_cell(packed):
        places, kind_here, allowed = packed
        matrices = jnp.where(allowed[:, None, None], couple_table[kind_here], jnp.zeros((), couple_table.dtype))
        return jnp.einsum('jrs,jsc->rc', matrices.astype(jnp.float32), flattened[places].astype(jnp.float32))
    result = lax.map(one_cell, (located, offset_kind, usable))
    return result.reshape(grid_rows, grid_cols, coef.shape[2], coef.shape[3])

def reference(positions, samples, leaf_basis, transfer_one, transfer_two, couplings, near_lists, far_zero, far_one, far_two):
    coef_zero = jnp.einsum('xypr,xypc->xyrc', leaf_basis.astype(jnp.float32), samples.astype(jnp.float32)).astype(jnp.bfloat16)
    coef_one = children_sum(transfer_one, coef_zero).astype(jnp.bfloat16)
    coef_two = children_sum(transfer_two, coef_one).astype(jnp.bfloat16)
    field_zero = far_level(coef_zero, far_zero, coupling_table(couplings[0]))
    field_one = far_level(coef_one, far_one, coupling_table(couplings[1]))
    field_two = far_level(coef_two, far_two, coupling_table(couplings[2]))
    down_two = field_two.astype(jnp.bfloat16)
    down_one = (field_one + descend(transfer_two, down_two)).astype(jnp.bfloat16)
    down_zero = (field_zero + descend(transfer_one, down_one)).astype(jnp.bfloat16)
    site_count = positions.shape[3]
    flat_samples = samples.reshape(-1, samples.shape[2], samples.shape[3])
    flat_positions = positions.reshape(-1, 2, site_count)
    near_ids = near_lists.reshape(-1, near_lists.shape[2])

    def one_leaf(packed):
        target, entries = packed
        allowed = entries >= 0
        clipped = jnp.maximum(entries, 0)
        kernel_tiles = matern_tiles(target[None], flat_positions[clipped], allowed)
        return jnp.einsum('jpq,jqc->pc', kernel_tiles.astype(jnp.float32), flat_samples[clipped].astype(jnp.float32))
    near_field = lax.map(one_leaf, (flat_positions, near_ids)).reshape(samples.shape)
    total_sum = near_field + jnp.einsum('xypr,xyrc->xypc', leaf_basis.astype(jnp.float32), down_zero.astype(jnp.float32))
    return total_sum.astype(jnp.bfloat16)
```

```python
import functools

import jax
import jax.numpy as jnp
import numpy as np
from jax import lax
from jax.experimental import pallas as pl
from jax.experimental.pallas import tpu as pltpu
from jax.sharding import PartitionSpec as P

root_three = 1.7320508075688772
length_scale = 1.0
VMEM = pltpu.VMEM
SMEM = pltpu.SMEM
F32 = jnp.float32
BF16 = jnp.bfloat16
BIG = 60 * 1024 * 1024


def nn(a, b):
    return lax.dot_general(a, b, (((1,), (0,)), ((), ())), preferred_element_type=F32)


def nt(a, b):
    return lax.dot_general(a, b, (((1,), (1,)), ((), ())), preferred_element_type=F32)


def tn(a, b):
    return lax.dot_general(a, b, (((0,), (0,)), ((), ())), preferred_element_type=F32)


def params():
    return pltpu.CompilerParams(vmem_limit_bytes=BIG)


def cost(products, bytes_accessed):
    return pl.CostEstimate(
        flops=products * 2 * 256**3, bytes_accessed=bytes_accessed, transcendentals=0
    )


def half_offsets():
    kept = []
    for u in range(-3, 4):
        for v in range(-3, 4):
            if max(abs(u), abs(v)) >= 2 and (u > 0 or (u == 0 and v > 0)):
                kept.append((u, v))
    return kept


HALF_OFFSETS = half_offsets()


def class_plan(a, b):
    plain, turned = [], []
    for w in range(36):
        u, v = w // 6 - 2 - a, w % 6 - 2 - b
        if max(abs(u), abs(v)) < 2:
            continue
        if (u, v) in HALF_OFFSETS:
            plain.append((w, HALF_OFFSETS.index((u, v))))
        else:
            turned.append((w, HALF_OFFSETS.index((-u, -v))))
    return plain, turned


def coef_kernel(samples, basis, t_one, t_two, top, bottom, left, right, upper, own_one):
    side = samples.shape[0]
    half = side // 2
    coef = {}
    for x in range(side):
        for y in range(side):
            value = tn(samples[x, y], basis[x, y]).astype(BF16)
            coef[x, y] = value
            if x < half:
                top[x * side + y] = value
            else:
                bottom[(x - half) * side + y] = value
            if y < 2:
                left[x * 2 + y] = value
            if y >= side - 2:
                right[x * 2 + y - (side - 2)] = value
    ones = []
    for x in range(half):
        for y in range(half):
            kids = [(2 * x + a, 2 * y + b) for a in range(2) for b in range(2)]
            lhs = jnp.concatenate([coef[k] for k in kids], axis=1)
            rhs = jnp.concatenate([t_one[k] for k in kids], axis=0)
            value = nn(lhs, rhs).astype(BF16)
            ones.append(value)
            upper[x * half + y] = value
    kids = [(a, b) for a in range(2) for b in range(2)]
    lhs = jnp.concatenate(ones, axis=1)
    rhs = jnp.concatenate([t_two[k] for k in kids], axis=0)
    upper[4] = nn(lhs, rhs).astype(BF16)
    own_one[...] = upper[0:4]


def coefficients(samples, basis, t_one, t_two):
    tile = lambda n: jax.ShapeDtypeStruct((n, 256, 256), BF16)
    return pl.pallas_call(
        coef_kernel,
        out_shape=(tile(8), tile(8), tile(8), tile(8), tile(5), tile(4)),
        compiler_params=params(),
        cost_estimate=cost(36, 12 << 20),
        name="coefficients",
    )(samples, basis, t_one, t_two)


def split3(x):
    first = x.astype(BF16).astype(F32)
    rest = x - first
    second = rest.astype(BF16).astype(F32)
    return first, second, rest - second


def near_kernel(
    grid_rows,
    grid_cols,
    corner,
    weight,
    positions,
    own,
    left,
    right,
    top,
    bottom,
    near,
    held,
    target_feat,
    source_feat,
    sems,
):
    side = 4
    copies = []

    def bring(src, dst):
        copy = pltpu.make_async_copy(src, dst, sems.at[len(copies)])
        copy.start()
        copies.append(copy)

    bring(top, held.at[0:6])
    bring(bottom, held.at[30:36])
    for x in range(side):
        base = (x + 1) * 6
        bring(left.at[x], held.at[base])
        bring(own.at[x], held.at[base + 1 : base + 5])
        bring(right.at[x], held.at[base + 5])

    first_row = corner[0]
    first_col = corner[1]
    mid_row = (first_row + 2).astype(F32)
    mid_col = (first_col + 2).astype(F32)
    row_number = lax.broadcasted_iota(jnp.int32, (32, 256), 0)

    def features(place, carry):
        r = jnp.clip(first_row + place // 6 - 1, 0, grid_rows - 1)
        c = jnp.clip(first_col + place % 6 - 1, 0, grid_cols - 1)
        here = positions[r * grid_cols + c]
        x = (here[0:1] - mid_row) * (root_three / length_scale)
        y = (here[1:2] - mid_col) * (root_three / length_scale)
        square = x * x + y * y
        xs, ys, squares = split3(x), split3(y), split3(square)
        one = jnp.ones_like(x)
        pairs = []
        for part in squares:
            pairs.append((part, one))
            pairs.append((one, part))
        for parts in (xs, ys):
            for m, n in ((0, 0), (0, 1), (1, 0), (1, 1), (0, 2), (2, 0)):
                pairs.append((-2.0 * parts[m], parts[n]))
        target = jnp.zeros((32, 256), F32)
        source = jnp.zeros((32, 256), F32)
        for k, (p, q) in enumerate(pairs):
            target = jnp.where(row_number == k, p, target)
            source = jnp.where(row_number == k, q, source)
        target_feat[place] = target.astype(BF16)
        source_feat[place] = source.astype(BF16)
        return carry

    lax.fori_loop(0, 36, features, 0)
    for copy in copies:
        copy.wait()

    def one_target(t, carry):
        r = t // side
        c = t % side
        place = (r + 1) * 6 + c + 1
        target = target_feat[place].astype(F32).T.astype(BF16)
        tiles = []
        blocks = []
        for k in range(9):
            at = (r + k // 3) * 6 + c + k % 3
            scaled_sq = jnp.maximum(nn(target, source_feat[at]), 1e-24)
            a = scaled_sq * lax.rsqrt(scaled_sq)
            w = weight[t, k]
            tiles.append(((a * w + w) * jnp.exp(-a)).astype(BF16))
            blocks.append(held[at])
        near[t] = nn(jnp.concatenate(tiles, axis=1), jnp.concatenate(blocks, axis=0))
        return carry

    lax.fori_loop(0, side * side, one_target, 0)


def near_field(grid_rows, grid_cols, corner, weight, positions, own, left, right, top, bottom):
    any_space = pl.BlockSpec(memory_space=pl.ANY)
    smem = pl.BlockSpec(memory_space=SMEM)
    return pl.pallas_call(
        functools.partial(near_kernel, grid_rows, grid_cols),
        out_shape=jax.ShapeDtypeStruct((16, 256, 256), F32),
        in_specs=[smem, smem, pl.BlockSpec(memory_space=VMEM)] + [any_space] * 5,
        out_specs=pl.BlockSpec(memory_space=VMEM),
        scratch_shapes=[
            VMEM((36, 256, 256), BF16),
            VMEM((36, 32, 256), BF16),
            VMEM((36, 32, 256), BF16),
            pltpu.SemaphoreType.DMA((14,)),
        ],
        compiler_params=params(),
        cost_estimate=cost(400, 12 << 20),
        name="near_field",
    )(corner, weight, positions, own, left, right, top, bottom)


def coupled(plan, couplings, held, places):
    plain, turned = plan
    total = None
    if plain:
        rows = len(places(plain[0][0]))
        lhs = jnp.concatenate(
            [
                jnp.concatenate([held[places(w)[n]] for w, _ in plain], axis=1)
                for n in range(rows)
            ],
            axis=0,
        )
        rhs = jnp.concatenate([couplings[k] for _, k in plain], axis=1)
        total = nt(lhs, rhs)
    if turned:
        rows = len(places(turned[0][0]))
        lhs = jnp.concatenate(
            [
                jnp.concatenate([held[places(w)[n]] for w, _ in turned], axis=1)
                for n in range(rows)
            ],
            axis=0,
        )
        rhs = jnp.concatenate([couplings[k] for _, k in turned], axis=0)
        part = nn(lhs, rhs)
        total = part if total is None else total + part
    return total


def upper_kernel(
    parity, at_one, at_two, couplings, t_two, row, row_e, row_d, cells, cells_e, down, held_one, held_two, field_two, sems
):
    n_one = row.shape[0]
    n_two = cells.shape[0]
    copies = []

    def bring(src, dst):
        copy = pltpu.make_async_copy(src, dst, sems.at[len(copies)])
        copy.start()
        copies.append(copy)

    bring(cells, held_two.at[0:n_two])
    bring(cells_e, held_two.at[n_two : 2 * n_two])
    bring(row, held_one.at[0:n_one])
    bring(row_e, held_one.at[n_one : 2 * n_one])
    bring(row_d, held_one.at[2 * n_one : 3 * n_one])
    held_one[3 * n_one] = jnp.zeros((256, 256), BF16)
    held_two[2 * n_two] = jnp.zeros((256, 256), BF16)
    for copy in copies:
        copy.wait()
    for a in range(2):
        for b in range(2):

            @pl.when((parity[0] == a) & (parity[1] == b))
            def _():
                field_two[...] = coupled(
                    class_plan(a, b), couplings.at[1], held_two, lambda w: [at_two[0, w]]
                ).astype(BF16)

    for a in range(2):
        for b in range(2):
            t = a * 2 + b
            field = coupled(class_plan(a, b), couplings.at[0], held_one, lambda w: [at_one[t, w]])
            down[t] = (field + nt(field_two[...], t_two[a, b])).astype(BF16)


def upper_levels(parity, at_one, at_two, couplings, t_two, row, row_e, row_d, cells, cells_e):
    any_space = pl.BlockSpec(memory_space=pl.ANY)
    smem = pl.BlockSpec(memory_space=SMEM)
    n_one, n_two = row.shape[0], cells.shape[0]
    return pl.pallas_call(
        upper_kernel,
        grid=(1,),
        out_shape=jax.ShapeDtypeStruct((4, 256, 256), BF16),
        in_specs=[
            smem,
            smem,
            smem,
            pl.BlockSpec((pl.Element(2), pl.Element(20), pl.Element(256), pl.Element(256)), lambda g: (1, 0, 0, 0)),
            pl.BlockSpec((2, 2, 256, 256), lambda g: (0, 0, 0, 0)),
        ]
        + [any_space] * 5,
        out_specs=pl.BlockSpec((4, 256, 256), lambda g: (0, 0, 0)),
        scratch_shapes=[
            VMEM((3 * n_one + 1, 256, 256), BF16),
            VMEM((2 * n_two + 1, 256, 256), BF16),
            VMEM((256, 256), BF16),
            pltpu.SemaphoreType.DMA((5,)),
        ],
        compiler_params=params(),
        cost_estimate=cost(140, 14 << 20),
        name="upper_levels",
    )(parity, at_one, at_two, couplings, t_two, row, row_e, row_d, cells, cells_e)


HELD_ZERO = 64


def held_place(r, c):
    rows_in = 2 <= r < 6
    cols_in = 2 <= c < 6
    if rows_in and cols_in:
        return (r - 2) * 4 + c - 2
    if rows_in:
        return (16 if c < 2 else 24) + (r - 2) * 2 + (c if c < 2 else c - 6)
    if cols_in:
        return (32 if r < 2 else 40) + (r if r < 2 else r - 6) * 4 + c - 2
    base = 48 if r < 2 else 56
    return base + (0 if c < 2 else 4) + (r if r < 2 else r - 6) * 2 + (c if c < 2 else c - 6)


def leaf_kernel(
    at, couplings, t_one, basis, down_one, near, *rest
):
    sources = rest[:8]
    out, held, sems = rest[8:]
    step = pl.program_id(0)

    @pl.when(step == 0)
    def _():
        copies = []
        for n, src in enumerate(sources):
            copy = pltpu.make_async_copy(src, held.at[8 * n : 8 * n + 8], sems.at[n])
            copy.start()
            copies.append(copy)
        held[HELD_ZERO] = jnp.zeros((256, 256), BF16)
        for copy in copies:
            copy.wait()

    for a in range(2):
        for b in range(2):

            @pl.when(step == a * 2 + b)
            def _():
                targets = [(x, y) for x in range(2) for y in range(2)]
                numbers = [(2 * x + a) * 4 + 2 * y + b for x, y in targets]
                field = coupled(
                    class_plan(a, b), couplings.at[0], held, lambda w: [at[n, w] for n in numbers]
                )
                for n, (x, y) in enumerate(targets):
                    down = field[n * 256 : n * 256 + 256] + nt(down_one[x * 2 + y], t_one[x, 0, y, 0])
                    down = down.astype(BF16)
                    total = near[x, 0, y, 0] + nt(basis[x, 0, y, 0], down)
                    out[x, 0, y, 0] = total.astype(BF16)


def leaf_level(at, couplings, t_one, basis, down_one, near, sources):
    any_space = pl.BlockSpec(memory_space=pl.ANY)
    smem = pl.BlockSpec(memory_space=SMEM)
    grouped = lambda x: x.reshape(2, 2, 2, 2, 256, 256)
    block = pl.BlockSpec((2, 1, 2, 1, 256, 256), lambda g: (0, g // 2, 0, g % 2, 0, 0))
    return pl.pallas_call(
        leaf_kernel,
        grid=(4,),
        out_shape=jax.ShapeDtypeStruct((2, 2, 2, 2, 256, 256), BF16),
        in_specs=[
            smem,
            pl.BlockSpec((1, 20, 256, 256), lambda g: (0, 0, 0, 0)),
            block,
            block,
            pl.BlockSpec((4, 256, 256), lambda g: (0, 0, 0)),
            block,
        ]
        + [any_space] * 8,
        out_specs=block,
        scratch_shapes=[VMEM((65, 256, 256), BF16), pltpu.SemaphoreType.DMA((8,))],
        compiler_params=params(),
        cost_estimate=cost(464, 24 << 20),
        name="leaf_level",
    )(at, couplings, grouped(t_one), grouped(basis), down_one, grouped(near), *sources)


def listed(lists, ids):
    return jnp.any(lists[:, None, :] == ids[:, :, None], axis=-1)


def window_ids(rows, cols, reach, grid_rows, grid_cols):
    step = np.arange(reach * reach)
    r = rows[:, None] + jnp.asarray(step // reach, jnp.int32)[None]
    c = cols[:, None] + jnp.asarray(step % reach, jnp.int32)[None]
    inside = (r >= 0) & (r < grid_rows) & (c >= 0) & (c < grid_cols)
    return jnp.where(inside, r * grid_cols + c, -2)


def per_device(
    positions,
    samples,
    leaf_basis,
    transfer_one,
    transfer_two,
    couplings,
    near_lists,
    far_zero,
    far_one,
    far_two,
):
    nx = lax.axis_size("qx")
    ny = lax.axis_size("qy")
    i = lax.axis_index("qx")
    j = lax.axis_index("qy")
    a = i % 2
    b = j % 2
    down_x = [(k, k + 1) for k in range(nx - 1)]
    up_x = [(k + 1, k) for k in range(nx - 1)]
    down_y = [(k, k + 1) for k in range(ny - 1)]
    up_y = [(k + 1, k) for k in range(ny - 1)]

    s_left = lax.ppermute(samples[:, 3], "qy", down_y)
    s_right = lax.ppermute(samples[:, 0], "qy", up_y)

    top, bottom, left, right, upper, own_one = coefficients(
        samples, leaf_basis, transfer_one, transfer_two
    )

    pair = lax.ppermute(upper, "qy", [(k, k ^ 1) for k in range(ny)])
    z_left = lax.ppermute(right, "qy", down_y)
    z_right = lax.ppermute(left, "qy", up_y)
    z_above = lax.ppermute(bottom, "qx", down_x)
    z_below = lax.ppermute(top, "qx", up_x)
    s_above = lax.ppermute(
        jnp.concatenate([s_left[3:], samples[3], s_right[3:]]), "qx", down_x
    )
    s_below = lax.ppermute(
        jnp.concatenate([s_left[:1], samples[0], s_right[:1]]), "qx", up_x
    )
    cell_pair = jnp.concatenate([upper[4:], pair[4:]])
    if nx == 4:
        others = [lax.ppermute(cell_pair, "qx", [(k, k ^ 2) for k in range(nx)])]
    else:
        others = [
            lax.ppermute(cell_pair, "qx", [(k, k + 2) for k in range(nx - 2)]),
            lax.ppermute(cell_pair, "qx", [(k + 2, k) for k in range(nx - 2)]),
        ]
    quad = jnp.concatenate([cell_pair] + others)
    outward = [(k, k + 2) for k in range(0, ny - 2, 2)] + [(k + 2, k) for k in range(1, ny - 2, 2)]
    inward = [(k + 2, k) for k in range(0, ny - 2, 2)] + [(k, k + 2) for k in range(1, ny - 2, 2)]
    along = lax.ppermute(jnp.concatenate([pair[:4], quad]), "qy", outward)
    quad_back = lax.ppermute(quad, "qy", inward)
    one_row = jnp.concatenate([own_one, pair[:4], along[:4]])
    two_row = jnp.concatenate([quad, along[4:], quad_back])
    swap_x = [(k, k ^ 1) for k in range(nx)]
    cross_x = [(k, k + 1) for k in range(1, nx - 1, 2)] + [(k + 1, k) for k in range(1, nx - 1, 2)]
    one_e = lax.ppermute(one_row, "qx", swap_x)
    one_d = lax.ppermute(one_row, "qx", cross_x)
    two_e = lax.ppermute(two_row, "qx", swap_x)
    z_corner_above = lax.ppermute(jnp.concatenate([z_left[4:], z_right[4:]]), "qx", down_x)
    z_corner_below = lax.ppermute(jnp.concatenate([z_left[:4], z_right[:4]]), "qx", up_x)

    rows0 = np.arange(16) // 4
    cols0 = np.arange(16) % 4
    base_r = 4 * i + jnp.asarray(rows0, jnp.int32)
    base_c = 4 * j + jnp.asarray(cols0, jnp.int32)
    near_ids = window_ids(base_r - 1, base_c - 1, 3, 4 * nx, 4 * ny)
    weight = jnp.where(listed(near_lists.reshape(16, -1), near_ids), F32(256 ** -0.5), F32(0.0))
    zero_ids = window_ids(base_r // 2 * 2 - 2, base_c // 2 * 2 - 2, 6, 4 * nx, 4 * ny)
    place0 = np.array(
        [
            [held_place(r // 2 * 2 + w // 6, c // 2 * 2 + w % 6) for w in range(36)]
            for r, c in zip(rows0, cols0)
        ],
        np.int32,
    )
    at_zero = jnp.where(listed(far_zero.reshape(16, -1), zero_ids), place0, HELD_ZERO)

    w = np.arange(36)
    wr, wc = w // 6, w % 6
    n_one = 12
    first = jnp.full((4,), 1, jnp.int32)
    one_ids = window_ids(first * (2 * i - 2), first * (2 * j - 2), 6, 2 * nx, 2 * ny)
    row_at = jnp.where(
        wr // 2 == 1, 0, jnp.where((wr // 2 == 2) == (a == 0), n_one, 2 * n_one)
    )
    col_at = jnp.where(wc // 2 == 1, 0, jnp.where((wc // 2 == 2) == (b == 0), 4, 8))
    place1 = row_at + col_at + (wr % 2) * 2 + wc % 2
    at_one = jnp.where(listed(far_one.reshape(4, -1), one_ids), place1[None], 3 * n_one)

    n_quad = quad.shape[0]
    n_two = 3 * n_quad
    two_ids = window_ids(
        first[:1] * (i // 2 * 2 - 2), first[:1] * (j // 2 * 2 - 2), 6, nx, ny
    )
    core_at = jnp.where(wr % 2 == a, 0, n_two)
    z_at = jnp.where(wc // 2 == 1, 0, jnp.where((wc // 2 == 0) == (b == 0), n_quad, 2 * n_quad))
    if nx == 4:
        y_at = np.where(wr // 2 == 1, 0, 2)
    else:
        y_at = np.where(wr // 2 == 1, 0, np.where(wr // 2 == 0, 2, 4))
    x_at = jnp.where(wc % 2 == b, 0, 1)
    place2 = core_at + z_at + y_at + x_at
    at_two = jnp.where(listed(far_two.reshape(1, -1), two_ids), place2[None], 2 * n_two)

    corner = jnp.stack([4 * i, 4 * j]).astype(jnp.int32)
    parity = jnp.stack([a, b]).astype(jnp.int32)
    near = near_field(
        4 * nx,
        4 * ny,
        corner,
        weight,
        positions.reshape(-1, 2, 256),
        samples,
        s_left,
        s_right,
        s_above,
        s_below,
    )
    down_one = upper_levels(
        parity, at_one, at_two, couplings, transfer_two, one_row, one_e, one_d, two_row, two_e
    )
    result = leaf_level(
        at_zero,
        couplings,
        transfer_one,
        leaf_basis,
        down_one,
        near,
        (top, bottom, z_left, z_right, z_above, z_below, z_corner_above, z_corner_below),
    )
    return result.reshape(4, 4, 256, 256)


def solution(mesh):
    return jax.shard_map(
        per_device,
        mesh=mesh,
        in_specs=(
            P(),
            P("qx", "qy", None, None),
            P("qx", "qy", None, None),
            P("qx", "qy", None, None),
            P("qx", "qy", None, None),
            P(),
            P("qx", "qy", None),
            P("qx", "qy", None),
            P("qx", "qy", None),
            P("qx", "qy", None),
        ),
        out_specs=P("qx", "qy", None, None),
        check_vma=False,
    )
```

```python
import functools

import jax
import jax.numpy as jnp
import numpy as np
from jax import lax
from jax.experimental import pallas as pl
from jax.experimental.pallas import tpu as pltpu
from jax.sharding import PartitionSpec as P

root_three = 1.7320508075688772
length_scale = 1.0
VMEM = pltpu.VMEM
SMEM = pltpu.SMEM
F32 = jnp.float32
BF16 = jnp.bfloat16
BIG = 60 * 1024 * 1024


def nn(a, b):
    return lax.dot_general(a, b, (((1,), (0,)), ((), ())), preferred_element_type=F32)


def nt(a, b):
    return lax.dot_general(a, b, (((1,), (1,)), ((), ())), preferred_element_type=F32)


def tn(a, b):
    return lax.dot_general(a, b, (((0,), (0,)), ((), ())), preferred_element_type=F32)


def params():
    return pltpu.CompilerParams(vmem_limit_bytes=BIG)


def cost(products, bytes_accessed):
    return pl.CostEstimate(
        flops=products * 2 * 256**3, bytes_accessed=bytes_accessed, transcendentals=0
    )


def half_offsets():
    kept = []
    for u in range(-3, 4):
        for v in range(-3, 4):
            if max(abs(u), abs(v)) >= 2 and (u > 0 or (u == 0 and v > 0)):
                kept.append((u, v))
    return kept


HALF_OFFSETS = half_offsets()


def class_plan(a, b):
    plain, turned = [], []
    for w in range(36):
        u, v = w // 6 - 2 - a, w % 6 - 2 - b
        if max(abs(u), abs(v)) < 2:
            continue
        if (u, v) in HALF_OFFSETS:
            plain.append((w, HALF_OFFSETS.index((u, v))))
        else:
            turned.append((w, HALF_OFFSETS.index((-u, -v))))
    return plain, turned


LOG2E = 1.4426950408889634


def tiles(n, dtype=BF16):
    return jax.ShapeDtypeStruct((n, 256, 256), dtype)


ANY_SPEC = pl.BlockSpec(memory_space=pl.ANY)
SMEM_SPEC = pl.BlockSpec(memory_space=SMEM)
VMEM_SPEC = pl.BlockSpec(memory_space=VMEM)


class Copies:
    def __init__(self, sems):
        self.sems = sems
        self.started = []

    def start(self, src, dst):
        copy = pltpu.make_async_copy(src, dst, self.sems.at[len(self.started)])
        copy.start()
        self.started.append(copy)
        return copy

    def wait(self):
        for copy in self.started:
            copy.wait()


def coef_kernel(
    samples, basis, t_one, t_two, up, down, left, right, upper,
    sv, bv, t1v, t2v, cv, uv, in_sems, out_sems,
):
    into = Copies(in_sems)
    out = Copies(out_sems)
    rows = []
    for x in range(4):
        rows.append(
            (
                into.start(samples.at[x], sv.at[x]),
                into.start(basis.at[x], bv.at[x]),
                into.start(t_one.at[x], t1v.at[x]),
            )
        )
    last = into.start(t_two, t2v)
    for x in range(4):
        rows[x][0].wait()
        rows[x][1].wait()
        for y in range(4):
            cv[x * 4 + y] = tn(sv[x, y], bv[x, y]).astype(BF16)
        own = cv.at[4 * x : 4 * x + 4]
        out.start(own, (up if x < 2 else down).at[4 * (x % 2) : 4 * (x % 2) + 4])
        out.start(cv.at[4 * x : 4 * x + 2], left.at[2 * x : 2 * x + 2])
        out.start(cv.at[4 * x + 2 : 4 * x + 4], right.at[2 * x : 2 * x + 2])
        out.start(sv.at[x, 0], left.at[8 + x])
        out.start(sv.at[x, 3], right.at[8 + x])
        if x == 0:
            out.start(sv.at[x], up.at[8:12])
        if x == 3:
            out.start(sv.at[x], down.at[8:12])
        if x % 2 == 1:
            rows[x - 1][2].wait()
            rows[x][2].wait()
            for y in range(2):
                kids = [(x - 1 + a, 2 * y + b) for a in range(2) for b in range(2)]
                lhs = jnp.concatenate([cv[k * 4 + m] for k, m in kids], axis=1)
                rhs = jnp.concatenate([t1v[k] for k in kids], axis=0)
                uv[x // 2 * 2 + y] = nn(lhs, rhs).astype(BF16)
    last.wait()
    lhs = jnp.concatenate([uv[k] for k in range(4)], axis=1)
    rhs = jnp.concatenate([t2v[k // 2, k % 2] for k in range(4)], axis=0)
    uv[4] = nn(lhs, rhs).astype(BF16)
    out.start(uv, upper)
    out.wait()


def coefficients(samples, basis, t_one, t_two):
    return pl.pallas_call(
        coef_kernel,
        out_shape=(tiles(12), tiles(12), tiles(12), tiles(12), tiles(5)),
        in_specs=[ANY_SPEC] * 4,
        out_specs=[ANY_SPEC] * 5,
        scratch_shapes=[
            VMEM((4, 4, 256, 256), BF16),
            VMEM((4, 4, 256, 256), BF16),
            VMEM((4, 4, 256, 256), BF16),
            VMEM((2, 2, 256, 256), BF16),
            VMEM((16, 256, 256), BF16),
            VMEM((5, 256, 256), BF16),
            pltpu.SemaphoreType.DMA((13,)),
            pltpu.SemaphoreType.DMA((23,)),
        ],
        compiler_params=params(),
        cost_estimate=cost(170, 12 << 20),
        name="coefficients",
    )(samples, basis, t_one, t_two)


def halo_places():
    numbers = {}
    for r in range(4):
        for c in range(4):
            for k in range(9):
                y, x = r + k // 3 - 1, c + k % 3 - 1
                if not (0 <= y < 4 and 0 <= x < 4):
                    numbers[r * 4 + c, k] = len(numbers)
    return numbers


HALO = halo_places()
N_HALO = len(HALO) // 2


def near_kernel(
    first, grid_rows, grid_cols, lists, positions, own, near, halo_tiles,
    held, plane_x, plane_y, weight, sems,
):
    copy = pltpu.make_async_copy(own, held.at[0:16], sems.at[0])
    copy.start()
    held[16] = jnp.zeros((256, 256), BF16)
    first_row = lax.axis_index("qx") * 4
    first_col = lax.axis_index("qy") * 4
    scale = root_three / length_scale * LOG2E
    weight_full = 256 ** -0.5

    def place_of(row, col):
        r = jnp.clip(row, 0, grid_rows - 1)
        c = jnp.clip(col, 0, grid_cols - 1)
        return r * grid_cols + c

    copy.wait()

    def one_target(t, carry):
        r = t // 4
        c = t % 4
        row = first_row + r
        col = first_col + c
        mid_row = row.astype(F32) + 0.5
        mid_col = col.astype(F32) + 0.5
        for k in range(9):
            weight[k] = 0.0
        for e in range(9):
            entry = lists[r, c, e]
            source_row = jnp.maximum(entry, 0) // grid_cols
            source_col = jnp.maximum(entry, 0) - source_row * grid_cols
            k = (source_row - row + 1) * 3 + source_col - col + 1
            weight[jnp.where(entry >= 0, k, 9)] = weight_full
        here = positions[place_of(row, col)]
        turn_x = jnp.broadcast_to((here[0:1] - mid_row) * scale, (8, 256)).T
        turn_y = jnp.broadcast_to((here[1:2] - mid_col) * scale, (8, 256)).T
        plane_x[...] = jnp.broadcast_to(turn_x[:, 0:1], (256, 128))
        plane_y[...] = jnp.broadcast_to(turn_y[:, 0:1], (256, 128))
        made = []
        blocks = []
        for k in range(9):
            dr, dc = k // 3 - 1, k % 3 - 1
            there = positions[place_of(row + dr, col + dc)]
            x = (there[0:1] - mid_row) * scale
            y = (there[1:2] - mid_col) * scale
            w = weight[k]
            halves = []
            for h in range(2):
                gap_x = plane_x[...] - x[:, 128 * h : 128 * h + 128]
                gap_y = plane_y[...] - y[:, 128 * h : 128 * h + 128]
                square = jnp.maximum(gap_x * gap_x + gap_y * gap_y, 1e-24)
                far = square * lax.rsqrt(square)
                halves.append(((far * (w / LOG2E) + w) * jnp.exp2(-far)).astype(BF16))
            tile = jnp.concatenate(halves, axis=1)
            inside = (r + dr >= 0) & (r + dr < 4) & (c + dc >= 0) & (c + dc < 4)
            halo_tiles[jnp.where(inside, 72, (t - first) * 9 + k)] = tile
            made.append(tile)
            blocks.append(held[jnp.where(inside, (r + dr) * 4 + c + dc, 16)])
        near[t - first] = nn(jnp.concatenate(made, axis=1), jnp.concatenate(blocks, axis=0))
        return carry

    lax.fori_loop(first, first + 8, one_target, 0)


def near_store_kernel(first, grid_rows, grid_cols, lists, positions, own, near, halo_out, *scratch):
    held, plane_x, plane_y, halo, weight, sems, halo_sems = scratch
    near_kernel(
        first, grid_rows, grid_cols, lists, positions, own, near, halo,
        held, plane_x, plane_y, weight, sems,
    )
    out = Copies(halo_sems)
    for (t, k), number in HALO.items():
        if first <= t < first + 8:
            out.start(halo.at[(t - first) * 9 + k], halo_out.at[number % N_HALO])
    out.wait()


def near_own(first, grid_rows, grid_cols, lists, positions, own):
    return pl.pallas_call(
        functools.partial(near_store_kernel, first, grid_rows, grid_cols),
        out_shape=(tiles(8, F32), tiles(N_HALO)),
        in_specs=[SMEM_SPEC, VMEM_SPEC, ANY_SPEC],
        out_specs=[VMEM_SPEC, ANY_SPEC],
        scratch_shapes=[
            VMEM((17, 256, 256), BF16),
            VMEM((256, 128), F32),
            VMEM((256, 128), F32),
            VMEM((73, 256, 256), BF16),
            pltpu.SMEM((10,), F32),
            pltpu.SemaphoreType.DMA((1,)),
            pltpu.SemaphoreType.DMA((N_HALO,)),
        ],
        compiler_params=params(),
        cost_estimate=cost(300, 8 << 20),
        name=f"near_own_{first}",
    )(lists, positions, own)


def mark_listed(entries, flags, n, first_row, first_col, grid_cols):
    for w in range(36):
        flags[n, w] = 0
    for e in range(27):
        entry = entries(e)
        row = jnp.maximum(entry, 0) // grid_cols
        col = jnp.maximum(entry, 0) - row * grid_cols
        w = (row - first_row) * 6 + col - first_col
        flags[n, jnp.where(entry >= 0, jnp.clip(w, 0, 35), 36)] = 1


def dot_group(held, couplings, turned, group):
    rows = len(group[0][1])
    lhs = [
        jnp.concatenate([held[places[n]] for _, places in group], axis=1) for n in range(rows)
    ]
    lhs = jnp.concatenate(lhs, axis=0) if rows > 1 else lhs[0]
    if turned:
        return nn(lhs, jnp.concatenate([couplings[k] for k, _ in group], axis=0))
    return nt(lhs, jnp.concatenate([couplings[k] for k, _ in group], axis=1))


def coupled(plan, couplings, held, places):
    total = None
    for turned in (0, 1):
        group = [(k, [places(w)]) for w, k in plan[turned]]
        part = dot_group(held, couplings, turned, group)
        total = part if total is None else total + part
    return total


def upper_kernel(
    grid_cols, far_one, far_two, couplings, t_two, row, row_e, row_d, cells, cells_e, down,
    held_one, held_two, field_two, flags, sems,
):
    n_one = row.shape[0]
    n_two = cells.shape[0]
    zero_one, zero_two = 3 * n_one, 2 * n_two
    copies = Copies(sems)
    copies.start(cells, held_two.at[0:n_two])
    copies.start(cells_e, held_two.at[n_two : 2 * n_two])
    copies.start(row, held_one.at[0:n_one])
    copies.start(row_e, held_one.at[n_one : 2 * n_one])
    copies.start(row_d, held_one.at[2 * n_one : 3 * n_one])
    held_one[zero_one] = jnp.zeros((256, 256), BF16)
    held_two[zero_two] = jnp.zeros((256, 256), BF16)
    i = lax.axis_index("qx")
    j = lax.axis_index("qy")
    a = i % 2
    b = j % 2
    for t in range(4):
        mark_listed(
            lambda e: far_one[t // 2, t % 2, e], flags, t, 2 * i - 2, 2 * j - 2, 2 * grid_cols
        )
    mark_listed(
        lambda e: far_two[0, 0, e], flags, 4, i // 2 * 2 - 2, j // 2 * 2 - 2, grid_cols
    )
    n_quad = n_two // 3
    core_at = [jnp.where(a == 0, 0, n_two), jnp.where(a == 0, n_two, 0)]
    z_at = [jnp.where(b == 0, n_quad, 2 * n_quad), 0, jnp.where(b == 0, 2 * n_quad, n_quad)]
    y_at = [2, 0, 2] if n_quad == 4 else [2, 0, 4]
    x_at = [b, 1 - b]

    def place_two(w):
        r, c = w // 6, w % 6
        place = core_at[r % 2] + z_at[c // 2] + y_at[r // 2] + x_at[c % 2]
        return jnp.where(flags[4, w] == 1, place, zero_two)

    row_at = [jnp.where(a == 0, 2 * n_one, n_one), 0, jnp.where(a == 0, n_one, 2 * n_one)]
    col_at = [jnp.where(b == 0, 8, 4), 0, jnp.where(b == 0, 4, 8)]

    def place_one(t, w):
        r, c = w // 6, w % 6
        place = row_at[r // 2] + col_at[c // 2] + (r % 2) * 2 + c % 2
        return jnp.where(flags[t, w] == 1, place, zero_one)

    copies.wait()
    for u in range(2):
        for v in range(2):

            @pl.when((a == u) & (b == v))
            def _():
                field_two[...] = coupled(
                    class_plan(u, v), couplings.at[1], held_two, place_two
                ).astype(BF16)

    for u in range(2):
        for v in range(2):
            t = u * 2 + v
            field = coupled(
                class_plan(u, v), couplings.at[0], held_one, functools.partial(place_one, t)
            )
            down[t] = (field + nt(field_two[...], t_two[u, v])).astype(BF16)


def upper_levels(grid_cols, far_one, far_two, couplings, t_two, row, row_e, row_d, cells, cells_e):
    n_one, n_two = row.shape[0], cells.shape[0]
    return pl.pallas_call(
        functools.partial(upper_kernel, grid_cols),
        grid=(1,),
        out_shape=tiles(4),
        in_specs=[
            SMEM_SPEC,
            SMEM_SPEC,
            pl.BlockSpec(
                (pl.Element(2), pl.Element(20), pl.Element(256), pl.Element(256)),
                lambda g: (1, 0, 0, 0),
            ),
            pl.BlockSpec((2, 2, 256, 256), lambda g: (0, 0, 0, 0)),
        ]
        + [ANY_SPEC] * 5,
        out_specs=pl.BlockSpec((4, 256, 256), lambda g: (0, 0, 0)),
        scratch_shapes=[
            VMEM((3 * n_one + 1, 256, 256), BF16),
            VMEM((2 * n_two + 1, 256, 256), BF16),
            VMEM((256, 256), BF16),
            pltpu.SMEM((5, 37), jnp.int32),
            pltpu.SemaphoreType.DMA((5,)),
        ],
        compiler_params=params(),
        cost_estimate=cost(340, 14 << 20),
        name="upper_levels",
    )(far_one, far_two, couplings, t_two, row, row_e, row_d, cells, cells_e)


def source_of(x, y, w):
    r, c = 2 * x + w // 6, 2 * y + w % 6
    rows_in, cols_in = 2 <= r < 6, 2 <= c < 6
    if cols_in:
        return "rows", r * 4 + c - 2
    if rows_in:
        return "sides", (0 if c < 2 else 8) + (r - 2) * 2 + (c if c < 2 else c - 6)
    base = 0 if r < 2 else 8
    return "corners", base + (0 if c < 2 else 4) + (r if r < 2 else r - 6) * 2 + (
        c if c < 2 else c - 6
    )


PARENTS = [(x, y) for x in range(2) for y in range(2)]


def number_of(a, b, parent):
    x, y = parent
    return (2 * x + a) * 4 + 2 * y + b


def level_zero_sums(kind, a, b, flags, couplings, held, zero):
    plan = class_plan(a, b)
    sums = {}
    for turned in (0, 1):
        groups = {}
        for w, k in plan[turned]:
            members = tuple(p for p in PARENTS if source_of(*p, w)[0] == kind)
            if members:
                groups.setdefault(members, []).append((w, k))
        for members, entries in groups.items():
            group = []
            for w, k in entries:
                places = [
                    jnp.where(flags[number_of(a, b, p), w] == 1, source_of(*p, w)[1], zero)
                    for p in members
                ]
                group.append((k, places))
            total = dot_group(held, couplings, turned, group)
            for n, p in enumerate(members):
                part = total[256 * n : 256 * n + 256]
                sums[p] = part if p not in sums else sums[p] + part
    return sums


def grouped(x):
    return x.reshape(2, 2, 2, 2, 256, 256)


CLASS_BLOCK = pl.BlockSpec((2, 1, 2, 1, 256, 256), lambda g: (0, g // 2, 0, g % 2, 0, 0))
COUPLING_BLOCK = pl.BlockSpec((1, 20, 256, 256), lambda g: (0, 0, 0, 0))
GROUPED_F32 = jax.ShapeDtypeStruct((2, 2, 2, 2, 256, 256), F32)


def each_class(step, body):
    for a in range(2):
        for b in range(2):
            pl.when(step == a * 2 + b)(functools.partial(body, a, b))


def rows_kernel(
    grid_cols, far_zero, couplings, up, down, above, below, field, flags, held, sems
):
    step = pl.program_id(0)

    @pl.when(step == 0)
    def _():
        copies = Copies(sems)
        for n, src in enumerate((above, up, down, below)):
            copies.start(src.at[0:8], held.at[8 * n : 8 * n + 8])
        held[32] = jnp.zeros((256, 256), BF16)
        first_row = lax.axis_index("qx") * 4
        first_col = lax.axis_index("qy") * 4

        def mark(t, carry):
            r, c = t // 4, t % 4
            mark_listed(
                lambda e: far_zero[r, c, e],
                flags,
                t,
                first_row + r // 2 * 2 - 2,
                first_col + c // 2 * 2 - 2,
                grid_cols,
            )
            return carry

        lax.fori_loop(0, 16, mark, 0)
        copies.wait()

    def body(a, b):
        sums = level_zero_sums("rows", a, b, flags, couplings.at[0], held, 32)
        for x, y in PARENTS:
            field[x, 0, y, 0] = sums[x, y]

    each_class(step, body)


def rows_level(grid_cols, far_zero, couplings, up, down, above, below):
    return pl.pallas_call(
        functools.partial(rows_kernel, grid_cols),
        grid=(4,),
        out_shape=(GROUPED_F32, jax.ShapeDtypeStruct((16, 37), jnp.int32)),
        in_specs=[SMEM_SPEC, COUPLING_BLOCK] + [ANY_SPEC] * 4,
        out_specs=[CLASS_BLOCK, SMEM_SPEC],
        scratch_shapes=[VMEM((33, 256, 256), BF16), pltpu.SemaphoreType.DMA((4,))],
        compiler_params=params(),
        cost_estimate=cost(420, 11 << 20),
        name="far_rows",
    )(far_zero, couplings, up, down, above, below)


def near_source(r, c):
    rows_in, cols_in = 1 <= r < 5, 1 <= c < 5
    if rows_in and cols_in:
        return "own", None
    if rows_in:
        return "side", (0 if c == 0 else 4) + r - 1
    if cols_in:
        return "side", (8 if r == 0 else 12) + c - 1
    return "corner", (0 if r == 0 else 2) + (0 if c == 0 else 1)


def near_part(kind, t, tile_of, held):
    r, c = t // 4, t % 4
    made, blocks = [], []
    for k in range(9):
        found, place = near_source(r + k // 3, c + k % 3)
        if found == kind:
            made.append(tile_of(HALO[t, k]))
            blocks.append(held[place])
    if not made:
        return None
    return nn(jnp.concatenate(made, axis=1), jnp.concatenate(blocks, axis=0))


SIDE_HALO = [n for (t, k), n in HALO.items() if near_source(t // 4 + k // 3, t % 4 + k % 3)[0] == "side"]
CORNER_HALO = [n for n in range(2 * N_HALO) if n not in SIDE_HALO]


def sides_kernel(
    flags, couplings, field_in, near_a, near_b, halo_a, halo_b, left, right, above, below,
    field, near, held, near_held, halo, sems,
):
    step = pl.program_id(0)

    @pl.when(step == 0)
    def _():
        copies = Copies(sems)
        copies.start(left.at[0:8], held.at[0:8])
        copies.start(right.at[0:8], held.at[8:16])
        for n, src in enumerate((left, right, above, below)):
            copies.start(src.at[8:12], near_held.at[4 * n : 4 * n + 4])
        copies.start(halo_a, halo.at[0:N_HALO])
        copies.start(halo_b, halo.at[N_HALO : 2 * N_HALO])
        held[16] = jnp.zeros((256, 256), BF16)
        copies.wait()

    def body(a, b):
        sums = level_zero_sums("sides", a, b, flags, couplings.at[0], held, 16)
        for x, y in PARENTS:
            field[x, 0, y, 0] = field_in[x, 0, y, 0] + sums[x, y]
            part = near_part("side", number_of(a, b, (x, y)), lambda n: halo[n], near_held)
            here = (near_b if x else near_a)[0, y, 0]
            near[x, 0, y, 0] = here if part is None else here + part

    each_class(step, body)


HALF_BLOCK = pl.BlockSpec((1, 2, 1, 256, 256), lambda g: (g // 2, 0, g % 2, 0, 0))


def sides_level(flags, couplings, field, near_a, near_b, halo_a, halo_b, left, right, above, below):
    half = lambda x: x.reshape(2, 2, 2, 256, 256)
    return pl.pallas_call(
        sides_kernel,
        grid=(4,),
        out_shape=(GROUPED_F32, GROUPED_F32),
        in_specs=[SMEM_SPEC, COUPLING_BLOCK, CLASS_BLOCK, HALF_BLOCK, HALF_BLOCK] + [ANY_SPEC] * 6,
        out_specs=[CLASS_BLOCK, CLASS_BLOCK],
        scratch_shapes=[
            VMEM((17, 256, 256), BF16),
            VMEM((16, 256, 256), BF16),
            VMEM((2 * N_HALO, 256, 256), BF16),
            pltpu.SemaphoreType.DMA((8,)),
        ],
        compiler_params=params(),
        cost_estimate=cost(300, 30 << 20),
        name="far_sides",
    )(
        flags, couplings, field, half(near_a), half(near_b), halo_a, halo_b, left, right, above, below
    )


def last_kernel(
    flags, couplings, t_one, basis, down_one, field, near, halo_a, halo_b, above, below, out,
    held, near_held, halo, sems,
):
    step = pl.program_id(0)

    @pl.when(step == 0)
    def _():
        copies = Copies(sems)
        copies.start(above.at[0:8], held.at[0:8])
        copies.start(below.at[0:8], held.at[8:16])
        copies.start(above.at[8:10], near_held.at[0:2])
        copies.start(below.at[8:10], near_held.at[2:4])
        for m, n in enumerate(CORNER_HALO):
            copies.start((halo_a if n < N_HALO else halo_b).at[n % N_HALO], halo.at[m])
        held[16] = jnp.zeros((256, 256), BF16)
        copies.wait()

    def body(a, b):
        sums = level_zero_sums("corners", a, b, flags, couplings.at[0], held, 16)
        for x, y in PARENTS:
            total = field[x, 0, y, 0] + nt(down_one[x * 2 + y], t_one[x, 0, y, 0])
            if (x, y) in sums:
                total = total + sums[x, y]
            result = near[x, 0, y, 0] + nt(basis[x, 0, y, 0], total.astype(BF16))
            part = near_part(
                "corner",
                number_of(a, b, (x, y)),
                lambda n: halo[CORNER_HALO.index(n)],
                near_held,
            )
            if part is not None:
                result = result + part
            out[x, 0, y, 0] = result.astype(BF16)

    each_class(step, body)


def last_level(
    flags, couplings, t_one, basis, down_one, field, near, halo_a, halo_b, above, below
):
    return pl.pallas_call(
        last_kernel,
        grid=(4,),
        out_shape=jax.ShapeDtypeStruct((2, 2, 2, 2, 256, 256), BF16),
        in_specs=[
            SMEM_SPEC,
            COUPLING_BLOCK,
            CLASS_BLOCK,
            CLASS_BLOCK,
            pl.BlockSpec((4, 256, 256), lambda g: (0, 0, 0)),
            CLASS_BLOCK,
            CLASS_BLOCK,
        ]
        + [ANY_SPEC] * 4,
        out_specs=CLASS_BLOCK,
        scratch_shapes=[
            VMEM((17, 256, 256), BF16),
            VMEM((4, 256, 256), BF16),
            VMEM((len(CORNER_HALO), 256, 256), BF16),
            pltpu.SemaphoreType.DMA((4 + len(CORNER_HALO),)),
        ],
        compiler_params=params(),
        cost_estimate=cost(270, 20 << 20),
        name="last_level",
    )(
        flags, couplings, grouped(t_one), grouped(basis), down_one, field, near, halo_a, halo_b,
        above, below,
    )


def per_device(
    positions,
    samples,
    leaf_basis,
    transfer_one,
    transfer_two,
    couplings,
    near_lists,
    far_zero,
    far_one,
    far_two,
):
    nx = lax.axis_size("qx")
    ny = lax.axis_size("qy")
    down_x = [(k, k + 1) for k in range(nx - 1)]
    up_x = [(k + 1, k) for k in range(nx - 1)]
    down_y = [(k, k + 1) for k in range(ny - 1)]
    up_y = [(k + 1, k) for k in range(ny - 1)]

    up, down, left, right, upper = coefficients(samples, leaf_basis, transfer_one, transfer_two)

    pair = lax.ppermute(upper, "qy", [(k, k ^ 1) for k in range(ny)])
    above = lax.ppermute(down, "qx", down_x)
    below = lax.ppermute(up, "qx", up_x)
    sites = positions.reshape(-1, 2, 256)
    flat_samples = samples.reshape(16, 256, 256)
    near_a, halo_a = near_own(0, 4 * nx, 4 * ny, near_lists, sites, flat_samples)
    pair, above, below, left, right, near_a = lax.optimization_barrier(
        (pair, above, below, left, right, near_a)
    )
    cell_pair = jnp.concatenate([upper[4:], pair[4:]])
    if nx == 4:
        others = [lax.ppermute(cell_pair, "qx", [(k, k ^ 2) for k in range(nx)])]
    else:
        others = [
            lax.ppermute(cell_pair, "qx", [(k, k + 2) for k in range(nx - 2)]),
            lax.ppermute(cell_pair, "qx", [(k + 2, k) for k in range(nx - 2)]),
        ]
    on_left = lax.ppermute(right, "qy", down_y)
    on_right = lax.ppermute(left, "qy", up_y)
    quad = jnp.concatenate([cell_pair] + others)
    quad, above, below, near_lists = lax.optimization_barrier((quad, above, below, near_lists))
    outward = [(k, k + 2) for k in range(0, ny - 2, 2)] + [(k + 2, k) for k in range(1, ny - 2, 2)]
    inward = [(k + 2, k) for k in range(0, ny - 2, 2)] + [(k, k + 2) for k in range(1, ny - 2, 2)]
    along = lax.ppermute(jnp.concatenate([pair[:4], quad]), "qy", outward)
    quad_back = lax.ppermute(quad, "qy", inward)
    near_b, halo_b = near_own(8, 4 * nx, 4 * ny, near_lists, sites, flat_samples)
    field, flags = rows_level(4 * ny, far_zero, couplings, up, down, above, below)
    one_row = jnp.concatenate([upper[:4], pair[:4], along[:4]])
    two_row = jnp.concatenate([quad, along[4:], quad_back])
    swap_x = [(k, k ^ 1) for k in range(nx)]
    cross_x = [(k, k + 1) for k in range(1, nx - 1, 2)] + [(k + 1, k) for k in range(1, nx - 1, 2)]
    one_d = lax.ppermute(one_row, "qx", cross_x)
    one_e = lax.ppermute(one_row, "qx", swap_x)
    two_e = lax.ppermute(two_row, "qx", swap_x)

    corner_down = jnp.concatenate([on_left[4:8], on_right[4:8], on_left[11:], on_right[11:]])
    corner_up = jnp.concatenate([on_left[:4], on_right[:4], on_left[8:9], on_right[8:9]])
    corner_above = lax.ppermute(corner_down, "qx", down_x)
    corner_below = lax.ppermute(corner_up, "qx", up_x)
    down_one = upper_levels(
        ny, far_one, far_two, couplings, transfer_two, one_row, one_e, one_d, two_row, two_e
    )
    field, down_one = lax.optimization_barrier((field, down_one))
    field, near = sides_level(
        flags, couplings, field, near_a, near_b, halo_a, halo_b, on_left, on_right, above, below
    )
    result = last_level(
        flags,
        couplings,
        transfer_one,
        leaf_basis,
        down_one,
        field,
        near,
        halo_a,
        halo_b,
        corner_above,
        corner_below,
    )
    return result.reshape(4, 4, 256, 256)


def solution(mesh):
    return jax.shard_map(
        per_device,
        mesh=mesh,
        in_specs=(
            P(),
            P("qx", "qy", None, None),
            P("qx", "qy", None, None),
            P("qx", "qy", None, None),
            P("qx", "qy", None, None),
            P(),
            P("qx", "qy", None),
            P("qx", "qy", None),
            P("qx", "qy", None),
            P("qx", "qy", None),
        ),
        out_specs=P("qx", "qy", None, None),
        check_vma=False,
    )
```

```python
import functools

import jax
import jax.numpy as jnp
import numpy as np
from jax import lax
from jax.experimental import pallas as pl
from jax.experimental.pallas import tpu as pltpu
from jax.sharding import PartitionSpec as P

root_three = 1.7320508075688772
length_scale = 1.0
VMEM = pltpu.VMEM
SMEM = pltpu.SMEM
F32 = jnp.float32
BF16 = jnp.bfloat16
BIG = 60 * 1024 * 1024


def nn(a, b):
    return lax.dot_general(a, b, (((1,), (0,)), ((), ())), preferred_element_type=F32)


def nt(a, b):
    return lax.dot_general(a, b, (((1,), (1,)), ((), ())), preferred_element_type=F32)


def tn(a, b):
    return lax.dot_general(a, b, (((0,), (0,)), ((), ())), preferred_element_type=F32)


def params():
    return pltpu.CompilerParams(vmem_limit_bytes=BIG)


def cost(products, bytes_accessed):
    return pl.CostEstimate(
        flops=products * 2 * 256**3 // 8, bytes_accessed=bytes_accessed // 8, transcendentals=0
    )


def half_offsets():
    kept = []
    for u in range(-3, 4):
        for v in range(-3, 4):
            if max(abs(u), abs(v)) >= 2 and (u > 0 or (u == 0 and v > 0)):
                kept.append((u, v))
    return kept


HALF_OFFSETS = half_offsets()


def class_plan(a, b):
    plain, turned = [], []
    for w in range(36):
        u, v = w // 6 - 2 - a, w % 6 - 2 - b
        if max(abs(u), abs(v)) < 2:
            continue
        if (u, v) in HALF_OFFSETS:
            plain.append((w, HALF_OFFSETS.index((u, v))))
        else:
            turned.append((w, HALF_OFFSETS.index((-u, -v))))
    return plain, turned


LOG2E = 1.4426950408889634
TILE_SCALE = 256 ** -0.5


def tiles(n, dtype=BF16):
    return jax.ShapeDtypeStruct((n, 256, 256), dtype)


ANY_SPEC = pl.BlockSpec(memory_space=pl.ANY)
SMEM_SPEC = pl.BlockSpec(memory_space=SMEM)
VMEM_SPEC = pl.BlockSpec(memory_space=VMEM)


class Copies:
    def __init__(self, sems):
        self.sems = sems
        self.started = []

    def start(self, src, dst):
        copy = pltpu.make_async_copy(src, dst, self.sems.at[len(self.started)])
        copy.start()
        self.started.append(copy)
        return copy

    def wait(self):
        for copy in self.started:
            copy.wait()


def coef_kernel(
    samples, basis, t_one, t_two, up, down, left, right, upper,
    sv, bv, t1v, t2v, cv, uv, in_sems, out_sems,
):
    into = Copies(in_sems)
    out = Copies(out_sems)
    rows = []
    for x in range(4):
        rows.append(
            (
                into.start(samples.at[x], sv.at[x]),
                into.start(basis.at[x], bv.at[x]),
                into.start(t_one.at[x], t1v.at[x]),
            )
        )
    last = into.start(t_two, t2v)
    for x in range(4):
        rows[x][0].wait()
        rows[x][1].wait()
        for y in range(4):
            cv[x * 4 + y] = tn(sv[x, y], bv[x, y]).astype(BF16)
        own = cv.at[4 * x : 4 * x + 4]
        out.start(own, (up if x < 2 else down).at[4 * (x % 2) : 4 * (x % 2) + 4])
        out.start(cv.at[4 * x : 4 * x + 2], left.at[2 * x : 2 * x + 2])
        out.start(cv.at[4 * x + 2 : 4 * x + 4], right.at[2 * x : 2 * x + 2])
        out.start(sv.at[x, 0], left.at[8 + x])
        out.start(sv.at[x, 3], right.at[8 + x])
        if x == 0:
            out.start(sv.at[x], up.at[8:12])
        if x == 3:
            out.start(sv.at[x], down.at[8:12])
        if x % 2 == 1:
            rows[x - 1][2].wait()
            rows[x][2].wait()
            for y in range(2):
                kids = [(x - 1 + a, 2 * y + b) for a in range(2) for b in range(2)]
                lhs = jnp.concatenate([cv[k * 4 + m] for k, m in kids], axis=1)
                rhs = jnp.concatenate([t1v[k] for k in kids], axis=0)
                uv[x // 2 * 2 + y] = nn(lhs, rhs).astype(BF16)
    last.wait()
    lhs = jnp.concatenate([uv[k] for k in range(4)], axis=1)
    rhs = jnp.concatenate([t2v[k // 2, k % 2] for k in range(4)], axis=0)
    uv[4] = nn(lhs, rhs).astype(BF16)
    out.start(uv, upper)
    out.wait()


def coefficients(samples, basis, t_one, t_two):
    return pl.pallas_call(
        coef_kernel,
        out_shape=(tiles(12), tiles(12), tiles(12), tiles(12), tiles(5)),
        in_specs=[ANY_SPEC] * 4,
        out_specs=[ANY_SPEC] * 5,
        scratch_shapes=[
            VMEM((4, 4, 256, 256), BF16),
            VMEM((4, 4, 256, 256), BF16),
            VMEM((4, 4, 256, 256), BF16),
            VMEM((2, 2, 256, 256), BF16),
            VMEM((16, 256, 256), BF16),
            VMEM((5, 256, 256), BF16),
            pltpu.SemaphoreType.DMA((13,)),
            pltpu.SemaphoreType.DMA((23,)),
        ],
        compiler_params=params(),
        cost_estimate=cost(170, 12 << 20),
        name="coefficients",
    )(samples, basis, t_one, t_two)


def assembled(name, sources, plans):
    sizes = [sum(n for _, _, n in plan) for plan in plans]
    count = sum(len(plan) for plan in plans)

    def kernel(*refs):
        ins, outs, sems = refs[: len(sources)], refs[len(sources) : -1], refs[-1]
        copies = Copies(sems)
        for plan, out in zip(plans, outs):
            at = 0
            for source, first, n in plan:
                copies.start(ins[source].at[first : first + n], out.at[at : at + n])
                at += n
        copies.wait()

    return pl.pallas_call(
        kernel,
        out_shape=[tiles(n) for n in sizes],
        in_specs=[ANY_SPEC] * len(sources),
        out_specs=[ANY_SPEC] * len(plans),
        scratch_shapes=[pltpu.SemaphoreType.DMA((count,))],
        cost_estimate=cost(35, 0),
        name=name,
    )(*sources)


def halo_places():
    numbers = {}
    for r in range(4):
        for c in range(4):
            for k in range(9):
                y, x = r + k // 3 - 1, c + k % 3 - 1
                if not (0 <= y < 4 and 0 <= x < 4):
                    numbers[r * 4 + c, k] = len(numbers)
    return numbers


HALO = halo_places()
N_HALO = len(HALO) // 2


def split3(x):
    first = x.astype(BF16).astype(F32)
    rest = x - first
    second = rest.astype(BF16).astype(F32)
    return first, second, rest - second


def site_features(x, y):
    n = lax.broadcasted_iota(jnp.int32, (8, 256), 0)
    square = x * x + y * y
    target, source = [], []
    for parts in (split3(x), split3(y)):
        first, second, third = parts
        target.append(jnp.where(n < 3, first, jnp.where(n < 5, second, jnp.where(n < 6, third, 0.0))))
        other = jnp.where(
            (n == 0) | (n == 3) | (n == 5),
            first,
            jnp.where((n == 1) | (n == 4), second, jnp.where(n == 2, third, 0.0)),
        )
        source.append(-2.0 * other)
    first, second, third = split3(square)
    low = jnp.where(n == 0, first, jnp.where(n == 1, second, third))
    high = jnp.where(n == 3, first, jnp.where(n == 4, second, third))
    one = jnp.where(n < 6, 1.0, 0.0)
    target.append(jnp.where(n < 3, low, one))
    source.append(jnp.where(n < 3, 1.0, jnp.where(n < 6, high, 0.0)))
    zero = jnp.zeros((8, 256), F32)
    return jnp.concatenate(target + [zero], axis=0), jnp.concatenate(source + [zero], axis=0)


def near_kernel(
    first, grid_rows, grid_cols, lists, positions, own, near, halo_out,
    held, target_feat, source_feat, halo, floors, sems, halo_sems,
):
    copy = pltpu.make_async_copy(own, held.at[0:16], sems.at[0])
    copy.start()
    held[16] = jnp.zeros((256, 256), BF16)
    first_row = lax.axis_index("qx") * 4
    first_col = lax.axis_index("qy") * 4
    scale = root_three / length_scale
    mid_row = first_row.astype(F32) + 2.0
    mid_col = first_col.astype(F32) + 2.0
    first_place = first // 4 * 6

    def features(n, carry):
        r = jnp.clip(first_row + (first_place + n) // 6 - 1, 0, grid_rows - 1)
        c = jnp.clip(first_col + n % 6 - 1, 0, grid_cols - 1)
        here = positions[r * grid_cols + c]
        target, source = site_features(
            (here[0:1] - mid_row) * scale, (here[1:2] - mid_col) * scale
        )
        target_feat[n] = target
        source_feat[n] = source.astype(BF16)
        return carry

    lax.fori_loop(0, 24, features, 0)
    copy.wait()

    def one_target(m, carry):
        t = first + m
        r = t // 4
        c = t % 4
        row = first_row + r
        col = first_col + c
        for k in range(9):
            floors[k] = 1e6
        for e in range(9):
            entry = lists[r, c, e]
            source_row = jnp.maximum(entry, 0) // grid_cols
            source_col = jnp.maximum(entry, 0) - source_row * grid_cols
            k = (source_row - row + 1) * 3 + source_col - col + 1
            floors[jnp.where(entry >= 0, k, 9)] = 1e-24
        place = (m // 4 + 1) * 6 + c + 1
        target = target_feat[place].T.astype(BF16)
        made = []
        blocks = []
        for k in range(9):
            dr, dc = k // 3 - 1, k % 3 - 1
            square = nn(target, source_feat[place + dr * 6 + dc])
            square = jnp.maximum(square, floors[k])
            far = square * lax.rsqrt(square)
            tile = ((far + 1.0) * jnp.exp2(far * -LOG2E)).astype(BF16)
            inside = (r + dr >= 0) & (r + dr < 4) & (c + dc >= 0) & (c + dc < 4)
            halo[jnp.where(inside, 72, m * 9 + k)] = tile
            made.append(tile)
            blocks.append(held[jnp.where(inside, (r + dr) * 4 + c + dc, 16)])
        near[m] = nn(jnp.concatenate(made, axis=1), jnp.concatenate(blocks, axis=0))
        return carry

    lax.fori_loop(0, 8, one_target, 0)
    out = Copies(halo_sems)
    for (t, k), number in HALO.items():
        if first <= t < first + 8:
            out.start(halo.at[(t - first) * 9 + k], halo_out.at[number % N_HALO])
    out.wait()


def near_own(first, grid_rows, grid_cols, lists, positions, own):
    return pl.pallas_call(
        functools.partial(near_kernel, first, grid_rows, grid_cols),
        out_shape=(tiles(8, F32), tiles(N_HALO)),
        in_specs=[SMEM_SPEC, VMEM_SPEC, ANY_SPEC],
        out_specs=[VMEM_SPEC, ANY_SPEC],
        scratch_shapes=[
            VMEM((17, 256, 256), BF16),
            VMEM((24, 32, 256), F32),
            VMEM((24, 32, 256), BF16),
            VMEM((73, 256, 256), BF16),
            pltpu.SMEM((10,), F32),
            pltpu.SemaphoreType.DMA((1,)),
            pltpu.SemaphoreType.DMA((N_HALO,)),
        ],
        compiler_params=params(),
        cost_estimate=cost(300, 8 << 20),
        name=f"near_own_{first}",
    )(lists, positions, own)


def mark_listed(entries, flags, n, first_row, first_col, grid_cols):
    for w in range(36):
        flags[n, w] = 0
    for e in range(27):
        entry = entries(e)
        row = jnp.maximum(entry, 0) // grid_cols
        col = jnp.maximum(entry, 0) - row * grid_cols
        w = (row - first_row) * 6 + col - first_col
        flags[n, jnp.where(entry >= 0, jnp.clip(w, 0, 35), 36)] = 1


def dot_group(held, couplings, turned, group):
    rows = len(group[0][1])
    lhs = [
        jnp.concatenate([held[places[n]] for _, places in group], axis=1) for n in range(rows)
    ]
    lhs = jnp.concatenate(lhs, axis=0) if rows > 1 else lhs[0]
    if turned:
        return nn(lhs, jnp.concatenate([couplings[k] for k, _ in group], axis=0))
    return nt(lhs, jnp.concatenate([couplings[k] for k, _ in group], axis=1))


def coupled(plan, couplings, held, places):
    total = None
    for turned in (0, 1):
        group = [(k, [places(w)]) for w, k in plan[turned]]
        part = dot_group(held, couplings, turned, group)
        total = part if total is None else total + part
    return total


def upper_kernel(grid_cols, n_others, far_one, far_two, couplings, t_two, *rest):
    row, row_e, row_d = rest[:3]
    others = rest[3 : 3 + 2 * n_others]
    down, held_one, held_two, field_two, flags, sems = rest[3 + 2 * n_others :]
    zero_one, zero_two = 36, 12 + 12 * n_others
    copies = Copies(sems)
    copies.start(row.at[12:18], held_two.at[0:6])
    copies.start(row_e.at[12:18], held_two.at[6:12])
    for n, other in enumerate(others):
        copies.start(other, held_two.at[12 + 6 * n : 18 + 6 * n])
    copies.start(row.at[0:12], held_one.at[0:12])
    copies.start(row_e.at[0:12], held_one.at[12:24])
    copies.start(row_d, held_one.at[24:36])
    held_one[zero_one] = jnp.zeros((256, 256), BF16)
    held_two[zero_two] = jnp.zeros((256, 256), BF16)
    i = lax.axis_index("qx")
    j = lax.axis_index("qy")
    a = i % 2
    b = j % 2
    for t in range(4):
        mark_listed(
            lambda e: far_one[t // 2, t % 2, e], flags, t, 2 * i - 2, 2 * j - 2, 2 * grid_cols
        )
    mark_listed(
        lambda e: far_two[0, 0, e], flags, 4, i // 2 * 2 - 2, j // 2 * 2 - 2, grid_cols
    )
    rows_at = []
    for r in range(6):
        if r // 2 == 1:
            rows_at.append(jnp.where(a == r % 2, 0, 6))
        else:
            n = 0 if r // 2 == 0 or n_others == 1 else 1
            rows_at.append(
                jnp.where(a == r % 2, 12 + 6 * n, 12 + 6 * (n_others + n))
            )
    z_at = [jnp.where(b == 0, 2, 4), 0, jnp.where(b == 0, 4, 2)]
    x_at = [b, 1 - b]

    def place_two(w):
        r, c = w // 6, w % 6
        place = rows_at[r] + z_at[c // 2] + x_at[c % 2]
        return jnp.where(flags[4, w] == 1, place, zero_two)

    row_at = [jnp.where(a == 0, 24, 12), 0, jnp.where(a == 0, 12, 24)]
    col_at = [jnp.where(b == 0, 8, 4), 0, jnp.where(b == 0, 4, 8)]

    def place_one(t, w):
        r, c = w // 6, w % 6
        place = row_at[r // 2] + col_at[c // 2] + (r % 2) * 2 + c % 2
        return jnp.where(flags[t, w] == 1, place, zero_one)

    for copy in copies.started[: 2 + 2 * n_others]:
        copy.wait()
    for u in range(2):
        for v in range(2):

            @pl.when((a == u) & (b == v))
            def _():
                field_two[...] = coupled(
                    class_plan(u, v), couplings.at[1], held_two, place_two
                ).astype(BF16)

    for copy in copies.started[2 + 2 * n_others :]:
        copy.wait()
    for u in range(2):
        for v in range(2):
            t = u * 2 + v
            field = coupled(
                class_plan(u, v), couplings.at[0], held_one, functools.partial(place_one, t)
            )
            down[t] = (field + nt(field_two[...], t_two[u, v])).astype(BF16)


def upper_levels(grid_cols, far_one, far_two, couplings, t_two, row, row_e, row_d, others):
    n_others = len(others) // 2
    return pl.pallas_call(
        functools.partial(upper_kernel, grid_cols, n_others),
        grid=(1,),
        out_shape=tiles(4),
        in_specs=[
            SMEM_SPEC,
            SMEM_SPEC,
            pl.BlockSpec(
                (pl.Element(2), pl.Element(20), pl.Element(256), pl.Element(256)),
                lambda g: (1, 0, 0, 0),
            ),
            pl.BlockSpec((2, 2, 256, 256), lambda g: (0, 0, 0, 0)),
        ]
        + [ANY_SPEC] * (3 + 2 * n_others),
        out_specs=pl.BlockSpec((4, 256, 256), lambda g: (0, 0, 0)),
        scratch_shapes=[
            VMEM((37, 256, 256), BF16),
            VMEM((13 + 12 * n_others, 256, 256), BF16),
            VMEM((256, 256), BF16),
            pltpu.SMEM((5, 37), jnp.int32),
            pltpu.SemaphoreType.DMA((5 + 2 * n_others,)),
        ],
        compiler_params=params(),
        cost_estimate=cost(340, 14 << 20),
        name="upper_levels",
    )(far_one, far_two, couplings, t_two, row, row_e, row_d, *others)


def source_of(x, y, w):
    r, c = 2 * x + w // 6, 2 * y + w % 6
    rows_in, cols_in = 2 <= r < 6, 2 <= c < 6
    if cols_in:
        return "rows", r * 4 + c - 2
    if rows_in:
        return "sides", (0 if c < 2 else 8) + (r - 2) * 2 + (c if c < 2 else c - 6)
    base = 0 if r < 2 else 8
    return "corners", base + (0 if c < 2 else 4) + (r if r < 2 else r - 6) * 2 + (
        c if c < 2 else c - 6
    )


PARENTS = [(x, y) for x in range(2) for y in range(2)]


def number_of(a, b, parent):
    x, y = parent
    return (2 * x + a) * 4 + 2 * y + b


def level_zero_sums(kind, a, b, flags, couplings, held, zero):
    plan = class_plan(a, b)
    sums = {}
    for turned in (0, 1):
        groups = {}
        for w, k in plan[turned]:
            members = tuple(p for p in PARENTS if source_of(*p, w)[0] == kind)
            if members:
                groups.setdefault(members, []).append((w, k))
        for members, entries in groups.items():
            group = []
            for w, k in entries:
                places = [
                    jnp.where(flags[number_of(a, b, p), w] == 1, source_of(*p, w)[1], zero)
                    for p in members
                ]
                group.append((k, places))
            total = dot_group(held, couplings, turned, group)
            for n, p in enumerate(members):
                part = total[256 * n : 256 * n + 256]
                sums[p] = part if p not in sums else sums[p] + part
    return sums


def grouped(x):
    return x.reshape(2, 2, 2, 2, 256, 256)


CLASS_BLOCK = pl.BlockSpec((2, 1, 2, 1, 256, 256), lambda g: (0, g // 2, 0, g % 2, 0, 0))
COUPLING_BLOCK = pl.BlockSpec((1, 20, 256, 256), lambda g: (0, 0, 0, 0))
GROUPED_F32 = jax.ShapeDtypeStruct((2, 2, 2, 2, 256, 256), F32)


def each_class(step, body):
    for a in range(2):
        for b in range(2):
            pl.when(step == a * 2 + b)(functools.partial(body, a, b))


def rows_kernel(
    grid_cols, far_zero, couplings, up, down, above, below, field, flags, held, sems
):
    step = pl.program_id(0)

    @pl.when(step == 0)
    def _():
        copies = Copies(sems)
        for n, src in enumerate((above, up, down, below)):
            copies.start(src.at[0:8], held.at[8 * n : 8 * n + 8])
        held[32] = jnp.zeros((256, 256), BF16)
        first_row = lax.axis_index("qx") * 4
        first_col = lax.axis_index("qy") * 4

        def mark(t, carry):
            r, c = t // 4, t % 4
            mark_listed(
                lambda e: far_zero[r, c, e],
                flags,
                t,
                first_row + r // 2 * 2 - 2,
                first_col + c // 2 * 2 - 2,
                grid_cols,
            )
            return carry

        lax.fori_loop(0, 16, mark, 0)
        copies.wait()

    def body(a, b):
        sums = level_zero_sums("rows", a, b, flags, couplings.at[0], held, 32)
        for x, y in PARENTS:
            field[x, 0, y, 0] = sums[x, y]

    each_class(step, body)


def rows_level(grid_cols, far_zero, couplings, up, down, above, below):
    return pl.pallas_call(
        functools.partial(rows_kernel, grid_cols),
        grid=(4,),
        out_shape=(GROUPED_F32, jax.ShapeDtypeStruct((16, 37), jnp.int32)),
        in_specs=[SMEM_SPEC, COUPLING_BLOCK] + [ANY_SPEC] * 4,
        out_specs=[CLASS_BLOCK, SMEM_SPEC],
        scratch_shapes=[VMEM((33, 256, 256), BF16), pltpu.SemaphoreType.DMA((4,))],
        compiler_params=params(),
        cost_estimate=cost(420, 11 << 20),
        name="far_rows",
    )(far_zero, couplings, up, down, above, below)


def near_source(r, c):
    rows_in, cols_in = 1 <= r < 5, 1 <= c < 5
    if rows_in and cols_in:
        return "own", None
    if rows_in:
        return "side", (0 if c == 0 else 4) + r - 1
    if cols_in:
        return "side", (8 if r == 0 else 12) + c - 1
    return "corner", (0 if r == 0 else 2) + (0 if c == 0 else 1)


def near_part(kind, t, tile_of, held):
    r, c = t // 4, t % 4
    made, blocks = [], []
    for k in range(9):
        found, place = near_source(r + k // 3, c + k % 3)
        if found == kind:
            made.append(tile_of(HALO[t, k]))
            blocks.append(held[place])
    if not made:
        return None
    return nn(jnp.concatenate(made, axis=1), jnp.concatenate(blocks, axis=0))


SIDE_HALO = [n for (t, k), n in HALO.items() if near_source(t // 4 + k // 3, t % 4 + k % 3)[0] == "side"]
CORNER_HALO = [n for n in range(2 * N_HALO) if n not in SIDE_HALO]


def sides_kernel(
    flags, couplings, field_in, near_a, near_b, halo_a, halo_b, left, right, above, below,
    field, near, held, near_held, halo, sems,
):
    step = pl.program_id(0)

    def copies():
        pairs = [(left.at[0:8], held.at[0:8]), (right.at[0:8], held.at[8:16])]
        for n, src in enumerate((left, right, above, below)):
            pairs.append((src.at[8:12], near_held.at[4 * n : 4 * n + 4]))
        pairs.append((halo_a, halo.at[0:N_HALO]))
        pairs.append((halo_b, halo.at[N_HALO : 2 * N_HALO]))
        return [pltpu.make_async_copy(src, dst, sems.at[n]) for n, (src, dst) in enumerate(pairs)]

    @pl.when(step == 0)
    def _():
        started = copies()
        for copy in started:
            copy.start()
        held[16] = jnp.zeros((256, 256), BF16)
        for copy in started[:2]:
            copy.wait()

    def body(a, b):
        sums = level_zero_sums("sides", a, b, flags, couplings.at[0], held, 16)
        for x, y in PARENTS:
            field[x, 0, y, 0] = field_in[x, 0, y, 0] + sums[x, y]
        if a == 0 and b == 0:
            for copy in copies()[2:]:
                copy.wait()
        for x, y in PARENTS:
            part = near_part("side", number_of(a, b, (x, y)), lambda n: halo[n], near_held)
            here = (near_b if x else near_a)[0, y, 0]
            near[x, 0, y, 0] = here if part is None else here + part

    each_class(step, body)


HALF_BLOCK = pl.BlockSpec((1, 2, 1, 256, 256), lambda g: (g // 2, 0, g % 2, 0, 0))


def sides_level(flags, couplings, field, near_a, near_b, halo_a, halo_b, left, right, above, below):
    half = lambda x: x.reshape(2, 2, 2, 256, 256)
    return pl.pallas_call(
        sides_kernel,
        grid=(4,),
        out_shape=(GROUPED_F32, GROUPED_F32),
        in_specs=[SMEM_SPEC, COUPLING_BLOCK, CLASS_BLOCK, HALF_BLOCK, HALF_BLOCK] + [ANY_SPEC] * 6,
        out_specs=[CLASS_BLOCK, CLASS_BLOCK],
        scratch_shapes=[
            VMEM((17, 256, 256), BF16),
            VMEM((16, 256, 256), BF16),
            VMEM((2 * N_HALO, 256, 256), BF16),
            pltpu.SemaphoreType.DMA((8,)),
        ],
        compiler_params=params(),
        cost_estimate=cost(300, 30 << 20),
        name="far_sides",
    )(
        flags, couplings, field, half(near_a), half(near_b), halo_a, halo_b, left, right, above, below
    )


def last_kernel(
    flags, couplings, t_one, basis, down_one, field, near, halo_a, halo_b, above, below, out,
    held, near_held, halo, sems,
):
    step = pl.program_id(0)

    @pl.when(step == 0)
    def _():
        copies = Copies(sems)
        copies.start(above.at[0:8], held.at[0:8])
        copies.start(below.at[0:8], held.at[8:16])
        copies.start(above.at[8:10], near_held.at[0:2])
        copies.start(below.at[8:10], near_held.at[2:4])
        for m, n in enumerate(CORNER_HALO):
            copies.start((halo_a if n < N_HALO else halo_b).at[n % N_HALO], halo.at[m])
        held[16] = jnp.zeros((256, 256), BF16)
        copies.wait()

    def body(a, b):
        sums = level_zero_sums("corners", a, b, flags, couplings.at[0], held, 16)
        for x, y in PARENTS:
            total = field[x, 0, y, 0] + nt(down_one[x * 2 + y], t_one[x, 0, y, 0])
            if (x, y) in sums:
                total = total + sums[x, y]
            far = nt(basis[x, 0, y, 0], total.astype(BF16))
            near_sum = near[x, 0, y, 0]
            part = near_part(
                "corner",
                number_of(a, b, (x, y)),
                lambda n: halo[CORNER_HALO.index(n)],
                near_held,
            )
            if part is not None:
                near_sum = near_sum + part
            out[x, 0, y, 0] = (near_sum * TILE_SCALE + far).astype(BF16)

    each_class(step, body)


def last_level(
    flags, couplings, t_one, basis, down_one, field, near, halo_a, halo_b, above, below
):
    return pl.pallas_call(
        last_kernel,
        grid=(4,),
        out_shape=jax.ShapeDtypeStruct((2, 2, 2, 2, 256, 256), BF16),
        in_specs=[
            SMEM_SPEC,
            COUPLING_BLOCK,
            CLASS_BLOCK,
            CLASS_BLOCK,
            pl.BlockSpec((4, 256, 256), lambda g: (0, 0, 0)),
            CLASS_BLOCK,
            CLASS_BLOCK,
        ]
        + [ANY_SPEC] * 4,
        out_specs=CLASS_BLOCK,
        scratch_shapes=[
            VMEM((17, 256, 256), BF16),
            VMEM((4, 256, 256), BF16),
            VMEM((len(CORNER_HALO), 256, 256), BF16),
            pltpu.SemaphoreType.DMA((4 + len(CORNER_HALO),)),
        ],
        compiler_params=params(),
        cost_estimate=cost(270, 20 << 20),
        name="last_level",
    )(
        flags, couplings, grouped(t_one), grouped(basis), down_one, field, near, halo_a, halo_b,
        above, below,
    )


def per_device(
    positions,
    samples,
    leaf_basis,
    transfer_one,
    transfer_two,
    couplings,
    near_lists,
    far_zero,
    far_one,
    far_two,
):
    nx = lax.axis_size("qx")
    ny = lax.axis_size("qy")
    down_x = [(k, k + 1) for k in range(nx - 1)]
    up_x = [(k + 1, k) for k in range(nx - 1)]
    down_y = [(k, k + 1) for k in range(ny - 1)]
    up_y = [(k + 1, k) for k in range(ny - 1)]

    up, down, left, right, upper = coefficients(samples, leaf_basis, transfer_one, transfer_two)

    above = lax.ppermute(down, "qx", down_x)
    below = lax.ppermute(up, "qx", up_x)
    pair = lax.ppermute(upper, "qy", [(k, k ^ 1) for k in range(ny)])
    sites = positions.reshape(-1, 2, 256)
    flat_samples = samples.reshape(16, 256, 256)
    near_a, halo_a = near_own(0, 4 * nx, 4 * ny, near_lists, sites, flat_samples)
    pair, above, below, left, right, near_a = lax.optimization_barrier(
        (pair, above, below, left, right, near_a)
    )
    outward = [(k, k + 2) for k in range(0, ny - 2, 2)] + [(k + 2, k) for k in range(1, ny - 2, 2)]
    inward = [(k + 2, k) for k in range(0, ny - 2, 2)] + [(k, k + 2) for k in range(1, ny - 2, 2)]
    to_out, to_in = assembled(
        "pair_payload", (upper, pair), [[(1, 0, 5), (0, 4, 1)], [(0, 4, 1), (1, 4, 1)]]
    )
    on_left = lax.ppermute(right, "qy", down_y)
    on_right = lax.ppermute(left, "qy", up_y)
    outer = lax.ppermute(to_out, "qy", outward)
    inner = lax.ppermute(to_in, "qy", inward)
    near_b, halo_b = near_own(8, 4 * nx, 4 * ny, near_lists, sites, flat_samples)
    inner, outer, near_b = lax.optimization_barrier((inner, outer, near_b))
    cells = [(0, 4, 1), (1, 4, 1), (2, 5, 1), (2, 4, 1), (3, 0, 2)]
    ones = [(0, 0, 4), (1, 0, 4), (2, 0, 4)]
    row, one_row, two_row = assembled(
        "row_payload", (upper, pair, outer, inner), [ones + cells, ones, cells]
    )
    swap_x = [(k, k ^ 1) for k in range(nx)]
    cross_x = [(k, k + 1) for k in range(1, nx - 1, 2)] + [(k + 1, k) for k in range(1, nx - 1, 2)]
    if nx == 4:
        others = [lax.ppermute(two_row, "qx", [(k, k ^ 2) for k in range(nx)])]
    else:
        others = [
            lax.ppermute(two_row, "qx", [(k, k + 2) for k in range(nx - 2)]),
            lax.ppermute(two_row, "qx", [(k + 2, k) for k in range(nx - 2)]),
        ]
    row_d = lax.ppermute(one_row, "qx", cross_x)
    row_e = lax.ppermute(row, "qx", swap_x)
    field, flags = rows_level(4 * ny, far_zero, couplings, up, down, above, below)
    others, field = lax.optimization_barrier((others, field))
    others = others + [lax.ppermute(x, "qx", swap_x) for x in others]
    down_one = upper_levels(
        ny, far_one, far_two, couplings, transfer_two, row, row_e, row_d, others
    )

    on_left, on_right, down_one = lax.optimization_barrier((on_left, on_right, down_one))
    corner_down, corner_up = assembled(
        "corner_payload",
        (on_left, on_right),
        [
            [(0, 4, 4), (1, 4, 4), (0, 11, 1), (1, 11, 1)],
            [(0, 0, 4), (1, 0, 4), (0, 8, 1), (1, 8, 1)],
        ],
    )
    corner_above = lax.ppermute(corner_down, "qx", down_x)
    corner_below = lax.ppermute(corner_up, "qx", up_x)
    field, near = sides_level(
        flags, couplings, field, near_a, near_b, halo_a, halo_b, on_left, on_right, above, below
    )
    result = last_level(
        flags,
        couplings,
        transfer_one,
        leaf_basis,
        down_one,
        field,
        near,
        halo_a,
        halo_b,
        corner_above,
        corner_below,
    )
    return result.reshape(4, 4, 256, 256)


def solution(mesh):
    return jax.shard_map(
        per_device,
        mesh=mesh,
        in_specs=(
            P(),
            P("qx", "qy", None, None),
            P("qx", "qy", None, None),
            P("qx", "qy", None, None),
            P("qx", "qy", None, None),
            P(),
            P("qx", "qy", None),
            P("qx", "qy", None),
            P("qx", "qy", None),
            P("qx", "qy", None),
        ),
        out_specs=P("qx", "qy", None, None),
        check_vma=False,
    )
```

```python
import functools

import jax
import jax.numpy as jnp
import numpy as np
from jax import lax
from jax.experimental import pallas as pl
from jax.experimental.pallas import tpu as pltpu
from jax.sharding import PartitionSpec as P

root_three = 1.7320508075688772
length_scale = 1.0
VMEM = pltpu.VMEM
SMEM = pltpu.SMEM
F32 = jnp.float32
BF16 = jnp.bfloat16
BIG = 60 * 1024 * 1024


def nn(a, b):
    return lax.dot_general(a, b, (((1,), (0,)), ((), ())), preferred_element_type=F32)


def nt(a, b):
    return lax.dot_general(a, b, (((1,), (1,)), ((), ())), preferred_element_type=F32)


def tn(a, b):
    return lax.dot_general(a, b, (((0,), (0,)), ((), ())), preferred_element_type=F32)


def params():
    return pltpu.CompilerParams(vmem_limit_bytes=BIG)


def cost(products, bytes_accessed):
    return pl.CostEstimate(
        flops=products * 2 * 256**3 // 8, bytes_accessed=bytes_accessed // 8, transcendentals=0
    )


def half_offsets():
    kept = []
    for u in range(-3, 4):
        for v in range(-3, 4):
            if max(abs(u), abs(v)) >= 2 and (u > 0 or (u == 0 and v > 0)):
                kept.append((u, v))
    return kept


HALF_OFFSETS = half_offsets()


def class_plan(a, b):
    plain, turned = [], []
    for w in range(36):
        u, v = w // 6 - 2 - a, w % 6 - 2 - b
        if max(abs(u), abs(v)) < 2:
            continue
        if (u, v) in HALF_OFFSETS:
            plain.append((w, HALF_OFFSETS.index((u, v))))
        else:
            turned.append((w, HALF_OFFSETS.index((-u, -v))))
    return plain, turned


LOG2E = 1.4426950408889634
TILE_SCALE = 256 ** -0.5


def tiles(n, dtype=BF16):
    return jax.ShapeDtypeStruct((n, 256, 256), dtype)


ANY_SPEC = pl.BlockSpec(memory_space=pl.ANY)
SMEM_SPEC = pl.BlockSpec(memory_space=SMEM)
VMEM_SPEC = pl.BlockSpec(memory_space=VMEM)


class Copies:
    def __init__(self, sems):
        self.sems = sems
        self.started = []

    def start(self, src, dst):
        copy = pltpu.make_async_copy(src, dst, self.sems.at[len(self.started)])
        copy.start()
        self.started.append(copy)
        return copy

    def wait(self):
        for copy in self.started:
            copy.wait()


def coef_kernel(
    samples, basis, t_one, t_two, up, down, left, right, upper,
    sv, bv, t1v, t2v, cv, uv, in_sems, out_sems,
):
    into = Copies(in_sems)
    out = Copies(out_sems)
    rows = []
    for x in range(4):
        rows.append(
            (
                into.start(samples.at[x], sv.at[x]),
                into.start(basis.at[x], bv.at[x]),
                into.start(t_one.at[x], t1v.at[x]),
            )
        )
    last = into.start(t_two, t2v)
    for x in range(4):
        rows[x][0].wait()
        rows[x][1].wait()
        for y in range(4):
            cv[x * 4 + y] = tn(sv[x, y], bv[x, y]).astype(BF16)
        own = cv.at[4 * x : 4 * x + 4]
        out.start(own, (up if x < 2 else down).at[4 * (x % 2) : 4 * (x % 2) + 4])
        out.start(cv.at[4 * x : 4 * x + 2], left.at[2 * x : 2 * x + 2])
        out.start(cv.at[4 * x + 2 : 4 * x + 4], right.at[2 * x : 2 * x + 2])
        out.start(sv.at[x, 0], left.at[8 + x])
        out.start(sv.at[x, 3], right.at[8 + x])
        if x == 0:
            out.start(sv.at[x], up.at[8:12])
        if x == 3:
            out.start(sv.at[x], down.at[8:12])
        if x % 2 == 1:
            rows[x - 1][2].wait()
            rows[x][2].wait()
            for y in range(2):
                kids = [(x - 1 + a, 2 * y + b) for a in range(2) for b in range(2)]
                lhs = jnp.concatenate([cv[k * 4 + m] for k, m in kids], axis=1)
                rhs = jnp.concatenate([t1v[k] for k in kids], axis=0)
                uv[x // 2 * 2 + y] = nn(lhs, rhs).astype(BF16)
    last.wait()
    lhs = jnp.concatenate([uv[k] for k in range(4)], axis=1)
    rhs = jnp.concatenate([t2v[k // 2, k % 2] for k in range(4)], axis=0)
    uv[4] = nn(lhs, rhs).astype(BF16)
    out.start(uv, upper)
    out.wait()


def coefficients(samples, basis, t_one, t_two):
    return pl.pallas_call(
        coef_kernel,
        out_shape=(tiles(12), tiles(12), tiles(12), tiles(12), tiles(5)),
        in_specs=[ANY_SPEC] * 4,
        out_specs=[ANY_SPEC] * 5,
        scratch_shapes=[
            VMEM((4, 4, 256, 256), BF16),
            VMEM((4, 4, 256, 256), BF16),
            VMEM((4, 4, 256, 256), BF16),
            VMEM((2, 2, 256, 256), BF16),
            VMEM((16, 256, 256), BF16),
            VMEM((5, 256, 256), BF16),
            pltpu.SemaphoreType.DMA((13,)),
            pltpu.SemaphoreType.DMA((23,)),
        ],
        compiler_params=params(),
        cost_estimate=cost(170, 12 << 20),
        name="coefficients",
    )(samples, basis, t_one, t_two)


def assembled(name, sources, pieces, ranges):
    count = sum(n for _, _, n in pieces)

    def kernel(*refs):
        ins, outs = refs[: len(sources)], refs[len(sources) : -3]
        held, in_sems, out_sems = refs[-3:]
        into = Copies(in_sems)
        at = 0
        for source, first, n in pieces:
            into.start(ins[source].at[first : first + n], held.at[at : at + n])
            at += n
        into.wait()
        out = Copies(out_sems)
        for (first, last), ref in zip(ranges, outs):
            out.start(held.at[first:last], ref)
        out.wait()

    return pl.pallas_call(
        kernel,
        out_shape=[tiles(last - first) for first, last in ranges],
        in_specs=[ANY_SPEC] * len(sources),
        out_specs=[ANY_SPEC] * len(ranges),
        scratch_shapes=[
            VMEM((count, 256, 256), BF16),
            pltpu.SemaphoreType.DMA((len(pieces),)),
            pltpu.SemaphoreType.DMA((len(ranges),)),
        ],
        compiler_params=params(),
        cost_estimate=cost(35, 0),
        name=name,
    )(*sources)


def halo_places():
    numbers = {}
    for r in range(4):
        for c in range(4):
            for k in range(9):
                y, x = r + k // 3 - 1, c + k % 3 - 1
                if not (0 <= y < 4 and 0 <= x < 4):
                    numbers[r * 4 + c, k] = len(numbers)
    return numbers


HALO = halo_places()
N_HALO = len(HALO) // 2


def split3(x):
    first = x.astype(BF16).astype(F32)
    rest = x - first
    second = rest.astype(BF16).astype(F32)
    return first, second, rest - second


def site_features(x, y):
    n = lax.broadcasted_iota(jnp.int32, (8, 256), 0)
    square = x * x + y * y
    target, source = [], []
    for parts in (split3(x), split3(y)):
        first, second, third = parts
        target.append(jnp.where(n < 3, first, jnp.where(n < 5, second, jnp.where(n < 6, third, 0.0))))
        other = jnp.where(
            (n == 0) | (n == 3) | (n == 5),
            first,
            jnp.where((n == 1) | (n == 4), second, jnp.where(n == 2, third, 0.0)),
        )
        source.append(-2.0 * other)
    first, second, third = split3(square)
    low = jnp.where(n == 0, first, jnp.where(n == 1, second, third))
    high = jnp.where(n == 3, first, jnp.where(n == 4, second, third))
    one = jnp.where(n < 6, 1.0, 0.0)
    target.append(jnp.where(n < 3, low, one))
    source.append(jnp.where(n < 3, 1.0, jnp.where(n < 6, high, 0.0)))
    zero = jnp.zeros((8, 256), F32)
    return jnp.concatenate(target + [zero], axis=0), jnp.concatenate(source + [zero], axis=0)


def near_kernel(
    first, grid_rows, grid_cols, lists, positions, own, near, halo_out,
    held, target_feat, source_feat, halo, made_a, made_b, floors_a, floors_b, sems, halo_sems,
):
    copy = pltpu.make_async_copy(own, held.at[0:16], sems.at[0])
    copy.start()
    held[16] = jnp.zeros((256, 256), BF16)
    first_row = lax.axis_index("qx") * 4
    first_col = lax.axis_index("qy") * 4
    scale = root_three / length_scale
    mid_row = first_row.astype(F32) + 2.0
    mid_col = first_col.astype(F32) + 2.0
    first_place = first // 4 * 6

    def features(n, carry):
        r = jnp.clip(first_row + (first_place + n) // 6 - 1, 0, grid_rows - 1)
        c = jnp.clip(first_col + n % 6 - 1, 0, grid_cols - 1)
        here = positions[r * grid_cols + c]
        target, source = site_features(
            (here[0:1] - mid_row) * scale, (here[1:2] - mid_col) * scale
        )
        target_feat[n] = target
        source_feat[n] = source.astype(BF16)
        return carry

    lax.fori_loop(0, 24, features, 0)
    copy.wait()

    def make(m, made, floors):
        r = (first + m) // 4
        c = (first + m) % 4
        row = first_row + r
        col = first_col + c
        for k in range(9):
            floors[k] = 1e6
        for e in range(9):
            entry = lists[r, c, e]
            source_row = jnp.maximum(entry, 0) // grid_cols
            source_col = jnp.maximum(entry, 0) - source_row * grid_cols
            k = (source_row - row + 1) * 3 + source_col - col + 1
            floors[jnp.where(entry >= 0, k, 9)] = 1e-24
        place = (m // 4 + 1) * 6 + c + 1
        target = target_feat[place].T.astype(BF16)
        for k in range(9):
            dr, dc = k // 3 - 1, k % 3 - 1
            square = nn(target, source_feat[place + dr * 6 + dc])
            square = jnp.maximum(square, floors[k])
            far = square * lax.rsqrt(square)
            tile = ((far + 1.0) * jnp.exp2(far * -LOG2E)).astype(BF16)
            inside = (r + dr >= 0) & (r + dr < 4) & (c + dc >= 0) & (c + dc < 4)
            halo[jnp.where(inside, 72, m * 9 + k)] = tile
            made[k] = tile

    def use(m, made):
        r = (first + m) // 4
        c = (first + m) % 4
        blocks = []
        for k in range(9):
            dr, dc = k // 3 - 1, k % 3 - 1
            inside = (r + dr >= 0) & (r + dr < 4) & (c + dc >= 0) & (c + dc < 4)
            blocks.append(held[jnp.where(inside, (r + dr) * 4 + c + dc, 16)])
        lhs = jnp.concatenate([made[k] for k in range(9)], axis=1)
        near[m] = nn(lhs, jnp.concatenate(blocks, axis=0))

    def two_targets(n, carry):
        use(2 * n, made_a)
        make(2 * n + 1, made_b, floors_b)
        use(2 * n + 1, made_b)
        make(2 * n + 2, made_a, floors_a)
        return carry

    make(0, made_a, floors_a)
    lax.fori_loop(0, 3, two_targets, 0)
    use(6, made_a)
    make(7, made_b, floors_b)
    use(7, made_b)
    out = Copies(halo_sems)
    for (t, k), number in HALO.items():
        if first <= t < first + 8:
            out.start(halo.at[(t - first) * 9 + k], halo_out.at[number % N_HALO])
    out.wait()


def near_own(first, grid_rows, grid_cols, lists, positions, own):
    return pl.pallas_call(
        functools.partial(near_kernel, first, grid_rows, grid_cols),
        out_shape=(tiles(8, F32), tiles(N_HALO)),
        in_specs=[SMEM_SPEC, VMEM_SPEC, ANY_SPEC],
        out_specs=[VMEM_SPEC, ANY_SPEC],
        scratch_shapes=[
            VMEM((17, 256, 256), BF16),
            VMEM((24, 32, 256), F32),
            VMEM((24, 32, 256), BF16),
            VMEM((73, 256, 256), BF16),
            VMEM((9, 256, 256), BF16),
            VMEM((9, 256, 256), BF16),
            pltpu.SMEM((10,), F32),
            pltpu.SMEM((10,), F32),
            pltpu.SemaphoreType.DMA((1,)),
            pltpu.SemaphoreType.DMA((N_HALO,)),
        ],
        compiler_params=params(),
        cost_estimate=cost(300, 8 << 20),
        name=f"near_own_{first}",
    )(lists, positions, own)


def mark_listed(entries, flags, n, first_row, first_col, grid_cols):
    for w in range(36):
        flags[n, w] = 0
    for e in range(27):
        entry = entries(e)
        row = jnp.maximum(entry, 0) // grid_cols
        col = jnp.maximum(entry, 0) - row * grid_cols
        w = (row - first_row) * 6 + col - first_col
        flags[n, jnp.where(entry >= 0, jnp.clip(w, 0, 35), 36)] = 1


def dot_group(held, couplings, turned, group):
    rows = len(group[0][1])
    lhs = [
        jnp.concatenate([held[places[n]] for _, places in group], axis=1) for n in range(rows)
    ]
    lhs = jnp.concatenate(lhs, axis=0) if rows > 1 else lhs[0]
    if turned:
        return nn(lhs, jnp.concatenate([couplings[k] for k, _ in group], axis=0))
    return nt(lhs, jnp.concatenate([couplings[k] for k, _ in group], axis=1))


def coupled(plan, couplings, held, places):
    total = None
    for turned in (0, 1):
        group = [(k, [places(w)]) for w, k in plan[turned]]
        part = dot_group(held, couplings, turned, group)
        total = part if total is None else total + part
    return total


def upper_kernel(grid_cols, n_others, far_one, far_two, couplings, t_two, *rest):
    row, row_e, row_d = rest[:3]
    others = rest[3 : 3 + 2 * n_others]
    down, held_one, held_two, field_two, flags, sems = rest[3 + 2 * n_others :]
    zero_one, zero_two = 36, 12 + 12 * n_others
    copies = Copies(sems)
    copies.start(row.at[12:18], held_two.at[0:6])
    copies.start(row_e.at[12:18], held_two.at[6:12])
    for n, other in enumerate(others):
        copies.start(other, held_two.at[12 + 6 * n : 18 + 6 * n])
    copies.start(row.at[0:12], held_one.at[0:12])
    copies.start(row_e.at[0:12], held_one.at[12:24])
    copies.start(row_d, held_one.at[24:36])
    held_one[zero_one] = jnp.zeros((256, 256), BF16)
    held_two[zero_two] = jnp.zeros((256, 256), BF16)
    i = lax.axis_index("qx")
    j = lax.axis_index("qy")
    a = i % 2
    b = j % 2
    for t in range(4):
        mark_listed(
            lambda e: far_one[t // 2, t % 2, e], flags, t, 2 * i - 2, 2 * j - 2, 2 * grid_cols
        )
    mark_listed(
        lambda e: far_two[0, 0, e], flags, 4, i // 2 * 2 - 2, j // 2 * 2 - 2, grid_cols
    )
    rows_at = []
    for r in range(6):
        if r // 2 == 1:
            rows_at.append(jnp.where(a == r % 2, 0, 6))
        else:
            n = 0 if r // 2 == 0 or n_others == 1 else 1
            rows_at.append(
                jnp.where(a == r % 2, 12 + 6 * n, 12 + 6 * (n_others + n))
            )
    z_at = [jnp.where(b == 0, 2, 4), 0, jnp.where(b == 0, 4, 2)]
    x_at = [b, 1 - b]

    def place_two(w):
        r, c = w // 6, w % 6
        place = rows_at[r] + z_at[c // 2] + x_at[c % 2]
        return jnp.where(flags[4, w] == 1, place, zero_two)

    row_at = [jnp.where(a == 0, 24, 12), 0, jnp.where(a == 0, 12, 24)]
    col_at = [jnp.where(b == 0, 8, 4), 0, jnp.where(b == 0, 4, 8)]

    def place_one(t, w):
        r, c = w // 6, w % 6
        place = row_at[r // 2] + col_at[c // 2] + (r % 2) * 2 + c % 2
        return jnp.where(flags[t, w] == 1, place, zero_one)

    for copy in copies.started[: 2 + 2 * n_others]:
        copy.wait()
    for u in range(2):
        for v in range(2):

            @pl.when((a == u) & (b == v))
            def _():
                field_two[...] = coupled(
                    class_plan(u, v), couplings.at[1], held_two, place_two
                ).astype(BF16)

    for copy in copies.started[2 + 2 * n_others :]:
        copy.wait()
    for u in range(2):
        for v in range(2):
            t = u * 2 + v
            field = coupled(
                class_plan(u, v), couplings.at[0], held_one, functools.partial(place_one, t)
            )
            down[t] = (field + nt(field_two[...], t_two[u, v])).astype(BF16)


def upper_levels(grid_cols, far_one, far_two, couplings, t_two, row, row_e, row_d, others):
    n_others = len(others) // 2
    return pl.pallas_call(
        functools.partial(upper_kernel, grid_cols, n_others),
        grid=(1,),
        out_shape=tiles(4),
        in_specs=[
            SMEM_SPEC,
            SMEM_SPEC,
            pl.BlockSpec(
                (pl.Element(2), pl.Element(20), pl.Element(256), pl.Element(256)),
                lambda g: (1, 0, 0, 0),
            ),
            pl.BlockSpec((2, 2, 256, 256), lambda g: (0, 0, 0, 0)),
        ]
        + [ANY_SPEC] * (3 + 2 * n_others),
        out_specs=pl.BlockSpec((4, 256, 256), lambda g: (0, 0, 0)),
        scratch_shapes=[
            VMEM((37, 256, 256), BF16),
            VMEM((13 + 12 * n_others, 256, 256), BF16),
            VMEM((256, 256), BF16),
            pltpu.SMEM((5, 37), jnp.int32),
            pltpu.SemaphoreType.DMA((5 + 2 * n_others,)),
        ],
        compiler_params=params(),
        cost_estimate=cost(340, 14 << 20),
        name="upper_levels",
    )(far_one, far_two, couplings, t_two, row, row_e, row_d, *others)


def source_of(x, y, w):
    r, c = 2 * x + w // 6, 2 * y + w % 6
    if 2 <= c < 6:
        return "inner", r * 4 + c - 2
    side = 0 if c < 2 else 1
    c = c if c < 2 else c - 6
    if 2 <= r < 6:
        return "outer", side * 8 + (r - 2) * 2 + c
    return "outer", (16 if r < 2 else 24) + side * 4 + (r if r < 2 else r - 6) * 2 + c


PARENTS = [(x, y) for x in range(2) for y in range(2)]


def number_of(a, b, parent):
    x, y = parent
    return (2 * x + a) * 4 + 2 * y + b


def level_zero_sums(kind, a, b, flags, couplings, held, zero):
    plan = class_plan(a, b)
    sums = {}
    for turned in (0, 1):
        groups = {}
        for w, k in plan[turned]:
            members = tuple(p for p in PARENTS if source_of(*p, w)[0] == kind)
            if members:
                groups.setdefault(members, []).append((w, k))
        for members, entries in groups.items():
            group = []
            for w, k in entries:
                places = [
                    jnp.where(flags[number_of(a, b, p), w] == 1, source_of(*p, w)[1], zero)
                    for p in members
                ]
                group.append((k, places))
            total = dot_group(held, couplings, turned, group)
            for n, p in enumerate(members):
                part = total[256 * n : 256 * n + 256]
                sums[p] = part if p not in sums else sums[p] + part
    return sums


def grouped(x):
    return x.reshape(2, 2, 2, 2, 256, 256)


CLASS_BLOCK = pl.BlockSpec((2, 1, 2, 1, 256, 256), lambda g: (0, g // 2, 0, g % 2, 0, 0))
COUPLING_BLOCK = pl.BlockSpec((1, 20, 256, 256), lambda g: (0, 0, 0, 0))
GROUPED_F32 = jax.ShapeDtypeStruct((2, 2, 2, 2, 256, 256), F32)


def each_class(step, body):
    for a in range(2):
        for b in range(2):
            pl.when(step == a * 2 + b)(functools.partial(body, a, b))


def rows_kernel(
    grid_cols, far_zero, couplings, up, down, above, below, field, flags, held, sems
):
    step = pl.program_id(0)

    @pl.when(step == 0)
    def _():
        copies = Copies(sems)
        for n, src in enumerate((above, up, down, below)):
            copies.start(src.at[0:8], held.at[8 * n : 8 * n + 8])
        held[32] = jnp.zeros((256, 256), BF16)
        first_row = lax.axis_index("qx") * 4
        first_col = lax.axis_index("qy") * 4

        def mark(t, carry):
            r, c = t // 4, t % 4
            mark_listed(
                lambda e: far_zero[r, c, e],
                flags,
                t,
                first_row + r // 2 * 2 - 2,
                first_col + c // 2 * 2 - 2,
                grid_cols,
            )
            return carry

        lax.fori_loop(0, 16, mark, 0)
        copies.wait()

    def body(a, b):
        sums = level_zero_sums("inner", a, b, flags, couplings.at[0], held, 32)
        for x, y in PARENTS:
            field[x, 0, y, 0] = sums[x, y]

    each_class(step, body)


def rows_level(grid_cols, far_zero, couplings, up, down, above, below):
    return pl.pallas_call(
        functools.partial(rows_kernel, grid_cols),
        grid=(4,),
        out_shape=(GROUPED_F32, jax.ShapeDtypeStruct((16, 37), jnp.int32)),
        in_specs=[SMEM_SPEC, COUPLING_BLOCK] + [ANY_SPEC] * 4,
        out_specs=[CLASS_BLOCK, SMEM_SPEC],
        scratch_shapes=[VMEM((33, 256, 256), BF16), pltpu.SemaphoreType.DMA((4,))],
        compiler_params=params(),
        cost_estimate=cost(420, 11 << 20),
        name="far_rows",
    )(far_zero, couplings, up, down, above, below)


def near_place(r, c):
    rows_in, cols_in = 1 <= r < 5, 1 <= c < 5
    if rows_in:
        return (0 if c == 0 else 4) + r - 1
    if cols_in:
        return (8 if r == 0 else 12) + c - 1
    return 16 + (0 if r == 0 else 2) + (0 if c == 0 else 1)


def near_part(t, halo, held):
    r, c = t // 4, t % 4
    found = [k for k in range(9) if (t, k) in HALO]
    if not found:
        return None
    lhs = jnp.concatenate([halo[HALO[t, k]] for k in found], axis=1)
    rhs = jnp.concatenate([held[near_place(r + k // 3, c + k % 3)] for k in found], axis=0)
    return nn(lhs, rhs)


def outer_kernel(
    flags, couplings, t_one, basis, down_one, field, near_a, near_b, halo_a, halo_b,
    left, right, above, below, corner_above, corner_below, out, held, near_held, halo, sems,
):
    step = pl.program_id(0)

    def copies():
        pairs = []
        for n, src in enumerate((left, right, corner_above, corner_below)):
            pairs.append((src.at[0:8], held.at[8 * n : 8 * n + 8]))
        for n, src in enumerate((left, right, above, below)):
            pairs.append((src.at[8:12], near_held.at[4 * n : 4 * n + 4]))
        pairs.append((corner_above.at[8:10], near_held.at[16:18]))
        pairs.append((corner_below.at[8:10], near_held.at[18:20]))
        pairs.append((halo_a, halo.at[0:N_HALO]))
        pairs.append((halo_b, halo.at[N_HALO : 2 * N_HALO]))
        return [pltpu.make_async_copy(src, dst, sems.at[n]) for n, (src, dst) in enumerate(pairs)]

    @pl.when(step == 0)
    def _():
        started = copies()
        for copy in started:
            copy.start()
        held[32] = jnp.zeros((256, 256), BF16)
        for copy in started[:4]:
            copy.wait()

    def body(a, b):
        sums = level_zero_sums("outer", a, b, flags, couplings.at[0], held, 32)
        if a == 0 and b == 0:
            for copy in copies()[4:]:
                copy.wait()
        for x, y in PARENTS:
            total = field[x, 0, y, 0] + sums[x, y]
            total = total + nt(down_one[x * 2 + y], t_one[x, 0, y, 0])
            far = nt(basis[x, 0, y, 0], total.astype(BF16))
            near = (near_b if x else near_a)[0, y, 0]
            part = near_part(number_of(a, b, (x, y)), halo, near_held)
            if part is not None:
                near = near + part
            out[x, 0, y, 0] = (near * TILE_SCALE + far).astype(BF16)

    each_class(step, body)


HALF_BLOCK = pl.BlockSpec((1, 2, 1, 256, 256), lambda g: (g // 2, 0, g % 2, 0, 0))


def outer_level(
    flags, couplings, t_one, basis, down_one, field, near_a, near_b, halo_a, halo_b, *received
):
    half = lambda x: x.reshape(2, 2, 2, 256, 256)
    return pl.pallas_call(
        outer_kernel,
        grid=(4,),
        out_shape=jax.ShapeDtypeStruct((2, 2, 2, 2, 256, 256), BF16),
        in_specs=[
            SMEM_SPEC,
            COUPLING_BLOCK,
            CLASS_BLOCK,
            CLASS_BLOCK,
            pl.BlockSpec((4, 256, 256), lambda g: (0, 0, 0)),
            CLASS_BLOCK,
            HALF_BLOCK,
            HALF_BLOCK,
        ]
        + [ANY_SPEC] * 8,
        out_specs=CLASS_BLOCK,
        scratch_shapes=[
            VMEM((33, 256, 256), BF16),
            VMEM((20, 256, 256), BF16),
            VMEM((2 * N_HALO, 256, 256), BF16),
            pltpu.SemaphoreType.DMA((12,)),
        ],
        compiler_params=params(),
        cost_estimate=cost(500, 34 << 20),
        name="leaf_outer",
    )(
        flags, couplings, grouped(t_one), grouped(basis), down_one, field, half(near_a),
        half(near_b), halo_a, halo_b, *received,
    )


def per_device(
    positions,
    samples,
    leaf_basis,
    transfer_one,
    transfer_two,
    couplings,
    near_lists,
    far_zero,
    far_one,
    far_two,
):
    nx = lax.axis_size("qx")
    ny = lax.axis_size("qy")
    down_x = [(k, k + 1) for k in range(nx - 1)]
    up_x = [(k + 1, k) for k in range(nx - 1)]
    down_y = [(k, k + 1) for k in range(ny - 1)]
    up_y = [(k + 1, k) for k in range(ny - 1)]

    up, down, left, right, upper = coefficients(samples, leaf_basis, transfer_one, transfer_two)

    above = lax.ppermute(down, "qx", down_x)
    below = lax.ppermute(up, "qx", up_x)
    pair = lax.ppermute(upper, "qy", [(k, k ^ 1) for k in range(ny)])
    sites = positions.reshape(-1, 2, 256)
    flat_samples = samples.reshape(16, 256, 256)
    near_a, halo_a = near_own(0, 4 * nx, 4 * ny, near_lists, sites, flat_samples)
    pair, above, below, left, right, near_a = lax.optimization_barrier(
        (pair, above, below, left, right, near_a)
    )
    outward = [(k, k + 2) for k in range(0, ny - 2, 2)] + [(k + 2, k) for k in range(1, ny - 2, 2)]
    inward = [(k + 2, k) for k in range(0, ny - 2, 2)] + [(k, k + 2) for k in range(1, ny - 2, 2)]
    to_out, to_in = assembled(
        "pair_payload", (upper, pair), [(1, 0, 5), (0, 4, 1)], [(0, 6), (4, 6)]
    )
    on_left = lax.ppermute(right, "qy", down_y)
    on_right = lax.ppermute(left, "qy", up_y)
    outer = lax.ppermute(to_out, "qy", outward)
    inner = lax.ppermute(to_in, "qy", inward)
    near_b, halo_b = near_own(8, 4 * nx, 4 * ny, near_lists, sites, flat_samples)
    inner, outer, near_b = lax.optimization_barrier((inner, outer, near_b))
    row, one_row, two_row = assembled(
        "row_payload",
        (upper, pair, outer, inner),
        [(0, 0, 4), (1, 0, 4), (2, 0, 4)]
        + [(0, 4, 1), (1, 4, 1), (2, 5, 1), (2, 4, 1), (3, 1, 1), (3, 0, 1)],
        [(0, 18), (0, 12), (12, 18)],
    )
    swap_x = [(k, k ^ 1) for k in range(nx)]
    cross_x = [(k, k + 1) for k in range(1, nx - 1, 2)] + [(k + 1, k) for k in range(1, nx - 1, 2)]
    if nx == 4:
        others = [lax.ppermute(two_row, "qx", [(k, k ^ 2) for k in range(nx)])]
    else:
        others = [
            lax.ppermute(two_row, "qx", [(k, k + 2) for k in range(nx - 2)]),
            lax.ppermute(two_row, "qx", [(k + 2, k) for k in range(nx - 2)]),
        ]
    row_d = lax.ppermute(one_row, "qx", cross_x)
    row_e = lax.ppermute(row, "qx", swap_x)
    field, flags = rows_level(4 * ny, far_zero, couplings, up, down, above, below)
    others, field = lax.optimization_barrier((others, field))
    others = others + [lax.ppermute(x, "qx", swap_x) for x in others]
    on_left, on_right, others = lax.optimization_barrier((on_left, on_right, others))

    corner_down, corner_up = assembled(
        "corner_payload",
        (on_left, on_right),
        [(0, 4, 4), (1, 4, 4), (0, 11, 1), (1, 11, 1)]
        + [(0, 0, 4), (1, 0, 4), (0, 8, 1), (1, 8, 1)],
        [(0, 10), (10, 20)],
    )
    corner_above = lax.ppermute(corner_down, "qx", down_x)
    corner_below = lax.ppermute(corner_up, "qx", up_x)
    down_one = upper_levels(
        ny, far_one, far_two, couplings, transfer_two, row, row_e, row_d, others
    )
    result = outer_level(
        flags,
        couplings,
        transfer_one,
        leaf_basis,
        down_one,
        field,
        near_a,
        near_b,
        halo_a,
        halo_b,
        on_left,
        on_right,
        above,
        below,
        corner_above,
        corner_below,
    )
    return result.reshape(4, 4, 256, 256)


def solution(mesh):
    return jax.shard_map(
        per_device,
        mesh=mesh,
        in_specs=(
            P(),
            P("qx", "qy", None, None),
            P("qx", "qy", None, None),
            P("qx", "qy", None, None),
            P("qx", "qy", None, None),
            P(),
            P("qx", "qy", None),
            P("qx", "qy", None),
            P("qx", "qy", None),
            P("qx", "qy", None),
        ),
        out_specs=P("qx", "qy", None, None),
        check_vma=False,
    )
```

```python
import functools

import jax
import jax.numpy as jnp
import numpy as np
from jax import lax
from jax.experimental import pallas as pl
from jax.experimental.pallas import tpu as pltpu
from jax.sharding import PartitionSpec as P

root_three = 1.7320508075688772
length_scale = 1.0
VMEM = pltpu.VMEM
SMEM = pltpu.SMEM
F32 = jnp.float32
BF16 = jnp.bfloat16
BIG = 60 * 1024 * 1024


def nn(a, b):
    return lax.dot_general(a, b, (((1,), (0,)), ((), ())), preferred_element_type=F32)


def nt(a, b):
    return lax.dot_general(a, b, (((1,), (1,)), ((), ())), preferred_element_type=F32)


def tn(a, b):
    return lax.dot_general(a, b, (((0,), (0,)), ((), ())), preferred_element_type=F32)


def params():
    return pltpu.CompilerParams(vmem_limit_bytes=BIG)


def cost(products, bytes_accessed):
    return pl.CostEstimate(
        flops=products * 2 * 256**3 // 8, bytes_accessed=bytes_accessed // 8, transcendentals=0
    )


def half_offsets():
    kept = []
    for u in range(-3, 4):
        for v in range(-3, 4):
            if max(abs(u), abs(v)) >= 2 and (u > 0 or (u == 0 and v > 0)):
                kept.append((u, v))
    return kept


HALF_OFFSETS = half_offsets()


def class_plan(a, b):
    plain, turned = [], []
    for w in range(36):
        u, v = w // 6 - 2 - a, w % 6 - 2 - b
        if max(abs(u), abs(v)) < 2:
            continue
        if (u, v) in HALF_OFFSETS:
            plain.append((w, HALF_OFFSETS.index((u, v))))
        else:
            turned.append((w, HALF_OFFSETS.index((-u, -v))))
    return plain, turned


LOG2E = 1.4426950408889634
TILE_SCALE = 256 ** -0.5


def tiles(n, dtype=BF16):
    return jax.ShapeDtypeStruct((n, 256, 256), dtype)


ANY_SPEC = pl.BlockSpec(memory_space=pl.ANY)
SMEM_SPEC = pl.BlockSpec(memory_space=SMEM)
VMEM_SPEC = pl.BlockSpec(memory_space=VMEM)


class Copies:
    def __init__(self, sems):
        self.sems = sems
        self.started = []

    def start(self, src, dst):
        copy = pltpu.make_async_copy(src, dst, self.sems.at[len(self.started)])
        copy.start()
        self.started.append(copy)
        return copy

    def wait(self):
        for copy in self.started:
            copy.wait()


def coef_kernel(
    samples, basis, t_one, t_two, up, down, left, right, upper,
    sv, bv, t1v, t2v, cv, uv, in_sems, out_sems,
):
    into = Copies(in_sems)
    out = Copies(out_sems)
    rows = []
    for x in range(4):
        rows.append(
            (
                into.start(samples.at[x], sv.at[x]),
                into.start(basis.at[x], bv.at[x]),
                into.start(t_one.at[x], t1v.at[x]),
            )
        )
    last = into.start(t_two, t2v)
    for x in range(4):
        rows[x][0].wait()
        rows[x][1].wait()
        for y in range(4):
            cv[x * 4 + y] = tn(sv[x, y], bv[x, y]).astype(BF16)
        own = cv.at[4 * x : 4 * x + 4]
        out.start(own, (up if x < 2 else down).at[4 * (x % 2) : 4 * (x % 2) + 4])
        out.start(cv.at[4 * x : 4 * x + 2], left.at[2 * x : 2 * x + 2])
        out.start(cv.at[4 * x + 2 : 4 * x + 4], right.at[2 * x : 2 * x + 2])
        out.start(sv.at[x, 0], left.at[8 + x])
        out.start(sv.at[x, 3], right.at[8 + x])
        if x == 0:
            out.start(sv.at[x], up.at[8:12])
        if x == 3:
            out.start(sv.at[x], down.at[8:12])
        if x % 2 == 1:
            rows[x - 1][2].wait()
            rows[x][2].wait()
            for y in range(2):
                kids = [(x - 1 + a, 2 * y + b) for a in range(2) for b in range(2)]
                lhs = jnp.concatenate([cv[k * 4 + m] for k, m in kids], axis=1)
                rhs = jnp.concatenate([t1v[k] for k in kids], axis=0)
                uv[x // 2 * 2 + y] = nn(lhs, rhs).astype(BF16)
    last.wait()
    lhs = jnp.concatenate([uv[k] for k in range(4)], axis=1)
    rhs = jnp.concatenate([t2v[k // 2, k % 2] for k in range(4)], axis=0)
    uv[4] = nn(lhs, rhs).astype(BF16)
    out.start(uv, upper)
    out.wait()


def coefficients(samples, basis, t_one, t_two):
    return pl.pallas_call(
        coef_kernel,
        out_shape=(tiles(12), tiles(12), tiles(12), tiles(12), tiles(5)),
        in_specs=[ANY_SPEC] * 4,
        out_specs=[ANY_SPEC] * 5,
        scratch_shapes=[
            VMEM((4, 4, 256, 256), BF16),
            VMEM((4, 4, 256, 256), BF16),
            VMEM((4, 4, 256, 256), BF16),
            VMEM((2, 2, 256, 256), BF16),
            VMEM((16, 256, 256), BF16),
            VMEM((5, 256, 256), BF16),
            pltpu.SemaphoreType.DMA((13,)),
            pltpu.SemaphoreType.DMA((23,)),
        ],
        compiler_params=params(),
        cost_estimate=cost(170, 12 << 20),
        name="coefficients",
    )(samples, basis, t_one, t_two)


def assembled(name, sources, pieces, ranges):
    count = sum(n for _, _, n in pieces)

    def kernel(*refs):
        ins, outs = refs[: len(sources)], refs[len(sources) : -3]
        held, in_sems, out_sems = refs[-3:]
        into = Copies(in_sems)
        at = 0
        for source, first, n in pieces:
            into.start(ins[source].at[first : first + n], held.at[at : at + n])
            at += n
        into.wait()
        out = Copies(out_sems)
        for (first, last), ref in zip(ranges, outs):
            out.start(held.at[first:last], ref)
        out.wait()

    return pl.pallas_call(
        kernel,
        out_shape=[tiles(last - first) for first, last in ranges],
        in_specs=[ANY_SPEC] * len(sources),
        out_specs=[ANY_SPEC] * len(ranges),
        scratch_shapes=[
            VMEM((count, 256, 256), BF16),
            pltpu.SemaphoreType.DMA((len(pieces),)),
            pltpu.SemaphoreType.DMA((len(ranges),)),
        ],
        compiler_params=params(),
        cost_estimate=cost(35, 0),
        name=name,
    )(*sources)


def halo_places():
    numbers = {}
    for r in range(4):
        for c in range(4):
            for k in range(9):
                y, x = r + k // 3 - 1, c + k % 3 - 1
                if not (0 <= y < 4 and 0 <= x < 4):
                    numbers[r * 4 + c, k] = len(numbers)
    return numbers


HALO = halo_places()
N_HALO = len(HALO) // 2


def split3(x):
    first = x.astype(BF16).astype(F32)
    rest = x - first
    second = rest.astype(BF16).astype(F32)
    return first, second, rest - second


def site_features(x, y):
    n = lax.broadcasted_iota(jnp.int32, (8, 256), 0)
    square = x * x + y * y
    target, source = [], []
    for parts in (split3(x), split3(y)):
        first, second, third = parts
        target.append(jnp.where(n < 3, first, jnp.where(n < 5, second, jnp.where(n < 6, third, 0.0))))
        other = jnp.where(
            (n == 0) | (n == 3) | (n == 5),
            first,
            jnp.where((n == 1) | (n == 4), second, jnp.where(n == 2, third, 0.0)),
        )
        source.append(-2.0 * other)
    first, second, third = split3(square)
    low = jnp.where(n == 0, first, jnp.where(n == 1, second, third))
    high = jnp.where(n == 3, first, jnp.where(n == 4, second, third))
    one = jnp.where(n < 6, 1.0, 0.0)
    target.append(jnp.where(n < 3, low, one))
    source.append(jnp.where(n < 3, 1.0, jnp.where(n < 6, high, 0.0)))
    zero = jnp.zeros((8, 256), F32)
    return jnp.concatenate(target + [zero], axis=0), jnp.concatenate(source + [zero], axis=0)


def near_kernel(
    first, grid_rows, grid_cols, lists, positions, own, near, halo_out,
    held, target_feat, source_feat, halo, made, floors, sems, halo_sems,
):
    copy = pltpu.make_async_copy(own, held, sems.at[0])
    copy.start()
    first_row = lax.axis_index("qx") * 4
    first_col = lax.axis_index("qy") * 4
    scale = root_three / length_scale
    mid_row = first_row.astype(F32) + 2.0
    mid_col = first_col.astype(F32) + 2.0
    first_place = first // 4 * 6

    def features(n, carry):
        r = jnp.clip(first_row + (first_place + n) // 6 - 1, 0, grid_rows - 1)
        c = jnp.clip(first_col + n % 6 - 1, 0, grid_cols - 1)
        here = positions[r * grid_cols + c]
        target, source = site_features(
            (here[0:1] - mid_row) * scale, (here[1:2] - mid_col) * scale
        )
        target_feat[n] = target
        source_feat[n] = source.astype(BF16)
        return carry

    lax.fori_loop(0, 24, features, 0)

    out = Copies(halo_sems)

    def make(m):
        t = first + m
        r, c = t // 4, t % 4
        slot = m % 2 * 9
        for k in range(9):
            floors[m * 10 + k] = 1e6
        for e in range(9):
            entry = lists[r, c, e]
            source_row = jnp.maximum(entry, 0) // grid_cols
            source_col = jnp.maximum(entry, 0) - source_row * grid_cols
            k = (source_row - first_row - r + 1) * 3 + source_col - first_col - c + 1
            floors[m * 10 + jnp.where(entry >= 0, k, 9)] = 1e-24
        place = (m // 4 + 1) * 6 + c + 1
        target = target_feat[place].T.astype(BF16)
        for k in range(9):
            square = nn(target, source_feat[place + (k // 3 - 1) * 6 + k % 3 - 1])
            square = jnp.maximum(square, floors[m * 10 + k])
            far = square * lax.rsqrt(square)
            tile = ((far + 1.0) * jnp.exp2(far * -LOG2E)).astype(BF16)
            if (t, k) in HALO:
                number = HALO[t, k] % N_HALO
                halo[number] = tile
                out.start(halo.at[number], halo_out.at[number])
            else:
                made[slot + k] = tile

    def use(m):
        t = first + m
        slot = m % 2 * 9
        found = [k for k in range(9) if (t, k) not in HALO]
        lhs = jnp.concatenate([made[slot + k] for k in found], axis=1)
        blocks = [held[t + (k // 3 - 1) * 4 + k % 3 - 1] for k in found]
        near[m] = nn(lhs, jnp.concatenate(blocks, axis=0))

    make(0)
    copy.wait()
    for m in range(1, 8):
        make(m)
        use(m - 1)
    use(7)
    out.wait()


def near_own(first, grid_rows, grid_cols, lists, positions, own):
    return pl.pallas_call(
        functools.partial(near_kernel, first, grid_rows, grid_cols),
        out_shape=(tiles(8, F32), tiles(N_HALO)),
        in_specs=[SMEM_SPEC, VMEM_SPEC, ANY_SPEC],
        out_specs=[VMEM_SPEC, ANY_SPEC],
        scratch_shapes=[
            VMEM((16, 256, 256), BF16),
            VMEM((24, 32, 256), F32),
            VMEM((24, 32, 256), BF16),
            VMEM((N_HALO, 256, 256), BF16),
            VMEM((18, 256, 256), BF16),
            pltpu.SMEM((80,), F32),
            pltpu.SemaphoreType.DMA((1,)),
            pltpu.SemaphoreType.DMA((N_HALO,)),
        ],
        compiler_params=params(),
        cost_estimate=cost(300, 8 << 20),
        name=f"near_own_{first}",
    )(lists, positions, own)


def mark_listed(entries, flags, n, first_row, first_col, grid_cols):
    for w in range(36):
        flags[n, w] = 0
    for e in range(27):
        entry = entries(e)
        row = jnp.maximum(entry, 0) // grid_cols
        col = jnp.maximum(entry, 0) - row * grid_cols
        w = (row - first_row) * 6 + col - first_col
        flags[n, jnp.where(entry >= 0, jnp.clip(w, 0, 35), 36)] = 1


def dot_group(held, couplings, turned, group):
    rows = len(group[0][1])
    lhs = [
        jnp.concatenate([held[places[n]] for _, places in group], axis=1) for n in range(rows)
    ]
    lhs = jnp.concatenate(lhs, axis=0) if rows > 1 else lhs[0]
    if turned:
        return nn(lhs, jnp.concatenate([couplings[k] for k, _ in group], axis=0))
    return nt(lhs, jnp.concatenate([couplings[k] for k, _ in group], axis=1))


def coupled(plan, couplings, held, places):
    total = None
    for turned in (0, 1):
        group = [(k, [places(w)]) for w, k in plan[turned]]
        part = dot_group(held, couplings, turned, group)
        total = part if total is None else total + part
    return total


def upper_kernel(grid_cols, n_others, far_one, far_two, couplings, t_two, *rest):
    row, row_e, row_d = rest[:3]
    others = rest[3 : 3 + 2 * n_others]
    down, held_one, held_two, field_two, flags, sems = rest[3 + 2 * n_others :]
    zero_one, zero_two = 36, 12 + 12 * n_others
    copies = Copies(sems)
    copies.start(row.at[12:18], held_two.at[0:6])
    copies.start(row_e.at[12:18], held_two.at[6:12])
    for n, other in enumerate(others):
        copies.start(other, held_two.at[12 + 6 * n : 18 + 6 * n])
    copies.start(row.at[0:12], held_one.at[0:12])
    copies.start(row_e.at[0:12], held_one.at[12:24])
    copies.start(row_d, held_one.at[24:36])
    held_one[zero_one] = jnp.zeros((256, 256), BF16)
    held_two[zero_two] = jnp.zeros((256, 256), BF16)
    i = lax.axis_index("qx")
    j = lax.axis_index("qy")
    a = i % 2
    b = j % 2
    for t in range(4):
        mark_listed(
            lambda e: far_one[t // 2, t % 2, e], flags, t, 2 * i - 2, 2 * j - 2, 2 * grid_cols
        )
    mark_listed(
        lambda e: far_two[0, 0, e], flags, 4, i // 2 * 2 - 2, j // 2 * 2 - 2, grid_cols
    )
    rows_at = []
    for r in range(6):
        if r // 2 == 1:
            rows_at.append(jnp.where(a == r % 2, 0, 6))
        else:
            n = 0 if r // 2 == 0 or n_others == 1 else 1
            rows_at.append(
                jnp.where(a == r % 2, 12 + 6 * n, 12 + 6 * (n_others + n))
            )
    z_at = [jnp.where(b == 0, 2, 4), 0, jnp.where(b == 0, 4, 2)]
    x_at = [b, 1 - b]

    def place_two(w):
        r, c = w // 6, w % 6
        place = rows_at[r] + z_at[c // 2] + x_at[c % 2]
        return jnp.where(flags[4, w] == 1, place, zero_two)

    row_at = [jnp.where(a == 0, 24, 12), 0, jnp.where(a == 0, 12, 24)]
    col_at = [jnp.where(b == 0, 8, 4), 0, jnp.where(b == 0, 4, 8)]

    def place_one(t, w):
        r, c = w // 6, w % 6
        place = row_at[r // 2] + col_at[c // 2] + (r % 2) * 2 + c % 2
        return jnp.where(flags[t, w] == 1, place, zero_one)

    for copy in copies.started[: 2 + 2 * n_others]:
        copy.wait()
    for u in range(2):
        for v in range(2):

            @pl.when((a == u) & (b == v))
            def _():
                field_two[...] = coupled(
                    class_plan(u, v), couplings.at[1], held_two, place_two
                ).astype(BF16)

    for copy in copies.started[2 + 2 * n_others :]:
        copy.wait()
    for u in range(2):
        for v in range(2):
            t = u * 2 + v
            field = coupled(
                class_plan(u, v), couplings.at[0], held_one, functools.partial(place_one, t)
            )
            down[t] = (field + nt(field_two[...], t_two[u, v])).astype(BF16)


def upper_levels(grid_cols, far_one, far_two, couplings, t_two, row, row_e, row_d, others):
    n_others = len(others) // 2
    return pl.pallas_call(
        functools.partial(upper_kernel, grid_cols, n_others),
        grid=(1,),
        out_shape=tiles(4),
        in_specs=[
            SMEM_SPEC,
            SMEM_SPEC,
            pl.BlockSpec(
                (pl.Element(2), pl.Element(20), pl.Element(256), pl.Element(256)),
                lambda g: (1, 0, 0, 0),
            ),
            pl.BlockSpec((2, 2, 256, 256), lambda g: (0, 0, 0, 0)),
        ]
        + [ANY_SPEC] * (3 + 2 * n_others),
        out_specs=pl.BlockSpec((4, 256, 256), lambda g: (0, 0, 0)),
        scratch_shapes=[
            VMEM((37, 256, 256), BF16),
            VMEM((13 + 12 * n_others, 256, 256), BF16),
            VMEM((256, 256), BF16),
            pltpu.SMEM((5, 37), jnp.int32),
            pltpu.SemaphoreType.DMA((5 + 2 * n_others,)),
        ],
        compiler_params=params(),
        cost_estimate=cost(340, 14 << 20),
        name="upper_levels",
    )(far_one, far_two, couplings, t_two, row, row_e, row_d, *others)


def source_of(x, y, w):
    r, c = 2 * x + w // 6, 2 * y + w % 6
    if 2 <= c < 6:
        return "inner", r * 4 + c - 2
    side = 0 if c < 2 else 1
    c = c if c < 2 else c - 6
    if 2 <= r < 6:
        return "outer", side * 8 + (r - 2) * 2 + c
    return "outer", (16 if r < 2 else 24) + side * 4 + (r if r < 2 else r - 6) * 2 + c


PARENTS = [(x, y) for x in range(2) for y in range(2)]


def number_of(a, b, parent):
    x, y = parent
    return (2 * x + a) * 4 + 2 * y + b


def level_zero_sums(kind, a, b, flags, couplings, held, zero):
    plan = class_plan(a, b)
    sums = {}
    for turned in (0, 1):
        groups = {}
        for w, k in plan[turned]:
            members = tuple(p for p in PARENTS if source_of(*p, w)[0] == kind)
            if members:
                groups.setdefault(members, []).append((w, k))
        for members, entries in groups.items():
            group = []
            for w, k in entries:
                places = [
                    jnp.where(flags[number_of(a, b, p), w] == 1, source_of(*p, w)[1], zero)
                    for p in members
                ]
                group.append((k, places))
            total = dot_group(held, couplings, turned, group)
            for n, p in enumerate(members):
                part = total[256 * n : 256 * n + 256]
                sums[p] = part if p not in sums else sums[p] + part
    return sums


def grouped(x):
    return x.reshape(2, 2, 2, 2, 256, 256)


CLASS_BLOCK = pl.BlockSpec((2, 1, 2, 1, 256, 256), lambda g: (0, g // 2, 0, g % 2, 0, 0))
COUPLING_BLOCK = pl.BlockSpec((1, 20, 256, 256), lambda g: (0, 0, 0, 0))
GROUPED_F32 = jax.ShapeDtypeStruct((2, 2, 2, 2, 256, 256), F32)


def each_class(step, body):
    for a in range(2):
        for b in range(2):
            pl.when(step == a * 2 + b)(functools.partial(body, a, b))


def rows_kernel(
    grid_cols, far_zero, couplings, up, down, above, below, field, flags, held, sems
):
    step = pl.program_id(0)

    @pl.when(step == 0)
    def _():
        copies = Copies(sems)
        for n, src in enumerate((above, up, down, below)):
            copies.start(src.at[0:8], held.at[8 * n : 8 * n + 8])
        held[32] = jnp.zeros((256, 256), BF16)
        first_row = lax.axis_index("qx") * 4
        first_col = lax.axis_index("qy") * 4

        def mark(t, carry):
            r, c = t // 4, t % 4
            mark_listed(
                lambda e: far_zero[r, c, e],
                flags,
                t,
                first_row + r // 2 * 2 - 2,
                first_col + c // 2 * 2 - 2,
                grid_cols,
            )
            return carry

        lax.fori_loop(0, 16, mark, 0)
        copies.wait()

    def body(a, b):
        sums = level_zero_sums("inner", a, b, flags, couplings.at[0], held, 32)
        for x, y in PARENTS:
            field[x, 0, y, 0] = sums[x, y]

    each_class(step, body)


def rows_level(grid_cols, far_zero, couplings, up, down, above, below):
    return pl.pallas_call(
        functools.partial(rows_kernel, grid_cols),
        grid=(4,),
        out_shape=(GROUPED_F32, jax.ShapeDtypeStruct((16, 37), jnp.int32)),
        in_specs=[SMEM_SPEC, COUPLING_BLOCK] + [ANY_SPEC] * 4,
        out_specs=[CLASS_BLOCK, SMEM_SPEC],
        scratch_shapes=[VMEM((33, 256, 256), BF16), pltpu.SemaphoreType.DMA((4,))],
        compiler_params=params(),
        cost_estimate=cost(420, 11 << 20),
        name="far_rows",
    )(far_zero, couplings, up, down, above, below)


def near_place(r, c):
    rows_in, cols_in = 1 <= r < 5, 1 <= c < 5
    if rows_in:
        return (0 if c == 0 else 4) + r - 1
    if cols_in:
        return (8 if r == 0 else 12) + c - 1
    return 16 + (0 if r == 0 else 2) + (0 if c == 0 else 1)


def near_part(t, halo, held):
    r, c = t // 4, t % 4
    found = [k for k in range(9) if (t, k) in HALO]
    if not found:
        return None
    lhs = jnp.concatenate([halo[HALO[t, k]] for k in found], axis=1)
    rhs = jnp.concatenate([held[near_place(r + k // 3, c + k % 3)] for k in found], axis=0)
    return nn(lhs, rhs)


def outer_kernel(
    flags, couplings, t_one, basis, down_one, field, near_a, near_b, halo_a, halo_b,
    left, right, above, below, corner_above, corner_below, out, held, near_held, halo, sems,
):
    step = pl.program_id(0)

    def copies():
        pairs = []
        for n, src in enumerate((left, right, corner_above, corner_below)):
            pairs.append((src.at[0:8], held.at[8 * n : 8 * n + 8]))
        for n, src in enumerate((left, right, above, below)):
            pairs.append((src.at[8:12], near_held.at[4 * n : 4 * n + 4]))
        pairs.append((corner_above.at[8:10], near_held.at[16:18]))
        pairs.append((corner_below.at[8:10], near_held.at[18:20]))
        pairs.append((halo_a, halo.at[0:N_HALO]))
        pairs.append((halo_b, halo.at[N_HALO : 2 * N_HALO]))
        return [pltpu.make_async_copy(src, dst, sems.at[n]) for n, (src, dst) in enumerate(pairs)]

    @pl.when(step == 0)
    def _():
        started = copies()
        for copy in started:
            copy.start()
        held[32] = jnp.zeros((256, 256), BF16)
        for copy in started[:4]:
            copy.wait()

    def body(a, b):
        sums = level_zero_sums("outer", a, b, flags, couplings.at[0], held, 32)
        if a == 0 and b == 0:
            for copy in copies()[4:]:
                copy.wait()
        for x, y in PARENTS:
            total = field[x, 0, y, 0] + sums[x, y]
            total = total + nt(down_one[x * 2 + y], t_one[x, 0, y, 0])
            far = nt(basis[x, 0, y, 0], total.astype(BF16))
            near = (near_b if x else near_a)[0, y, 0]
            part = near_part(number_of(a, b, (x, y)), halo, near_held)
            if part is not None:
                near = near + part
            out[x, 0, y, 0] = (near * TILE_SCALE + far).astype(BF16)

    each_class(step, body)


HALF_BLOCK = pl.BlockSpec((1, 2, 1, 256, 256), lambda g: (g // 2, 0, g % 2, 0, 0))


def outer_level(
    flags, couplings, t_one, basis, down_one, field, near_a, near_b, halo_a, halo_b, *received
):
    half = lambda x: x.reshape(2, 2, 2, 256, 256)
    return pl.pallas_call(
        outer_kernel,
        grid=(4,),
        out_shape=jax.ShapeDtypeStruct((2, 2, 2, 2, 256, 256), BF16),
        in_specs=[
            SMEM_SPEC,
            COUPLING_BLOCK,
            CLASS_BLOCK,
            CLASS_BLOCK,
            pl.BlockSpec((4, 256, 256), lambda g: (0, 0, 0)),
            CLASS_BLOCK,
            HALF_BLOCK,
            HALF_BLOCK,
        ]
        + [ANY_SPEC] * 8,
        out_specs=CLASS_BLOCK,
        scratch_shapes=[
            VMEM((33, 256, 256), BF16),
            VMEM((20, 256, 256), BF16),
            VMEM((2 * N_HALO, 256, 256), BF16),
            pltpu.SemaphoreType.DMA((12,)),
        ],
        compiler_params=params(),
        cost_estimate=cost(500, 34 << 20),
        name="leaf_outer",
    )(
        flags, couplings, grouped(t_one), grouped(basis), down_one, field, half(near_a),
        half(near_b), halo_a, halo_b, *received,
    )


def per_device(
    positions,
    samples,
    leaf_basis,
    transfer_one,
    transfer_two,
    couplings,
    near_lists,
    far_zero,
    far_one,
    far_two,
):
    nx = lax.axis_size("qx")
    ny = lax.axis_size("qy")
    down_x = [(k, k + 1) for k in range(nx - 1)]
    up_x = [(k + 1, k) for k in range(nx - 1)]
    down_y = [(k, k + 1) for k in range(ny - 1)]
    up_y = [(k + 1, k) for k in range(ny - 1)]

    up, down, left, right, upper = coefficients(samples, leaf_basis, transfer_one, transfer_two)

    above = lax.ppermute(down, "qx", down_x)
    below = lax.ppermute(up, "qx", up_x)
    pair = lax.ppermute(upper, "qy", [(k, k ^ 1) for k in range(ny)])
    sites = positions.reshape(-1, 2, 256)
    flat_samples = samples.reshape(16, 256, 256)
    near_a, halo_a = near_own(0, 4 * nx, 4 * ny, near_lists, sites, flat_samples)
    pair, above, below, left, right, near_a = lax.optimization_barrier(
        (pair, above, below, left, right, near_a)
    )
    outward = [(k, k + 2) for k in range(0, ny - 2, 2)] + [(k + 2, k) for k in range(1, ny - 2, 2)]
    inward = [(k + 2, k) for k in range(0, ny - 2, 2)] + [(k, k + 2) for k in range(1, ny - 2, 2)]
    to_out, to_in = assembled(
        "pair_payload", (upper, pair), [(1, 0, 5), (0, 4, 1)], [(0, 6), (4, 6)]
    )
    on_left = lax.ppermute(right, "qy", down_y)
    on_right = lax.ppermute(left, "qy", up_y)
    outer = lax.ppermute(to_out, "qy", outward)
    inner = lax.ppermute(to_in, "qy", inward)
    near_b, halo_b = near_own(8, 4 * nx, 4 * ny, near_lists, sites, flat_samples)
    inner, outer, near_b = lax.optimization_barrier((inner, outer, near_b))
    row, one_row, two_row = assembled(
        "row_payload",
        (upper, pair, outer, inner),
        [(0, 0, 4), (1, 0, 4), (2, 0, 4)]
        + [(0, 4, 1), (1, 4, 1), (2, 5, 1), (2, 4, 1), (3, 1, 1), (3, 0, 1)],
        [(0, 18), (0, 12), (12, 18)],
    )
    swap_x = [(k, k ^ 1) for k in range(nx)]
    cross_x = [(k, k + 1) for k in range(1, nx - 1, 2)] + [(k + 1, k) for k in range(1, nx - 1, 2)]
    if nx == 4:
        others = [lax.ppermute(two_row, "qx", [(k, k ^ 2) for k in range(nx)])]
    else:
        others = [
            lax.ppermute(two_row, "qx", [(k, k + 2) for k in range(nx - 2)]),
            lax.ppermute(two_row, "qx", [(k + 2, k) for k in range(nx - 2)]),
        ]
    row_d = lax.ppermute(one_row, "qx", cross_x)
    row_e = lax.ppermute(row, "qx", swap_x)
    field, flags = rows_level(4 * ny, far_zero, couplings, up, down, above, below)
    others, field = lax.optimization_barrier((others, field))
    others = others + [lax.ppermute(x, "qx", swap_x) for x in others]
    on_left, on_right, field = lax.optimization_barrier((on_left, on_right, field))

    corner_down, corner_up = assembled(
        "corner_payload",
        (on_left, on_right),
        [(0, 4, 4), (1, 4, 4), (0, 11, 1), (1, 11, 1)]
        + [(0, 0, 4), (1, 0, 4), (0, 8, 1), (1, 8, 1)],
        [(0, 10), (10, 20)],
    )
    corner_above = lax.ppermute(corner_down, "qx", down_x)
    corner_below = lax.ppermute(corner_up, "qx", up_x)
    down_one = upper_levels(
        ny, far_one, far_two, couplings, transfer_two, row, row_e, row_d, others
    )
    result = outer_level(
        flags,
        couplings,
        transfer_one,
        leaf_basis,
        down_one,
        field,
        near_a,
        near_b,
        halo_a,
        halo_b,
        on_left,
        on_right,
        above,
        below,
        corner_above,
        corner_below,
    )
    return result.reshape(4, 4, 256, 256)


def solution(mesh):
    return jax.shard_map(
        per_device,
        mesh=mesh,
        in_specs=(
            P(),
            P("qx", "qy", None, None),
            P("qx", "qy", None, None),
            P("qx", "qy", None, None),
            P("qx", "qy", None, None),
            P(),
            P("qx", "qy", None),
            P("qx", "qy", None),
            P("qx", "qy", None),
            P("qx", "qy", None),
        ),
        out_specs=P("qx", "qy", None, None),
        check_vma=False,
    )
```

```python
import functools

import jax
import jax.numpy as jnp
import numpy as np
from jax import lax
from jax.experimental import pallas as pl
from jax.experimental.pallas import tpu as pltpu
from jax.sharding import PartitionSpec as P

root_three = 1.7320508075688772
length_scale = 1.0
VMEM = pltpu.VMEM
SMEM = pltpu.SMEM
F32 = jnp.float32
BF16 = jnp.bfloat16
BIG = 64 * 1024 * 1024 - 256 * 1024


def nn(a, b):
    return lax.dot_general(a, b, (((1,), (0,)), ((), ())), preferred_element_type=F32)


def nt(a, b):
    return lax.dot_general(a, b, (((1,), (1,)), ((), ())), preferred_element_type=F32)


def tn(a, b):
    return lax.dot_general(a, b, (((0,), (0,)), ((), ())), preferred_element_type=F32)


def params():
    return pltpu.CompilerParams(vmem_limit_bytes=BIG)


def cost(products, bytes_accessed):
    return pl.CostEstimate(
        flops=products * 2 * 256**3 // 8, bytes_accessed=bytes_accessed // 8, transcendentals=0
    )


def half_offsets():
    kept = []
    for u in range(-3, 4):
        for v in range(-3, 4):
            if max(abs(u), abs(v)) >= 2 and (u > 0 or (u == 0 and v > 0)):
                kept.append((u, v))
    return kept


HALF_OFFSETS = half_offsets()


def class_plan(a, b):
    plain, turned = [], []
    for w in range(36):
        u, v = w // 6 - 2 - a, w % 6 - 2 - b
        if max(abs(u), abs(v)) < 2:
            continue
        if (u, v) in HALF_OFFSETS:
            plain.append((w, HALF_OFFSETS.index((u, v))))
        else:
            turned.append((w, HALF_OFFSETS.index((-u, -v))))
    return plain, turned


LOG2E = 1.4426950408889634
TILE_SCALE = 256 ** -0.5


def tiles(n, dtype=BF16):
    return jax.ShapeDtypeStruct((n, 256, 256), dtype)


ANY_SPEC = pl.BlockSpec(memory_space=pltpu.HBM)
SMEM_SPEC = pl.BlockSpec(memory_space=SMEM)
VMEM_SPEC = pl.BlockSpec(memory_space=VMEM)


class Copies:
    def __init__(self, sems):
        self.sems = sems
        self.started = []

    def start(self, src, dst):
        copy = pltpu.make_async_copy(src, dst, self.sems.at[len(self.started)])
        copy.start()
        self.started.append(copy)
        return copy

    def wait(self):
        for copy in self.started:
            copy.wait()


def coef_kernel(
    samples, basis, t_one, t_two, up, down, left, right, upper,
    sv, bv, t1v, t2v, cv, uv, in_sems, out_sems,
):
    into = Copies(in_sems)
    out = Copies(out_sems)
    rows = []
    for x in range(4):
        rows.append(
            (
                into.start(samples.at[x], sv.at[x]),
                into.start(basis.at[x], bv.at[x]),
                into.start(t_one.at[x], t1v.at[x]),
            )
        )
    last = into.start(t_two, t2v)
    for x in range(4):
        rows[x][0].wait()
        rows[x][1].wait()
        for y in range(4):
            cv[x * 4 + y] = tn(sv[x, y], bv[x, y]).astype(BF16)
        own = cv.at[4 * x : 4 * x + 4]
        out.start(own, (up if x < 2 else down).at[4 * (x % 2) : 4 * (x % 2) + 4])
        out.start(cv.at[4 * x : 4 * x + 2], left.at[2 * x : 2 * x + 2])
        out.start(cv.at[4 * x + 2 : 4 * x + 4], right.at[2 * x : 2 * x + 2])
        out.start(sv.at[x, 0], left.at[8 + x])
        out.start(sv.at[x, 3], right.at[8 + x])
        if x == 0:
            out.start(sv.at[x], up.at[8:12])
        if x == 3:
            out.start(sv.at[x], down.at[8:12])
        if x % 2 == 1:
            rows[x - 1][2].wait()
            rows[x][2].wait()
            for y in range(2):
                kids = [(x - 1 + a, 2 * y + b) for a in range(2) for b in range(2)]
                lhs = jnp.concatenate([cv[k * 4 + m] for k, m in kids], axis=1)
                rhs = jnp.concatenate([t1v[k] for k in kids], axis=0)
                uv[x // 2 * 2 + y] = nn(lhs, rhs).astype(BF16)
    last.wait()
    lhs = jnp.concatenate([uv[k] for k in range(4)], axis=1)
    rhs = jnp.concatenate([t2v[k // 2, k % 2] for k in range(4)], axis=0)
    uv[4] = nn(lhs, rhs).astype(BF16)
    out.start(uv, upper)
    out.wait()


def coefficients(samples, basis, t_one, t_two):
    return pl.pallas_call(
        coef_kernel,
        out_shape=(tiles(12), tiles(12), tiles(12), tiles(12), tiles(5)),
        in_specs=[ANY_SPEC] * 4,
        out_specs=[ANY_SPEC] * 5,
        scratch_shapes=[
            VMEM((4, 4, 256, 256), BF16),
            VMEM((4, 4, 256, 256), BF16),
            VMEM((4, 4, 256, 256), BF16),
            VMEM((2, 2, 256, 256), BF16),
            VMEM((16, 256, 256), BF16),
            VMEM((5, 256, 256), BF16),
            pltpu.SemaphoreType.DMA((13,)),
            pltpu.SemaphoreType.DMA((23,)),
        ],
        compiler_params=params(),
        cost_estimate=cost(170, 12 << 20),
        name="coefficients",
    )(samples, basis, t_one, t_two)


def assembled(name, sources, pieces, ranges):
    count = sum(n for _, _, n in pieces)

    def kernel(*refs):
        ins, outs = refs[: len(sources)], refs[len(sources) : -3]
        held, in_sems, out_sems = refs[-3:]
        into = Copies(in_sems)
        at = 0
        for source, first, n in pieces:
            into.start(ins[source].at[first : first + n], held.at[at : at + n])
            at += n
        into.wait()
        out = Copies(out_sems)
        for (first, last), ref in zip(ranges, outs):
            out.start(held.at[first:last], ref)
        out.wait()

    return pl.pallas_call(
        kernel,
        out_shape=[tiles(last - first) for first, last in ranges],
        in_specs=[ANY_SPEC] * len(sources),
        out_specs=[ANY_SPEC] * len(ranges),
        scratch_shapes=[
            VMEM((count, 256, 256), BF16),
            pltpu.SemaphoreType.DMA((len(pieces),)),
            pltpu.SemaphoreType.DMA((len(ranges),)),
        ],
        compiler_params=params(),
        cost_estimate=cost(35, 0),
        name=name,
    )(*sources)


def halo_places():
    numbers = {}
    for r in range(4):
        for c in range(4):
            for k in range(9):
                y, x = r + k // 3 - 1, c + k % 3 - 1
                if not (0 <= y < 4 and 0 <= x < 4):
                    numbers[r * 4 + c, k] = len(numbers)
    return numbers


HALO = halo_places()
N_HALO = len(HALO) // 2


def split3(x):
    first = x.astype(BF16).astype(F32)
    rest = x - first
    second = rest.astype(BF16).astype(F32)
    return first, second, rest - second


def site_features(x, y):
    n = lax.broadcasted_iota(jnp.int32, (8, 256), 0)
    square = x * x + y * y
    target, source = [], []
    for parts in (split3(x), split3(y)):
        first, second, third = parts
        target.append(jnp.where(n < 3, first, jnp.where(n < 5, second, jnp.where(n < 6, third, 0.0))))
        other = jnp.where(
            (n == 0) | (n == 3) | (n == 5),
            first,
            jnp.where((n == 1) | (n == 4), second, jnp.where(n == 2, third, 0.0)),
        )
        source.append(-2.0 * other)
    first, second, third = split3(square)
    low = jnp.where(n == 0, first, jnp.where(n == 1, second, third))
    high = jnp.where(n == 3, first, jnp.where(n == 4, second, third))
    one = jnp.where(n < 6, 1.0, 0.0)
    target.append(jnp.where(n < 3, low, one))
    source.append(jnp.where(n < 3, 1.0, jnp.where(n < 6, high, 0.0)))
    zero = jnp.zeros((8, 256), F32)
    return jnp.concatenate(target + [zero], axis=0), jnp.concatenate(source + [zero], axis=0)


def near_kernel(
    first, with_far, grid_rows, grid_cols, lists, far_zero, positions, own, *rest
):
    if with_far:
        flags, couplings, up, down, above, below, near_out, halo_out, field_out = rest[:9]
        table, far_held, field, far_sems, field_sems = rest[9:14]
        rest = rest[14:]
    else:
        near_out, halo_out, flags = rest[:3]
        rest = rest[3:]
    held, target_feat, source_feat, halo, made, near, floors, sems, halo_sems, near_sems = rest
    copy = pltpu.make_async_copy(own, held, sems.at[0])
    copy.start()
    out = Copies(halo_sems)
    sums_out = Copies(near_sems)
    if with_far:
        far_in = Copies(far_sems)
        far_in.start(couplings.at[0], table)
        for n, src in enumerate((above, up, down, below)):
            far_in.start(src.at[0:8], far_held.at[8 * n : 8 * n + 8])
        far_held[32] = jnp.zeros((256, 256), BF16)
        field_copies = Copies(field_sems)
    first_row = lax.axis_index("qx") * 4
    first_col = lax.axis_index("qy") * 4
    scale = root_three / length_scale
    mid_row = first_row.astype(F32) + 2.0
    mid_col = first_col.astype(F32) + 2.0
    first_place = first // 4 * 6

    def features(n, carry):
        r = jnp.clip(first_row + (first_place + n) // 6 - 1, 0, grid_rows - 1)
        c = jnp.clip(first_col + n % 6 - 1, 0, grid_cols - 1)
        here = positions[r * grid_cols + c]
        target, source = site_features(
            (here[0:1] - mid_row) * scale, (here[1:2] - mid_col) * scale
        )
        target_feat[n] = target
        source_feat[n] = source.astype(BF16)
        return carry

    lax.fori_loop(0, 24, features, 0)

    if not with_far:

        def mark(t, carry):
            r, c = t // 4, t % 4
            mark_listed(
                lambda e: far_zero[r, c, e],
                flags,
                t,
                first_row + r // 2 * 2 - 2,
                first_col + c // 2 * 2 - 2,
                grid_cols,
            )
            return carry

        lax.fori_loop(0, 16, mark, 0)

    def make(m):
        t = first + m
        r, c = t // 4, t % 4
        slot = m % 2 * 9
        for k in range(9):
            floors[m * 10 + k] = 1e6
        for e in range(9):
            entry = lists[r, c, e]
            source_row = jnp.maximum(entry, 0) // grid_cols
            source_col = jnp.maximum(entry, 0) - source_row * grid_cols
            k = (source_row - first_row - r + 1) * 3 + source_col - first_col - c + 1
            floors[m * 10 + jnp.where(entry >= 0, k, 9)] = 1e-24
        place = (m // 4 + 1) * 6 + c + 1
        target = target_feat[place].T.astype(BF16)
        for k in range(9):
            square = nn(target, source_feat[place + (k // 3 - 1) * 6 + k % 3 - 1])
            square = jnp.maximum(square, floors[m * 10 + k])
            far = square * lax.rsqrt(square)
            tile = ((far + 1.0) * jnp.exp2(far * -LOG2E)).astype(BF16)
            if (t, k) in HALO:
                number = HALO[t, k] % N_HALO
                halo[number] = tile
                out.start(halo.at[number], halo_out.at[number])
            else:
                made[slot + k] = tile

    def use(m):
        t = first + m
        slot = m % 2 * 9
        found = [k for k in range(9) if (t, k) not in HALO]
        lhs = jnp.concatenate([made[slot + k] for k in found], axis=1)
        blocks = [held[t + (k // 3 - 1) * 4 + k % 3 - 1] for k in found]
        near[m] = nn(lhs, jnp.concatenate(blocks, axis=0))
        sums_out.start(near.at[m], near_out.at[m])

    make(0)
    copy.wait()
    if with_far:
        far_in.wait()
    for m in range(1, 8):
        make(m)
        if with_far and m % 2 == 1:
            a, b = m // 4, m // 2 % 2
            sums = level_zero_sums("inner", a, b, flags, table, far_held, 32)
            for p in PARENTS:
                t = number_of(a, b, p)
                field[t] = sums[p]
                field_copies.start(field.at[t], field_out.at[t])
        use(m - 1)
    use(7)
    out.wait()
    sums_out.wait()
    if with_far:
        field_copies.wait()


def near_call(first, grid_rows, grid_cols, lists, far_zero, positions, own, far=()):
    out_shape = [tiles(8, F32), tiles(N_HALO)]
    out_specs = [ANY_SPEC, ANY_SPEC]
    scratch = []
    if far:
        out_shape.append(tiles(16, F32))
        out_specs.append(ANY_SPEC)
        scratch = [
            VMEM((20, 256, 256), BF16),
            VMEM((33, 256, 256), BF16),
            VMEM((16, 256, 256), F32),
            pltpu.SemaphoreType.DMA((5,)),
            pltpu.SemaphoreType.DMA((16,)),
        ]
    else:
        out_shape.append(jax.ShapeDtypeStruct((16, 37), jnp.int32))
        out_specs.append(SMEM_SPEC)
    return pl.pallas_call(
        functools.partial(near_kernel, first, bool(far), grid_rows, grid_cols),
        out_shape=out_shape,
        in_specs=[SMEM_SPEC, SMEM_SPEC, VMEM_SPEC, ANY_SPEC]
        + ([SMEM_SPEC] + [ANY_SPEC] * 5 if far else []),
        out_specs=out_specs,
        scratch_shapes=scratch
        + [
            VMEM((16, 256, 256), BF16),
            VMEM((24, 32, 256), F32),
            VMEM((24, 32, 256), BF16),
            VMEM((N_HALO, 256, 256), BF16),
            VMEM((18, 256, 256), BF16),
            VMEM((8, 256, 256), F32),
            pltpu.SMEM((80,), F32),
            pltpu.SemaphoreType.DMA((1,)),
            pltpu.SemaphoreType.DMA((N_HALO,)),
            pltpu.SemaphoreType.DMA((8,)),
        ],
        compiler_params=params(),
        cost_estimate=cost(600 if far else 12000, 8 << 20),
        name="near_and_inner_far" if far else "near_first",
    )(lists, far_zero, positions, own, *far)


def mark_listed(entries, flags, n, first_row, first_col, grid_cols):
    for w in range(36):
        flags[n, w] = 0
    for e in range(27):
        entry = entries(e)
        row = jnp.maximum(entry, 0) // grid_cols
        col = jnp.maximum(entry, 0) - row * grid_cols
        w = (row - first_row) * 6 + col - first_col
        flags[n, jnp.where(entry >= 0, jnp.clip(w, 0, 35), 36)] = 1


def dot_group(held, couplings, turned, group):
    rows = len(group[0][1])
    lhs = [
        jnp.concatenate([held[places[n]] for _, places in group], axis=1) for n in range(rows)
    ]
    lhs = jnp.concatenate(lhs, axis=0) if rows > 1 else lhs[0]
    if turned:
        return nn(lhs, jnp.concatenate([couplings[k] for k, _ in group], axis=0))
    return nt(lhs, jnp.concatenate([couplings[k] for k, _ in group], axis=1))


def coupled(plan, couplings, held, places):
    total = None
    for turned in (0, 1):
        group = [(k, [places(w)]) for w, k in plan[turned]]
        part = dot_group(held, couplings, turned, group)
        total = part if total is None else total + part
    return total


def upper_kernel(grid_cols, n_others, far_one, far_two, couplings, t_two, *rest):
    row, row_e, row_d = rest[:3]
    others = rest[3 : 3 + 2 * n_others]
    down, held_one, held_two, field_two, flags, sems = rest[3 + 2 * n_others :]
    zero_one, zero_two = 36, 12 + 12 * n_others
    copies = Copies(sems)
    copies.start(row.at[12:18], held_two.at[0:6])
    copies.start(row_e.at[12:18], held_two.at[6:12])
    for n, other in enumerate(others):
        copies.start(other, held_two.at[12 + 6 * n : 18 + 6 * n])
    copies.start(row.at[0:12], held_one.at[0:12])
    copies.start(row_e.at[0:12], held_one.at[12:24])
    copies.start(row_d, held_one.at[24:36])
    held_one[zero_one] = jnp.zeros((256, 256), BF16)
    held_two[zero_two] = jnp.zeros((256, 256), BF16)
    i = lax.axis_index("qx")
    j = lax.axis_index("qy")
    a = i % 2
    b = j % 2
    for t in range(4):
        mark_listed(
            lambda e: far_one[t // 2, t % 2, e], flags, t, 2 * i - 2, 2 * j - 2, 2 * grid_cols
        )
    mark_listed(
        lambda e: far_two[0, 0, e], flags, 4, i // 2 * 2 - 2, j // 2 * 2 - 2, grid_cols
    )
    rows_at = []
    for r in range(6):
        if r // 2 == 1:
            rows_at.append(jnp.where(a == r % 2, 0, 6))
        else:
            n = 0 if r // 2 == 0 or n_others == 1 else 1
            rows_at.append(
                jnp.where(a == r % 2, 12 + 6 * n, 12 + 6 * (n_others + n))
            )
    z_at = [jnp.where(b == 0, 2, 4), 0, jnp.where(b == 0, 4, 2)]
    x_at = [b, 1 - b]

    def place_two(w):
        r, c = w // 6, w % 6
        place = rows_at[r] + z_at[c // 2] + x_at[c % 2]
        return jnp.where(flags[4, w] == 1, place, zero_two)

    row_at = [jnp.where(a == 0, 24, 12), 0, jnp.where(a == 0, 12, 24)]
    col_at = [jnp.where(b == 0, 8, 4), 0, jnp.where(b == 0, 4, 8)]

    def place_one(t, w):
        r, c = w // 6, w % 6
        place = row_at[r // 2] + col_at[c // 2] + (r % 2) * 2 + c % 2
        return jnp.where(flags[t, w] == 1, place, zero_one)

    for copy in copies.started[: 2 + 2 * n_others]:
        copy.wait()
    for u in range(2):
        for v in range(2):

            @pl.when((a == u) & (b == v))
            def _():
                field_two[...] = coupled(
                    class_plan(u, v), couplings.at[1], held_two, place_two
                ).astype(BF16)

    for copy in copies.started[2 + 2 * n_others :]:
        copy.wait()
    for u in range(2):
        for v in range(2):
            t = u * 2 + v
            field = coupled(
                class_plan(u, v), couplings.at[0], held_one, functools.partial(place_one, t)
            )
            down[t] = (field + nt(field_two[...], t_two[u, v])).astype(BF16)


def upper_levels(grid_cols, far_one, far_two, couplings, t_two, row, row_e, row_d, others):
    n_others = len(others) // 2
    return pl.pallas_call(
        functools.partial(upper_kernel, grid_cols, n_others),
        grid=(1,),
        out_shape=tiles(4),
        in_specs=[
            SMEM_SPEC,
            SMEM_SPEC,
            pl.BlockSpec(
                (pl.Element(2), pl.Element(20), pl.Element(256), pl.Element(256)),
                lambda g: (1, 0, 0, 0),
            ),
            pl.BlockSpec((2, 2, 256, 256), lambda g: (0, 0, 0, 0)),
        ]
        + [ANY_SPEC] * (3 + 2 * n_others),
        out_specs=pl.BlockSpec((4, 256, 256), lambda g: (0, 0, 0)),
        scratch_shapes=[
            VMEM((37, 256, 256), BF16),
            VMEM((13 + 12 * n_others, 256, 256), BF16),
            VMEM((256, 256), BF16),
            pltpu.SMEM((5, 37), jnp.int32),
            pltpu.SemaphoreType.DMA((5 + 2 * n_others,)),
        ],
        compiler_params=params(),
        cost_estimate=cost(340, 14 << 20),
        name="upper_levels",
    )(far_one, far_two, couplings, t_two, row, row_e, row_d, *others)


def source_of(x, y, w):
    r, c = 2 * x + w // 6, 2 * y + w % 6
    if 2 <= c < 6:
        return "inner", r * 4 + c - 2
    side = 0 if c < 2 else 1
    c = c if c < 2 else c - 6
    if 2 <= r < 6:
        return "outer", side * 8 + (r - 2) * 2 + c
    return "outer", (16 if r < 2 else 24) + side * 4 + (r if r < 2 else r - 6) * 2 + c


PARENTS = [(x, y) for x in range(2) for y in range(2)]


def number_of(a, b, parent):
    x, y = parent
    return (2 * x + a) * 4 + 2 * y + b


def level_zero_sums(kind, a, b, flags, couplings, held, zero):
    plan = class_plan(a, b)
    sums = {}
    for turned in (0, 1):
        groups = {}
        for w, k in plan[turned]:
            members = tuple(p for p in PARENTS if source_of(*p, w)[0] == kind)
            if members:
                groups.setdefault(members, []).append((w, k))
        for members, entries in groups.items():
            group = []
            for w, k in entries:
                places = [
                    jnp.where(flags[number_of(a, b, p), w] == 1, source_of(*p, w)[1], zero)
                    for p in members
                ]
                group.append((k, places))
            total = dot_group(held, couplings, turned, group)
            for n, p in enumerate(members):
                part = total[256 * n : 256 * n + 256]
                sums[p] = part if p not in sums else sums[p] + part
    return sums


def grouped(x):
    return x.reshape(2, 2, 2, 2, 256, 256)


CLASS_BLOCK = pl.BlockSpec((2, 1, 2, 1, 256, 256), lambda g: (0, g // 2, 0, g % 2, 0, 0))
COUPLING_BLOCK = pl.BlockSpec((1, 20, 256, 256), lambda g: (0, 0, 0, 0))
GROUPED_F32 = jax.ShapeDtypeStruct((2, 2, 2, 2, 256, 256), F32)


def each_class(step, body):
    for a in range(2):
        for b in range(2):
            pl.when(step == a * 2 + b)(functools.partial(body, a, b))


def near_place(r, c):
    rows_in, cols_in = 1 <= r < 5, 1 <= c < 5
    if rows_in:
        return (0 if c == 0 else 4) + r - 1
    if cols_in:
        return (8 if r == 0 else 12) + c - 1
    return 16 + (0 if r == 0 else 2) + (0 if c == 0 else 1)


def near_part(t, halo, held):
    r, c = t // 4, t % 4
    found = [k for k in range(9) if (t, k) in HALO]
    if not found:
        return None
    lhs = jnp.concatenate([halo[HALO[t, k]] for k in found], axis=1)
    rhs = jnp.concatenate([held[near_place(r + k // 3, c + k % 3)] for k in found], axis=0)
    return nn(lhs, rhs)


def outer_kernel(
    flags, couplings, t_one, basis, down_one, field, near_a, near_b, halo_a, halo_b,
    left, right, above, below, corner_above, corner_below, out, held, near_held, halo, sems,
):
    step = pl.program_id(0)

    def copies():
        pairs = []
        for n, src in enumerate((left, right, corner_above, corner_below)):
            pairs.append((src.at[0:8], held.at[8 * n : 8 * n + 8]))
        for n, src in enumerate((left, right, above, below)):
            pairs.append((src.at[8:12], near_held.at[4 * n : 4 * n + 4]))
        pairs.append((corner_above.at[8:10], near_held.at[16:18]))
        pairs.append((corner_below.at[8:10], near_held.at[18:20]))
        pairs.append((halo_a, halo.at[0:N_HALO]))
        pairs.append((halo_b, halo.at[N_HALO : 2 * N_HALO]))
        return [pltpu.make_async_copy(src, dst, sems.at[n]) for n, (src, dst) in enumerate(pairs)]

    @pl.when(step == 0)
    def _():
        started = copies()
        for copy in started:
            copy.start()
        held[32] = jnp.zeros((256, 256), BF16)
        for copy in started[:4]:
            copy.wait()

    def body(a, b):
        sums = level_zero_sums("outer", a, b, flags, couplings.at[0], held, 32)
        if a == 0 and b == 0:
            for copy in copies()[4:]:
                copy.wait()
        for x, y in PARENTS:
            total = field[x, 0, y, 0] + sums[x, y]
            total = total + nt(down_one[x * 2 + y], t_one[x, 0, y, 0])
            far = nt(basis[x, 0, y, 0], total.astype(BF16))
            near = (near_b if x else near_a)[0, y, 0]
            part = near_part(number_of(a, b, (x, y)), halo, near_held)
            if part is not None:
                near = near + part
            out[x, 0, y, 0] = (near * TILE_SCALE + far).astype(BF16)

    each_class(step, body)


HALF_BLOCK = pl.BlockSpec((1, 2, 1, 256, 256), lambda g: (g // 2, 0, g % 2, 0, 0))


def outer_level(
    flags, couplings, t_one, basis, down_one, field, near_a, near_b, halo_a, halo_b, *received
):
    half = lambda x: x.reshape(2, 2, 2, 256, 256)
    return pl.pallas_call(
        outer_kernel,
        grid=(4,),
        out_shape=jax.ShapeDtypeStruct((2, 2, 2, 2, 256, 256), BF16),
        in_specs=[
            SMEM_SPEC,
            COUPLING_BLOCK,
            CLASS_BLOCK,
            CLASS_BLOCK,
            pl.BlockSpec((4, 256, 256), lambda g: (0, 0, 0)),
            CLASS_BLOCK,
            HALF_BLOCK,
            HALF_BLOCK,
        ]
        + [ANY_SPEC] * 8,
        out_specs=CLASS_BLOCK,
        scratch_shapes=[
            VMEM((33, 256, 256), BF16),
            VMEM((20, 256, 256), BF16),
            VMEM((2 * N_HALO, 256, 256), BF16),
            pltpu.SemaphoreType.DMA((12,)),
        ],
        compiler_params=params(),
        cost_estimate=cost(500, 34 << 20),
        name="leaf_outer",
    )(
        flags, couplings, grouped(t_one), grouped(basis), down_one, field, half(near_a),
        half(near_b), halo_a, halo_b, *received,
    )


def per_device(
    positions,
    samples,
    leaf_basis,
    transfer_one,
    transfer_two,
    couplings,
    near_lists,
    far_zero,
    far_one,
    far_two,
):
    nx = lax.axis_size("qx")
    ny = lax.axis_size("qy")
    down_x = [(k, k + 1) for k in range(nx - 1)]
    up_x = [(k + 1, k) for k in range(nx - 1)]
    down_y = [(k, k + 1) for k in range(ny - 1)]
    up_y = [(k + 1, k) for k in range(ny - 1)]

    up, down, left, right, upper = coefficients(samples, leaf_basis, transfer_one, transfer_two)

    pair = lax.ppermute(upper, "qy", [(k, k ^ 1) for k in range(ny)])
    sites = positions.reshape(-1, 2, 256)
    flat_samples = samples.reshape(16, 256, 256)
    near_a, halo_a, flags = near_call(
        0, 4 * nx, 4 * ny, near_lists, far_zero, sites, flat_samples
    )
    above = lax.ppermute(down, "qx", down_x)
    below = lax.ppermute(up, "qx", up_x)
    pair, above, below, left, right, near_a = lax.optimization_barrier(
        (pair, above, below, left, right, near_a)
    )
    outward = [(k, k + 2) for k in range(0, ny - 2, 2)] + [(k + 2, k) for k in range(1, ny - 2, 2)]
    inward = [(k + 2, k) for k in range(0, ny - 2, 2)] + [(k, k + 2) for k in range(1, ny - 2, 2)]
    (across,) = assembled("pair_payload", (upper, pair), [(1, 0, 5), (0, 4, 1)], [(0, 6)])
    outer = lax.ppermute(across, "qy", outward)
    inner = lax.ppermute(across, "qy", inward)
    on_left = lax.ppermute(right, "qy", down_y)
    on_right = lax.ppermute(left, "qy", up_y)
    across, above, below = lax.optimization_barrier((across, above, below))
    near_b, halo_b, field = near_call(
        8,
        4 * nx,
        4 * ny,
        near_lists,
        far_zero,
        sites,
        flat_samples,
        (flags, couplings, up, down, above, below),
    )
    inner, outer, near_b = lax.optimization_barrier((inner, outer, near_b))
    row, one_row, two_row = assembled(
        "row_payload",
        (upper, pair, outer, inner),
        [(0, 0, 4), (1, 0, 4), (2, 0, 4)]
        + [(0, 4, 1), (1, 4, 1), (2, 5, 1), (2, 4, 1), (3, 5, 1), (3, 4, 1)],
        [(0, 18), (0, 12), (12, 18)],
    )
    swap_x = [(k, k ^ 1) for k in range(nx)]
    cross_x = [(k, k + 1) for k in range(1, nx - 1, 2)] + [(k + 1, k) for k in range(1, nx - 1, 2)]
    if nx == 4:
        others = [lax.ppermute(two_row, "qx", [(k, k ^ 2) for k in range(nx)])]
    else:
        others = [
            lax.ppermute(two_row, "qx", [(k, k + 2) for k in range(nx - 2)]),
            lax.ppermute(two_row, "qx", [(k + 2, k) for k in range(nx - 2)]),
        ]
    row_d = lax.ppermute(one_row, "qx", cross_x)
    row_e = lax.ppermute(row, "qx", swap_x)
    others = others + [lax.ppermute(x, "qx", swap_x) for x in others]

    corner_down, corner_up = assembled(
        "corner_payload",
        (on_left, on_right),
        [(0, 4, 4), (1, 4, 4), (0, 11, 1), (1, 11, 1)]
        + [(0, 0, 4), (1, 0, 4), (0, 8, 1), (1, 8, 1)],
        [(0, 10), (10, 20)],
    )
    corner_above = lax.ppermute(corner_down, "qx", down_x)
    corner_below = lax.ppermute(corner_up, "qx", up_x)
    down_one = upper_levels(
        ny, far_one, far_two, couplings, transfer_two, row, row_e, row_d, others
    )
    result = outer_level(
        flags,
        couplings,
        transfer_one,
        leaf_basis,
        down_one,
        grouped(field),
        near_a,
        near_b,
        halo_a,
        halo_b,
        on_left,
        on_right,
        above,
        below,
        corner_above,
        corner_below,
    )
    return result.reshape(4, 4, 256, 256)


def solution(mesh):
    return jax.shard_map(
        per_device,
        mesh=mesh,
        in_specs=(
            P(),
            P("qx", "qy", None, None),
            P("qx", "qy", None, None),
            P("qx", "qy", None, None),
            P("qx", "qy", None, None),
            P(),
            P("qx", "qy", None),
            P("qx", "qy", None),
            P("qx", "qy", None),
            P("qx", "qy", None),
        ),
        out_specs=P("qx", "qy", None, None),
        check_vma=False,
    )
```

```python
import functools

import jax
import jax.numpy as jnp
import numpy as np
from jax import lax
from jax.experimental import pallas as pl
from jax.experimental.pallas import tpu as pltpu
from jax.sharding import PartitionSpec as P

root_three = 1.7320508075688772
length_scale = 1.0
VMEM = pltpu.VMEM
SMEM = pltpu.SMEM
F32 = jnp.float32
BF16 = jnp.bfloat16
BIG = 64 * 1024 * 1024 - 256 * 1024


def nn(a, b):
    return lax.dot_general(a, b, (((1,), (0,)), ((), ())), preferred_element_type=F32)


def nt(a, b):
    return lax.dot_general(a, b, (((1,), (1,)), ((), ())), preferred_element_type=F32)


def tn(a, b):
    return lax.dot_general(a, b, (((0,), (0,)), ((), ())), preferred_element_type=F32)


def params():
    return pltpu.CompilerParams(vmem_limit_bytes=BIG)


def cost(products, bytes_accessed):
    return pl.CostEstimate(
        flops=products * 2 * 256**3 // 8, bytes_accessed=bytes_accessed // 8, transcendentals=0
    )


def half_offsets():
    kept = []
    for u in range(-3, 4):
        for v in range(-3, 4):
            if max(abs(u), abs(v)) >= 2 and (u > 0 or (u == 0 and v > 0)):
                kept.append((u, v))
    return kept


HALF_OFFSETS = half_offsets()


def class_plan(a, b):
    plain, turned = [], []
    for w in range(36):
        u, v = w // 6 - 2 - a, w % 6 - 2 - b
        if max(abs(u), abs(v)) < 2:
            continue
        if (u, v) in HALF_OFFSETS:
            plain.append((w, HALF_OFFSETS.index((u, v))))
        else:
            turned.append((w, HALF_OFFSETS.index((-u, -v))))
    return plain, turned


LOG2E = 1.4426950408889634
TILE_SCALE = 256 ** -0.5


def tiles(n, dtype=BF16):
    return jax.ShapeDtypeStruct((n, 256, 256), dtype)


ANY_SPEC = pl.BlockSpec(memory_space=pltpu.HBM)
SMEM_SPEC = pl.BlockSpec(memory_space=SMEM)
VMEM_SPEC = pl.BlockSpec(memory_space=VMEM)


class Copies:
    def __init__(self, sems):
        self.sems = sems
        self.started = []

    def start(self, src, dst):
        copy = pltpu.make_async_copy(src, dst, self.sems.at[len(self.started)])
        copy.start()
        self.started.append(copy)
        return copy

    def wait(self):
        for copy in self.started:
            copy.wait()


def coef_kernel(
    samples, basis, t_one, t_two, up, down, left, right, upper,
    sv, bv, t1v, t2v, cv, uv, in_sems, out_sems,
):
    into = Copies(in_sems)
    out = Copies(out_sems)
    rows = []
    for x in range(4):
        rows.append(
            (
                into.start(samples.at[x], sv.at[x]),
                into.start(basis.at[x], bv.at[x]),
                into.start(t_one.at[x], t1v.at[x]),
            )
        )
    last = into.start(t_two, t2v)
    for x in range(4):
        rows[x][0].wait()
        rows[x][1].wait()
        for y in range(4):
            cv[x * 4 + y] = tn(sv[x, y], bv[x, y]).astype(BF16)
        own = cv.at[4 * x : 4 * x + 4]
        out.start(own, (up if x < 2 else down).at[4 * (x % 2) : 4 * (x % 2) + 4])
        out.start(cv.at[4 * x : 4 * x + 2], left.at[2 * x : 2 * x + 2])
        out.start(cv.at[4 * x + 2 : 4 * x + 4], right.at[2 * x : 2 * x + 2])
        out.start(sv.at[x, 0], left.at[8 + x])
        out.start(sv.at[x, 3], right.at[8 + x])
        if x == 0:
            out.start(sv.at[x], up.at[8:12])
        if x == 3:
            out.start(sv.at[x], down.at[8:12])
        if x % 2 == 1:
            rows[x - 1][2].wait()
            rows[x][2].wait()
            for y in range(2):
                kids = [(x - 1 + a, 2 * y + b) for a in range(2) for b in range(2)]
                lhs = jnp.concatenate([cv[k * 4 + m] for k, m in kids], axis=1)
                rhs = jnp.concatenate([t1v[k] for k in kids], axis=0)
                uv[x // 2 * 2 + y] = nn(lhs, rhs).astype(BF16)
    last.wait()
    lhs = jnp.concatenate([uv[k] for k in range(4)], axis=1)
    rhs = jnp.concatenate([t2v[k // 2, k % 2] for k in range(4)], axis=0)
    uv[4] = nn(lhs, rhs).astype(BF16)
    out.start(uv, upper)
    out.wait()


def coefficients(samples, basis, t_one, t_two):
    return pl.pallas_call(
        coef_kernel,
        out_shape=(tiles(12), tiles(12), tiles(12), tiles(12), tiles(5)),
        in_specs=[ANY_SPEC] * 4,
        out_specs=[ANY_SPEC] * 5,
        scratch_shapes=[
            VMEM((4, 4, 256, 256), BF16),
            VMEM((4, 4, 256, 256), BF16),
            VMEM((4, 4, 256, 256), BF16),
            VMEM((2, 2, 256, 256), BF16),
            VMEM((16, 256, 256), BF16),
            VMEM((5, 256, 256), BF16),
            pltpu.SemaphoreType.DMA((13,)),
            pltpu.SemaphoreType.DMA((23,)),
        ],
        compiler_params=params(),
        cost_estimate=cost(170, 12 << 20),
        name="coefficients",
    )(samples, basis, t_one, t_two)


def assembled(name, sources, pieces, ranges, stated=35):
    count = sum(n for _, _, n in pieces)

    def kernel(*refs):
        ins, outs = refs[: len(sources)], refs[len(sources) : -3]
        held, in_sems, out_sems = refs[-3:]
        into = Copies(in_sems)
        at = 0
        for source, first, n in pieces:
            into.start(ins[source].at[first : first + n], held.at[at : at + n])
            at += n
        into.wait()
        out = Copies(out_sems)
        for (first, last), ref in zip(ranges, outs):
            out.start(held.at[first:last], ref)
        out.wait()

    return pl.pallas_call(
        kernel,
        out_shape=[tiles(last - first) for first, last in ranges],
        in_specs=[ANY_SPEC] * len(sources),
        out_specs=[ANY_SPEC] * len(ranges),
        scratch_shapes=[
            VMEM((count, 256, 256), BF16),
            pltpu.SemaphoreType.DMA((len(pieces),)),
            pltpu.SemaphoreType.DMA((len(ranges),)),
        ],
        compiler_params=params(),
        cost_estimate=cost(stated, 0),
        name=name,
    )(*sources)


def halo_places():
    numbers = {}
    for r in range(4):
        for c in range(4):
            for k in range(9):
                y, x = r + k // 3 - 1, c + k % 3 - 1
                if not (0 <= y < 4 and 0 <= x < 4):
                    numbers[r * 4 + c, k] = len(numbers)
    return numbers


HALO = halo_places()
N_HALO = len(HALO) // 2


def split3(x):
    first = x.astype(BF16).astype(F32)
    rest = x - first
    second = rest.astype(BF16).astype(F32)
    return first, second, rest - second


def site_features(x, y):
    n = lax.broadcasted_iota(jnp.int32, (8, 256), 0)
    square = x * x + y * y
    target, source = [], []
    for parts in (split3(x), split3(y)):
        first, second, third = parts
        target.append(jnp.where(n < 3, first, jnp.where(n < 5, second, jnp.where(n < 6, third, 0.0))))
        other = jnp.where(
            (n == 0) | (n == 3) | (n == 5),
            first,
            jnp.where((n == 1) | (n == 4), second, jnp.where(n == 2, third, 0.0)),
        )
        source.append(-2.0 * other)
    first, second, third = split3(square)
    low = jnp.where(n == 0, first, jnp.where(n == 1, second, third))
    high = jnp.where(n == 3, first, jnp.where(n == 4, second, third))
    one = jnp.where(n < 6, 1.0, 0.0)
    target.append(jnp.where(n < 3, low, one))
    source.append(jnp.where(n < 3, 1.0, jnp.where(n < 6, high, 0.0)))
    zero = jnp.zeros((8, 256), F32)
    return jnp.concatenate(target + [zero], axis=0), jnp.concatenate(source + [zero], axis=0)


def near_kernel(
    first, with_far, grid_rows, grid_cols, lists, far_zero, positions, own, *rest
):
    if with_far:
        flags, couplings, up, down, above, below, near_out, halo_out, field_out = rest[:9]
        table, far_held, field, far_sems, field_sems = rest[9:14]
        rest = rest[14:]
    else:
        near_out, halo_out, flags = rest[:3]
        rest = rest[3:]
    held, target_feat, source_feat, halo, made, near, floors, sems, halo_sems, near_sems = rest
    copy = pltpu.make_async_copy(own, held, sems.at[0])
    copy.start()
    out = Copies(halo_sems)
    sums_out = Copies(near_sems)
    if with_far:
        far_in = Copies(far_sems)
        far_in.start(couplings.at[0], table)
        for n, src in enumerate((above, up, down, below)):
            far_in.start(src.at[0:8], far_held.at[8 * n : 8 * n + 8])
        far_held[32] = jnp.zeros((256, 256), BF16)
        field_copies = Copies(field_sems)
    first_row = lax.axis_index("qx") * 4
    first_col = lax.axis_index("qy") * 4
    scale = root_three / length_scale
    mid_row = first_row.astype(F32) + 2.0
    mid_col = first_col.astype(F32) + 2.0
    first_place = first // 4 * 6

    def features(n, carry):
        r = jnp.clip(first_row + (first_place + n) // 6 - 1, 0, grid_rows - 1)
        c = jnp.clip(first_col + n % 6 - 1, 0, grid_cols - 1)
        here = positions[r * grid_cols + c]
        target, source = site_features(
            (here[0:1] - mid_row) * scale, (here[1:2] - mid_col) * scale
        )
        target_feat[n] = target
        source_feat[n] = source.astype(BF16)
        return carry

    lax.fori_loop(0, 24, features, 0)

    if not with_far:

        def mark(t, carry):
            r, c = t // 4, t % 4
            mark_listed(
                lambda e: far_zero[r, c, e],
                flags,
                t,
                first_row + r // 2 * 2 - 2,
                first_col + c // 2 * 2 - 2,
                grid_cols,
            )
            return carry

        lax.fori_loop(0, 16, mark, 0)

    def make(m):
        t = first + m
        r, c = t // 4, t % 4
        slot = m % 2 * 9
        for k in range(9):
            floors[m * 10 + k] = 1e6
        for e in range(9):
            entry = lists[r, c, e]
            source_row = jnp.maximum(entry, 0) // grid_cols
            source_col = jnp.maximum(entry, 0) - source_row * grid_cols
            k = (source_row - first_row - r + 1) * 3 + source_col - first_col - c + 1
            floors[m * 10 + jnp.where(entry >= 0, k, 9)] = 1e-24
        place = (m // 4 + 1) * 6 + c + 1
        target = target_feat[place].T.astype(BF16)
        for k in range(9):
            square = nn(target, source_feat[place + (k // 3 - 1) * 6 + k % 3 - 1])
            square = jnp.maximum(square, floors[m * 10 + k])
            far = square * lax.rsqrt(square)
            tile = ((far + 1.0) * jnp.exp2(far * -LOG2E)).astype(BF16)
            if (t, k) in HALO:
                number = HALO[t, k] % N_HALO
                halo[number] = tile
                out.start(halo.at[number], halo_out.at[number])
            else:
                made[slot + k] = tile

    def use(m):
        t = first + m
        slot = m % 2 * 9
        found = [k for k in range(9) if (t, k) not in HALO]
        lhs = jnp.concatenate([made[slot + k] for k in found], axis=1)
        blocks = [held[t + (k // 3 - 1) * 4 + k % 3 - 1] for k in found]
        near[m] = nn(lhs, jnp.concatenate(blocks, axis=0))
        sums_out.start(near.at[m], near_out.at[m])

    make(0)
    copy.wait()
    if with_far:
        far_in.wait()
    for m in range(1, 8):
        make(m)
        if with_far and m % 2 == 1:
            a, b = m // 4, m // 2 % 2
            sums = level_zero_sums("inner", a, b, flags, table, far_held, 32)
            for p in PARENTS:
                t = number_of(a, b, p)
                field[t] = sums[p]
                field_copies.start(field.at[t], field_out.at[t])
        use(m - 1)
    use(7)
    out.wait()
    sums_out.wait()
    if with_far:
        field_copies.wait()


def near_call(first, grid_rows, grid_cols, lists, far_zero, positions, own, far=()):
    out_shape = [tiles(8, F32), tiles(N_HALO)]
    out_specs = [ANY_SPEC, ANY_SPEC]
    scratch = []
    if far:
        out_shape.append(tiles(16, F32))
        out_specs.append(ANY_SPEC)
        scratch = [
            VMEM((20, 256, 256), BF16),
            VMEM((33, 256, 256), BF16),
            VMEM((16, 256, 256), F32),
            pltpu.SemaphoreType.DMA((5,)),
            pltpu.SemaphoreType.DMA((16,)),
        ]
    else:
        out_shape.append(jax.ShapeDtypeStruct((16, 37), jnp.int32))
        out_specs.append(SMEM_SPEC)
    return pl.pallas_call(
        functools.partial(near_kernel, first, bool(far), grid_rows, grid_cols),
        out_shape=out_shape,
        in_specs=[SMEM_SPEC, SMEM_SPEC, VMEM_SPEC, ANY_SPEC]
        + ([SMEM_SPEC] + [ANY_SPEC] * 5 if far else []),
        out_specs=out_specs,
        scratch_shapes=scratch
        + [
            VMEM((16, 256, 256), BF16),
            VMEM((24, 32, 256), F32),
            VMEM((24, 32, 256), BF16),
            VMEM((N_HALO, 256, 256), BF16),
            VMEM((18, 256, 256), BF16),
            VMEM((8, 256, 256), F32),
            pltpu.SMEM((80,), F32),
            pltpu.SemaphoreType.DMA((1,)),
            pltpu.SemaphoreType.DMA((N_HALO,)),
            pltpu.SemaphoreType.DMA((8,)),
        ],
        compiler_params=params(),
        cost_estimate=cost(600 if far else 12000, 8 << 20),
        name="near_and_inner_far" if far else "near_first",
    )(lists, far_zero, positions, own, *far)


def mark_listed(entries, flags, n, first_row, first_col, grid_cols):
    for w in range(36):
        flags[n, w] = 0
    for e in range(27):
        entry = entries(e)
        row = jnp.maximum(entry, 0) // grid_cols
        col = jnp.maximum(entry, 0) - row * grid_cols
        w = (row - first_row) * 6 + col - first_col
        flags[n, jnp.where(entry >= 0, jnp.clip(w, 0, 35), 36)] = 1


def dot_group(held, couplings, turned, group):
    rows = len(group[0][1])
    lhs = [
        jnp.concatenate([held[places[n]] for _, places in group], axis=1) for n in range(rows)
    ]
    lhs = jnp.concatenate(lhs, axis=0) if rows > 1 else lhs[0]
    if turned:
        return nn(lhs, jnp.concatenate([couplings[k] for k, _ in group], axis=0))
    return nt(lhs, jnp.concatenate([couplings[k] for k, _ in group], axis=1))


def coupled(plan, couplings, held, places):
    total = None
    for turned in (0, 1):
        group = [(k, [places(w)]) for w, k in plan[turned]]
        part = dot_group(held, couplings, turned, group)
        total = part if total is None else total + part
    return total


def upper_kernel(grid_cols, n_others, far_one, far_two, couplings, t_two, *rest):
    row, row_e, row_d = rest[:3]
    others = rest[3 : 3 + 2 * n_others]
    down, held_one, held_two, field_two, flags, sems = rest[3 + 2 * n_others :]
    zero_one, zero_two = 36, 12 + 12 * n_others
    copies = Copies(sems)
    copies.start(row.at[12:18], held_two.at[0:6])
    copies.start(row_e.at[12:18], held_two.at[6:12])
    for n, other in enumerate(others):
        copies.start(other, held_two.at[12 + 6 * n : 18 + 6 * n])
    copies.start(row.at[0:12], held_one.at[0:12])
    copies.start(row_e.at[0:12], held_one.at[12:24])
    copies.start(row_d, held_one.at[24:36])
    held_one[zero_one] = jnp.zeros((256, 256), BF16)
    held_two[zero_two] = jnp.zeros((256, 256), BF16)
    i = lax.axis_index("qx")
    j = lax.axis_index("qy")
    a = i % 2
    b = j % 2
    for t in range(4):
        mark_listed(
            lambda e: far_one[t // 2, t % 2, e], flags, t, 2 * i - 2, 2 * j - 2, 2 * grid_cols
        )
    mark_listed(
        lambda e: far_two[0, 0, e], flags, 4, i // 2 * 2 - 2, j // 2 * 2 - 2, grid_cols
    )
    rows_at = []
    for r in range(6):
        if r // 2 == 1:
            rows_at.append(jnp.where(a == r % 2, 0, 6))
        else:
            n = 0 if r // 2 == 0 or n_others == 1 else 1
            rows_at.append(
                jnp.where(a == r % 2, 12 + 6 * n, 12 + 6 * (n_others + n))
            )
    z_at = [jnp.where(b == 0, 2, 4), 0, jnp.where(b == 0, 4, 2)]
    x_at = [b, 1 - b]

    def place_two(w):
        r, c = w // 6, w % 6
        place = rows_at[r] + z_at[c // 2] + x_at[c % 2]
        return jnp.where(flags[4, w] == 1, place, zero_two)

    row_at = [jnp.where(a == 0, 24, 12), 0, jnp.where(a == 0, 12, 24)]
    col_at = [jnp.where(b == 0, 8, 4), 0, jnp.where(b == 0, 4, 8)]

    def place_one(t, w):
        r, c = w // 6, w % 6
        place = row_at[r // 2] + col_at[c // 2] + (r % 2) * 2 + c % 2
        return jnp.where(flags[t, w] == 1, place, zero_one)

    for copy in copies.started[: 2 + 2 * n_others]:
        copy.wait()
    for u in range(2):
        for v in range(2):

            @pl.when((a == u) & (b == v))
            def _():
                field_two[...] = coupled(
                    class_plan(u, v), couplings.at[1], held_two, place_two
                ).astype(BF16)

    for copy in copies.started[2 + 2 * n_others :]:
        copy.wait()
    for u in range(2):
        for v in range(2):
            t = u * 2 + v
            field = coupled(
                class_plan(u, v), couplings.at[0], held_one, functools.partial(place_one, t)
            )
            down[t] = (field + nt(field_two[...], t_two[u, v])).astype(BF16)


def upper_levels(grid_cols, far_one, far_two, couplings, t_two, row, row_e, row_d, others):
    n_others = len(others) // 2
    return pl.pallas_call(
        functools.partial(upper_kernel, grid_cols, n_others),
        grid=(1,),
        out_shape=tiles(4),
        in_specs=[
            SMEM_SPEC,
            SMEM_SPEC,
            pl.BlockSpec(
                (pl.Element(2), pl.Element(20), pl.Element(256), pl.Element(256)),
                lambda g: (1, 0, 0, 0),
            ),
            pl.BlockSpec((2, 2, 256, 256), lambda g: (0, 0, 0, 0)),
        ]
        + [ANY_SPEC] * (3 + 2 * n_others),
        out_specs=pl.BlockSpec((4, 256, 256), lambda g: (0, 0, 0)),
        scratch_shapes=[
            VMEM((37, 256, 256), BF16),
            VMEM((13 + 12 * n_others, 256, 256), BF16),
            VMEM((256, 256), BF16),
            pltpu.SMEM((5, 37), jnp.int32),
            pltpu.SemaphoreType.DMA((5 + 2 * n_others,)),
        ],
        compiler_params=params(),
        cost_estimate=cost(340, 14 << 20),
        name="upper_levels",
    )(far_one, far_two, couplings, t_two, row, row_e, row_d, *others)


def source_of(x, y, w):
    r, c = 2 * x + w // 6, 2 * y + w % 6
    if 2 <= c < 6:
        return "inner", r * 4 + c - 2
    side = 0 if c < 2 else 1
    c = c if c < 2 else c - 6
    if 2 <= r < 6:
        return "outer", side * 8 + (r - 2) * 2 + c
    return "outer", (16 if r < 2 else 24) + side * 4 + (r if r < 2 else r - 6) * 2 + c


PARENTS = [(x, y) for x in range(2) for y in range(2)]


def number_of(a, b, parent):
    x, y = parent
    return (2 * x + a) * 4 + 2 * y + b


def level_zero_sums(kind, a, b, flags, couplings, held, zero):
    plan = class_plan(a, b)
    sums = {}
    for turned in (0, 1):
        groups = {}
        for w, k in plan[turned]:
            members = tuple(p for p in PARENTS if source_of(*p, w)[0] == kind)
            if members:
                groups.setdefault(members, []).append((w, k))
        for members, entries in groups.items():
            group = []
            for w, k in entries:
                places = [
                    jnp.where(flags[number_of(a, b, p), w] == 1, source_of(*p, w)[1], zero)
                    for p in members
                ]
                group.append((k, places))
            total = dot_group(held, couplings, turned, group)
            for n, p in enumerate(members):
                part = total[256 * n : 256 * n + 256]
                sums[p] = part if p not in sums else sums[p] + part
    return sums


def grouped(x):
    return x.reshape(2, 2, 2, 2, 256, 256)


CLASS_BLOCK = pl.BlockSpec((2, 1, 2, 1, 256, 256), lambda g: (0, g // 2, 0, g % 2, 0, 0))
COUPLING_BLOCK = pl.BlockSpec((1, 20, 256, 256), lambda g: (0, 0, 0, 0))
GROUPED_F32 = jax.ShapeDtypeStruct((2, 2, 2, 2, 256, 256), F32)


def each_class(step, body):
    for a in range(2):
        for b in range(2):
            pl.when(step == a * 2 + b)(functools.partial(body, a, b))


def near_place(r, c):
    rows_in, cols_in = 1 <= r < 5, 1 <= c < 5
    if rows_in:
        return (0 if c == 0 else 4) + r - 1
    if cols_in:
        return (8 if r == 0 else 12) + c - 1
    return 16 + (0 if r == 0 else 2) + (0 if c == 0 else 1)


def near_part(t, halo, held):
    r, c = t // 4, t % 4
    found = [k for k in range(9) if (t, k) in HALO]
    if not found:
        return None
    lhs = jnp.concatenate([halo[HALO[t, k]] for k in found], axis=1)
    rhs = jnp.concatenate([held[near_place(r + k // 3, c + k % 3)] for k in found], axis=0)
    return nn(lhs, rhs)


def outer_kernel(
    flags, couplings, t_one, basis, down_one, field, near_a, near_b, halo_a, halo_b,
    left, right, above, below, corner_above, corner_below, out, held, near_held, halo, sems,
):
    step = pl.program_id(0)

    def copies():
        pairs = []
        for n, src in enumerate((left, right, corner_above, corner_below)):
            pairs.append((src.at[0:8], held.at[8 * n : 8 * n + 8]))
        for n, src in enumerate((left, right, above, below)):
            pairs.append((src.at[8:12], near_held.at[4 * n : 4 * n + 4]))
        pairs.append((corner_above.at[8:10], near_held.at[16:18]))
        pairs.append((corner_below.at[8:10], near_held.at[18:20]))
        pairs.append((halo_a, halo.at[0:N_HALO]))
        pairs.append((halo_b, halo.at[N_HALO : 2 * N_HALO]))
        return [pltpu.make_async_copy(src, dst, sems.at[n]) for n, (src, dst) in enumerate(pairs)]

    @pl.when(step == 0)
    def _():
        started = copies()
        for copy in started:
            copy.start()
        held[32] = jnp.zeros((256, 256), BF16)
        for copy in started[:4]:
            copy.wait()

    def body(a, b):
        sums = level_zero_sums("outer", a, b, flags, couplings.at[0], held, 32)
        if a == 0 and b == 0:
            for copy in copies()[4:]:
                copy.wait()
        for x, y in PARENTS:
            total = field[x, 0, y, 0] + sums[x, y]
            total = total + nt(down_one[x * 2 + y], t_one[x, 0, y, 0])
            far = nt(basis[x, 0, y, 0], total.astype(BF16))
            near = (near_b if x else near_a)[0, y, 0]
            part = near_part(number_of(a, b, (x, y)), halo, near_held)
            if part is not None:
                near = near + part
            out[x, 0, y, 0] = (near * TILE_SCALE + far).astype(BF16)

    each_class(step, body)


HALF_BLOCK = pl.BlockSpec((1, 2, 1, 256, 256), lambda g: (g // 2, 0, g % 2, 0, 0))


def outer_level(
    flags, couplings, t_one, basis, down_one, field, near_a, near_b, halo_a, halo_b, *received
):
    half = lambda x: x.reshape(2, 2, 2, 256, 256)
    return pl.pallas_call(
        outer_kernel,
        grid=(4,),
        out_shape=jax.ShapeDtypeStruct((2, 2, 2, 2, 256, 256), BF16),
        in_specs=[
            SMEM_SPEC,
            COUPLING_BLOCK,
            CLASS_BLOCK,
            CLASS_BLOCK,
            pl.BlockSpec((4, 256, 256), lambda g: (0, 0, 0)),
            CLASS_BLOCK,
            HALF_BLOCK,
            HALF_BLOCK,
        ]
        + [ANY_SPEC] * 8,
        out_specs=CLASS_BLOCK,
        scratch_shapes=[
            VMEM((33, 256, 256), BF16),
            VMEM((20, 256, 256), BF16),
            VMEM((2 * N_HALO, 256, 256), BF16),
            pltpu.SemaphoreType.DMA((12,)),
        ],
        compiler_params=params(),
        cost_estimate=cost(500, 34 << 20),
        name="leaf_outer",
    )(
        flags, couplings, grouped(t_one), grouped(basis), down_one, field, half(near_a),
        half(near_b), halo_a, halo_b, *received,
    )


def per_device(
    positions,
    samples,
    leaf_basis,
    transfer_one,
    transfer_two,
    couplings,
    near_lists,
    far_zero,
    far_one,
    far_two,
):
    nx = lax.axis_size("qx")
    ny = lax.axis_size("qy")
    down_x = [(k, k + 1) for k in range(nx - 1)]
    up_x = [(k + 1, k) for k in range(nx - 1)]
    down_y = [(k, k + 1) for k in range(ny - 1)]
    up_y = [(k + 1, k) for k in range(ny - 1)]

    up, down, left, right, upper = coefficients(samples, leaf_basis, transfer_one, transfer_two)

    pair = lax.ppermute(upper, "qy", [(k, k ^ 1) for k in range(ny)])
    sites = positions.reshape(-1, 2, 256)
    flat_samples = samples.reshape(16, 256, 256)
    near_a, halo_a, flags = near_call(
        0, 4 * nx, 4 * ny, near_lists, far_zero, sites, flat_samples
    )
    above = lax.ppermute(down, "qx", down_x)
    below = lax.ppermute(up, "qx", up_x)
    on_left = lax.ppermute(right, "qy", down_y)
    on_right = lax.ppermute(left, "qy", up_y)
    pair, above, below, near_a = lax.optimization_barrier((pair, above, below, near_a))
    outward = [(k, k + 2) for k in range(0, ny - 2, 2)] + [(k + 2, k) for k in range(1, ny - 2, 2)]
    inward = [(k + 2, k) for k in range(0, ny - 2, 2)] + [(k, k + 2) for k in range(1, ny - 2, 2)]
    to_out, to_in = assembled(
        "pair_payload", (upper, pair), [(1, 0, 5), (0, 4, 1)], [(0, 6), (4, 6)]
    )
    outer = lax.ppermute(to_out, "qy", outward)
    inner = lax.ppermute(to_in, "qy", inward)
    near_b, halo_b, field = near_call(
        8,
        4 * nx,
        4 * ny,
        near_lists,
        far_zero,
        sites,
        flat_samples,
        (flags, couplings, up, down, above, below),
    )
    inner, outer, near_b = lax.optimization_barrier((inner, outer, near_b))
    row, one_row, two_row = assembled(
        "row_payload",
        (upper, pair, outer, inner),
        [(0, 0, 4), (1, 0, 4), (2, 0, 4)]
        + [(0, 4, 1), (1, 4, 1), (2, 5, 1), (2, 4, 1), (3, 1, 1), (3, 0, 1)],
        [(0, 18), (0, 12), (12, 18)],
    )
    swap_x = [(k, k ^ 1) for k in range(nx)]
    cross_x = [(k, k + 1) for k in range(1, nx - 1, 2)] + [(k + 1, k) for k in range(1, nx - 1, 2)]
    if nx == 4:
        others = [lax.ppermute(two_row, "qx", [(k, k ^ 2) for k in range(nx)])]
    else:
        others = [
            lax.ppermute(two_row, "qx", [(k, k + 2) for k in range(nx - 2)]),
            lax.ppermute(two_row, "qx", [(k + 2, k) for k in range(nx - 2)]),
        ]
    row_d = lax.ppermute(one_row, "qx", cross_x)
    row_e = lax.ppermute(row, "qx", swap_x)
    others = others + [lax.ppermute(x, "qx", swap_x) for x in others]

    corner_down, corner_up = assembled(
        "corner_payload",
        (on_left, on_right),
        [(0, 4, 4), (1, 4, 4), (0, 11, 1), (1, 11, 1)]
        + [(0, 0, 4), (1, 0, 4), (0, 8, 1), (1, 8, 1)],
        [(0, 10), (10, 20)],
        stated=6000,
    )
    corner_above = lax.ppermute(corner_down, "qx", down_x)
    corner_below = lax.ppermute(corner_up, "qx", up_x)
    down_one = upper_levels(
        ny, far_one, far_two, couplings, transfer_two, row, row_e, row_d, others
    )
    result = outer_level(
        flags,
        couplings,
        transfer_one,
        leaf_basis,
        down_one,
        grouped(field),
        near_a,
        near_b,
        halo_a,
        halo_b,
        on_left,
        on_right,
        above,
        below,
        corner_above,
        corner_below,
    )
    return result.reshape(4, 4, 256, 256)


def solution(mesh):
    return jax.shard_map(
        per_device,
        mesh=mesh,
        in_specs=(
            P(),
            P("qx", "qy", None, None),
            P("qx", "qy", None, None),
            P("qx", "qy", None, None),
            P("qx", "qy", None, None),
            P(),
            P("qx", "qy", None),
            P("qx", "qy", None),
            P("qx", "qy", None),
            P("qx", "qy", None),
        ),
        out_specs=P("qx", "qy", None, None),
        check_vma=False,
    )
```

```python
import functools

import jax
import jax.numpy as jnp
import numpy as np
from jax import lax
from jax.experimental import pallas as pl
from jax.experimental.pallas import tpu as pltpu
from jax.sharding import PartitionSpec as P

root_three = 1.7320508075688772
length_scale = 1.0
VMEM = pltpu.VMEM
SMEM = pltpu.SMEM
F32 = jnp.float32
BF16 = jnp.bfloat16
BIG = 64 * 1024 * 1024 - 256 * 1024


def nn(a, b):
    return lax.dot_general(a, b, (((1,), (0,)), ((), ())), preferred_element_type=F32)


def nt(a, b):
    return lax.dot_general(a, b, (((1,), (1,)), ((), ())), preferred_element_type=F32)


def tn(a, b):
    return lax.dot_general(a, b, (((0,), (0,)), ((), ())), preferred_element_type=F32)


def params():
    return pltpu.CompilerParams(vmem_limit_bytes=BIG)


def cost(products, bytes_accessed):
    return pl.CostEstimate(
        flops=products * 2 * 256**3 // 8, bytes_accessed=bytes_accessed // 8, transcendentals=0
    )


def half_offsets():
    kept = []
    for u in range(-3, 4):
        for v in range(-3, 4):
            if max(abs(u), abs(v)) >= 2 and (u > 0 or (u == 0 and v > 0)):
                kept.append((u, v))
    return kept


HALF_OFFSETS = half_offsets()


def class_plan(a, b):
    plain, turned = [], []
    for w in range(36):
        u, v = w // 6 - 2 - a, w % 6 - 2 - b
        if max(abs(u), abs(v)) < 2:
            continue
        if (u, v) in HALF_OFFSETS:
            plain.append((w, HALF_OFFSETS.index((u, v))))
        else:
            turned.append((w, HALF_OFFSETS.index((-u, -v))))
    return plain, turned


LOG2E = 1.4426950408889634
TILE_SCALE = 256 ** -0.5


def tiles(n, dtype=BF16):
    return jax.ShapeDtypeStruct((n, 256, 256), dtype)


ANY_SPEC = pl.BlockSpec(memory_space=pltpu.HBM)
SMEM_SPEC = pl.BlockSpec(memory_space=SMEM)
VMEM_SPEC = pl.BlockSpec(memory_space=VMEM)


class Copies:
    def __init__(self, sems):
        self.sems = sems
        self.started = []

    def start(self, src, dst):
        copy = pltpu.make_async_copy(src, dst, self.sems.at[len(self.started)])
        copy.start()
        self.started.append(copy)
        return copy

    def wait(self):
        for copy in self.started:
            copy.wait()


def coef_kernel(
    samples, basis, t_one, t_two, up, down, left, right, s_left, s_right, upper, cell,
    sv, bv, t1v, t2v, cv, uv, in_sems, out_sems,
):
    into = Copies(in_sems)
    out = Copies(out_sems)
    rows = []
    for x in range(4):
        rows.append(
            (
                into.start(samples.at[x], sv.at[x]),
                into.start(basis.at[x], bv.at[x]),
                into.start(t_one.at[x], t1v.at[x]),
            )
        )
    last = into.start(t_two, t2v)
    for x in range(4):
        rows[x][0].wait()
        rows[x][1].wait()
        for y in range(4):
            cv[x * 4 + y] = tn(sv[x, y], bv[x, y]).astype(BF16)
        own = cv.at[4 * x : 4 * x + 4]
        out.start(own, (up if x < 2 else down).at[4 * (x % 2) : 4 * (x % 2) + 4])
        out.start(cv.at[4 * x : 4 * x + 2], left.at[2 * x : 2 * x + 2])
        out.start(cv.at[4 * x + 2 : 4 * x + 4], right.at[2 * x : 2 * x + 2])
        out.start(sv.at[x, 0], s_left.at[x])
        out.start(sv.at[x, 3], s_right.at[x])
        if x == 0:
            out.start(sv.at[x], up.at[8:12])
        if x == 3:
            out.start(sv.at[x], down.at[8:12])
        if x % 2 == 1:
            rows[x - 1][2].wait()
            rows[x][2].wait()
            for y in range(2):
                kids = [(x - 1 + a, 2 * y + b) for a in range(2) for b in range(2)]
                lhs = jnp.concatenate([cv[k * 4 + m] for k, m in kids], axis=1)
                rhs = jnp.concatenate([t1v[k] for k in kids], axis=0)
                uv[x // 2 * 2 + y] = nn(lhs, rhs).astype(BF16)
    last.wait()
    lhs = jnp.concatenate([uv[k] for k in range(4)], axis=1)
    rhs = jnp.concatenate([t2v[k // 2, k % 2] for k in range(4)], axis=0)
    uv[4] = nn(lhs, rhs).astype(BF16)
    out.start(uv, upper)
    out.start(uv.at[4:5], cell)
    out.wait()


def coefficients(samples, basis, t_one, t_two):
    return pl.pallas_call(
        coef_kernel,
        out_shape=[tiles(n) for n in (12, 12, 8, 8, 4, 4, 5, 1)],
        in_specs=[ANY_SPEC] * 4,
        out_specs=[ANY_SPEC] * 8,
        scratch_shapes=[
            VMEM((4, 4, 256, 256), BF16),
            VMEM((4, 4, 256, 256), BF16),
            VMEM((4, 4, 256, 256), BF16),
            VMEM((2, 2, 256, 256), BF16),
            VMEM((16, 256, 256), BF16),
            VMEM((5, 256, 256), BF16),
            pltpu.SemaphoreType.DMA((13,)),
            pltpu.SemaphoreType.DMA((24,)),
        ],
        compiler_params=params(),
        cost_estimate=cost(170, 12 << 20),
        name="coefficients",
    )(samples, basis, t_one, t_two)


def assembled(name, sources, pieces, ranges, stated=35):
    count = sum(n for _, _, n in pieces)

    def kernel(*refs):
        ins, outs = refs[: len(sources)], refs[len(sources) : -3]
        held, in_sems, out_sems = refs[-3:]
        into = Copies(in_sems)
        at = 0
        for source, first, n in pieces:
            into.start(ins[source].at[first : first + n], held.at[at : at + n])
            at += n
        into.wait()
        out = Copies(out_sems)
        for (first, last), ref in zip(ranges, outs):
            out.start(held.at[first:last], ref)
        out.wait()

    return pl.pallas_call(
        kernel,
        out_shape=[tiles(last - first) for first, last in ranges],
        in_specs=[ANY_SPEC] * len(sources),
        out_specs=[ANY_SPEC] * len(ranges),
        scratch_shapes=[
            VMEM((count, 256, 256), BF16),
            pltpu.SemaphoreType.DMA((len(pieces),)),
            pltpu.SemaphoreType.DMA((len(ranges),)),
        ],
        compiler_params=params(),
        cost_estimate=cost(stated, 0),
        name=name,
    )(*sources)


def halo_places():
    numbers = {}
    for r in range(4):
        for c in range(4):
            for k in range(9):
                y, x = r + k // 3 - 1, c + k % 3 - 1
                if not (0 <= y < 4 and 0 <= x < 4):
                    numbers[r * 4 + c, k] = len(numbers)
    return numbers


HALO = halo_places()
N_HALO = len(HALO) // 2


def split3(x):
    first = x.astype(BF16).astype(F32)
    rest = x - first
    second = rest.astype(BF16).astype(F32)
    return first, second, rest - second


def site_features(x, y):
    n = lax.broadcasted_iota(jnp.int32, (8, 256), 0)
    square = x * x + y * y
    target, source = [], []
    for parts in (split3(x), split3(y)):
        first, second, third = parts
        target.append(jnp.where(n < 3, first, jnp.where(n < 5, second, jnp.where(n < 6, third, 0.0))))
        other = jnp.where(
            (n == 0) | (n == 3) | (n == 5),
            first,
            jnp.where((n == 1) | (n == 4), second, jnp.where(n == 2, third, 0.0)),
        )
        source.append(-2.0 * other)
    first, second, third = split3(square)
    low = jnp.where(n == 0, first, jnp.where(n == 1, second, third))
    high = jnp.where(n == 3, first, jnp.where(n == 4, second, third))
    one = jnp.where(n < 6, 1.0, 0.0)
    target.append(jnp.where(n < 3, low, one))
    source.append(jnp.where(n < 3, 1.0, jnp.where(n < 6, high, 0.0)))
    zero = jnp.zeros((8, 256), F32)
    return jnp.concatenate(target + [zero], axis=0), jnp.concatenate(source + [zero], axis=0)


def near_kernel(
    first, with_far, grid_rows, grid_cols, lists, far_zero, positions, own, *rest
):
    if with_far:
        flags, couplings, up, down, above, below, near_out, halo_out, field_out = rest[:9]
        table, far_held, field, far_sems, field_sems = rest[9:14]
        rest = rest[14:]
    else:
        near_out, halo_out, flags = rest[:3]
        rest = rest[3:]
    held, target_feat, source_feat, halo, made, near, floors, sems, halo_sems, near_sems = rest
    copy = pltpu.make_async_copy(own, held, sems.at[0])
    copy.start()
    out = Copies(halo_sems)
    sums_out = Copies(near_sems)
    if with_far:
        far_in = Copies(far_sems)
        far_in.start(couplings.at[0], table)
        for n, src in enumerate((above, up, down, below)):
            far_in.start(src.at[0:8], far_held.at[8 * n : 8 * n + 8])
        far_held[32] = jnp.zeros((256, 256), BF16)
        field_copies = Copies(field_sems)
    first_row = lax.axis_index("qx") * 4
    first_col = lax.axis_index("qy") * 4
    scale = root_three / length_scale
    mid_row = first_row.astype(F32) + 2.0
    mid_col = first_col.astype(F32) + 2.0
    first_place = first // 4 * 6

    def features(n, carry):
        r = jnp.clip(first_row + (first_place + n) // 6 - 1, 0, grid_rows - 1)
        c = jnp.clip(first_col + n % 6 - 1, 0, grid_cols - 1)
        here = positions[r * grid_cols + c]
        target, source = site_features(
            (here[0:1] - mid_row) * scale, (here[1:2] - mid_col) * scale
        )
        target_feat[n] = target
        source_feat[n] = source.astype(BF16)
        return carry

    lax.fori_loop(0, 24, features, 0)

    if not with_far:

        def mark(t, carry):
            r, c = t // 4, t % 4
            mark_listed(
                lambda e: far_zero[r, c, e],
                flags,
                t,
                first_row + r // 2 * 2 - 2,
                first_col + c // 2 * 2 - 2,
                grid_cols,
            )
            return carry

        lax.fori_loop(0, 16, mark, 0)

    def make(m):
        t = first + m
        r, c = t // 4, t % 4
        slot = m % 2 * 9
        for k in range(9):
            floors[m * 10 + k] = 1e6
        for e in range(9):
            entry = lists[r, c, e]
            source_row = jnp.maximum(entry, 0) // grid_cols
            source_col = jnp.maximum(entry, 0) - source_row * grid_cols
            k = (source_row - first_row - r + 1) * 3 + source_col - first_col - c + 1
            floors[m * 10 + jnp.where(entry >= 0, k, 9)] = 1e-24
        place = (m // 4 + 1) * 6 + c + 1
        target = target_feat[place].T.astype(BF16)
        for k in range(9):
            square = nn(target, source_feat[place + (k // 3 - 1) * 6 + k % 3 - 1])
            square = jnp.maximum(square, floors[m * 10 + k])
            far = square * lax.rsqrt(square)
            tile = ((far + 1.0) * jnp.exp2(far * -LOG2E)).astype(BF16)
            if (t, k) in HALO:
                number = HALO[t, k] % N_HALO
                halo[number] = tile
                out.start(halo.at[number], halo_out.at[number])
            else:
                made[slot + k] = tile

    def use(m):
        t = first + m
        slot = m % 2 * 9
        found = [k for k in range(9) if (t, k) not in HALO]
        lhs = jnp.concatenate([made[slot + k] for k in found], axis=1)
        blocks = [held[t + (k // 3 - 1) * 4 + k % 3 - 1] for k in found]
        near[m] = nn(lhs, jnp.concatenate(blocks, axis=0))
        sums_out.start(near.at[m], near_out.at[m])

    make(0)
    copy.wait()
    if with_far:
        far_in.wait()
    for m in range(1, 8):
        make(m)
        if with_far and m % 2 == 1:
            a, b = m // 4, m // 2 % 2
            sums = level_zero_sums("inner", a, b, flags, table, far_held, 32)
            for p in PARENTS:
                t = number_of(a, b, p)
                field[t] = sums[p]
                field_copies.start(field.at[t], field_out.at[t])
        use(m - 1)
    use(7)
    out.wait()
    sums_out.wait()
    if with_far:
        field_copies.wait()


def near_call(first, grid_rows, grid_cols, lists, far_zero, positions, own, far=()):
    out_shape = [tiles(8, F32), tiles(N_HALO)]
    out_specs = [ANY_SPEC, ANY_SPEC]
    scratch = []
    if far:
        out_shape.append(tiles(16, F32))
        out_specs.append(ANY_SPEC)
        scratch = [
            VMEM((20, 256, 256), BF16),
            VMEM((33, 256, 256), BF16),
            VMEM((16, 256, 256), F32),
            pltpu.SemaphoreType.DMA((5,)),
            pltpu.SemaphoreType.DMA((16,)),
        ]
    else:
        out_shape.append(jax.ShapeDtypeStruct((16, 37), jnp.int32))
        out_specs.append(SMEM_SPEC)
    return pl.pallas_call(
        functools.partial(near_kernel, first, bool(far), grid_rows, grid_cols),
        out_shape=out_shape,
        in_specs=[SMEM_SPEC, SMEM_SPEC, VMEM_SPEC, ANY_SPEC]
        + ([SMEM_SPEC] + [ANY_SPEC] * 5 if far else []),
        out_specs=out_specs,
        scratch_shapes=scratch
        + [
            VMEM((16, 256, 256), BF16),
            VMEM((24, 32, 256), F32),
            VMEM((24, 32, 256), BF16),
            VMEM((N_HALO, 256, 256), BF16),
            VMEM((18, 256, 256), BF16),
            VMEM((8, 256, 256), F32),
            pltpu.SMEM((80,), F32),
            pltpu.SemaphoreType.DMA((1,)),
            pltpu.SemaphoreType.DMA((N_HALO,)),
            pltpu.SemaphoreType.DMA((8,)),
        ],
        compiler_params=params(),
        cost_estimate=cost(600 if far else 12000, 8 << 20),
        name="near_and_inner_far" if far else "near_first",
    )(lists, far_zero, positions, own, *far)


def mark_listed(entries, flags, n, first_row, first_col, grid_cols):
    for w in range(36):
        flags[n, w] = 0
    for e in range(27):
        entry = entries(e)
        row = jnp.maximum(entry, 0) // grid_cols
        col = jnp.maximum(entry, 0) - row * grid_cols
        w = (row - first_row) * 6 + col - first_col
        flags[n, jnp.where(entry >= 0, jnp.clip(w, 0, 35), 36)] = 1


def dot_group(held, couplings, turned, group):
    rows = len(group[0][1])
    lhs = [
        jnp.concatenate([held[places[n]] for _, places in group], axis=1) for n in range(rows)
    ]
    lhs = jnp.concatenate(lhs, axis=0) if rows > 1 else lhs[0]
    if turned:
        return nn(lhs, jnp.concatenate([couplings[k] for k, _ in group], axis=0))
    return nt(lhs, jnp.concatenate([couplings[k] for k, _ in group], axis=1))


def coupled(plan, couplings, held, places):
    total = None
    for turned in (0, 1):
        group = [(k, [places(w)]) for w, k in plan[turned]]
        part = dot_group(held, couplings, turned, group)
        total = part if total is None else total + part
    return total


def upper_kernel(
    grid_cols, n_rows, far_one, far_two, couplings, t_two, row, row_e, row_d, down,
    held_one, held_two, field_two, flags, sems,
):
    n_two = 6 * n_rows
    zero_one, zero_two = 36, 2 * n_two
    copies = Copies(sems)
    copies.start(row.at[12 : 12 + n_two], held_two.at[0:n_two])
    copies.start(row_e.at[12 : 12 + n_two], held_two.at[n_two : 2 * n_two])
    copies.start(row.at[0:12], held_one.at[0:12])
    copies.start(row_e.at[0:12], held_one.at[12:24])
    copies.start(row_d, held_one.at[24:36])
    held_one[zero_one] = jnp.zeros((256, 256), BF16)
    held_two[zero_two] = jnp.zeros((256, 256), BF16)
    i = lax.axis_index("qx")
    j = lax.axis_index("qy")
    a = i % 2
    b = j % 2
    for t in range(4):
        mark_listed(
            lambda e: far_one[t // 2, t % 2, e], flags, t, 2 * i - 2, 2 * j - 2, 2 * grid_cols
        )
    mark_listed(
        lambda e: far_two[0, 0, e], flags, 4, i // 2 * 2 - 2, j // 2 * 2 - 2, grid_cols
    )
    core_at = [jnp.where(a == 0, 0, n_two), jnp.where(a == 0, n_two, 0)]
    y_at = [2, 0, 2] if n_rows == 2 else [2, 0, 4]
    pair_tiles = 2 * n_rows
    z_at = [
        jnp.where(b == 0, pair_tiles, 2 * pair_tiles),
        0,
        jnp.where(b == 0, 2 * pair_tiles, pair_tiles),
    ]
    x_at = [b, 1 - b]

    def place_two(w):
        r, c = w // 6, w % 6
        place = core_at[r % 2] + y_at[r // 2] + z_at[c // 2] + x_at[c % 2]
        return jnp.where(flags[4, w] == 1, place, zero_two)

    row_at = [jnp.where(a == 0, 24, 12), 0, jnp.where(a == 0, 12, 24)]
    col_at = [jnp.where(b == 0, 8, 4), 0, jnp.where(b == 0, 4, 8)]

    def place_one(t, w):
        r, c = w // 6, w % 6
        place = row_at[r // 2] + col_at[c // 2] + (r % 2) * 2 + c % 2
        return jnp.where(flags[t, w] == 1, place, zero_one)

    for copy in copies.started[:2]:
        copy.wait()
    for u in range(2):
        for v in range(2):

            @pl.when((a == u) & (b == v))
            def _():
                field_two[...] = coupled(
                    class_plan(u, v), couplings.at[1], held_two, place_two
                ).astype(BF16)

    for copy in copies.started[2:]:
        copy.wait()
    for u in range(2):
        for v in range(2):
            t = u * 2 + v
            field = coupled(
                class_plan(u, v), couplings.at[0], held_one, functools.partial(place_one, t)
            )
            down[t] = (field + nt(field_two[...], t_two[u, v])).astype(BF16)


def upper_levels(grid_cols, far_one, far_two, couplings, t_two, row, row_e, row_d):
    n_two = row.shape[0] - 12
    return pl.pallas_call(
        functools.partial(upper_kernel, grid_cols, n_two // 6),
        grid=(1,),
        out_shape=tiles(4),
        in_specs=[
            SMEM_SPEC,
            SMEM_SPEC,
            pl.BlockSpec(
                (pl.Element(2), pl.Element(20), pl.Element(256), pl.Element(256)),
                lambda g: (1, 0, 0, 0),
            ),
            pl.BlockSpec((2, 2, 256, 256), lambda g: (0, 0, 0, 0)),
        ]
        + [ANY_SPEC] * 3,
        out_specs=pl.BlockSpec((4, 256, 256), lambda g: (0, 0, 0)),
        scratch_shapes=[
            VMEM((37, 256, 256), BF16),
            VMEM((2 * n_two + 1, 256, 256), BF16),
            VMEM((256, 256), BF16),
            pltpu.SMEM((5, 37), jnp.int32),
            pltpu.SemaphoreType.DMA((5,)),
        ],
        compiler_params=params(),
        cost_estimate=cost(340, 14 << 20),
        name="upper_levels",
    )(far_one, far_two, couplings, t_two, row, row_e, row_d)


def source_of(x, y, w):
    r, c = 2 * x + w // 6, 2 * y + w % 6
    if 2 <= c < 6:
        return "inner", r * 4 + c - 2
    side = 0 if c < 2 else 1
    c = c if c < 2 else c - 6
    if 2 <= r < 6:
        return "outer", side * 8 + (r - 2) * 2 + c
    return "outer", (16 if r < 2 else 24) + side * 4 + (r if r < 2 else r - 6) * 2 + c


PARENTS = [(x, y) for x in range(2) for y in range(2)]


def number_of(a, b, parent):
    x, y = parent
    return (2 * x + a) * 4 + 2 * y + b


def level_zero_sums(kind, a, b, flags, couplings, held, zero):
    plan = class_plan(a, b)
    sums = {}
    for turned in (0, 1):
        groups = {}
        for w, k in plan[turned]:
            members = tuple(p for p in PARENTS if source_of(*p, w)[0] == kind)
            if members:
                groups.setdefault(members, []).append((w, k))
        for members, entries in groups.items():
            group = []
            for w, k in entries:
                places = [
                    jnp.where(flags[number_of(a, b, p), w] == 1, source_of(*p, w)[1], zero)
                    for p in members
                ]
                group.append((k, places))
            total = dot_group(held, couplings, turned, group)
            for n, p in enumerate(members):
                part = total[256 * n : 256 * n + 256]
                sums[p] = part if p not in sums else sums[p] + part
    return sums


def grouped(x):
    return x.reshape(2, 2, 2, 2, 256, 256)


CLASS_BLOCK = pl.BlockSpec((2, 1, 2, 1, 256, 256), lambda g: (0, g // 2, 0, g % 2, 0, 0))
COUPLING_BLOCK = pl.BlockSpec((1, 20, 256, 256), lambda g: (0, 0, 0, 0))
GROUPED_F32 = jax.ShapeDtypeStruct((2, 2, 2, 2, 256, 256), F32)


def each_class(step, body):
    for a in range(2):
        for b in range(2):
            pl.when(step == a * 2 + b)(functools.partial(body, a, b))


def near_place(r, c):
    rows_in, cols_in = 1 <= r < 5, 1 <= c < 5
    if rows_in:
        return (0 if c == 0 else 4) + r - 1
    if cols_in:
        return (8 if r == 0 else 12) + c - 1
    return 16 + (0 if r == 0 else 2) + (0 if c == 0 else 1)


def near_part(t, halo, held):
    r, c = t // 4, t % 4
    found = [k for k in range(9) if (t, k) in HALO]
    if not found:
        return None
    lhs = jnp.concatenate([halo[HALO[t, k]] for k in found], axis=1)
    rhs = jnp.concatenate([held[near_place(r + k // 3, c + k % 3)] for k in found], axis=0)
    return nn(lhs, rhs)


def outer_kernel(
    flags, couplings, t_one, basis, down_one, field, near_a, near_b, halo_a, halo_b,
    left, right, s_left, s_right, above, below, corner_above, corner_below, out,
    held, near_held, halo, sems,
):
    step = pl.program_id(0)

    def copies():
        pairs = []
        for n, src in enumerate((left, right, corner_above.at[0:8], corner_below.at[0:8])):
            pairs.append((src, held.at[8 * n : 8 * n + 8]))
        for n, src in enumerate((s_left, s_right, above.at[8:12], below.at[8:12])):
            pairs.append((src, near_held.at[4 * n : 4 * n + 4]))
        pairs.append((corner_above.at[8:10], near_held.at[16:18]))
        pairs.append((corner_below.at[8:10], near_held.at[18:20]))
        pairs.append((halo_a, halo.at[0:N_HALO]))
        pairs.append((halo_b, halo.at[N_HALO : 2 * N_HALO]))
        return [pltpu.make_async_copy(src, dst, sems.at[n]) for n, (src, dst) in enumerate(pairs)]

    @pl.when(step == 0)
    def _():
        started = copies()
        for copy in started:
            copy.start()
        held[32] = jnp.zeros((256, 256), BF16)
        for copy in started[:4]:
            copy.wait()

    def body(a, b):
        sums = level_zero_sums("outer", a, b, flags, couplings.at[0], held, 32)
        if a == 0 and b == 0:
            for copy in copies()[4:]:
                copy.wait()
        for x, y in PARENTS:
            total = field[x, 0, y, 0] + sums[x, y]
            total = total + nt(down_one[x * 2 + y], t_one[x, 0, y, 0])
            far = nt(basis[x, 0, y, 0], total.astype(BF16))
            near = (near_b if x else near_a)[0, y, 0]
            part = near_part(number_of(a, b, (x, y)), halo, near_held)
            if part is not None:
                near = near + part
            out[x, 0, y, 0] = (near * TILE_SCALE + far).astype(BF16)

    each_class(step, body)


HALF_BLOCK = pl.BlockSpec((1, 2, 1, 256, 256), lambda g: (g // 2, 0, g % 2, 0, 0))


def outer_level(
    flags, couplings, t_one, basis, down_one, field, near_a, near_b, halo_a, halo_b, *received
):
    half = lambda x: x.reshape(2, 2, 2, 256, 256)
    return pl.pallas_call(
        outer_kernel,
        grid=(4,),
        out_shape=jax.ShapeDtypeStruct((2, 2, 2, 2, 256, 256), BF16),
        in_specs=[
            SMEM_SPEC,
            COUPLING_BLOCK,
            CLASS_BLOCK,
            CLASS_BLOCK,
            pl.BlockSpec((4, 256, 256), lambda g: (0, 0, 0)),
            CLASS_BLOCK,
            HALF_BLOCK,
            HALF_BLOCK,
        ]
        + [ANY_SPEC] * 10,
        out_specs=CLASS_BLOCK,
        scratch_shapes=[
            VMEM((33, 256, 256), BF16),
            VMEM((20, 256, 256), BF16),
            VMEM((2 * N_HALO, 256, 256), BF16),
            pltpu.SemaphoreType.DMA((12,)),
        ],
        compiler_params=params(),
        cost_estimate=cost(500, 34 << 20),
        name="leaf_outer",
    )(
        flags, couplings, grouped(t_one), grouped(basis), down_one, field, half(near_a),
        half(near_b), halo_a, halo_b, *received,
    )


def per_device(
    positions,
    samples,
    leaf_basis,
    transfer_one,
    transfer_two,
    couplings,
    near_lists,
    far_zero,
    far_one,
    far_two,
):
    nx = lax.axis_size("qx")
    ny = lax.axis_size("qy")
    down_x = [(k, k + 1) for k in range(nx - 1)]
    up_x = [(k + 1, k) for k in range(nx - 1)]
    down_y = [(k, k + 1) for k in range(ny - 1)]
    up_y = [(k + 1, k) for k in range(ny - 1)]

    up, down, left, right, to_left, to_right, upper, cell = coefficients(
        samples, leaf_basis, transfer_one, transfer_two
    )

    swap_y = [(k, k ^ 1) for k in range(ny)]
    swap_x = [(k, k ^ 1) for k in range(nx)]
    cross_x = [(k, k + 1) for k in range(1, nx - 1, 2)] + [(k + 1, k) for k in range(1, nx - 1, 2)]
    pair = lax.ppermute(upper, "qy", swap_y)
    if nx == 4:
        others = [lax.ppermute(cell, "qx", [(k, k ^ 2) for k in range(nx)])]
    else:
        others = [
            lax.ppermute(cell, "qx", [(k, k + 2) for k in range(nx - 2)]),
            lax.ppermute(cell, "qx", [(k + 2, k) for k in range(nx - 2)]),
        ]
    others_pair = [lax.ppermute(x, "qy", swap_y) for x in others]
    s_left = lax.ppermute(to_right, "qy", down_y)
    above = lax.ppermute(down, "qx", down_x)
    sites = positions.reshape(-1, 2, 256)
    flat_samples = samples.reshape(16, 256, 256)
    near_a, halo_a, flags = near_call(
        0, 4 * nx, 4 * ny, near_lists, far_zero, sites, flat_samples
    )
    pair, others_pair, s_left, near_a, to_left, up = lax.optimization_barrier(
        (pair, others_pair, s_left, near_a, to_left, up)
    )
    s_right = lax.ppermute(to_left, "qy", up_y)
    below = lax.ppermute(up, "qx", up_x)
    outward = [(k, k + 2) for k in range(0, ny - 2, 2)] + [(k + 2, k) for k in range(1, ny - 2, 2)]
    inward = [(k + 2, k) for k in range(0, ny - 2, 2)] + [(k, k + 2) for k in range(1, ny - 2, 2)]
    n_others = len(others)
    quad = [(0, 4, 1), (1, 4, 1)]
    for n in range(n_others):
        quad += [(2 + n, 0, 1), (2 + n_others + n, 0, 1)]
    n_quad = len(quad)
    across, cells = assembled(
        "pair_payload",
        (upper, pair, *others, *others_pair),
        [(1, 0, 4)] + quad,
        [(0, 4 + n_quad), (4, 4 + n_quad)],
    )
    outer = lax.ppermute(across, "qy", outward)
    inner = lax.ppermute(across, "qy", inward)
    left, right, s_left, s_right, above = lax.optimization_barrier(
        (left, right, s_left, s_right, above)
    )
    on_left = lax.ppermute(right, "qy", down_y)
    on_right = lax.ppermute(left, "qy", up_y)
    near_b, halo_b, field = near_call(
        8,
        4 * nx,
        4 * ny,
        near_lists,
        far_zero,
        sites,
        flat_samples,
        (flags, couplings, up, down, above, below),
    )
    inner, outer, near_b = lax.optimization_barrier((inner, outer, near_b))
    row, one_row = assembled(
        "row_payload",
        (upper, pair, outer, inner, cells),
        [(0, 0, 4), (1, 0, 4), (2, 0, 4), (4, 0, n_quad), (2, 4, n_quad), (3, 4, n_quad)],
        [(0, 12 + 3 * n_quad), (0, 12)],
    )
    row_d = lax.ppermute(one_row, "qx", cross_x)
    row_e = lax.ppermute(row, "qx", swap_x)

    corner_down, corner_up = assembled(
        "corner_payload",
        (on_left, on_right, s_left, s_right),
        [(0, 4, 4), (1, 4, 4), (2, 3, 1), (3, 3, 1)]
        + [(0, 0, 4), (1, 0, 4), (2, 0, 1), (3, 0, 1)],
        [(0, 10), (10, 20)],
        stated=6000,
    )
    corner_above = lax.ppermute(corner_down, "qx", down_x)
    corner_below = lax.ppermute(corner_up, "qx", up_x)
    down_one = upper_levels(
        ny, far_one, far_two, couplings, transfer_two, row, row_e, row_d
    )
    result = outer_level(
        flags,
        couplings,
        transfer_one,
        leaf_basis,
        down_one,
        grouped(field),
        near_a,
        near_b,
        halo_a,
        halo_b,
        on_left,
        on_right,
        s_left,
        s_right,
        above,
        below,
        corner_above,
        corner_below,
    )
    return result.reshape(4, 4, 256, 256)


def solution(mesh):
    return jax.shard_map(
        per_device,
        mesh=mesh,
        in_specs=(
            P(),
            P("qx", "qy", None, None),
            P("qx", "qy", None, None),
            P("qx", "qy", None, None),
            P("qx", "qy", None, None),
            P(),
            P("qx", "qy", None),
            P("qx", "qy", None),
            P("qx", "qy", None),
            P("qx", "qy", None),
        ),
        out_specs=P("qx", "qy", None, None),
        check_vma=False,
    )
```

```python
import functools

import jax
import jax.numpy as jnp
import numpy as np
from jax import lax
from jax.experimental import pallas as pl
from jax.experimental.pallas import tpu as pltpu
from jax.sharding import PartitionSpec as P

root_three = 1.7320508075688772
length_scale = 1.0
VMEM = pltpu.VMEM
SMEM = pltpu.SMEM
F32 = jnp.float32
BF16 = jnp.bfloat16
BIG = 64 * 1024 * 1024 - 256 * 1024


def nn(a, b):
    return lax.dot_general(a, b, (((1,), (0,)), ((), ())), preferred_element_type=F32)


def nt(a, b):
    return lax.dot_general(a, b, (((1,), (1,)), ((), ())), preferred_element_type=F32)


def tn(a, b):
    return lax.dot_general(a, b, (((0,), (0,)), ((), ())), preferred_element_type=F32)


def params():
    return pltpu.CompilerParams(vmem_limit_bytes=BIG)


def cost(products, bytes_accessed):
    return pl.CostEstimate(
        flops=products * 2 * 256**3 // 8, bytes_accessed=bytes_accessed // 8, transcendentals=0
    )


def half_offsets():
    kept = []
    for u in range(-3, 4):
        for v in range(-3, 4):
            if max(abs(u), abs(v)) >= 2 and (u > 0 or (u == 0 and v > 0)):
                kept.append((u, v))
    return kept


HALF_OFFSETS = half_offsets()


def class_plan(a, b):
    plain, turned = [], []
    for w in range(36):
        u, v = w // 6 - 2 - a, w % 6 - 2 - b
        if max(abs(u), abs(v)) < 2:
            continue
        if (u, v) in HALF_OFFSETS:
            plain.append((w, HALF_OFFSETS.index((u, v))))
        else:
            turned.append((w, HALF_OFFSETS.index((-u, -v))))
    return plain, turned


LOG2E = 1.4426950408889634
TILE_SCALE = 256 ** -0.5


def tiles(n, dtype=BF16):
    return jax.ShapeDtypeStruct((n, 256, 256), dtype)


ANY_SPEC = pl.BlockSpec(memory_space=pltpu.HBM)
SMEM_SPEC = pl.BlockSpec(memory_space=SMEM)
VMEM_SPEC = pl.BlockSpec(memory_space=VMEM)


class Copies:
    def __init__(self, sems):
        self.sems = sems
        self.started = []

    def start(self, src, dst):
        copy = pltpu.make_async_copy(src, dst, self.sems.at[len(self.started)])
        copy.start()
        self.started.append(copy)
        return copy

    def wait(self):
        for copy in self.started:
            copy.wait()


def coef_kernel(
    samples, basis, t_one, t_two, up, down, left, right, upper, cell,
    sv, bv, t1v, t2v, cv, uv, in_sems, out_sems,
):
    into = Copies(in_sems)
    out = Copies(out_sems)
    rows = []
    for x in range(4):
        rows.append(
            (
                into.start(samples.at[x], sv.at[x]),
                into.start(basis.at[x], bv.at[x]),
                into.start(t_one.at[x], t1v.at[x]),
            )
        )
    last = into.start(t_two, t2v)
    for x in range(4):
        rows[x][0].wait()
        rows[x][1].wait()
        for y in range(4):
            cv[x * 4 + y] = tn(sv[x, y], bv[x, y]).astype(BF16)
        own = cv.at[4 * x : 4 * x + 4]
        out.start(own, (up if x < 2 else down).at[4 * (x % 2) : 4 * (x % 2) + 4])
        out.start(cv.at[4 * x : 4 * x + 2], left.at[2 * x : 2 * x + 2])
        out.start(cv.at[4 * x + 2 : 4 * x + 4], right.at[2 * x : 2 * x + 2])
        out.start(sv.at[x, 0], left.at[8 + x])
        out.start(sv.at[x, 3], right.at[8 + x])
        if x == 0:
            out.start(sv.at[x], up.at[8:12])
        if x == 3:
            out.start(sv.at[x], down.at[8:12])
        if x % 2 == 1:
            rows[x - 1][2].wait()
            rows[x][2].wait()
            for y in range(2):
                kids = [(x - 1 + a, 2 * y + b) for a in range(2) for b in range(2)]
                lhs = jnp.concatenate([cv[k * 4 + m] for k, m in kids], axis=1)
                rhs = jnp.concatenate([t1v[k] for k in kids], axis=0)
                uv[x // 2 * 2 + y] = nn(lhs, rhs).astype(BF16)
    last.wait()
    lhs = jnp.concatenate([uv[k] for k in range(4)], axis=1)
    rhs = jnp.concatenate([t2v[k // 2, k % 2] for k in range(4)], axis=0)
    uv[4] = nn(lhs, rhs).astype(BF16)
    out.start(uv, upper)
    out.start(uv.at[4:5], cell)
    out.wait()


def coefficients(samples, basis, t_one, t_two):
    return pl.pallas_call(
        coef_kernel,
        out_shape=[tiles(n) for n in (12, 12, 12, 12, 5, 1)],
        in_specs=[ANY_SPEC] * 4,
        out_specs=[ANY_SPEC] * 6,
        scratch_shapes=[
            VMEM((4, 4, 256, 256), BF16),
            VMEM((4, 4, 256, 256), BF16),
            VMEM((4, 4, 256, 256), BF16),
            VMEM((2, 2, 256, 256), BF16),
            VMEM((16, 256, 256), BF16),
            VMEM((5, 256, 256), BF16),
            pltpu.SemaphoreType.DMA((13,)),
            pltpu.SemaphoreType.DMA((24,)),
        ],
        compiler_params=params(),
        cost_estimate=cost(170, 12 << 20),
        name="coefficients",
    )(samples, basis, t_one, t_two)


def assembled(name, sources, pieces, ranges, stated=35):
    count = sum(n for _, _, n in pieces)

    def kernel(*refs):
        ins, outs = refs[: len(sources)], refs[len(sources) : -3]
        held, in_sems, out_sems = refs[-3:]
        into = Copies(in_sems)
        at = 0
        for source, first, n in pieces:
            into.start(ins[source].at[first : first + n], held.at[at : at + n])
            at += n
        into.wait()
        out = Copies(out_sems)
        for (first, last), ref in zip(ranges, outs):
            out.start(held.at[first:last], ref)
        out.wait()

    return pl.pallas_call(
        kernel,
        out_shape=[tiles(last - first) for first, last in ranges],
        in_specs=[ANY_SPEC] * len(sources),
        out_specs=[ANY_SPEC] * len(ranges),
        scratch_shapes=[
            VMEM((count, 256, 256), BF16),
            pltpu.SemaphoreType.DMA((len(pieces),)),
            pltpu.SemaphoreType.DMA((len(ranges),)),
        ],
        compiler_params=params(),
        cost_estimate=cost(stated, 0),
        name=name,
    )(*sources)


def halo_places():
    numbers = {}
    for r in range(4):
        for c in range(4):
            for k in range(9):
                y, x = r + k // 3 - 1, c + k % 3 - 1
                if not (0 <= y < 4 and 0 <= x < 4):
                    numbers[r * 4 + c, k] = len(numbers)
    return numbers


HALO = halo_places()
N_HALO = len(HALO) // 2


def split3(x):
    first = x.astype(BF16).astype(F32)
    rest = x - first
    second = rest.astype(BF16).astype(F32)
    return first, second, rest - second


def site_features(x, y):
    n = lax.broadcasted_iota(jnp.int32, (8, 256), 0)
    square = x * x + y * y
    target, source = [], []
    for parts in (split3(x), split3(y)):
        first, second, third = parts
        target.append(jnp.where(n < 3, first, jnp.where(n < 5, second, jnp.where(n < 6, third, 0.0))))
        other = jnp.where(
            (n == 0) | (n == 3) | (n == 5),
            first,
            jnp.where((n == 1) | (n == 4), second, jnp.where(n == 2, third, 0.0)),
        )
        source.append(-2.0 * other)
    first, second, third = split3(square)
    low = jnp.where(n == 0, first, jnp.where(n == 1, second, third))
    high = jnp.where(n == 3, first, jnp.where(n == 4, second, third))
    one = jnp.where(n < 6, 1.0, 0.0)
    target.append(jnp.where(n < 3, low, one))
    source.append(jnp.where(n < 3, 1.0, jnp.where(n < 6, high, 0.0)))
    zero = jnp.zeros((8, 256), F32)
    return jnp.concatenate(target + [zero], axis=0), jnp.concatenate(source + [zero], axis=0)


def near_kernel(
    first, with_far, grid_rows, grid_cols, lists, far_zero, positions, own, *rest
):
    if with_far:
        flags, couplings, up, down, above, below, near_out, halo_out, field_out = rest[:9]
        table, far_held, field, far_sems, field_sems = rest[9:14]
        rest = rest[14:]
    else:
        near_out, halo_out, flags = rest[:3]
        rest = rest[3:]
    held, target_feat, source_feat, halo, made, near, floors, sems, halo_sems, near_sems = rest
    copy = pltpu.make_async_copy(own, held, sems.at[0])
    copy.start()
    out = Copies(halo_sems)
    sums_out = Copies(near_sems)
    if with_far:
        far_in = Copies(far_sems)
        far_in.start(couplings.at[0], table)
        for n, src in enumerate((above, up, down, below)):
            far_in.start(src.at[0:8], far_held.at[8 * n : 8 * n + 8])
        far_held[32] = jnp.zeros((256, 256), BF16)
        field_copies = Copies(field_sems)
    first_row = lax.axis_index("qx") * 4
    first_col = lax.axis_index("qy") * 4
    scale = root_three / length_scale
    mid_row = first_row.astype(F32) + 2.0
    mid_col = first_col.astype(F32) + 2.0
    first_place = first // 4 * 6

    def features(n, carry):
        r = jnp.clip(first_row + (first_place + n) // 6 - 1, 0, grid_rows - 1)
        c = jnp.clip(first_col + n % 6 - 1, 0, grid_cols - 1)
        here = positions[r * grid_cols + c]
        target, source = site_features(
            (here[0:1] - mid_row) * scale, (here[1:2] - mid_col) * scale
        )
        target_feat[n] = target
        source_feat[n] = source.astype(BF16)
        return carry

    lax.fori_loop(0, 24, features, 0)

    def mark(t):
        r, c = t // 4, t % 4
        mark_listed(
            lambda e: far_zero[r, c, e],
            flags,
            t,
            first_row + r // 2 * 2 - 2,
            first_col + c // 2 * 2 - 2,
            grid_cols,
        )

    def make(m):
        t = first + m
        r, c = t // 4, t % 4
        slot = m % 2 * 9
        for k in range(9):
            floors[m * 10 + k] = 1e6
        for e in range(9):
            entry = lists[r, c, e]
            source_row = jnp.maximum(entry, 0) // grid_cols
            source_col = jnp.maximum(entry, 0) - source_row * grid_cols
            k = (source_row - first_row - r + 1) * 3 + source_col - first_col - c + 1
            floors[m * 10 + jnp.where(entry >= 0, k, 9)] = 1e-24
        if not with_far:
            mark(2 * m)
            mark(2 * m + 1)
        place = (m // 4 + 1) * 6 + c + 1
        target = target_feat[place].T.astype(BF16)
        for k in range(9):
            square = nn(target, source_feat[place + (k // 3 - 1) * 6 + k % 3 - 1])
            square = jnp.maximum(square, floors[m * 10 + k])
            far = square * lax.rsqrt(square)
            tile = ((far + 1.0) * jnp.exp2(far * -LOG2E)).astype(BF16)
            if (t, k) in HALO:
                number = HALO[t, k] % N_HALO
                halo[number] = tile
                out.start(halo.at[number], halo_out.at[number])
            else:
                made[slot + k] = tile

    def use(m):
        t = first + m
        slot = m % 2 * 9
        found = [k for k in range(9) if (t, k) not in HALO]
        lhs = jnp.concatenate([made[slot + k] for k in found], axis=1)
        blocks = [held[t + (k // 3 - 1) * 4 + k % 3 - 1] for k in found]
        near[m] = nn(lhs, jnp.concatenate(blocks, axis=0))
        sums_out.start(near.at[m], near_out.at[m])

    make(0)
    copy.wait()
    if with_far:
        far_in.wait()
    for m in range(1, 8):
        make(m)
        if with_far and m % 2 == 1:
            a, b = m // 4, m // 2 % 2
            sums = level_zero_sums("inner", a, b, flags, table, far_held, 32)
            for p in PARENTS:
                t = number_of(a, b, p)
                field[t] = sums[p]
                field_copies.start(field.at[t], field_out.at[t])
        use(m - 1)
    use(7)
    out.wait()
    sums_out.wait()
    if with_far:
        field_copies.wait()


def near_call(first, grid_rows, grid_cols, lists, far_zero, positions, own, far=()):
    out_shape = [tiles(8, F32), tiles(N_HALO)]
    out_specs = [ANY_SPEC, ANY_SPEC]
    scratch = []
    if far:
        out_shape.append(tiles(16, F32))
        out_specs.append(ANY_SPEC)
        scratch = [
            VMEM((20, 256, 256), BF16),
            VMEM((33, 256, 256), BF16),
            VMEM((16, 256, 256), F32),
            pltpu.SemaphoreType.DMA((5,)),
            pltpu.SemaphoreType.DMA((16,)),
        ]
    else:
        out_shape.append(jax.ShapeDtypeStruct((16, 37), jnp.int32))
        out_specs.append(SMEM_SPEC)
    return pl.pallas_call(
        functools.partial(near_kernel, first, bool(far), grid_rows, grid_cols),
        out_shape=out_shape,
        in_specs=[SMEM_SPEC, SMEM_SPEC, VMEM_SPEC, ANY_SPEC]
        + ([SMEM_SPEC] + [ANY_SPEC] * 5 if far else []),
        out_specs=out_specs,
        scratch_shapes=scratch
        + [
            VMEM((16, 256, 256), BF16),
            VMEM((24, 32, 256), F32),
            VMEM((24, 32, 256), BF16),
            VMEM((N_HALO, 256, 256), BF16),
            VMEM((18, 256, 256), BF16),
            VMEM((8, 256, 256), F32),
            pltpu.SMEM((80,), F32),
            pltpu.SemaphoreType.DMA((1,)),
            pltpu.SemaphoreType.DMA((N_HALO,)),
            pltpu.SemaphoreType.DMA((8,)),
        ],
        compiler_params=params(),
        cost_estimate=cost(600 if far else 12000, 8 << 20),
        name="near_and_inner_far" if far else "near_first",
    )(lists, far_zero, positions, own, *far)


def mark_listed(entries, flags, n, first_row, first_col, grid_cols):
    for w in range(36):
        flags[n, w] = 0
    for e in range(27):
        entry = entries(e)
        row = jnp.maximum(entry, 0) // grid_cols
        col = jnp.maximum(entry, 0) - row * grid_cols
        w = (row - first_row) * 6 + col - first_col
        flags[n, jnp.where(entry >= 0, jnp.clip(w, 0, 35), 36)] = 1


def dot_group(held, couplings, turned, group):
    rows = len(group[0][1])
    lhs = [
        jnp.concatenate([held[places[n]] for _, places in group], axis=1) for n in range(rows)
    ]
    lhs = jnp.concatenate(lhs, axis=0) if rows > 1 else lhs[0]
    if turned:
        return nn(lhs, jnp.concatenate([couplings[k] for k, _ in group], axis=0))
    return nt(lhs, jnp.concatenate([couplings[k] for k, _ in group], axis=1))


def coupled(plan, couplings, held, places):
    total = None
    for turned in (0, 1):
        group = [(k, [places(w)]) for w, k in plan[turned]]
        part = dot_group(held, couplings, turned, group)
        total = part if total is None else total + part
    return total


def upper_kernel(
    grid_cols, n_rows, far_one, far_two, couplings, t_two, row, row_e, row_d, cells, cells_e, down,
    held_one, held_two, field_two, flags, sems,
):
    n_two = 6 * n_rows
    zero_one, zero_two = 36, 2 * n_two
    copies = Copies(sems)
    copies.start(cells, held_two.at[0:n_two])
    copies.start(cells_e, held_two.at[n_two : 2 * n_two])
    copies.start(row, held_one.at[0:12])
    copies.start(row_e, held_one.at[12:24])
    copies.start(row_d, held_one.at[24:36])
    held_one[zero_one] = jnp.zeros((256, 256), BF16)
    held_two[zero_two] = jnp.zeros((256, 256), BF16)
    i = lax.axis_index("qx")
    j = lax.axis_index("qy")
    a = i % 2
    b = j % 2
    for t in range(4):
        mark_listed(
            lambda e: far_one[t // 2, t % 2, e], flags, t, 2 * i - 2, 2 * j - 2, 2 * grid_cols
        )
    mark_listed(
        lambda e: far_two[0, 0, e], flags, 4, i // 2 * 2 - 2, j // 2 * 2 - 2, grid_cols
    )
    core_at = [jnp.where(a == 0, 0, n_two), jnp.where(a == 0, n_two, 0)]
    y_at = [2, 0, 2] if n_rows == 2 else [2, 0, 4]
    pair_tiles = 2 * n_rows
    z_at = [
        jnp.where(b == 0, pair_tiles, 2 * pair_tiles),
        0,
        jnp.where(b == 0, 2 * pair_tiles, pair_tiles),
    ]
    x_at = [b, 1 - b]

    def place_two(w):
        r, c = w // 6, w % 6
        place = core_at[r % 2] + y_at[r // 2] + z_at[c // 2] + x_at[c % 2]
        return jnp.where(flags[4, w] == 1, place, zero_two)

    row_at = [jnp.where(a == 0, 24, 12), 0, jnp.where(a == 0, 12, 24)]
    col_at = [jnp.where(b == 0, 8, 4), 0, jnp.where(b == 0, 4, 8)]

    def place_one(t, w):
        r, c = w // 6, w % 6
        place = row_at[r // 2] + col_at[c // 2] + (r % 2) * 2 + c % 2
        return jnp.where(flags[t, w] == 1, place, zero_one)

    for copy in copies.started[:2]:
        copy.wait()
    for u in range(2):
        for v in range(2):

            @pl.when((a == u) & (b == v))
            def _():
                field_two[...] = coupled(
                    class_plan(u, v), couplings.at[1], held_two, place_two
                ).astype(BF16)

    for copy in copies.started[2:]:
        copy.wait()
    for u in range(2):
        for v in range(2):
            t = u * 2 + v
            field = coupled(
                class_plan(u, v), couplings.at[0], held_one, functools.partial(place_one, t)
            )
            down[t] = (field + nt(field_two[...], t_two[u, v])).astype(BF16)


def upper_levels(grid_cols, far_one, far_two, couplings, t_two, row, row_e, row_d, cells, cells_e):
    n_two = cells.shape[0]
    return pl.pallas_call(
        functools.partial(upper_kernel, grid_cols, n_two // 6),
        grid=(1,),
        out_shape=tiles(4),
        in_specs=[
            SMEM_SPEC,
            SMEM_SPEC,
            pl.BlockSpec(
                (pl.Element(2), pl.Element(20), pl.Element(256), pl.Element(256)),
                lambda g: (1, 0, 0, 0),
            ),
            pl.BlockSpec((2, 2, 256, 256), lambda g: (0, 0, 0, 0)),
        ]
        + [ANY_SPEC] * 5,
        out_specs=pl.BlockSpec((4, 256, 256), lambda g: (0, 0, 0)),
        scratch_shapes=[
            VMEM((37, 256, 256), BF16),
            VMEM((2 * n_two + 1, 256, 256), BF16),
            VMEM((256, 256), BF16),
            pltpu.SMEM((5, 37), jnp.int32),
            pltpu.SemaphoreType.DMA((5,)),
        ],
        compiler_params=params(),
        cost_estimate=cost(340, 14 << 20),
        name="upper_levels",
    )(far_one, far_two, couplings, t_two, row, row_e, row_d, cells, cells_e)


def source_of(x, y, w):
    r, c = 2 * x + w // 6, 2 * y + w % 6
    if 2 <= c < 6:
        return "inner", r * 4 + c - 2
    side = 0 if c < 2 else 1
    c = c if c < 2 else c - 6
    if 2 <= r < 6:
        return "sides", side * 8 + (r - 2) * 2 + c
    return "corners", (0 if r < 2 else 8) + side * 4 + (r if r < 2 else r - 6) * 2 + c


PARENTS = [(x, y) for x in range(2) for y in range(2)]


def number_of(a, b, parent):
    x, y = parent
    return (2 * x + a) * 4 + 2 * y + b


def level_zero_sums(kind, a, b, flags, couplings, held, zero):
    plan = class_plan(a, b)
    sums = {}
    for turned in (0, 1):
        groups = {}
        for w, k in plan[turned]:
            members = tuple(p for p in PARENTS if source_of(*p, w)[0] == kind)
            if members:
                groups.setdefault(members, []).append((w, k))
        for members, entries in groups.items():
            group = []
            for w, k in entries:
                places = [
                    jnp.where(flags[number_of(a, b, p), w] == 1, source_of(*p, w)[1], zero)
                    for p in members
                ]
                group.append((k, places))
            total = dot_group(held, couplings, turned, group)
            for n, p in enumerate(members):
                part = total[256 * n : 256 * n + 256]
                sums[p] = part if p not in sums else sums[p] + part
    return sums


def grouped(x):
    return x.reshape(2, 2, 2, 2, 256, 256)


CLASS_BLOCK = pl.BlockSpec((2, 1, 2, 1, 256, 256), lambda g: (0, g // 2, 0, g % 2, 0, 0))
COUPLING_BLOCK = pl.BlockSpec((1, 20, 256, 256), lambda g: (0, 0, 0, 0))
GROUPED_F32 = jax.ShapeDtypeStruct((2, 2, 2, 2, 256, 256), F32)


def each_class(step, body):
    for a in range(2):
        for b in range(2):
            pl.when(step == a * 2 + b)(functools.partial(body, a, b))


def near_source(r, c):
    rows_in, cols_in = 1 <= r < 5, 1 <= c < 5
    if rows_in and cols_in:
        return "own", None
    if rows_in:
        return "sides", (0 if c == 0 else 4) + r - 1
    if cols_in:
        return "sides", (8 if r == 0 else 12) + c - 1
    return "corners", (0 if r == 0 else 2) + (0 if c == 0 else 1)


CORNER_HALO = [
    n for (t, k), n in HALO.items() if near_source(t // 4 + k // 3, t % 4 + k % 3)[0] == "corners"
]


def near_part(kind, t, tile_of, held):
    r, c = t // 4, t % 4
    made, blocks = [], []
    for k in range(9):
        found, place = near_source(r + k // 3, c + k % 3)
        if found == kind:
            made.append(tile_of(HALO[t, k]))
            blocks.append(held[place])
    if not made:
        return None
    return nn(jnp.concatenate(made, axis=1), jnp.concatenate(blocks, axis=0))


def sides_kernel(
    flags, couplings, field_in, near_a, near_b, halo_a, halo_b, left, right, above, below,
    field, near, held, near_held, halo, sems,
):
    step = pl.program_id(0)

    def copies():
        pairs = [(left.at[0:8], held.at[0:8]), (right.at[0:8], held.at[8:16])]
        for n, src in enumerate((left, right, above, below)):
            pairs.append((src.at[8:12], near_held.at[4 * n : 4 * n + 4]))
        pairs.append((halo_a, halo.at[0:N_HALO]))
        pairs.append((halo_b, halo.at[N_HALO : 2 * N_HALO]))
        return [pltpu.make_async_copy(src, dst, sems.at[n]) for n, (src, dst) in enumerate(pairs)]

    @pl.when(step == 0)
    def _():
        started = copies()
        for copy in started:
            copy.start()
        held[16] = jnp.zeros((256, 256), BF16)
        for copy in started[:2]:
            copy.wait()

    def body(a, b):
        sums = level_zero_sums("sides", a, b, flags, couplings.at[0], held, 16)
        for x, y in PARENTS:
            field[x, 0, y, 0] = field_in[x, 0, y, 0] + sums[x, y]
        if a == 0 and b == 0:
            for copy in copies()[2:]:
                copy.wait()
        for x, y in PARENTS:
            part = near_part("sides", number_of(a, b, (x, y)), lambda n: halo[n], near_held)
            here = (near_b if x else near_a)[0, y, 0]
            near[x, 0, y, 0] = here if part is None else here + part

    each_class(step, body)


HALF_BLOCK = pl.BlockSpec((1, 2, 1, 256, 256), lambda g: (g // 2, 0, g % 2, 0, 0))


def sides_level(flags, couplings, field, near_a, near_b, *received):
    half = lambda x: x.reshape(2, 2, 2, 256, 256)
    return pl.pallas_call(
        sides_kernel,
        grid=(4,),
        out_shape=(GROUPED_F32, GROUPED_F32),
        in_specs=[SMEM_SPEC, COUPLING_BLOCK, CLASS_BLOCK, HALF_BLOCK, HALF_BLOCK] + [ANY_SPEC] * 6,
        out_specs=[CLASS_BLOCK, CLASS_BLOCK],
        scratch_shapes=[
            VMEM((17, 256, 256), BF16),
            VMEM((16, 256, 256), BF16),
            VMEM((2 * N_HALO, 256, 256), BF16),
            pltpu.SemaphoreType.DMA((8,)),
        ],
        compiler_params=params(),
        cost_estimate=cost(300, 30 << 20),
        name="far_sides",
    )(flags, couplings, field, half(near_a), half(near_b), *received)


def last_kernel(
    flags, couplings, t_one, basis, down_one, field, near, halo_a, halo_b, above, below, out,
    held, near_held, halo, sems,
):
    step = pl.program_id(0)

    @pl.when(step == 0)
    def _():
        copies = Copies(sems)
        copies.start(above.at[0:8], held.at[0:8])
        copies.start(below.at[0:8], held.at[8:16])
        copies.start(above.at[8:10], near_held.at[0:2])
        copies.start(below.at[8:10], near_held.at[2:4])
        for m, n in enumerate(CORNER_HALO):
            copies.start((halo_a if n < N_HALO else halo_b).at[n % N_HALO], halo.at[m])
        held[16] = jnp.zeros((256, 256), BF16)
        copies.wait()

    def body(a, b):
        sums = level_zero_sums("corners", a, b, flags, couplings.at[0], held, 16)
        for x, y in PARENTS:
            total = field[x, 0, y, 0] + nt(down_one[x * 2 + y], t_one[x, 0, y, 0])
            if (x, y) in sums:
                total = total + sums[x, y]
            far = nt(basis[x, 0, y, 0], total.astype(BF16))
            near_sum = near[x, 0, y, 0]
            part = near_part(
                "corners",
                number_of(a, b, (x, y)),
                lambda n: halo[CORNER_HALO.index(n)],
                near_held,
            )
            if part is not None:
                near_sum = near_sum + part
            out[x, 0, y, 0] = (near_sum * TILE_SCALE + far).astype(BF16)

    each_class(step, body)


def last_level(flags, couplings, t_one, basis, *rest):
    return pl.pallas_call(
        last_kernel,
        grid=(4,),
        out_shape=jax.ShapeDtypeStruct((2, 2, 2, 2, 256, 256), BF16),
        in_specs=[
            SMEM_SPEC,
            COUPLING_BLOCK,
            CLASS_BLOCK,
            CLASS_BLOCK,
            pl.BlockSpec((4, 256, 256), lambda g: (0, 0, 0)),
            CLASS_BLOCK,
            CLASS_BLOCK,
        ]
        + [ANY_SPEC] * 4,
        out_specs=CLASS_BLOCK,
        scratch_shapes=[
            VMEM((17, 256, 256), BF16),
            VMEM((4, 256, 256), BF16),
            VMEM((len(CORNER_HALO), 256, 256), BF16),
            pltpu.SemaphoreType.DMA((4 + len(CORNER_HALO),)),
        ],
        compiler_params=params(),
        cost_estimate=cost(270, 20 << 20),
        name="last_level",
    )(flags, couplings, grouped(t_one), grouped(basis), *rest)


def per_device(
    positions,
    samples,
    leaf_basis,
    transfer_one,
    transfer_two,
    couplings,
    near_lists,
    far_zero,
    far_one,
    far_two,
):
    nx = lax.axis_size("qx")
    ny = lax.axis_size("qy")
    down_x = [(k, k + 1) for k in range(nx - 1)]
    up_x = [(k + 1, k) for k in range(nx - 1)]
    down_y = [(k, k + 1) for k in range(ny - 1)]
    up_y = [(k + 1, k) for k in range(ny - 1)]

    up, down, left, right, upper, cell = coefficients(
        samples, leaf_basis, transfer_one, transfer_two
    )

    swap_y = [(k, k ^ 1) for k in range(ny)]
    swap_x = [(k, k ^ 1) for k in range(nx)]
    cross_x = [(k, k + 1) for k in range(1, nx - 1, 2)] + [(k + 1, k) for k in range(1, nx - 1, 2)]
    pair = lax.ppermute(upper, "qy", swap_y)
    if nx == 4:
        others = [lax.ppermute(cell, "qx", [(k, k ^ 2) for k in range(nx)])]
    else:
        others = [
            lax.ppermute(cell, "qx", [(k, k + 2) for k in range(nx - 2)]),
            lax.ppermute(cell, "qx", [(k + 2, k) for k in range(nx - 2)]),
        ]
    others_pair = [lax.ppermute(x, "qy", swap_y) for x in others]
    above = lax.ppermute(down, "qx", down_x)
    below = lax.ppermute(up, "qx", up_x)
    sites = positions.reshape(-1, 2, 256)
    flat_samples = samples.reshape(16, 256, 256)
    near_a, halo_a, flags = near_call(
        0, 4 * nx, 4 * ny, near_lists, far_zero, sites, flat_samples
    )
    pair, others_pair, near_a = lax.optimization_barrier((pair, others_pair, near_a))
    outward = [(k, k + 2) for k in range(0, ny - 2, 2)] + [(k + 2, k) for k in range(1, ny - 2, 2)]
    inward = [(k + 2, k) for k in range(0, ny - 2, 2)] + [(k, k + 2) for k in range(1, ny - 2, 2)]
    n_others = len(others)
    quad = [(0, 4, 1), (1, 4, 1)]
    for n in range(n_others):
        quad += [(2 + n, 0, 1), (2 + n_others + n, 0, 1)]
    n_quad = len(quad)
    across, cells = assembled(
        "pair_payload",
        (upper, pair, *others, *others_pair),
        [(1, 0, 4)] + quad,
        [(0, 4 + n_quad), (4, 4 + n_quad)],
    )
    across, above, below, left, right = lax.optimization_barrier(
        (across, above, below, left, right)
    )
    outer = lax.ppermute(across, "qy", outward)
    inner = lax.ppermute(across, "qy", inward)
    on_right = lax.ppermute(left, "qy", up_y)
    on_right, right = lax.optimization_barrier((on_right, right))
    on_left = lax.ppermute(right, "qy", down_y)
    near_b, halo_b, field = near_call(
        8,
        4 * nx,
        4 * ny,
        near_lists,
        far_zero,
        sites,
        flat_samples,
        (flags, couplings, up, down, above, below),
    )
    inner, outer, near_b = lax.optimization_barrier((inner, outer, near_b))
    row, cells_row = assembled(
        "row_payload",
        (upper, pair, outer, inner, cells),
        [(0, 0, 4), (1, 0, 4), (2, 0, 4), (4, 0, n_quad), (2, 4, n_quad), (3, 4, n_quad)],
        [(0, 12), (12, 12 + 3 * n_quad)],
    )
    row_d = lax.ppermute(row, "qx", cross_x)
    row_e = lax.ppermute(row, "qx", swap_x)
    cells_e = lax.ppermute(cells_row, "qx", swap_x)

    down_one = upper_levels(
        ny, far_one, far_two, couplings, transfer_two, row, row_e, row_d, cells_row, cells_e
    )

    on_left, on_right, down_one = lax.optimization_barrier((on_left, on_right, down_one))
    corner_down, corner_up = assembled(
        "corner_payload",
        (on_left, on_right),
        [(0, 4, 4), (1, 4, 4), (0, 11, 1), (1, 11, 1)]
        + [(0, 0, 4), (1, 0, 4), (0, 8, 1), (1, 8, 1)],
        [(0, 10), (10, 20)],
        stated=6000,
    )
    corner_above = lax.ppermute(corner_down, "qx", down_x)
    corner_below = lax.ppermute(corner_up, "qx", up_x)
    field, near = sides_level(
        flags, couplings, grouped(field), near_a, near_b, halo_a, halo_b,
        on_left, on_right, above, below,
    )
    result = last_level(
        flags, couplings, transfer_one, leaf_basis, down_one, field, near, halo_a, halo_b,
        corner_above, corner_below,
    )
    return result.reshape(4, 4, 256, 256)


def solution(mesh):
    return jax.shard_map(
        per_device,
        mesh=mesh,
        in_specs=(
            P(),
            P("qx", "qy", None, None),
            P("qx", "qy", None, None),
            P("qx", "qy", None, None),
            P("qx", "qy", None, None),
            P(),
            P("qx", "qy", None),
            P("qx", "qy", None),
            P("qx", "qy", None),
            P("qx", "qy", None),
        ),
        out_specs=P("qx", "qy", None, None),
        check_vma=False,
    )
```

```python
import functools

import jax
import jax.numpy as jnp
import numpy as np
from jax import lax
from jax.experimental import pallas as pl
from jax.experimental.pallas import tpu as pltpu
from jax.sharding import PartitionSpec as P

root_three = 1.7320508075688772
length_scale = 1.0
VMEM = pltpu.VMEM
SMEM = pltpu.SMEM
F32 = jnp.float32
BF16 = jnp.bfloat16
BIG = 64 * 1024 * 1024 - 256 * 1024


def nn(a, b):
    return lax.dot_general(a, b, (((1,), (0,)), ((), ())), preferred_element_type=F32)


def nt(a, b):
    return lax.dot_general(a, b, (((1,), (1,)), ((), ())), preferred_element_type=F32)


def tn(a, b):
    return lax.dot_general(a, b, (((0,), (0,)), ((), ())), preferred_element_type=F32)


def params():
    return pltpu.CompilerParams(vmem_limit_bytes=BIG)


def cost(products, bytes_accessed):
    return pl.CostEstimate(
        flops=products * 2 * 256**3 // 8, bytes_accessed=bytes_accessed // 8, transcendentals=0
    )


def half_offsets():
    kept = []
    for u in range(-3, 4):
        for v in range(-3, 4):
            if max(abs(u), abs(v)) >= 2 and (u > 0 or (u == 0 and v > 0)):
                kept.append((u, v))
    return kept


HALF_OFFSETS = half_offsets()


def class_plan(a, b):
    plain, turned = [], []
    for w in range(36):
        u, v = w // 6 - 2 - a, w % 6 - 2 - b
        if max(abs(u), abs(v)) < 2:
            continue
        if (u, v) in HALF_OFFSETS:
            plain.append((w, HALF_OFFSETS.index((u, v))))
        else:
            turned.append((w, HALF_OFFSETS.index((-u, -v))))
    return plain, turned


LOG2E = 1.4426950408889634
TILE_SCALE = 256 ** -0.5


def tiles(n, dtype=BF16):
    return jax.ShapeDtypeStruct((n, 256, 256), dtype)


ANY_SPEC = pl.BlockSpec(memory_space=pltpu.HBM)
SMEM_SPEC = pl.BlockSpec(memory_space=SMEM)
VMEM_SPEC = pl.BlockSpec(memory_space=VMEM)


class Copies:
    def __init__(self, sems):
        self.sems = sems
        self.started = []

    def start(self, src, dst):
        copy = pltpu.make_async_copy(src, dst, self.sems.at[len(self.started)])
        copy.start()
        self.started.append(copy)
        return copy

    def wait(self):
        for copy in self.started:
            copy.wait()


def coef_kernel(
    samples, basis, t_one, t_two, up, down, left, right, upper, cell,
    sv, bv, t1v, t2v, cv, uv, in_sems, out_sems,
):
    into = Copies(in_sems)
    out = Copies(out_sems)
    rows = []
    for x in range(4):
        rows.append(
            (
                into.start(samples.at[x], sv.at[x]),
                into.start(basis.at[x], bv.at[x]),
                into.start(t_one.at[x], t1v.at[x]),
            )
        )
    last = into.start(t_two, t2v)
    for x in range(4):
        rows[x][0].wait()
        rows[x][1].wait()
        for y in range(4):
            cv[x * 4 + y] = tn(sv[x, y], bv[x, y]).astype(BF16)
        own = cv.at[4 * x : 4 * x + 4]
        out.start(own, (up if x < 2 else down).at[4 * (x % 2) : 4 * (x % 2) + 4])
        out.start(cv.at[4 * x : 4 * x + 2], left.at[2 * x : 2 * x + 2])
        out.start(cv.at[4 * x + 2 : 4 * x + 4], right.at[2 * x : 2 * x + 2])
        out.start(sv.at[x, 0], left.at[8 + x])
        out.start(sv.at[x, 3], right.at[8 + x])
        if x == 0:
            out.start(sv.at[x], up.at[8:12])
        if x == 3:
            out.start(sv.at[x], down.at[8:12])
        if x % 2 == 1:
            rows[x - 1][2].wait()
            rows[x][2].wait()
            for y in range(2):
                kids = [(x - 1 + a, 2 * y + b) for a in range(2) for b in range(2)]
                lhs = jnp.concatenate([cv[k * 4 + m] for k, m in kids], axis=1)
                rhs = jnp.concatenate([t1v[k] for k in kids], axis=0)
                uv[x // 2 * 2 + y] = nn(lhs, rhs).astype(BF16)
    last.wait()
    lhs = jnp.concatenate([uv[k] for k in range(4)], axis=1)
    rhs = jnp.concatenate([t2v[k // 2, k % 2] for k in range(4)], axis=0)
    uv[4] = nn(lhs, rhs).astype(BF16)
    out.start(uv.at[0:4], up.at[12:16])
    out.start(uv.at[0:4], down.at[12:16])
    out.start(uv, upper)
    out.start(uv.at[4:5], cell)
    out.wait()


def coefficients(samples, basis, t_one, t_two):
    return pl.pallas_call(
        coef_kernel,
        out_shape=[tiles(n) for n in (16, 16, 12, 12, 5, 1)],
        in_specs=[ANY_SPEC] * 4,
        out_specs=[ANY_SPEC] * 6,
        scratch_shapes=[
            VMEM((4, 4, 256, 256), BF16),
            VMEM((4, 4, 256, 256), BF16),
            VMEM((4, 4, 256, 256), BF16),
            VMEM((2, 2, 256, 256), BF16),
            VMEM((16, 256, 256), BF16),
            VMEM((5, 256, 256), BF16),
            pltpu.SemaphoreType.DMA((13,)),
            pltpu.SemaphoreType.DMA((26,)),
        ],
        compiler_params=params(),
        cost_estimate=cost(170, 12 << 20),
        name="coefficients",
    )(samples, basis, t_one, t_two)


def assembled(name, sources, pieces, ranges, stated=35):
    count = sum(n for _, _, n in pieces)

    def kernel(*refs):
        ins, outs = refs[: len(sources)], refs[len(sources) : -3]
        held, in_sems, out_sems = refs[-3:]
        into = Copies(in_sems)
        at = 0
        for source, first, n in pieces:
            into.start(ins[source].at[first : first + n], held.at[at : at + n])
            at += n
        into.wait()
        out = Copies(out_sems)
        for (first, last), ref in zip(ranges, outs):
            out.start(held.at[first:last], ref)
        out.wait()

    return pl.pallas_call(
        kernel,
        out_shape=[tiles(last - first) for first, last in ranges],
        in_specs=[ANY_SPEC] * len(sources),
        out_specs=[ANY_SPEC] * len(ranges),
        scratch_shapes=[
            VMEM((count, 256, 256), BF16),
            pltpu.SemaphoreType.DMA((len(pieces),)),
            pltpu.SemaphoreType.DMA((len(ranges),)),
        ],
        compiler_params=params(),
        cost_estimate=cost(stated, 0),
        name=name,
    )(*sources)


def halo_places():
    numbers = {}
    for r in range(4):
        for c in range(4):
            for k in range(9):
                y, x = r + k // 3 - 1, c + k % 3 - 1
                if not (0 <= y < 4 and 0 <= x < 4):
                    numbers[r * 4 + c, k] = len(numbers)
    return numbers


HALO = halo_places()
N_HALO = len(HALO) // 2


def split3(x):
    first = x.astype(BF16).astype(F32)
    rest = x - first
    second = rest.astype(BF16).astype(F32)
    return first, second, rest - second


def site_features(x, y):
    n = lax.broadcasted_iota(jnp.int32, (8, 256), 0)
    square = x * x + y * y
    target, source = [], []
    for parts in (split3(x), split3(y)):
        first, second, third = parts
        target.append(jnp.where(n < 3, first, jnp.where(n < 5, second, jnp.where(n < 6, third, 0.0))))
        other = jnp.where(
            (n == 0) | (n == 3) | (n == 5),
            first,
            jnp.where((n == 1) | (n == 4), second, jnp.where(n == 2, third, 0.0)),
        )
        source.append(-2.0 * other)
    first, second, third = split3(square)
    low = jnp.where(n == 0, first, jnp.where(n == 1, second, third))
    high = jnp.where(n == 3, first, jnp.where(n == 4, second, third))
    one = jnp.where(n < 6, 1.0, 0.0)
    target.append(jnp.where(n < 3, low, one))
    source.append(jnp.where(n < 3, 1.0, jnp.where(n < 6, high, 0.0)))
    zero = jnp.zeros((8, 256), F32)
    return jnp.concatenate(target + [zero], axis=0), jnp.concatenate(source + [zero], axis=0)


def near_kernel(
    first, with_far, grid_rows, grid_cols, lists, far_zero, positions, own, *rest
):
    if with_far:
        flags, couplings, up, down, above, below, near_out, halo_out, field_out = rest[:9]
        table, far_held, field, far_sems, field_sems = rest[9:14]
        rest = rest[14:]
    else:
        near_out, halo_out, flags = rest[:3]
        rest = rest[3:]
    held, target_feat, source_feat, halo, made, near, floors, sems, halo_sems, near_sems = rest
    copy = pltpu.make_async_copy(own, held, sems.at[0])
    copy.start()
    out = Copies(halo_sems)
    sums_out = Copies(near_sems)
    if with_far:
        far_in = Copies(far_sems)
        far_in.start(couplings.at[0], table)
        for n, src in enumerate((above, up, down, below)):
            far_in.start(src.at[0:8], far_held.at[8 * n : 8 * n + 8])
        far_held[32] = jnp.zeros((256, 256), BF16)
        field_copies = Copies(field_sems)
    first_row = lax.axis_index("qx") * 4
    first_col = lax.axis_index("qy") * 4
    scale = root_three / length_scale
    mid_row = first_row.astype(F32) + 2.0
    mid_col = first_col.astype(F32) + 2.0
    first_place = first // 4 * 6

    def features(n, carry):
        r = jnp.clip(first_row + (first_place + n) // 6 - 1, 0, grid_rows - 1)
        c = jnp.clip(first_col + n % 6 - 1, 0, grid_cols - 1)
        here = positions[r * grid_cols + c]
        target, source = site_features(
            (here[0:1] - mid_row) * scale, (here[1:2] - mid_col) * scale
        )
        target_feat[n] = target
        source_feat[n] = source.astype(BF16)
        return carry

    lax.fori_loop(0, 24, features, 0)

    def mark(t):
        r, c = t // 4, t % 4
        mark_listed(
            lambda e: far_zero[r, c, e],
            flags,
            t,
            first_row + r // 2 * 2 - 2,
            first_col + c // 2 * 2 - 2,
            grid_cols,
        )

    def make(m):
        t = first + m
        r, c = t // 4, t % 4
        slot = m % 2 * 9
        for k in range(9):
            floors[m * 10 + k] = 1e6
        for e in range(9):
            entry = lists[r, c, e]
            source_row = jnp.maximum(entry, 0) // grid_cols
            source_col = jnp.maximum(entry, 0) - source_row * grid_cols
            k = (source_row - first_row - r + 1) * 3 + source_col - first_col - c + 1
            floors[m * 10 + jnp.where(entry >= 0, k, 9)] = 1e-24
        if not with_far:
            mark(2 * m)
            mark(2 * m + 1)
        place = (m // 4 + 1) * 6 + c + 1
        target = target_feat[place].T.astype(BF16)
        for k in range(9):
            square = nn(target, source_feat[place + (k // 3 - 1) * 6 + k % 3 - 1])
            square = jnp.maximum(square, floors[m * 10 + k])
            far = square * lax.rsqrt(square)
            tile = ((far + 1.0) * jnp.exp2(far * -LOG2E)).astype(BF16)
            if (t, k) in HALO:
                number = HALO[t, k] % N_HALO
                halo[number] = tile
                out.start(halo.at[number], halo_out.at[number])
            else:
                made[slot + k] = tile

    def use(m):
        t = first + m
        slot = m % 2 * 9
        found = [k for k in range(9) if (t, k) not in HALO]
        lhs = jnp.concatenate([made[slot + k] for k in found], axis=1)
        blocks = [held[t + (k // 3 - 1) * 4 + k % 3 - 1] for k in found]
        near[m] = nn(lhs, jnp.concatenate(blocks, axis=0))
        sums_out.start(near.at[m], near_out.at[m])

    make(0)
    copy.wait()
    if with_far:
        far_in.wait()
    for m in range(1, 8):
        make(m)
        if with_far and m % 2 == 1:
            a, b = m // 4, m // 2 % 2
            sums = level_zero_sums("inner", a, b, flags, table, far_held, 32)
            for p in PARENTS:
                t = number_of(a, b, p)
                field[t] = sums[p]
                field_copies.start(field.at[t], field_out.at[t])
        use(m - 1)
    use(7)
    out.wait()
    sums_out.wait()
    if with_far:
        field_copies.wait()


def near_call(first, grid_rows, grid_cols, lists, far_zero, positions, own, far=()):
    out_shape = [tiles(8, F32), tiles(N_HALO)]
    out_specs = [ANY_SPEC, ANY_SPEC]
    scratch = []
    if far:
        out_shape.append(tiles(16, F32))
        out_specs.append(ANY_SPEC)
        scratch = [
            VMEM((20, 256, 256), BF16),
            VMEM((33, 256, 256), BF16),
            VMEM((16, 256, 256), F32),
            pltpu.SemaphoreType.DMA((5,)),
            pltpu.SemaphoreType.DMA((16,)),
        ]
    else:
        out_shape.append(jax.ShapeDtypeStruct((16, 37), jnp.int32))
        out_specs.append(SMEM_SPEC)
    return pl.pallas_call(
        functools.partial(near_kernel, first, bool(far), grid_rows, grid_cols),
        out_shape=out_shape,
        in_specs=[SMEM_SPEC, SMEM_SPEC, VMEM_SPEC, ANY_SPEC]
        + ([SMEM_SPEC] + [ANY_SPEC] * 5 if far else []),
        out_specs=out_specs,
        scratch_shapes=scratch
        + [
            VMEM((16, 256, 256), BF16),
            VMEM((24, 32, 256), F32),
            VMEM((24, 32, 256), BF16),
            VMEM((N_HALO, 256, 256), BF16),
            VMEM((18, 256, 256), BF16),
            VMEM((8, 256, 256), F32),
            pltpu.SMEM((80,), F32),
            pltpu.SemaphoreType.DMA((1,)),
            pltpu.SemaphoreType.DMA((N_HALO,)),
            pltpu.SemaphoreType.DMA((8,)),
        ],
        compiler_params=params(),
        cost_estimate=cost(600 if far else 12000, 8 << 20),
        name="near_and_inner_far" if far else "near_first",
    )(lists, far_zero, positions, own, *far)


def mark_listed(entries, flags, n, first_row, first_col, grid_cols):
    for w in range(36):
        flags[n, w] = 0
    for e in range(27):
        entry = entries(e)
        row = jnp.maximum(entry, 0) // grid_cols
        col = jnp.maximum(entry, 0) - row * grid_cols
        w = (row - first_row) * 6 + col - first_col
        flags[n, jnp.where(entry >= 0, jnp.clip(w, 0, 35), 36)] = 1


def dot_group(held, couplings, turned, group):
    rows = len(group[0][1])
    lhs = [
        jnp.concatenate([held[places[n]] for _, places in group], axis=1) for n in range(rows)
    ]
    lhs = jnp.concatenate(lhs, axis=0) if rows > 1 else lhs[0]
    if turned:
        return nn(lhs, jnp.concatenate([couplings[k] for k, _ in group], axis=0))
    return nt(lhs, jnp.concatenate([couplings[k] for k, _ in group], axis=1))


def coupled(plan, couplings, held, places):
    total = None
    for turned in (0, 1):
        group = [(k, [places(w)]) for w, k in plan[turned]]
        part = dot_group(held, couplings, turned, group)
        total = part if total is None else total + part
    return total


def upper_kernel(
    grid_cols, n_rows, far_one, far_two, couplings, t_two, upper, above, below, row, row_e, row_d,
    cells, cells_e, quads, quads_e, down, held_one, held_two, field_two, flags, sems,
):
    n_cells = 2 * n_rows
    n_two = 3 * n_cells
    zero_one, zero_two = 36, 2 * n_two
    copies = Copies(sems)
    copies.start(cells, held_two.at[0:n_cells])
    copies.start(quads, held_two.at[n_cells:n_two])
    copies.start(cells_e, held_two.at[n_two : n_two + n_cells])
    copies.start(quads_e, held_two.at[n_two + n_cells : 2 * n_two])
    copies.start(upper.at[0:4], held_one.at[0:4])
    copies.start(row, held_one.at[4:12])
    copies.start(above.at[12:16], held_one.at[12:16])
    copies.start(below.at[12:16], held_one.at[16:20])
    copies.start(row_e, held_one.at[20:28])
    copies.start(row_d, held_one.at[28:36])
    held_one[zero_one] = jnp.zeros((256, 256), BF16)
    held_two[zero_two] = jnp.zeros((256, 256), BF16)
    i = lax.axis_index("qx")
    j = lax.axis_index("qy")
    a = i % 2
    b = j % 2
    for t in range(4):
        mark_listed(
            lambda e: far_one[t // 2, t % 2, e], flags, t, 2 * i - 2, 2 * j - 2, 2 * grid_cols
        )
    mark_listed(
        lambda e: far_two[0, 0, e], flags, 4, i // 2 * 2 - 2, j // 2 * 2 - 2, grid_cols
    )
    core_at = [jnp.where(a == 0, 0, n_two), jnp.where(a == 0, n_two, 0)]
    y_at = [2, 0, 2] if n_rows == 2 else [2, 0, 4]
    pair_tiles = 2 * n_rows
    z_at = [
        jnp.where(b == 0, pair_tiles, 2 * pair_tiles),
        0,
        jnp.where(b == 0, 2 * pair_tiles, pair_tiles),
    ]
    x_at = [b, 1 - b]

    def place_two(w):
        r, c = w // 6, w % 6
        place = core_at[r % 2] + y_at[r // 2] + z_at[c // 2] + x_at[c % 2]
        return jnp.where(flags[4, w] == 1, place, zero_two)

    own_at = [12, 0, 16]
    pair_at = [jnp.where(a == 0, 28, 20), 4, jnp.where(a == 0, 20, 28)]
    col_at = [jnp.where(b == 0, 4, 0), None, jnp.where(b == 0, 0, 4)]

    def place_one(t, w):
        r, c = w // 6, w % 6
        base = own_at[r // 2] if c // 2 == 1 else pair_at[r // 2] + col_at[c // 2]
        place = base + (r % 2) * 2 + c % 2
        return jnp.where(flags[t, w] == 1, place, zero_one)

    for copy in copies.started[:4]:
        copy.wait()
    for u in range(2):
        for v in range(2):

            @pl.when((a == u) & (b == v))
            def _():
                field_two[...] = coupled(
                    class_plan(u, v), couplings.at[1], held_two, place_two
                ).astype(BF16)

    for copy in copies.started[4:]:
        copy.wait()
    for u in range(2):
        for v in range(2):
            t = u * 2 + v
            field = coupled(
                class_plan(u, v), couplings.at[0], held_one, functools.partial(place_one, t)
            )
            down[t] = (field + nt(field_two[...], t_two[u, v])).astype(BF16)


def upper_levels(grid_cols, far_one, far_two, couplings, t_two, *received):
    n_two = 3 * received[6].shape[0]
    return pl.pallas_call(
        functools.partial(upper_kernel, grid_cols, n_two // 6),
        grid=(1,),
        out_shape=tiles(4),
        in_specs=[
            SMEM_SPEC,
            SMEM_SPEC,
            pl.BlockSpec(
                (pl.Element(2), pl.Element(20), pl.Element(256), pl.Element(256)),
                lambda g: (1, 0, 0, 0),
            ),
            pl.BlockSpec((2, 2, 256, 256), lambda g: (0, 0, 0, 0)),
        ]
        + [ANY_SPEC] * 10,
        out_specs=pl.BlockSpec((4, 256, 256), lambda g: (0, 0, 0)),
        scratch_shapes=[
            VMEM((37, 256, 256), BF16),
            VMEM((2 * n_two + 1, 256, 256), BF16),
            VMEM((256, 256), BF16),
            pltpu.SMEM((5, 37), jnp.int32),
            pltpu.SemaphoreType.DMA((10,)),
        ],
        compiler_params=params(),
        cost_estimate=cost(340, 14 << 20),
        name="upper_levels",
    )(far_one, far_two, couplings, t_two, *received)


def source_of(x, y, w):
    r, c = 2 * x + w // 6, 2 * y + w % 6
    if 2 <= c < 6:
        return "inner", r * 4 + c - 2
    side = 0 if c < 2 else 1
    c = c if c < 2 else c - 6
    if 2 <= r < 6:
        return "sides", side * 8 + (r - 2) * 2 + c
    return "corners", (0 if r < 2 else 8) + side * 4 + (r if r < 2 else r - 6) * 2 + c


PARENTS = [(x, y) for x in range(2) for y in range(2)]


def number_of(a, b, parent):
    x, y = parent
    return (2 * x + a) * 4 + 2 * y + b


def level_zero_sums(kind, a, b, flags, couplings, held, zero):
    plan = class_plan(a, b)
    sums = {}
    for turned in (0, 1):
        groups = {}
        for w, k in plan[turned]:
            members = tuple(p for p in PARENTS if source_of(*p, w)[0] == kind)
            if members:
                groups.setdefault(members, []).append((w, k))
        for members, entries in groups.items():
            group = []
            for w, k in entries:
                places = [
                    jnp.where(flags[number_of(a, b, p), w] == 1, source_of(*p, w)[1], zero)
                    for p in members
                ]
                group.append((k, places))
            total = dot_group(held, couplings, turned, group)
            for n, p in enumerate(members):
                part = total[256 * n : 256 * n + 256]
                sums[p] = part if p not in sums else sums[p] + part
    return sums


def grouped(x):
    return x.reshape(2, 2, 2, 2, 256, 256)


CLASS_BLOCK = pl.BlockSpec((2, 1, 2, 1, 256, 256), lambda g: (0, g // 2, 0, g % 2, 0, 0))
COUPLING_BLOCK = pl.BlockSpec((1, 20, 256, 256), lambda g: (0, 0, 0, 0))
GROUPED_F32 = jax.ShapeDtypeStruct((2, 2, 2, 2, 256, 256), F32)


def each_class(step, body):
    for a in range(2):
        for b in range(2):
            pl.when(step == a * 2 + b)(functools.partial(body, a, b))


def near_source(r, c):
    rows_in, cols_in = 1 <= r < 5, 1 <= c < 5
    if rows_in and cols_in:
        return "own", None
    if rows_in:
        return "sides", (0 if c == 0 else 4) + r - 1
    if cols_in:
        return "sides", (8 if r == 0 else 12) + c - 1
    return "corners", (0 if r == 0 else 2) + (0 if c == 0 else 1)


CORNER_HALO = [
    n for (t, k), n in HALO.items() if near_source(t // 4 + k // 3, t % 4 + k % 3)[0] == "corners"
]


def near_part(kind, t, tile_of, held):
    r, c = t // 4, t % 4
    made, blocks = [], []
    for k in range(9):
        found, place = near_source(r + k // 3, c + k % 3)
        if found == kind:
            made.append(tile_of(HALO[t, k]))
            blocks.append(held[place])
    if not made:
        return None
    return nn(jnp.concatenate(made, axis=1), jnp.concatenate(blocks, axis=0))


def sides_kernel(
    flags, couplings, field_in, near_a, near_b, halo_a, halo_b, left, right, above, below,
    field, near, held, near_held, halo, sems,
):
    step = pl.program_id(0)

    def copies():
        pairs = [(left.at[0:8], held.at[0:8]), (right.at[0:8], held.at[8:16])]
        for n, src in enumerate((left, right, above, below)):
            pairs.append((src.at[8:12], near_held.at[4 * n : 4 * n + 4]))
        pairs.append((halo_a, halo.at[0:N_HALO]))
        pairs.append((halo_b, halo.at[N_HALO : 2 * N_HALO]))
        return [pltpu.make_async_copy(src, dst, sems.at[n]) for n, (src, dst) in enumerate(pairs)]

    @pl.when(step == 0)
    def _():
        started = copies()
        for copy in started:
            copy.start()
        held[16] = jnp.zeros((256, 256), BF16)
        for copy in started[:2]:
            copy.wait()

    def body(a, b):
        sums = level_zero_sums("sides", a, b, flags, couplings.at[0], held, 16)
        for x, y in PARENTS:
            field[x, 0, y, 0] = field_in[x, 0, y, 0] + sums[x, y]
        if a == 0 and b == 0:
            for copy in copies()[2:]:
                copy.wait()
        for x, y in PARENTS:
            part = near_part("sides", number_of(a, b, (x, y)), lambda n: halo[n], near_held)
            here = (near_b if x else near_a)[0, y, 0]
            near[x, 0, y, 0] = here if part is None else here + part

    each_class(step, body)


HALF_BLOCK = pl.BlockSpec((1, 2, 1, 256, 256), lambda g: (g // 2, 0, g % 2, 0, 0))


def sides_level(flags, couplings, field, near_a, near_b, *received):
    half = lambda x: x.reshape(2, 2, 2, 256, 256)
    return pl.pallas_call(
        sides_kernel,
        grid=(4,),
        out_shape=(GROUPED_F32, GROUPED_F32),
        in_specs=[SMEM_SPEC, COUPLING_BLOCK, CLASS_BLOCK, HALF_BLOCK, HALF_BLOCK] + [ANY_SPEC] * 6,
        out_specs=[CLASS_BLOCK, CLASS_BLOCK],
        scratch_shapes=[
            VMEM((17, 256, 256), BF16),
            VMEM((16, 256, 256), BF16),
            VMEM((2 * N_HALO, 256, 256), BF16),
            pltpu.SemaphoreType.DMA((8,)),
        ],
        compiler_params=params(),
        cost_estimate=cost(300, 30 << 20),
        name="far_sides",
    )(flags, couplings, field, half(near_a), half(near_b), *received)


def last_kernel(
    flags, couplings, t_one, basis, down_one, field, near, halo_a, halo_b, above, below, out,
    held, near_held, halo, sems,
):
    step = pl.program_id(0)

    @pl.when(step == 0)
    def _():
        copies = Copies(sems)
        copies.start(above.at[0:8], held.at[0:8])
        copies.start(below.at[0:8], held.at[8:16])
        copies.start(above.at[8:10], near_held.at[0:2])
        copies.start(below.at[8:10], near_held.at[2:4])
        for m, n in enumerate(CORNER_HALO):
            copies.start((halo_a if n < N_HALO else halo_b).at[n % N_HALO], halo.at[m])
        held[16] = jnp.zeros((256, 256), BF16)
        copies.wait()

    def body(a, b):
        sums = level_zero_sums("corners", a, b, flags, couplings.at[0], held, 16)
        for x, y in PARENTS:
            total = field[x, 0, y, 0] + nt(down_one[x * 2 + y], t_one[x, 0, y, 0])
            if (x, y) in sums:
                total = total + sums[x, y]
            far = nt(basis[x, 0, y, 0], total.astype(BF16))
            near_sum = near[x, 0, y, 0]
            part = near_part(
                "corners",
                number_of(a, b, (x, y)),
                lambda n: halo[CORNER_HALO.index(n)],
                near_held,
            )
            if part is not None:
                near_sum = near_sum + part
            out[x, 0, y, 0] = (near_sum * TILE_SCALE + far).astype(BF16)

    each_class(step, body)


def last_level(flags, couplings, t_one, basis, *rest):
    return pl.pallas_call(
        last_kernel,
        grid=(4,),
        out_shape=jax.ShapeDtypeStruct((2, 2, 2, 2, 256, 256), BF16),
        in_specs=[
            SMEM_SPEC,
            COUPLING_BLOCK,
            CLASS_BLOCK,
            CLASS_BLOCK,
            pl.BlockSpec((4, 256, 256), lambda g: (0, 0, 0)),
            CLASS_BLOCK,
            CLASS_BLOCK,
        ]
        + [ANY_SPEC] * 4,
        out_specs=CLASS_BLOCK,
        scratch_shapes=[
            VMEM((17, 256, 256), BF16),
            VMEM((4, 256, 256), BF16),
            VMEM((len(CORNER_HALO), 256, 256), BF16),
            pltpu.SemaphoreType.DMA((4 + len(CORNER_HALO),)),
        ],
        compiler_params=params(),
        cost_estimate=cost(270, 20 << 20),
        name="last_level",
    )(flags, couplings, grouped(t_one), grouped(basis), *rest)


def per_device(
    positions,
    samples,
    leaf_basis,
    transfer_one,
    transfer_two,
    couplings,
    near_lists,
    far_zero,
    far_one,
    far_two,
):
    nx = lax.axis_size("qx")
    ny = lax.axis_size("qy")
    down_x = [(k, k + 1) for k in range(nx - 1)]
    up_x = [(k + 1, k) for k in range(nx - 1)]
    down_y = [(k, k + 1) for k in range(ny - 1)]
    up_y = [(k + 1, k) for k in range(ny - 1)]

    up, down, left, right, upper, cell = coefficients(
        samples, leaf_basis, transfer_one, transfer_two
    )

    swap_y = [(k, k ^ 1) for k in range(ny)]
    swap_x = [(k, k ^ 1) for k in range(nx)]
    cross_x = [(k, k + 1) for k in range(1, nx - 1, 2)] + [(k + 1, k) for k in range(1, nx - 1, 2)]
    pair = lax.ppermute(upper, "qy", swap_y)
    if nx == 4:
        others = [lax.ppermute(cell, "qx", [(k, k ^ 2) for k in range(nx)])]
    else:
        others = [
            lax.ppermute(cell, "qx", [(k, k + 2) for k in range(nx - 2)]),
            lax.ppermute(cell, "qx", [(k + 2, k) for k in range(nx - 2)]),
        ]
    others_pair = [lax.ppermute(x, "qy", swap_y) for x in others]
    above = lax.ppermute(down, "qx", down_x)
    below = lax.ppermute(up, "qx", up_x)
    sites = positions.reshape(-1, 2, 256)
    flat_samples = samples.reshape(16, 256, 256)
    near_a, halo_a, flags = near_call(
        0, 4 * nx, 4 * ny, near_lists, far_zero, sites, flat_samples
    )
    pair, others_pair, near_a = lax.optimization_barrier((pair, others_pair, near_a))
    outward = [(k, k + 2) for k in range(0, ny - 2, 2)] + [(k + 2, k) for k in range(1, ny - 2, 2)]
    inward = [(k + 2, k) for k in range(0, ny - 2, 2)] + [(k, k + 2) for k in range(1, ny - 2, 2)]
    n_others = len(others)
    quad = [(0, 4, 1), (1, 4, 1)]
    for n in range(n_others):
        quad += [(2 + n, 0, 1), (2 + n_others + n, 0, 1)]
    n_quad = len(quad)
    across, cells = assembled(
        "pair_payload",
        (upper, pair, *others, *others_pair),
        [(1, 0, 4)] + quad,
        [(0, 4 + n_quad), (4, 4 + n_quad)],
    )
    across, cells, left, right = lax.optimization_barrier((across, cells, left, right))
    outer = lax.ppermute(across, "qy", outward)
    inner = lax.ppermute(cells, "qy", inward)
    cells_e = lax.ppermute(cells, "qx", swap_x)
    on_left = lax.ppermute(right, "qy", down_y)
    on_right = lax.ppermute(left, "qy", up_y)
    near_b, halo_b, field = near_call(
        8,
        4 * nx,
        4 * ny,
        near_lists,
        far_zero,
        sites,
        flat_samples,
        (flags, couplings, up, down, above, below),
    )
    inner, outer, near_b = lax.optimization_barrier((inner, outer, near_b))
    row, quads = assembled(
        "row_payload",
        (pair, outer, inner),
        [(0, 0, 4), (1, 0, 4), (1, 4, n_quad), (2, 0, n_quad)],
        [(0, 8), (8, 8 + 2 * n_quad)],
    )
    row_d = lax.ppermute(row, "qx", cross_x)
    row_e = lax.ppermute(row, "qx", swap_x)
    quads_e = lax.ppermute(quads, "qx", swap_x)
    down_one = upper_levels(
        ny, far_one, far_two, couplings, transfer_two, upper, above, below, row, row_e, row_d,
        cells, cells_e, quads, quads_e,
    )

    on_left, on_right, down_one = lax.optimization_barrier((on_left, on_right, down_one))
    corner_down, corner_up = assembled(
        "corner_payload",
        (on_left, on_right),
        [(0, 4, 4), (1, 4, 4), (0, 11, 1), (1, 11, 1)]
        + [(0, 0, 4), (1, 0, 4), (0, 8, 1), (1, 8, 1)],
        [(0, 10), (10, 20)],
        stated=35,
    )
    corner_above = lax.ppermute(corner_down, "qx", down_x)
    corner_below = lax.ppermute(corner_up, "qx", up_x)
    field, near = sides_level(
        flags, couplings, grouped(field), near_a, near_b, halo_a, halo_b,
        on_left, on_right, above, below,
    )
    result = last_level(
        flags, couplings, transfer_one, leaf_basis, down_one, field, near, halo_a, halo_b,
        corner_above, corner_below,
    )
    return result.reshape(4, 4, 256, 256)


def solution(mesh):
    return jax.shard_map(
        per_device,
        mesh=mesh,
        in_specs=(
            P(),
            P("qx", "qy", None, None),
            P("qx", "qy", None, None),
            P("qx", "qy", None, None),
            P("qx", "qy", None, None),
            P(),
            P("qx", "qy", None),
            P("qx", "qy", None),
            P("qx", "qy", None),
            P("qx", "qy", None),
        ),
        out_specs=P("qx", "qy", None, None),
        check_vma=False,
    )
```

```python
import functools

import jax
import jax.numpy as jnp
import numpy as np
from jax import lax
from jax.experimental import pallas as pl
from jax.experimental.pallas import tpu as pltpu
from jax.sharding import PartitionSpec as P

root_three = 1.7320508075688772
length_scale = 1.0
VMEM = pltpu.VMEM
SMEM = pltpu.SMEM
F32 = jnp.float32
BF16 = jnp.bfloat16
BIG = 64 * 1024 * 1024 - 256 * 1024


def nn(a, b):
    return lax.dot_general(a, b, (((1,), (0,)), ((), ())), preferred_element_type=F32)


def nt(a, b):
    return lax.dot_general(a, b, (((1,), (1,)), ((), ())), preferred_element_type=F32)


def tn(a, b):
    return lax.dot_general(a, b, (((0,), (0,)), ((), ())), preferred_element_type=F32)


def params():
    return pltpu.CompilerParams(vmem_limit_bytes=BIG)


def cost(products, bytes_accessed):
    return pl.CostEstimate(
        flops=products * 2 * 256**3 // 8, bytes_accessed=bytes_accessed // 8, transcendentals=0
    )


def half_offsets():
    kept = []
    for u in range(-3, 4):
        for v in range(-3, 4):
            if max(abs(u), abs(v)) >= 2 and (u > 0 or (u == 0 and v > 0)):
                kept.append((u, v))
    return kept


HALF_OFFSETS = half_offsets()


def class_plan(a, b):
    plain, turned = [], []
    for w in range(36):
        u, v = w // 6 - 2 - a, w % 6 - 2 - b
        if max(abs(u), abs(v)) < 2:
            continue
        if (u, v) in HALF_OFFSETS:
            plain.append((w, HALF_OFFSETS.index((u, v))))
        else:
            turned.append((w, HALF_OFFSETS.index((-u, -v))))
    return plain, turned


LOG2E = 1.4426950408889634
TILE_SCALE = 256 ** -0.5


def tiles(n, dtype=BF16):
    return jax.ShapeDtypeStruct((n, 256, 256), dtype)


ANY_SPEC = pl.BlockSpec(memory_space=pltpu.HBM)
SMEM_SPEC = pl.BlockSpec(memory_space=SMEM)
VMEM_SPEC = pl.BlockSpec(memory_space=VMEM)


class Copies:
    def __init__(self, sems):
        self.sems = sems
        self.started = []

    def start(self, src, dst):
        copy = pltpu.make_async_copy(src, dst, self.sems.at[len(self.started)])
        copy.start()
        self.started.append(copy)
        return copy

    def wait(self):
        for copy in self.started:
            copy.wait()


def coef_kernel(
    samples, basis, t_one, t_two, up, down, left, right, upper, cell,
    sv, bv, t1v, t2v, cv, uv, in_sems, out_sems,
):
    into = Copies(in_sems)
    out = Copies(out_sems)
    rows = []
    for x in range(4):
        rows.append(
            (
                into.start(samples.at[x], sv.at[x]),
                into.start(basis.at[x], bv.at[x]),
                into.start(t_one.at[x], t1v.at[x]),
            )
        )
    last = into.start(t_two, t2v)
    for x in range(4):
        rows[x][0].wait()
        rows[x][1].wait()
        for y in range(4):
            cv[x * 4 + y] = tn(sv[x, y], bv[x, y]).astype(BF16)
        own = cv.at[4 * x : 4 * x + 4]
        out.start(own, (up if x < 2 else down).at[4 * (x % 2) : 4 * (x % 2) + 4])
        out.start(cv.at[4 * x : 4 * x + 2], left.at[2 * x : 2 * x + 2])
        out.start(cv.at[4 * x + 2 : 4 * x + 4], right.at[2 * x : 2 * x + 2])
        out.start(sv.at[x, 0], left.at[8 + x])
        out.start(sv.at[x, 3], right.at[8 + x])
        if x == 0:
            out.start(sv.at[x], up.at[8:12])
        if x == 3:
            out.start(sv.at[x], down.at[8:12])
        if x % 2 == 1:
            rows[x - 1][2].wait()
            rows[x][2].wait()
            for y in range(2):
                kids = [(x - 1 + a, 2 * y + b) for a in range(2) for b in range(2)]
                lhs = jnp.concatenate([cv[k * 4 + m] for k, m in kids], axis=1)
                rhs = jnp.concatenate([t1v[k] for k in kids], axis=0)
                uv[x // 2 * 2 + y] = nn(lhs, rhs).astype(BF16)
    last.wait()
    lhs = jnp.concatenate([uv[k] for k in range(4)], axis=1)
    rhs = jnp.concatenate([t2v[k // 2, k % 2] for k in range(4)], axis=0)
    uv[4] = nn(lhs, rhs).astype(BF16)
    out.start(uv.at[0:4], up.at[12:16])
    out.start(uv.at[0:4], down.at[12:16])
    out.start(uv, upper)
    out.start(uv.at[4:5], cell)
    out.wait()


def coefficients(samples, basis, t_one, t_two):
    return pl.pallas_call(
        coef_kernel,
        out_shape=[tiles(n) for n in (16, 16, 12, 12, 5, 1)],
        in_specs=[ANY_SPEC] * 4,
        out_specs=[ANY_SPEC] * 6,
        scratch_shapes=[
            VMEM((4, 4, 256, 256), BF16),
            VMEM((4, 4, 256, 256), BF16),
            VMEM((4, 4, 256, 256), BF16),
            VMEM((2, 2, 256, 256), BF16),
            VMEM((16, 256, 256), BF16),
            VMEM((5, 256, 256), BF16),
            pltpu.SemaphoreType.DMA((13,)),
            pltpu.SemaphoreType.DMA((26,)),
        ],
        compiler_params=params(),
        cost_estimate=cost(170, 12 << 20),
        name="coefficients",
    )(samples, basis, t_one, t_two)


def assembled(name, sources, pieces, ranges, stated=35):
    count = sum(n for _, _, n in pieces)

    def kernel(*refs):
        ins, outs = refs[: len(sources)], refs[len(sources) : -3]
        held, in_sems, out_sems = refs[-3:]
        into = Copies(in_sems)
        at = 0
        for source, first, n in pieces:
            into.start(ins[source].at[first : first + n], held.at[at : at + n])
            at += n
        into.wait()
        out = Copies(out_sems)
        for (first, last), ref in zip(ranges, outs):
            out.start(held.at[first:last], ref)
        out.wait()

    return pl.pallas_call(
        kernel,
        out_shape=[tiles(last - first) for first, last in ranges],
        in_specs=[ANY_SPEC] * len(sources),
        out_specs=[ANY_SPEC] * len(ranges),
        scratch_shapes=[
            VMEM((count, 256, 256), BF16),
            pltpu.SemaphoreType.DMA((len(pieces),)),
            pltpu.SemaphoreType.DMA((len(ranges),)),
        ],
        compiler_params=params(),
        cost_estimate=cost(stated, 0),
        name=name,
    )(*sources)


def halo_places():
    numbers = {}
    for r in range(4):
        for c in range(4):
            for k in range(9):
                y, x = r + k // 3 - 1, c + k % 3 - 1
                if not (0 <= y < 4 and 0 <= x < 4):
                    numbers[r * 4 + c, k] = len(numbers)
    return numbers


HALO = halo_places()
N_HALO = len(HALO) // 2


def split3(x):
    first = x.astype(BF16).astype(F32)
    rest = x - first
    second = rest.astype(BF16).astype(F32)
    return first, second, rest - second


def site_features(x, y):
    n = lax.broadcasted_iota(jnp.int32, (8, 256), 0)
    square = x * x + y * y
    target, source = [], []
    for parts in (split3(x), split3(y)):
        first, second, third = parts
        target.append(jnp.where(n < 3, first, jnp.where(n < 5, second, jnp.where(n < 6, third, 0.0))))
        other = jnp.where(
            (n == 0) | (n == 3) | (n == 5),
            first,
            jnp.where((n == 1) | (n == 4), second, jnp.where(n == 2, third, 0.0)),
        )
        source.append(-2.0 * other)
    first, second, third = split3(square)
    low = jnp.where(n == 0, first, jnp.where(n == 1, second, third))
    high = jnp.where(n == 3, first, jnp.where(n == 4, second, third))
    one = jnp.where(n < 6, 1.0, 0.0)
    target.append(jnp.where(n < 3, low, one))
    source.append(jnp.where(n < 3, 1.0, jnp.where(n < 6, high, 0.0)))
    zero = jnp.zeros((8, 256), F32)
    return jnp.concatenate(target + [zero], axis=0), jnp.concatenate(source + [zero], axis=0)


def near_kernel(
    first, with_far, grid_rows, grid_cols, lists, far_zero, positions, own, *rest
):
    if with_far:
        couplings, up, down, above, below, near_out, halo_out, field_out, flags = rest[:9]
        table, far_held, field, far_sems, field_sems = rest[9:14]
        rest = rest[14:]
    else:
        near_out, halo_out = rest[:2]
        rest = rest[2:]
    held, target_feat, source_feat, halo, made, near, floors, sems, halo_sems, near_sems = rest
    copy = pltpu.make_async_copy(own, held, sems.at[0])
    copy.start()
    out = Copies(halo_sems)
    sums_out = Copies(near_sems)
    if with_far:
        far_in = Copies(far_sems)
        far_in.start(couplings.at[0], table)
        for n, src in enumerate((above, up, down, below)):
            far_in.start(src.at[0:8], far_held.at[8 * n : 8 * n + 8])
        far_held[32] = jnp.zeros((256, 256), BF16)
        field_copies = Copies(field_sems)
    first_row = lax.axis_index("qx") * 4
    first_col = lax.axis_index("qy") * 4
    scale = root_three / length_scale
    mid_row = first_row.astype(F32) + 2.0
    mid_col = first_col.astype(F32) + 2.0
    first_place = first // 4 * 6

    def features(n, carry):
        r = jnp.clip(first_row + (first_place + n) // 6 - 1, 0, grid_rows - 1)
        c = jnp.clip(first_col + n % 6 - 1, 0, grid_cols - 1)
        here = positions[r * grid_cols + c]
        target, source = site_features(
            (here[0:1] - mid_row) * scale, (here[1:2] - mid_col) * scale
        )
        target_feat[n] = target
        source_feat[n] = source.astype(BF16)
        return carry

    lax.fori_loop(0, 24, features, 0)

    def mark(t):
        r, c = t // 4, t % 4
        mark_listed(
            lambda e: far_zero[r, c, e],
            flags,
            t,
            first_row + r // 2 * 2 - 2,
            first_col + c // 2 * 2 - 2,
            grid_cols,
        )

    def make(m):
        t = first + m
        r, c = t // 4, t % 4
        slot = m % 2 * 9
        for k in range(9):
            floors[m * 10 + k] = 1e6
        for e in range(9):
            entry = lists[r, c, e]
            source_row = jnp.maximum(entry, 0) // grid_cols
            source_col = jnp.maximum(entry, 0) - source_row * grid_cols
            k = (source_row - first_row - r + 1) * 3 + source_col - first_col - c + 1
            floors[m * 10 + jnp.where(entry >= 0, k, 9)] = 1e-24
        place = (m // 4 + 1) * 6 + c + 1
        target = target_feat[place].T.astype(BF16)
        for k in range(9):
            square = nn(target, source_feat[place + (k // 3 - 1) * 6 + k % 3 - 1])
            square = jnp.maximum(square, floors[m * 10 + k])
            far = square * lax.rsqrt(square)
            tile = ((far + 1.0) * jnp.exp2(far * -LOG2E)).astype(BF16)
            if (t, k) in HALO:
                number = HALO[t, k] % N_HALO
                halo[number] = tile
                out.start(halo.at[number], halo_out.at[number])
            else:
                made[slot + k] = tile

    def use(m):
        t = first + m
        slot = m % 2 * 9
        found = [k for k in range(9) if (t, k) not in HALO]
        lhs = jnp.concatenate([made[slot + k] for k in found], axis=1)
        blocks = [held[t + (k // 3 - 1) * 4 + k % 3 - 1] for k in found]
        near[m] = nn(lhs, jnp.concatenate(blocks, axis=0))
        sums_out.start(near.at[m], near_out.at[m])

    make(0)
    copy.wait()
    if with_far:
        far_in.wait()
    for m in range(1, 8):
        make(m)
        if with_far and m % 2 == 1:
            a, b = m // 4, m // 2 % 2
            for p in PARENTS:
                mark(number_of(a, b, p))
            sums = level_zero_sums("inner", a, b, flags, table, far_held, 32)
            for p in PARENTS:
                t = number_of(a, b, p)
                field[t] = sums[p]
                field_copies.start(field.at[t], field_out.at[t])
        use(m - 1)
    use(7)
    out.wait()
    sums_out.wait()
    if with_far:
        field_copies.wait()


def near_call(first, grid_rows, grid_cols, lists, far_zero, positions, own, far=()):
    out_shape = [tiles(8, F32), tiles(N_HALO)]
    out_specs = [ANY_SPEC, ANY_SPEC]
    scratch = []
    if far:
        out_shape += [tiles(16, F32), jax.ShapeDtypeStruct((16, 37), jnp.int32)]
        out_specs += [ANY_SPEC, SMEM_SPEC]
        scratch = [
            VMEM((20, 256, 256), BF16),
            VMEM((33, 256, 256), BF16),
            VMEM((16, 256, 256), F32),
            pltpu.SemaphoreType.DMA((5,)),
            pltpu.SemaphoreType.DMA((16,)),
        ]
    return pl.pallas_call(
        functools.partial(near_kernel, first, bool(far), grid_rows, grid_cols),
        out_shape=out_shape,
        in_specs=[SMEM_SPEC, SMEM_SPEC, VMEM_SPEC, ANY_SPEC]
        + ([ANY_SPEC] * 5 if far else []),
        out_specs=out_specs,
        scratch_shapes=scratch
        + [
            VMEM((16, 256, 256), BF16),
            VMEM((24, 32, 256), F32),
            VMEM((24, 32, 256), BF16),
            VMEM((N_HALO, 256, 256), BF16),
            VMEM((18, 256, 256), BF16),
            VMEM((8, 256, 256), F32),
            pltpu.SMEM((80,), F32),
            pltpu.SemaphoreType.DMA((1,)),
            pltpu.SemaphoreType.DMA((N_HALO,)),
            pltpu.SemaphoreType.DMA((8,)),
        ],
        compiler_params=params(),
        cost_estimate=cost(600 if far else 12000, 8 << 20),
        name="near_and_inner_far" if far else "near_first",
    )(lists, far_zero, positions, own, *far)


def mark_listed(entries, flags, n, first_row, first_col, grid_cols):
    for w in range(36):
        flags[n, w] = 0
    for e in range(27):
        entry = entries(e)
        row = jnp.maximum(entry, 0) // grid_cols
        col = jnp.maximum(entry, 0) - row * grid_cols
        w = (row - first_row) * 6 + col - first_col
        flags[n, jnp.where(entry >= 0, jnp.clip(w, 0, 35), 36)] = 1


def dot_group(held, couplings, turned, group):
    rows = len(group[0][1])
    lhs = [
        jnp.concatenate([held[places[n]] for _, places in group], axis=1) for n in range(rows)
    ]
    lhs = jnp.concatenate(lhs, axis=0) if rows > 1 else lhs[0]
    if turned:
        return nn(lhs, jnp.concatenate([couplings[k] for k, _ in group], axis=0))
    return nt(lhs, jnp.concatenate([couplings[k] for k, _ in group], axis=1))


def coupled(plan, couplings, held, places):
    total = None
    for turned in (0, 1):
        group = [(k, [places(w)]) for w, k in plan[turned]]
        part = dot_group(held, couplings, turned, group)
        total = part if total is None else total + part
    return total


def upper_kernel(
    grid_cols, n_rows, far_one, far_two, couplings, t_two, upper, above, below, row, row_e, row_d,
    cells, cells_e, quads, quads_e, down, held_one, held_two, field_two, flags, sems,
):
    n_cells = 2 * n_rows
    n_two = 3 * n_cells
    zero_one, zero_two = 36, 2 * n_two
    copies = Copies(sems)
    copies.start(cells, held_two.at[0:n_cells])
    copies.start(quads, held_two.at[n_cells:n_two])
    copies.start(cells_e, held_two.at[n_two : n_two + n_cells])
    copies.start(quads_e, held_two.at[n_two + n_cells : 2 * n_two])
    copies.start(upper.at[0:4], held_one.at[0:4])
    copies.start(row, held_one.at[4:12])
    copies.start(above.at[12:16], held_one.at[12:16])
    copies.start(below.at[12:16], held_one.at[16:20])
    copies.start(row_e, held_one.at[20:28])
    copies.start(row_d, held_one.at[28:36])
    held_one[zero_one] = jnp.zeros((256, 256), BF16)
    held_two[zero_two] = jnp.zeros((256, 256), BF16)
    i = lax.axis_index("qx")
    j = lax.axis_index("qy")
    a = i % 2
    b = j % 2
    for t in range(4):
        mark_listed(
            lambda e: far_one[t // 2, t % 2, e], flags, t, 2 * i - 2, 2 * j - 2, 2 * grid_cols
        )
    mark_listed(
        lambda e: far_two[0, 0, e], flags, 4, i // 2 * 2 - 2, j // 2 * 2 - 2, grid_cols
    )
    core_at = [jnp.where(a == 0, 0, n_two), jnp.where(a == 0, n_two, 0)]
    y_at = [2, 0, 2] if n_rows == 2 else [2, 0, 4]
    pair_tiles = 2 * n_rows
    z_at = [
        jnp.where(b == 0, pair_tiles, 2 * pair_tiles),
        0,
        jnp.where(b == 0, 2 * pair_tiles, pair_tiles),
    ]
    x_at = [b, 1 - b]

    def place_two(w):
        r, c = w // 6, w % 6
        place = core_at[r % 2] + y_at[r // 2] + z_at[c // 2] + x_at[c % 2]
        return jnp.where(flags[4, w] == 1, place, zero_two)

    own_at = [12, 0, 16]
    pair_at = [jnp.where(a == 0, 28, 20), 4, jnp.where(a == 0, 20, 28)]
    col_at = [jnp.where(b == 0, 4, 0), None, jnp.where(b == 0, 0, 4)]

    def place_one(t, w):
        r, c = w // 6, w % 6
        base = own_at[r // 2] if c // 2 == 1 else pair_at[r // 2] + col_at[c // 2]
        place = base + (r % 2) * 2 + c % 2
        return jnp.where(flags[t, w] == 1, place, zero_one)

    for copy in copies.started[:4]:
        copy.wait()
    for u in range(2):
        for v in range(2):

            @pl.when((a == u) & (b == v))
            def _():
                field_two[...] = coupled(
                    class_plan(u, v), couplings.at[1], held_two, place_two
                ).astype(BF16)

    for copy in copies.started[4:]:
        copy.wait()
    for u in range(2):
        for v in range(2):
            t = u * 2 + v
            field = coupled(
                class_plan(u, v), couplings.at[0], held_one, functools.partial(place_one, t)
            )
            down[t] = (field + nt(field_two[...], t_two[u, v])).astype(BF16)


def upper_levels(grid_cols, far_one, far_two, couplings, t_two, *received):
    n_two = 3 * received[6].shape[0]
    return pl.pallas_call(
        functools.partial(upper_kernel, grid_cols, n_two // 6),
        grid=(1,),
        out_shape=tiles(4),
        in_specs=[
            SMEM_SPEC,
            SMEM_SPEC,
            pl.BlockSpec(
                (pl.Element(2), pl.Element(20), pl.Element(256), pl.Element(256)),
                lambda g: (1, 0, 0, 0),
            ),
            pl.BlockSpec((2, 2, 256, 256), lambda g: (0, 0, 0, 0)),
        ]
        + [ANY_SPEC] * 10,
        out_specs=pl.BlockSpec((4, 256, 256), lambda g: (0, 0, 0)),
        scratch_shapes=[
            VMEM((37, 256, 256), BF16),
            VMEM((2 * n_two + 1, 256, 256), BF16),
            VMEM((256, 256), BF16),
            pltpu.SMEM((5, 37), jnp.int32),
            pltpu.SemaphoreType.DMA((10,)),
        ],
        compiler_params=params(),
        cost_estimate=cost(340, 14 << 20),
        name="upper_levels",
    )(far_one, far_two, couplings, t_two, *received)


def source_of(x, y, w):
    r, c = 2 * x + w // 6, 2 * y + w % 6
    if 2 <= c < 6:
        return "inner", r * 4 + c - 2
    side = 0 if c < 2 else 1
    c = c if c < 2 else c - 6
    if 2 <= r < 6:
        return ("left", "right")[side], (r - 2) * 2 + c
    return "corners", (0 if r < 2 else 8) + side * 4 + (r if r < 2 else r - 6) * 2 + c


PARENTS = [(x, y) for x in range(2) for y in range(2)]


def number_of(a, b, parent):
    x, y = parent
    return (2 * x + a) * 4 + 2 * y + b


def level_zero_sums(kind, a, b, flags, couplings, held, zero):
    plan = class_plan(a, b)
    sums = {}
    for turned in (0, 1):
        groups = {}
        for w, k in plan[turned]:
            members = tuple(p for p in PARENTS if source_of(*p, w)[0] == kind)
            if members:
                groups.setdefault(members, []).append((w, k))
        for members, entries in groups.items():
            group = []
            for w, k in entries:
                places = [
                    jnp.where(flags[number_of(a, b, p), w] == 1, source_of(*p, w)[1], zero)
                    for p in members
                ]
                group.append((k, places))
            total = dot_group(held, couplings, turned, group)
            for n, p in enumerate(members):
                part = total[256 * n : 256 * n + 256]
                sums[p] = part if p not in sums else sums[p] + part
    return sums


def grouped(x):
    return x.reshape(2, 2, 2, 2, 256, 256)


CLASS_BLOCK = pl.BlockSpec((2, 1, 2, 1, 256, 256), lambda g: (0, g // 2, 0, g % 2, 0, 0))
COUPLING_BLOCK = pl.BlockSpec((1, 20, 256, 256), lambda g: (0, 0, 0, 0))
GROUPED_F32 = jax.ShapeDtypeStruct((2, 2, 2, 2, 256, 256), F32)


def each_class(step, body):
    for a in range(2):
        for b in range(2):
            pl.when(step == a * 2 + b)(functools.partial(body, a, b))


def near_source(r, c):
    rows_in, cols_in = 1 <= r < 5, 1 <= c < 5
    if rows_in and cols_in:
        return "own", None
    if rows_in:
        return ("left" if c == 0 else "right"), r - 1
    if cols_in:
        return "rows", (0 if r == 0 else 4) + c - 1
    return "corners", (0 if r == 0 else 2) + (0 if c == 0 else 1)


def halo_of(kinds):
    return [
        n for (t, k), n in HALO.items() if near_source(t // 4 + k // 3, t % 4 + k % 3)[0] in kinds
    ]


EARLY_HALO = halo_of(("left", "rows"))
LATE_HALO = halo_of(("right", "corners"))


def near_part(at, t, halo, numbers, held):
    r, c = t // 4, t % 4
    made, blocks = [], []
    for k in range(9):
        found, place = near_source(r + k // 3, c + k % 3)
        if found in at:
            made.append(halo[numbers.index(HALO[t, k])])
            blocks.append(held[at[found] + place])
    if not made:
        return None
    return nn(jnp.concatenate(made, axis=1), jnp.concatenate(blocks, axis=0))


def halo_pairs(numbers, halo_a, halo_b, halo):
    return [
        ((halo_a if n < N_HALO else halo_b).at[n % N_HALO], halo.at[m])
        for m, n in enumerate(numbers)
    ]


def started_first(step, pairs, sems, first):
    def copies():
        return [pltpu.make_async_copy(src, dst, sems.at[n]) for n, (src, dst) in enumerate(pairs)]

    @pl.when(step == 0)
    def _():
        started = copies()
        for copy in started:
            copy.start()
        for copy in started[:first]:
            copy.wait()

    def rest():
        for copy in copies()[first:]:
            copy.wait()

    return rest


def left_kernel(
    flags, couplings, field_in, near_a, near_b, halo_a, halo_b, left, above, below,
    field, near, held, near_held, halo, sems,
):
    step = pl.program_id(0)
    pairs = [(left.at[0:8], held.at[0:8])]
    for n, src in enumerate((left, above, below)):
        pairs.append((src.at[8:12], near_held.at[4 * n : 4 * n + 4]))
    pairs += halo_pairs(EARLY_HALO, halo_a, halo_b, halo)
    held[8] = jnp.zeros((256, 256), BF16)
    wait_rest = started_first(step, pairs, sems, 1)

    def body(a, b):
        sums = level_zero_sums("left", a, b, flags, couplings.at[0], held, 8)
        for x, y in PARENTS:
            value = field_in[x, 0, y, 0]
            field[x, 0, y, 0] = value + sums[x, y] if (x, y) in sums else value
        if a == 0 and b == 0:
            wait_rest()
        for x, y in PARENTS:
            part = near_part(
                {"left": 0, "rows": 4}, number_of(a, b, (x, y)), halo, EARLY_HALO, near_held
            )
            here = (near_b if x else near_a)[0, y, 0]
            near[x, 0, y, 0] = here if part is None else here + part

    each_class(step, body)


HALF_BLOCK = pl.BlockSpec((1, 2, 1, 256, 256), lambda g: (g // 2, 0, g % 2, 0, 0))


def left_level(flags, couplings, field, near_a, near_b, *received):
    half = lambda x: x.reshape(2, 2, 2, 256, 256)
    return pl.pallas_call(
        left_kernel,
        grid=(4,),
        out_shape=(GROUPED_F32, GROUPED_F32),
        in_specs=[SMEM_SPEC, COUPLING_BLOCK, CLASS_BLOCK, HALF_BLOCK, HALF_BLOCK] + [ANY_SPEC] * 5,
        out_specs=[CLASS_BLOCK, CLASS_BLOCK],
        scratch_shapes=[
            VMEM((9, 256, 256), BF16),
            VMEM((12, 256, 256), BF16),
            VMEM((len(EARLY_HALO), 256, 256), BF16),
            pltpu.SemaphoreType.DMA((4 + len(EARLY_HALO),)),
        ],
        compiler_params=params(),
        cost_estimate=cost(300, 30 << 20),
        name="far_left",
    )(flags, couplings, grouped(field), half(near_a), half(near_b), *received)


def right_kernel(flags, couplings, field_in, right, field, held, sems):
    step = pl.program_id(0)
    held[8] = jnp.zeros((256, 256), BF16)
    started_first(step, [(right.at[0:8], held.at[0:8])], sems, 1)

    def body(a, b):
        sums = level_zero_sums("right", a, b, flags, couplings.at[0], held, 8)
        for x, y in PARENTS:
            value = field_in[x, 0, y, 0]
            field[x, 0, y, 0] = value + sums[x, y] if (x, y) in sums else value

    each_class(step, body)


def right_level(flags, couplings, field, right):
    return pl.pallas_call(
        right_kernel,
        grid=(4,),
        out_shape=GROUPED_F32,
        in_specs=[SMEM_SPEC, COUPLING_BLOCK, CLASS_BLOCK, ANY_SPEC],
        out_specs=CLASS_BLOCK,
        scratch_shapes=[VMEM((9, 256, 256), BF16), pltpu.SemaphoreType.DMA((1,))],
        compiler_params=params(),
        cost_estimate=cost(200, 12 << 20),
        name="far_right",
    )(flags, couplings, field, right)


def last_kernel(
    flags, couplings, t_one, basis, down_one, field, near, halo_a, halo_b, right,
    left_above, left_below, right_above, right_below, out, held, near_held, halo, sems,
):
    step = pl.program_id(0)
    corners = (left_above, right_above, left_below, right_below)
    pairs = [(src.at[0:4], held.at[4 * n : 4 * n + 4]) for n, src in enumerate(corners)]
    pairs += [(src.at[4:5], near_held.at[n : n + 1]) for n, src in enumerate(corners)]
    pairs.append((right.at[8:12], near_held.at[4:8]))
    pairs += halo_pairs(LATE_HALO, halo_a, halo_b, halo)
    held[16] = jnp.zeros((256, 256), BF16)
    wait_rest = started_first(step, pairs, sems, 4)

    def body(a, b):
        sums = level_zero_sums("corners", a, b, flags, couplings.at[0], held, 16)
        if a == 0 and b == 0:
            wait_rest()
        for x, y in PARENTS:
            total = field[x, 0, y, 0] + nt(down_one[x * 2 + y], t_one[x, 0, y, 0])
            if (x, y) in sums:
                total = total + sums[x, y]
            far = nt(basis[x, 0, y, 0], total.astype(BF16))
            near_sum = near[x, 0, y, 0]
            part = near_part(
                {"corners": 0, "right": 4}, number_of(a, b, (x, y)), halo, LATE_HALO, near_held
            )
            if part is not None:
                near_sum = near_sum + part
            out[x, 0, y, 0] = (near_sum * TILE_SCALE + far).astype(BF16)

    each_class(step, body)


def last_level(flags, couplings, t_one, basis, *rest):
    return pl.pallas_call(
        last_kernel,
        grid=(4,),
        out_shape=jax.ShapeDtypeStruct((2, 2, 2, 2, 256, 256), BF16),
        in_specs=[
            SMEM_SPEC,
            COUPLING_BLOCK,
            CLASS_BLOCK,
            CLASS_BLOCK,
            pl.BlockSpec((4, 256, 256), lambda g: (0, 0, 0)),
            CLASS_BLOCK,
            CLASS_BLOCK,
        ]
        + [ANY_SPEC] * 7,
        out_specs=CLASS_BLOCK,
        scratch_shapes=[
            VMEM((17, 256, 256), BF16),
            VMEM((8, 256, 256), BF16),
            VMEM((len(LATE_HALO), 256, 256), BF16),
            pltpu.SemaphoreType.DMA((9 + len(LATE_HALO),)),
        ],
        compiler_params=params(),
        cost_estimate=cost(270, 20 << 20),
        name="last_level",
    )(flags, couplings, grouped(t_one), grouped(basis), *rest)


def per_device(
    positions,
    samples,
    leaf_basis,
    transfer_one,
    transfer_two,
    couplings,
    near_lists,
    far_zero,
    far_one,
    far_two,
):
    nx = lax.axis_size("qx")
    ny = lax.axis_size("qy")
    down_x = [(k, k + 1) for k in range(nx - 1)]
    up_x = [(k + 1, k) for k in range(nx - 1)]
    down_y = [(k, k + 1) for k in range(ny - 1)]
    up_y = [(k + 1, k) for k in range(ny - 1)]

    up, down, left, right, upper, cell = coefficients(
        samples, leaf_basis, transfer_one, transfer_two
    )

    swap_y = [(k, k ^ 1) for k in range(ny)]
    swap_x = [(k, k ^ 1) for k in range(nx)]
    cross_x = [(k, k + 1) for k in range(1, nx - 1, 2)] + [(k + 1, k) for k in range(1, nx - 1, 2)]
    pair = lax.ppermute(upper, "qy", swap_y)
    on_left = lax.ppermute(right, "qy", down_y)
    if nx == 4:
        others = [lax.ppermute(cell, "qx", [(k, k ^ 2) for k in range(nx)])]
    else:
        others = [
            lax.ppermute(cell, "qx", [(k, k + 2) for k in range(nx - 2)]),
            lax.ppermute(cell, "qx", [(k + 2, k) for k in range(nx - 2)]),
        ]
    others_pair = [lax.ppermute(x, "qy", swap_y) for x in others]
    above = lax.ppermute(down, "qx", down_x)
    below = lax.ppermute(up, "qx", up_x)
    sites = positions.reshape(-1, 2, 256)
    flat_samples = samples.reshape(16, 256, 256)
    near_a, halo_a = near_call(
        0, 4 * nx, 4 * ny, near_lists, far_zero, sites, flat_samples
    )
    pair, others_pair, near_a = lax.optimization_barrier((pair, others_pair, near_a))
    outward = [(k, k + 2) for k in range(0, ny - 2, 2)] + [(k + 2, k) for k in range(1, ny - 2, 2)]
    inward = [(k + 2, k) for k in range(0, ny - 2, 2)] + [(k, k + 2) for k in range(1, ny - 2, 2)]
    n_others = len(others)
    quad = [(0, 4, 1), (1, 4, 1)]
    for n in range(n_others):
        quad += [(2 + n, 0, 1), (2 + n_others + n, 0, 1)]
    n_quad = len(quad)
    across, cells = assembled(
        "pair_payload",
        (upper, pair, *others, *others_pair),
        [(1, 0, 4)] + quad,
        [(0, 4 + n_quad), (4, 4 + n_quad)],
    )
    across, cells, left = lax.optimization_barrier((across, cells, left))
    outer = lax.ppermute(across, "qy", outward)
    inner = lax.ppermute(cells, "qy", inward)
    cells_e = lax.ppermute(cells, "qx", swap_x)
    on_right = lax.ppermute(left, "qy", up_y)
    near_b, halo_b, field, flags = near_call(
        8,
        4 * nx,
        4 * ny,
        near_lists,
        far_zero,
        sites,
        flat_samples,
        (couplings, up, down, above, below),
    )
    inner, outer, near_b, on_left = lax.optimization_barrier((inner, outer, near_b, on_left))
    row, quads = assembled(
        "row_payload",
        (pair, outer, inner),
        [(0, 0, 4), (1, 0, 4), (1, 4, n_quad), (2, 0, n_quad)],
        [(0, 8), (8, 8 + 2 * n_quad)],
    )
    row_d = lax.ppermute(row, "qx", cross_x)
    row_e = lax.ppermute(row, "qx", swap_x)
    quads_e = lax.ppermute(quads, "qx", swap_x)
    down_one = upper_levels(
        ny, far_one, far_two, couplings, transfer_two, upper, above, below, row, row_e, row_d,
        cells, cells_e, quads, quads_e,
    )

    def corners(name, halo):
        to_down, to_up = assembled(
            name, (halo,), [(0, 4, 4), (0, 11, 1), (0, 0, 4), (0, 8, 1)], [(0, 5), (5, 10)]
        )
        return [lax.ppermute(to_down, "qx", down_x), lax.ppermute(to_up, "qx", up_x)]

    left_corners = corners("left_corners", on_left)
    field, near = left_level(
        flags, couplings, field, near_a, near_b, halo_a, halo_b, on_left, above, below
    )
    on_right, down_one, near = lax.optimization_barrier((on_right, down_one, near))
    right_corners = corners("right_corners", on_right)
    field = right_level(flags, couplings, field, on_right)
    result = last_level(
        flags, couplings, transfer_one, leaf_basis, down_one, field, near, halo_a, halo_b,
        on_right, *left_corners, *right_corners,
    )
    return result.reshape(4, 4, 256, 256)


def solution(mesh):
    return jax.shard_map(
        per_device,
        mesh=mesh,
        in_specs=(
            P(),
            P("qx", "qy", None, None),
            P("qx", "qy", None, None),
            P("qx", "qy", None, None),
            P("qx", "qy", None, None),
            P(),
            P("qx", "qy", None),
            P("qx", "qy", None),
            P("qx", "qy", None),
            P("qx", "qy", None),
        ),
        out_specs=P("qx", "qy", None, None),
        check_vma=False,
    )
```

```python
import functools

import jax
import jax.numpy as jnp
import numpy as np
from jax import lax
from jax.experimental import pallas as pl
from jax.experimental.pallas import tpu as pltpu
from jax.sharding import PartitionSpec as P

root_three = 1.7320508075688772
length_scale = 1.0
VMEM = pltpu.VMEM
SMEM = pltpu.SMEM
F32 = jnp.float32
BF16 = jnp.bfloat16
BIG = 64 * 1024 * 1024 - 256 * 1024


def nn(a, b):
    return lax.dot_general(a, b, (((1,), (0,)), ((), ())), preferred_element_type=F32)


def nt(a, b):
    return lax.dot_general(a, b, (((1,), (1,)), ((), ())), preferred_element_type=F32)


def tn(a, b):
    return lax.dot_general(a, b, (((0,), (0,)), ((), ())), preferred_element_type=F32)


def params():
    return pltpu.CompilerParams(vmem_limit_bytes=BIG)


def cost(products, bytes_accessed):
    return pl.CostEstimate(
        flops=products * 2 * 256**3 // 8, bytes_accessed=bytes_accessed // 8, transcendentals=0
    )


def half_offsets():
    kept = []
    for u in range(-3, 4):
        for v in range(-3, 4):
            if max(abs(u), abs(v)) >= 2 and (u > 0 or (u == 0 and v > 0)):
                kept.append((u, v))
    return kept


HALF_OFFSETS = half_offsets()


def class_plan(a, b):
    plain, turned = [], []
    for w in range(36):
        u, v = w // 6 - 2 - a, w % 6 - 2 - b
        if max(abs(u), abs(v)) < 2:
            continue
        if (u, v) in HALF_OFFSETS:
            plain.append((w, HALF_OFFSETS.index((u, v))))
        else:
            turned.append((w, HALF_OFFSETS.index((-u, -v))))
    return plain, turned


LOG2E = 1.4426950408889634
TILE_SCALE = 256 ** -0.5


def tiles(n, dtype=BF16):
    return jax.ShapeDtypeStruct((n, 256, 256), dtype)


ANY_SPEC = pl.BlockSpec(memory_space=pltpu.HBM)
SMEM_SPEC = pl.BlockSpec(memory_space=SMEM)
VMEM_SPEC = pl.BlockSpec(memory_space=VMEM)


class Copies:
    def __init__(self, sems):
        self.sems = sems
        self.started = []

    def start(self, src, dst):
        copy = pltpu.make_async_copy(src, dst, self.sems.at[len(self.started)])
        copy.start()
        self.started.append(copy)
        return copy

    def wait(self):
        for copy in self.started:
            copy.wait()


def coef_kernel(
    samples, basis, t_one, t_two, up, down, left, right, upper, cell,
    sv, bv, t1v, t2v, cv, uv, in_sems, out_sems,
):
    into = Copies(in_sems)
    out = Copies(out_sems)
    rows = []
    for x in range(4):
        rows.append(
            (
                into.start(samples.at[x], sv.at[x]),
                into.start(basis.at[x], bv.at[x]),
                into.start(t_one.at[x], t1v.at[x]),
            )
        )
    last = into.start(t_two, t2v)
    for x in range(4):
        rows[x][0].wait()
        rows[x][1].wait()
        for y in range(4):
            cv[x * 4 + y] = tn(sv[x, y], bv[x, y]).astype(BF16)
        own = cv.at[4 * x : 4 * x + 4]
        out.start(own, (up if x < 2 else down).at[4 * (x % 2) : 4 * (x % 2) + 4])
        out.start(cv.at[4 * x : 4 * x + 2], left.at[2 * x : 2 * x + 2])
        out.start(cv.at[4 * x + 2 : 4 * x + 4], right.at[2 * x : 2 * x + 2])
        out.start(sv.at[x, 0], left.at[8 + x])
        out.start(sv.at[x, 3], right.at[8 + x])
        if x == 0:
            out.start(sv.at[x], up.at[8:12])
        if x == 3:
            out.start(sv.at[x], down.at[8:12])
        if x % 2 == 1:
            rows[x - 1][2].wait()
            rows[x][2].wait()
            for y in range(2):
                kids = [(x - 1 + a, 2 * y + b) for a in range(2) for b in range(2)]
                lhs = jnp.concatenate([cv[k * 4 + m] for k, m in kids], axis=1)
                rhs = jnp.concatenate([t1v[k] for k in kids], axis=0)
                uv[x // 2 * 2 + y] = nn(lhs, rhs).astype(BF16)
    last.wait()
    lhs = jnp.concatenate([uv[k] for k in range(4)], axis=1)
    rhs = jnp.concatenate([t2v[k // 2, k % 2] for k in range(4)], axis=0)
    uv[4] = nn(lhs, rhs).astype(BF16)
    out.start(uv.at[0:4], up.at[12:16])
    out.start(uv.at[0:4], down.at[12:16])
    out.start(uv, upper)
    out.start(uv.at[4:5], cell)
    out.wait()


def coefficients(samples, basis, t_one, t_two):
    return pl.pallas_call(
        coef_kernel,
        out_shape=[tiles(n) for n in (16, 16, 12, 12, 5, 1)],
        in_specs=[ANY_SPEC] * 4,
        out_specs=[ANY_SPEC] * 6,
        scratch_shapes=[
            VMEM((4, 4, 256, 256), BF16),
            VMEM((4, 4, 256, 256), BF16),
            VMEM((4, 4, 256, 256), BF16),
            VMEM((2, 2, 256, 256), BF16),
            VMEM((16, 256, 256), BF16),
            VMEM((5, 256, 256), BF16),
            pltpu.SemaphoreType.DMA((13,)),
            pltpu.SemaphoreType.DMA((26,)),
        ],
        compiler_params=params(),
        cost_estimate=cost(170, 12 << 20),
        name="coefficients",
    )(samples, basis, t_one, t_two)


def assembled(name, sources, pieces, ranges, stated=35):
    count = sum(n for _, _, n in pieces)

    def kernel(*refs):
        ins, outs = refs[: len(sources)], refs[len(sources) : -3]
        held, in_sems, out_sems = refs[-3:]
        into = Copies(in_sems)
        at = 0
        for source, first, n in pieces:
            into.start(ins[source].at[first : first + n], held.at[at : at + n])
            at += n
        into.wait()
        out = Copies(out_sems)
        for (first, last), ref in zip(ranges, outs):
            out.start(held.at[first:last], ref)
        out.wait()

    return pl.pallas_call(
        kernel,
        out_shape=[tiles(last - first) for first, last in ranges],
        in_specs=[ANY_SPEC] * len(sources),
        out_specs=[ANY_SPEC] * len(ranges),
        scratch_shapes=[
            VMEM((count, 256, 256), BF16),
            pltpu.SemaphoreType.DMA((len(pieces),)),
            pltpu.SemaphoreType.DMA((len(ranges),)),
        ],
        compiler_params=params(),
        cost_estimate=cost(stated, 0),
        name=name,
    )(*sources)


def halo_places():
    numbers = {}
    for r in range(4):
        for c in range(4):
            for k in range(9):
                y, x = r + k // 3 - 1, c + k % 3 - 1
                if not (0 <= y < 4 and 0 <= x < 4):
                    numbers[r * 4 + c, k] = len(numbers)
    return numbers


HALO = halo_places()
N_HALO = len(HALO) // 2


def split3(x):
    first = x.astype(BF16).astype(F32)
    rest = x - first
    second = rest.astype(BF16).astype(F32)
    return first, second, rest - second


def site_features(x, y):
    n = lax.broadcasted_iota(jnp.int32, (8, 256), 0)
    square = x * x + y * y
    target, source = [], []
    for parts in (split3(x), split3(y)):
        first, second, third = parts
        target.append(jnp.where(n < 3, first, jnp.where(n < 5, second, jnp.where(n < 6, third, 0.0))))
        other = jnp.where(
            (n == 0) | (n == 3) | (n == 5),
            first,
            jnp.where((n == 1) | (n == 4), second, jnp.where(n == 2, third, 0.0)),
        )
        source.append(-2.0 * other)
    first, second, third = split3(square)
    low = jnp.where(n == 0, first, jnp.where(n == 1, second, third))
    high = jnp.where(n == 3, first, jnp.where(n == 4, second, third))
    one = jnp.where(n < 6, 1.0, 0.0)
    target.append(jnp.where(n < 3, low, one))
    source.append(jnp.where(n < 3, 1.0, jnp.where(n < 6, high, 0.0)))
    zero = jnp.zeros((8, 256), F32)
    return jnp.concatenate(target + [zero], axis=0), jnp.concatenate(source + [zero], axis=0)


def near_kernel(
    first, with_far, grid_rows, grid_cols, lists, far_zero, positions, own, *rest
):
    if with_far:
        couplings, up, down, above, below, near_out, halo_out, field_out, flags = rest[:9]
        table, far_held, field, far_sems, field_sems = rest[9:14]
        rest = rest[14:]
    else:
        near_out, halo_out = rest[:2]
        rest = rest[2:]
    held, target_feat, source_feat, halo, made, near, floors, sems, halo_sems, near_sems = rest
    copy = pltpu.make_async_copy(own, held, sems.at[0])
    copy.start()
    out = Copies(halo_sems)
    sums_out = Copies(near_sems)
    if with_far:
        far_in = Copies(far_sems)
        far_in.start(couplings.at[0], table)
        for n, src in enumerate((above, up, down, below)):
            far_in.start(src.at[0:8], far_held.at[8 * n : 8 * n + 8])
        far_held[32] = jnp.zeros((256, 256), BF16)
        field_copies = Copies(field_sems)
    first_row = lax.axis_index("qx") * 4
    first_col = lax.axis_index("qy") * 4
    scale = root_three / length_scale
    mid_row = first_row.astype(F32) + 2.0
    mid_col = first_col.astype(F32) + 2.0
    first_place = first // 4 * 6

    def features(n, carry):
        r = jnp.clip(first_row + (first_place + n) // 6 - 1, 0, grid_rows - 1)
        c = jnp.clip(first_col + n % 6 - 1, 0, grid_cols - 1)
        here = positions[r * grid_cols + c]
        target, source = site_features(
            (here[0:1] - mid_row) * scale, (here[1:2] - mid_col) * scale
        )
        target_feat[n] = target
        source_feat[n] = source.astype(BF16)
        return carry

    lax.fori_loop(0, 24, features, 0)

    def mark(t):
        r, c = t // 4, t % 4
        mark_listed(
            lambda e: far_zero[r, c, e],
            flags,
            t,
            first_row + r // 2 * 2 - 2,
            first_col + c // 2 * 2 - 2,
            grid_cols,
        )

    def make(m):
        t = first + m
        r, c = t // 4, t % 4
        slot = m % 2 * 9
        for k in range(9):
            floors[m * 10 + k] = 1e6
        for e in range(9):
            entry = lists[r, c, e]
            source_row = jnp.maximum(entry, 0) // grid_cols
            source_col = jnp.maximum(entry, 0) - source_row * grid_cols
            k = (source_row - first_row - r + 1) * 3 + source_col - first_col - c + 1
            floors[m * 10 + jnp.where(entry >= 0, k, 9)] = 1e-24
        place = (m // 4 + 1) * 6 + c + 1
        target = target_feat[place].T.astype(BF16)
        for k in range(9):
            square = nn(target, source_feat[place + (k // 3 - 1) * 6 + k % 3 - 1])
            square = jnp.maximum(square, floors[m * 10 + k])
            far = square * lax.rsqrt(square)
            tile = ((far + 1.0) * jnp.exp2(far * -LOG2E)).astype(BF16)
            if (t, k) in HALO:
                number = HALO[t, k] % N_HALO
                halo[number] = tile
                out.start(halo.at[number], halo_out.at[number])
            else:
                made[slot + k] = tile

    def use(m):
        t = first + m
        slot = m % 2 * 9
        found = [k for k in range(9) if (t, k) not in HALO]
        lhs = jnp.concatenate([made[slot + k] for k in found], axis=1)
        blocks = [held[t + (k // 3 - 1) * 4 + k % 3 - 1] for k in found]
        near[m] = nn(lhs, jnp.concatenate(blocks, axis=0))
        sums_out.start(near.at[m], near_out.at[m])

    make(0)
    copy.wait()
    if with_far:
        far_in.wait()
    for m in range(1, 8):
        make(m)
        if with_far and m % 2 == 1:
            a, b = m // 4, m // 2 % 2
            for p in PARENTS:
                mark(number_of(a, b, p))
            sums = level_zero_sums("inner", a, b, flags, table, far_held, 32)
            for p in PARENTS:
                t = number_of(a, b, p)
                field[t] = sums[p]
                field_copies.start(field.at[t], field_out.at[t])
        use(m - 1)
    use(7)
    out.wait()
    sums_out.wait()
    if with_far:
        field_copies.wait()


def near_call(first, grid_rows, grid_cols, lists, far_zero, positions, own, far=()):
    out_shape = [tiles(8, F32), tiles(N_HALO)]
    out_specs = [ANY_SPEC, ANY_SPEC]
    scratch = []
    if far:
        out_shape += [tiles(16, F32), jax.ShapeDtypeStruct((16, 37), jnp.int32)]
        out_specs += [ANY_SPEC, SMEM_SPEC]
        scratch = [
            VMEM((20, 256, 256), BF16),
            VMEM((33, 256, 256), BF16),
            VMEM((16, 256, 256), F32),
            pltpu.SemaphoreType.DMA((5,)),
            pltpu.SemaphoreType.DMA((16,)),
        ]
    return pl.pallas_call(
        functools.partial(near_kernel, first, bool(far), grid_rows, grid_cols),
        out_shape=out_shape,
        in_specs=[SMEM_SPEC, SMEM_SPEC, VMEM_SPEC, ANY_SPEC]
        + ([ANY_SPEC] * 5 if far else []),
        out_specs=out_specs,
        scratch_shapes=scratch
        + [
            VMEM((16, 256, 256), BF16),
            VMEM((24, 32, 256), F32),
            VMEM((24, 32, 256), BF16),
            VMEM((N_HALO, 256, 256), BF16),
            VMEM((18, 256, 256), BF16),
            VMEM((8, 256, 256), F32),
            pltpu.SMEM((80,), F32),
            pltpu.SemaphoreType.DMA((1,)),
            pltpu.SemaphoreType.DMA((N_HALO,)),
            pltpu.SemaphoreType.DMA((8,)),
        ],
        compiler_params=params(),
        cost_estimate=cost(600 if far else 12000, 8 << 20),
        name="near_and_inner_far" if far else "near_first",
    )(lists, far_zero, positions, own, *far)


def mark_listed(entries, flags, n, first_row, first_col, grid_cols):
    for w in range(36):
        flags[n, w] = 0
    for e in range(27):
        entry = entries(e)
        row = jnp.maximum(entry, 0) // grid_cols
        col = jnp.maximum(entry, 0) - row * grid_cols
        w = (row - first_row) * 6 + col - first_col
        flags[n, jnp.where(entry >= 0, jnp.clip(w, 0, 35), 36)] = 1


def dot_group(held, couplings, turned, group):
    rows = len(group[0][1])
    lhs = [
        jnp.concatenate([held[places[n]] for _, places in group], axis=1) for n in range(rows)
    ]
    lhs = jnp.concatenate(lhs, axis=0) if rows > 1 else lhs[0]
    if turned:
        return nn(lhs, jnp.concatenate([couplings[k] for k, _ in group], axis=0))
    return nt(lhs, jnp.concatenate([couplings[k] for k, _ in group], axis=1))


def coupled(plan, couplings, held, places):
    total = None
    for turned in (0, 1):
        group = [(k, [places(w)]) for w, k in plan[turned]]
        part = dot_group(held, couplings, turned, group)
        total = part if total is None else total + part
    return total


def upper_kernel(
    grid_cols, n_rows, far_one, far_two, couplings, t_two, upper, above, below, row, row_e, row_d,
    cells, cells_e, quads, quads_e, down, held_one, held_two, field_two, flags, sems,
):
    n_cells = 2 * n_rows
    n_two = 3 * n_cells
    zero_one, zero_two = 36, 2 * n_two
    copies = Copies(sems)
    copies.start(cells, held_two.at[0:n_cells])
    copies.start(quads, held_two.at[n_cells:n_two])
    copies.start(cells_e, held_two.at[n_two : n_two + n_cells])
    copies.start(quads_e, held_two.at[n_two + n_cells : 2 * n_two])
    copies.start(upper.at[0:4], held_one.at[0:4])
    copies.start(row, held_one.at[4:12])
    copies.start(above.at[12:16], held_one.at[12:16])
    copies.start(below.at[12:16], held_one.at[16:20])
    copies.start(row_e, held_one.at[20:28])
    copies.start(row_d, held_one.at[28:36])
    held_one[zero_one] = jnp.zeros((256, 256), BF16)
    held_two[zero_two] = jnp.zeros((256, 256), BF16)
    i = lax.axis_index("qx")
    j = lax.axis_index("qy")
    a = i % 2
    b = j % 2
    for t in range(4):
        mark_listed(
            lambda e: far_one[t // 2, t % 2, e], flags, t, 2 * i - 2, 2 * j - 2, 2 * grid_cols
        )
    mark_listed(
        lambda e: far_two[0, 0, e], flags, 4, i // 2 * 2 - 2, j // 2 * 2 - 2, grid_cols
    )
    core_at = [jnp.where(a == 0, 0, n_two), jnp.where(a == 0, n_two, 0)]
    y_at = [2, 0, 2] if n_rows == 2 else [2, 0, 4]
    pair_tiles = 2 * n_rows
    z_at = [
        jnp.where(b == 0, pair_tiles, 2 * pair_tiles),
        0,
        jnp.where(b == 0, 2 * pair_tiles, pair_tiles),
    ]
    x_at = [b, 1 - b]

    def place_two(w):
        r, c = w // 6, w % 6
        place = core_at[r % 2] + y_at[r // 2] + z_at[c // 2] + x_at[c % 2]
        return jnp.where(flags[4, w] == 1, place, zero_two)

    own_at = [12, 0, 16]
    pair_at = [jnp.where(a == 0, 28, 20), 4, jnp.where(a == 0, 20, 28)]
    col_at = [jnp.where(b == 0, 4, 0), None, jnp.where(b == 0, 0, 4)]

    def place_one(t, w):
        r, c = w // 6, w % 6
        base = own_at[r // 2] if c // 2 == 1 else pair_at[r // 2] + col_at[c // 2]
        place = base + (r % 2) * 2 + c % 2
        return jnp.where(flags[t, w] == 1, place, zero_one)

    for copy in copies.started[:4]:
        copy.wait()
    for u in range(2):
        for v in range(2):

            @pl.when((a == u) & (b == v))
            def _():
                field_two[...] = coupled(
                    class_plan(u, v), couplings.at[1], held_two, place_two
                ).astype(BF16)

    for copy in copies.started[4:]:
        copy.wait()
    for u in range(2):
        for v in range(2):
            t = u * 2 + v
            field = coupled(
                class_plan(u, v), couplings.at[0], held_one, functools.partial(place_one, t)
            )
            down[t] = (field + nt(field_two[...], t_two[u, v])).astype(BF16)


def upper_levels(grid_cols, far_one, far_two, couplings, t_two, *received):
    n_two = 3 * received[6].shape[0]
    return pl.pallas_call(
        functools.partial(upper_kernel, grid_cols, n_two // 6),
        grid=(1,),
        out_shape=tiles(4),
        in_specs=[
            SMEM_SPEC,
            SMEM_SPEC,
            pl.BlockSpec(
                (pl.Element(2), pl.Element(20), pl.Element(256), pl.Element(256)),
                lambda g: (1, 0, 0, 0),
            ),
            pl.BlockSpec((2, 2, 256, 256), lambda g: (0, 0, 0, 0)),
        ]
        + [ANY_SPEC] * 10,
        out_specs=pl.BlockSpec((4, 256, 256), lambda g: (0, 0, 0)),
        scratch_shapes=[
            VMEM((37, 256, 256), BF16),
            VMEM((2 * n_two + 1, 256, 256), BF16),
            VMEM((256, 256), BF16),
            pltpu.SMEM((5, 37), jnp.int32),
            pltpu.SemaphoreType.DMA((10,)),
        ],
        compiler_params=params(),
        cost_estimate=cost(340, 14 << 20),
        name="upper_levels",
    )(far_one, far_two, couplings, t_two, *received)


def source_of(x, y, w):
    r, c = 2 * x + w // 6, 2 * y + w % 6
    if 2 <= c < 6:
        return "inner", r * 4 + c - 2
    side = 0 if c < 2 else 1
    c = c if c < 2 else c - 6
    if 2 <= r < 6:
        return ("left", "right")[side], (r - 2) * 2 + c
    return "corners", (0 if r < 2 else 8) + side * 4 + (r if r < 2 else r - 6) * 2 + c


PARENTS = [(x, y) for x in range(2) for y in range(2)]


def number_of(a, b, parent):
    x, y = parent
    return (2 * x + a) * 4 + 2 * y + b


def level_zero_sums(kind, a, b, flags, couplings, held, zero):
    plan = class_plan(a, b)
    sums = {}
    for turned in (0, 1):
        groups = {}
        for w, k in plan[turned]:
            members = tuple(p for p in PARENTS if source_of(*p, w)[0] == kind)
            if members:
                groups.setdefault(members, []).append((w, k))
        for members, entries in groups.items():
            group = []
            for w, k in entries:
                places = [
                    jnp.where(flags[number_of(a, b, p), w] == 1, source_of(*p, w)[1], zero)
                    for p in members
                ]
                group.append((k, places))
            total = dot_group(held, couplings, turned, group)
            for n, p in enumerate(members):
                part = total[256 * n : 256 * n + 256]
                sums[p] = part if p not in sums else sums[p] + part
    return sums


def grouped(x):
    return x.reshape(2, 2, 2, 2, 256, 256)


CLASS_BLOCK = pl.BlockSpec((2, 1, 2, 1, 256, 256), lambda g: (0, g // 2, 0, g % 2, 0, 0))
COUPLING_BLOCK = pl.BlockSpec((1, 20, 256, 256), lambda g: (0, 0, 0, 0))
GROUPED_F32 = jax.ShapeDtypeStruct((2, 2, 2, 2, 256, 256), F32)


def each_class(step, body):
    for a in range(2):
        for b in range(2):
            pl.when(step == a * 2 + b)(functools.partial(body, a, b))


def near_source(r, c):
    rows_in, cols_in = 1 <= r < 5, 1 <= c < 5
    if rows_in and cols_in:
        return "own", None
    if rows_in:
        return ("left" if c == 0 else "right"), r - 1
    if cols_in:
        return "rows", (0 if r == 0 else 4) + c - 1
    return "corners", (0 if r == 0 else 2) + (0 if c == 0 else 1)


def halo_of(kinds):
    return [
        n for (t, k), n in HALO.items() if near_source(t // 4 + k // 3, t % 4 + k % 3)[0] in kinds
    ]


EARLY_HALO = halo_of(("left", "rows"))
LATE_HALO = halo_of(("right", "corners"))


def near_part(at, t, halo, numbers, held):
    r, c = t // 4, t % 4
    made, blocks = [], []
    for k in range(9):
        found, place = near_source(r + k // 3, c + k % 3)
        if found in at:
            made.append(halo[numbers.index(HALO[t, k])])
            blocks.append(held[at[found] + place])
    if not made:
        return None
    return nn(jnp.concatenate(made, axis=1), jnp.concatenate(blocks, axis=0))


def halo_pairs(numbers, halo_a, halo_b, halo):
    return [
        ((halo_a if n < N_HALO else halo_b).at[n % N_HALO], halo.at[m])
        for m, n in enumerate(numbers)
    ]


def started_first(step, pairs, sems, first):
    def copies():
        return [pltpu.make_async_copy(src, dst, sems.at[n]) for n, (src, dst) in enumerate(pairs)]

    @pl.when(step == 0)
    def _():
        started = copies()
        for copy in started:
            copy.start()
        for copy in started[:first]:
            copy.wait()

    def rest():
        for copy in copies()[first:]:
            copy.wait()

    return rest


def left_kernel(
    flags, couplings, field_in, near_a, near_b, halo_a, halo_b, left, above, below,
    field, near, held, near_held, halo, sems,
):
    step = pl.program_id(0)
    pairs = [(left.at[0:8], held.at[0:8])]
    for n, src in enumerate((left, above, below)):
        pairs.append((src.at[8:12], near_held.at[4 * n : 4 * n + 4]))
    pairs += halo_pairs(EARLY_HALO, halo_a, halo_b, halo)
    held[8] = jnp.zeros((256, 256), BF16)
    wait_rest = started_first(step, pairs, sems, 1)

    def body(a, b):
        sums = level_zero_sums("left", a, b, flags, couplings.at[0], held, 8)
        for x, y in PARENTS:
            value = field_in[x, 0, y, 0]
            field[x, 0, y, 0] = value + sums[x, y] if (x, y) in sums else value
        if a == 0 and b == 0:
            wait_rest()
        for x, y in PARENTS:
            part = near_part(
                {"left": 0, "rows": 4}, number_of(a, b, (x, y)), halo, EARLY_HALO, near_held
            )
            here = (near_b if x else near_a)[0, y, 0]
            near[x, 0, y, 0] = here if part is None else here + part

    each_class(step, body)


HALF_BLOCK = pl.BlockSpec((1, 2, 1, 256, 256), lambda g: (g // 2, 0, g % 2, 0, 0))


def left_level(flags, couplings, field, near_a, near_b, *received):
    half = lambda x: x.reshape(2, 2, 2, 256, 256)
    return pl.pallas_call(
        left_kernel,
        grid=(4,),
        out_shape=(GROUPED_F32, GROUPED_F32),
        in_specs=[SMEM_SPEC, COUPLING_BLOCK, CLASS_BLOCK, HALF_BLOCK, HALF_BLOCK] + [ANY_SPEC] * 5,
        out_specs=[CLASS_BLOCK, CLASS_BLOCK],
        scratch_shapes=[
            VMEM((9, 256, 256), BF16),
            VMEM((12, 256, 256), BF16),
            VMEM((len(EARLY_HALO), 256, 256), BF16),
            pltpu.SemaphoreType.DMA((4 + len(EARLY_HALO),)),
        ],
        compiler_params=params(),
        cost_estimate=cost(300, 30 << 20),
        name="far_left",
    )(flags, couplings, grouped(field), half(near_a), half(near_b), *received)


def right_kernel(flags, couplings, field_in, right, field, held, sems):
    step = pl.program_id(0)
    held[8] = jnp.zeros((256, 256), BF16)
    started_first(step, [(right.at[0:8], held.at[0:8])], sems, 1)

    def body(a, b):
        sums = level_zero_sums("right", a, b, flags, couplings.at[0], held, 8)
        for x, y in PARENTS:
            value = field_in[x, 0, y, 0]
            field[x, 0, y, 0] = value + sums[x, y] if (x, y) in sums else value

    each_class(step, body)


def right_level(flags, couplings, field, right):
    return pl.pallas_call(
        right_kernel,
        grid=(4,),
        out_shape=GROUPED_F32,
        in_specs=[SMEM_SPEC, COUPLING_BLOCK, CLASS_BLOCK, ANY_SPEC],
        out_specs=CLASS_BLOCK,
        scratch_shapes=[VMEM((9, 256, 256), BF16), pltpu.SemaphoreType.DMA((1,))],
        compiler_params=params(),
        cost_estimate=cost(200, 12 << 20),
        name="far_right",
    )(flags, couplings, field, right)


def last_kernel(
    flags, couplings, t_one, basis, down_one, field, near, halo_a, halo_b, right,
    left_above, left_below, right_above, right_below, out, held, near_held, halo, sems,
):
    step = pl.program_id(0)
    corners = (left_above, right_above, left_below, right_below)
    pairs = [(src.at[0:4], held.at[4 * n : 4 * n + 4]) for n, src in enumerate(corners)]
    pairs += [(src.at[4:5], near_held.at[n : n + 1]) for n, src in enumerate(corners)]
    pairs.append((right.at[8:12], near_held.at[4:8]))
    pairs += halo_pairs(LATE_HALO, halo_a, halo_b, halo)
    held[16] = jnp.zeros((256, 256), BF16)
    wait_rest = started_first(step, pairs, sems, 4)

    def body(a, b):
        sums = level_zero_sums("corners", a, b, flags, couplings.at[0], held, 16)
        if a == 0 and b == 0:
            wait_rest()
        for x, y in PARENTS:
            total = field[x, 0, y, 0] + nt(down_one[x * 2 + y], t_one[x, 0, y, 0])
            if (x, y) in sums:
                total = total + sums[x, y]
            far = nt(basis[x, 0, y, 0], total.astype(BF16))
            near_sum = near[x, 0, y, 0]
            part = near_part(
                {"corners": 0, "right": 4}, number_of(a, b, (x, y)), halo, LATE_HALO, near_held
            )
            if part is not None:
                near_sum = near_sum + part
            out[x, 0, y, 0] = (near_sum * TILE_SCALE + far).astype(BF16)

    each_class(step, body)


def last_level(flags, couplings, t_one, basis, *rest):
    return pl.pallas_call(
        last_kernel,
        grid=(4,),
        out_shape=jax.ShapeDtypeStruct((2, 2, 2, 2, 256, 256), BF16),
        in_specs=[
            SMEM_SPEC,
            COUPLING_BLOCK,
            CLASS_BLOCK,
            CLASS_BLOCK,
            pl.BlockSpec((4, 256, 256), lambda g: (0, 0, 0)),
            CLASS_BLOCK,
            CLASS_BLOCK,
        ]
        + [ANY_SPEC] * 7,
        out_specs=CLASS_BLOCK,
        scratch_shapes=[
            VMEM((17, 256, 256), BF16),
            VMEM((8, 256, 256), BF16),
            VMEM((len(LATE_HALO), 256, 256), BF16),
            pltpu.SemaphoreType.DMA((9 + len(LATE_HALO),)),
        ],
        compiler_params=params(),
        cost_estimate=cost(270, 20 << 20),
        name="last_level",
    )(flags, couplings, grouped(t_one), grouped(basis), *rest)


def per_device(
    positions,
    samples,
    leaf_basis,
    transfer_one,
    transfer_two,
    couplings,
    near_lists,
    far_zero,
    far_one,
    far_two,
):
    nx = lax.axis_size("qx")
    ny = lax.axis_size("qy")
    down_x = [(k, k + 1) for k in range(nx - 1)]
    up_x = [(k + 1, k) for k in range(nx - 1)]
    down_y = [(k, k + 1) for k in range(ny - 1)]
    up_y = [(k + 1, k) for k in range(ny - 1)]

    up, down, left, right, upper, cell = coefficients(
        samples, leaf_basis, transfer_one, transfer_two
    )

    swap_y = [(k, k ^ 1) for k in range(ny)]
    swap_x = [(k, k ^ 1) for k in range(nx)]
    cross_x = [(k, k + 1) for k in range(1, nx - 1, 2)] + [(k + 1, k) for k in range(1, nx - 1, 2)]
    pair = lax.ppermute(upper, "qy", swap_y)
    if nx == 4:
        others = [lax.ppermute(cell, "qx", [(k, k ^ 2) for k in range(nx)])]
    else:
        others = [
            lax.ppermute(cell, "qx", [(k, k + 2) for k in range(nx - 2)]),
            lax.ppermute(cell, "qx", [(k + 2, k) for k in range(nx - 2)]),
        ]
    others_pair = [lax.ppermute(x, "qy", swap_y) for x in others]
    above = lax.ppermute(down, "qx", down_x)
    below = lax.ppermute(up, "qx", up_x)
    sites = positions.reshape(-1, 2, 256)
    flat_samples = samples.reshape(16, 256, 256)
    near_a, halo_a = near_call(
        0, 4 * nx, 4 * ny, near_lists, far_zero, sites, flat_samples
    )
    pair, others_pair, near_a = lax.optimization_barrier((pair, others_pair, near_a))
    outward = [(k, k + 2) for k in range(0, ny - 2, 2)] + [(k + 2, k) for k in range(1, ny - 2, 2)]
    inward = [(k + 2, k) for k in range(0, ny - 2, 2)] + [(k, k + 2) for k in range(1, ny - 2, 2)]
    n_others = len(others)
    quad = [(0, 4, 1), (1, 4, 1)]
    for n in range(n_others):
        quad += [(2 + n, 0, 1), (2 + n_others + n, 0, 1)]
    n_quad = len(quad)
    across, cells = assembled(
        "pair_payload",
        (upper, pair, *others, *others_pair),
        [(1, 0, 4)] + quad,
        [(0, 4 + n_quad), (4, 4 + n_quad)],
    )
    across, cells, left, right = lax.optimization_barrier((across, cells, left, right))
    outer = lax.ppermute(across, "qy", outward)
    inner = lax.ppermute(cells, "qy", inward)
    cells_e = lax.ppermute(cells, "qx", swap_x)
    on_left = lax.ppermute(right, "qy", down_y)
    _, above, below = lax.optimization_barrier((across, above, below))
    near_b, halo_b, field, flags = near_call(
        8,
        4 * nx,
        4 * ny,
        near_lists,
        far_zero,
        sites,
        flat_samples,
        (couplings, up, down, above, below),
    )
    inner, outer, near_b = lax.optimization_barrier((inner, outer, near_b))
    row, quads = assembled(
        "row_payload",
        (pair, outer, inner),
        [(0, 0, 4), (1, 0, 4), (1, 4, n_quad), (2, 0, n_quad)],
        [(0, 8), (8, 8 + 2 * n_quad)],
    )
    row_d = lax.ppermute(row, "qx", cross_x)
    row_e = lax.ppermute(row, "qx", swap_x)
    quads_e = lax.ppermute(quads, "qx", swap_x)
    on_left, left, row_e = lax.optimization_barrier((on_left, left, row_e))
    on_right = lax.ppermute(left, "qy", up_y)
    down_one = upper_levels(
        ny, far_one, far_two, couplings, transfer_two, upper, above, below, row, row_e, row_d,
        cells, cells_e, quads, quads_e,
    )

    def corners(name, halo):
        to_down, to_up = assembled(
            name, (halo,), [(0, 4, 4), (0, 11, 1), (0, 0, 4), (0, 8, 1)], [(0, 5), (5, 10)]
        )
        return [lax.ppermute(to_down, "qx", down_x), lax.ppermute(to_up, "qx", up_x)]

    left_corners = corners("left_corners", on_left)
    field, near = left_level(
        flags, couplings, field, near_a, near_b, halo_a, halo_b, on_left, above, below
    )
    on_right, down_one, near = lax.optimization_barrier((on_right, down_one, near))
    right_corners = corners("right_corners", on_right)
    field = right_level(flags, couplings, field, on_right)
    result = last_level(
        flags, couplings, transfer_one, leaf_basis, down_one, field, near, halo_a, halo_b,
        on_right, *left_corners, *right_corners,
    )
    return result.reshape(4, 4, 256, 256)


def solution(mesh):
    return jax.shard_map(
        per_device,
        mesh=mesh,
        in_specs=(
            P(),
            P("qx", "qy", None, None),
            P("qx", "qy", None, None),
            P("qx", "qy", None, None),
            P("qx", "qy", None, None),
            P(),
            P("qx", "qy", None),
            P("qx", "qy", None),
            P("qx", "qy", None),
            P("qx", "qy", None),
        ),
        out_specs=P("qx", "qy", None, None),
        check_vma=False,
    )
```

```python
import functools

import jax
import jax.numpy as jnp
import numpy as np
from jax import lax
from jax.experimental import pallas as pl
from jax.experimental.pallas import tpu as pltpu
from jax.sharding import PartitionSpec as P

root_three = 1.7320508075688772
length_scale = 1.0
VMEM = pltpu.VMEM
SMEM = pltpu.SMEM
F32 = jnp.float32
BF16 = jnp.bfloat16
BIG = 64 * 1024 * 1024 - 256 * 1024


def nn(a, b):
    return lax.dot_general(a, b, (((1,), (0,)), ((), ())), preferred_element_type=F32)


def nt(a, b):
    return lax.dot_general(a, b, (((1,), (1,)), ((), ())), preferred_element_type=F32)


def tn(a, b):
    return lax.dot_general(a, b, (((0,), (0,)), ((), ())), preferred_element_type=F32)


def params():
    return pltpu.CompilerParams(vmem_limit_bytes=BIG)


def cost(products, bytes_accessed):
    return pl.CostEstimate(
        flops=products * 2 * 256**3 // 8, bytes_accessed=bytes_accessed // 8, transcendentals=0
    )


def half_offsets():
    kept = []
    for u in range(-3, 4):
        for v in range(-3, 4):
            if max(abs(u), abs(v)) >= 2 and (u > 0 or (u == 0 and v > 0)):
                kept.append((u, v))
    return kept


HALF_OFFSETS = half_offsets()


def class_plan(a, b):
    plain, turned = [], []
    for w in range(36):
        u, v = w // 6 - 2 - a, w % 6 - 2 - b
        if max(abs(u), abs(v)) < 2:
            continue
        if (u, v) in HALF_OFFSETS:
            plain.append((w, HALF_OFFSETS.index((u, v))))
        else:
            turned.append((w, HALF_OFFSETS.index((-u, -v))))
    return plain, turned


LOG2E = 1.4426950408889634
TILE_SCALE = 256 ** -0.5


def tiles(n, dtype=BF16):
    return jax.ShapeDtypeStruct((n, 256, 256), dtype)


ANY_SPEC = pl.BlockSpec(memory_space=pltpu.HBM)
SMEM_SPEC = pl.BlockSpec(memory_space=SMEM)
VMEM_SPEC = pl.BlockSpec(memory_space=VMEM)


class Copies:
    def __init__(self, sems):
        self.sems = sems
        self.started = []

    def start(self, src, dst):
        copy = pltpu.make_async_copy(src, dst, self.sems.at[len(self.started)])
        copy.start()
        self.started.append(copy)
        return copy

    def wait(self):
        for copy in self.started:
            copy.wait()


def coef_kernel(
    samples, basis, t_one, t_two, up, down, left, right, upper, cell,
    sv, bv, t1v, t2v, cv, uv, in_sems, out_sems,
):
    into = Copies(in_sems)
    out = Copies(out_sems)
    rows = []
    for x in range(4):
        rows.append(
            (
                into.start(samples.at[x], sv.at[x]),
                into.start(basis.at[x], bv.at[x]),
                into.start(t_one.at[x], t1v.at[x]),
            )
        )
    last = into.start(t_two, t2v)
    for x in range(4):
        rows[x][0].wait()
        rows[x][1].wait()
        for y in range(4):
            cv[x * 4 + y] = tn(sv[x, y], bv[x, y]).astype(BF16)
        own = cv.at[4 * x : 4 * x + 4]
        out.start(own, (up if x < 2 else down).at[4 * (x % 2) : 4 * (x % 2) + 4])
        out.start(cv.at[4 * x : 4 * x + 2], left.at[2 * x : 2 * x + 2])
        out.start(cv.at[4 * x + 2 : 4 * x + 4], right.at[2 * x : 2 * x + 2])
        out.start(sv.at[x, 0], left.at[8 + x])
        out.start(sv.at[x, 3], right.at[8 + x])
        if x == 0:
            out.start(sv.at[x], up.at[8:12])
        if x == 3:
            out.start(sv.at[x], down.at[8:12])
        if x % 2 == 1:
            rows[x - 1][2].wait()
            rows[x][2].wait()
            for y in range(2):
                kids = [(x - 1 + a, 2 * y + b) for a in range(2) for b in range(2)]
                lhs = jnp.concatenate([cv[k * 4 + m] for k, m in kids], axis=1)
                rhs = jnp.concatenate([t1v[k] for k in kids], axis=0)
                uv[x // 2 * 2 + y] = nn(lhs, rhs).astype(BF16)
    last.wait()
    lhs = jnp.concatenate([uv[k] for k in range(4)], axis=1)
    rhs = jnp.concatenate([t2v[k // 2, k % 2] for k in range(4)], axis=0)
    uv[4] = nn(lhs, rhs).astype(BF16)
    out.start(uv.at[0:4], up.at[12:16])
    out.start(uv.at[0:4], down.at[12:16])
    out.start(uv, upper)
    out.start(uv.at[4:5], cell)
    out.wait()


def coefficients(samples, basis, t_one, t_two):
    return pl.pallas_call(
        coef_kernel,
        out_shape=[tiles(n) for n in (16, 16, 12, 12, 5, 1)],
        in_specs=[ANY_SPEC] * 4,
        out_specs=[ANY_SPEC] * 6,
        scratch_shapes=[
            VMEM((4, 4, 256, 256), BF16),
            VMEM((4, 4, 256, 256), BF16),
            VMEM((4, 4, 256, 256), BF16),
            VMEM((2, 2, 256, 256), BF16),
            VMEM((16, 256, 256), BF16),
            VMEM((5, 256, 256), BF16),
            pltpu.SemaphoreType.DMA((13,)),
            pltpu.SemaphoreType.DMA((26,)),
        ],
        compiler_params=params(),
        cost_estimate=cost(170, 12 << 20),
        name="coefficients",
    )(samples, basis, t_one, t_two)


def assembled(name, sources, pieces, ranges, stated=35):
    count = sum(n for _, _, n in pieces)

    def kernel(*refs):
        ins, outs = refs[: len(sources)], refs[len(sources) : -3]
        held, in_sems, out_sems = refs[-3:]
        into = Copies(in_sems)
        at = 0
        for source, first, n in pieces:
            into.start(ins[source].at[first : first + n], held.at[at : at + n])
            at += n
        into.wait()
        out = Copies(out_sems)
        for (first, last), ref in zip(ranges, outs):
            out.start(held.at[first:last], ref)
        out.wait()

    return pl.pallas_call(
        kernel,
        out_shape=[tiles(last - first) for first, last in ranges],
        in_specs=[ANY_SPEC] * len(sources),
        out_specs=[ANY_SPEC] * len(ranges),
        scratch_shapes=[
            VMEM((count, 256, 256), BF16),
            pltpu.SemaphoreType.DMA((len(pieces),)),
            pltpu.SemaphoreType.DMA((len(ranges),)),
        ],
        compiler_params=params(),
        cost_estimate=cost(stated, 0),
        name=name,
    )(*sources)


def halo_places():
    numbers = {}
    for r in range(4):
        for c in range(4):
            for k in range(9):
                y, x = r + k // 3 - 1, c + k % 3 - 1
                if not (0 <= y < 4 and 0 <= x < 4):
                    numbers[r * 4 + c, k] = len(numbers)
    return numbers


HALO = halo_places()
N_HALO = len(HALO) // 2


def split3(x):
    first = x.astype(BF16).astype(F32)
    rest = x - first
    second = rest.astype(BF16).astype(F32)
    return first, second, rest - second


def site_features(x, y):
    n = lax.broadcasted_iota(jnp.int32, (8, 256), 0)
    square = x * x + y * y
    target, source = [], []
    for parts in (split3(x), split3(y)):
        first, second, third = parts
        target.append(jnp.where(n < 3, first, jnp.where(n < 5, second, jnp.where(n < 6, third, 0.0))))
        other = jnp.where(
            (n == 0) | (n == 3) | (n == 5),
            first,
            jnp.where((n == 1) | (n == 4), second, jnp.where(n == 2, third, 0.0)),
        )
        source.append(-2.0 * other)
    first, second, third = split3(square)
    low = jnp.where(n == 0, first, jnp.where(n == 1, second, third))
    high = jnp.where(n == 3, first, jnp.where(n == 4, second, third))
    one = jnp.where(n < 6, 1.0, 0.0)
    target.append(jnp.where(n < 3, low, one))
    source.append(jnp.where(n < 3, 1.0, jnp.where(n < 6, high, 0.0)))
    zero = jnp.zeros((8, 256), F32)
    return jnp.concatenate(target + [zero], axis=0), jnp.concatenate(source + [zero], axis=0)


def near_kernel(
    first, with_far, grid_rows, grid_cols, lists, far_zero, positions, own, *rest
):
    if with_far:
        couplings, up, down, above, below, near_out, halo_out, field_out, flags = rest[:9]
        table, far_held, field, far_sems, field_sems = rest[9:14]
        rest = rest[14:]
    else:
        near_out, halo_out = rest[:2]
        rest = rest[2:]
    held, target_feat, source_feat, halo, made, near, floors, sems, halo_sems, near_sems = rest
    copy = pltpu.make_async_copy(own, held.at[0:16], sems.at[0])
    copy.start()
    out = Copies(halo_sems)
    sums_out = Copies(near_sems)
    if with_far:
        far_in = Copies(far_sems)
        far_in.start(couplings.at[0], table)
        for n, src in enumerate((above, up, down, below)):
            far_in.start(src.at[0:8], far_held.at[8 * n : 8 * n + 8])
        far_held[32] = jnp.zeros((256, 256), BF16)
        field_copies = Copies(field_sems)
    first_row = lax.axis_index("qx") * 4
    first_col = lax.axis_index("qy") * 4
    scale = root_three / length_scale
    mid_row = first_row.astype(F32) + 2.0
    mid_col = first_col.astype(F32) + 2.0
    first_place = first // 4 * 6

    def features(n, carry):
        r = jnp.clip(first_row + (first_place + n) // 6 - 1, 0, grid_rows - 1)
        c = jnp.clip(first_col + n % 6 - 1, 0, grid_cols - 1)
        here = positions[r * grid_cols + c]
        target, source = site_features(
            (here[0:1] - mid_row) * scale, (here[1:2] - mid_col) * scale
        )
        target_feat[n] = target
        source_feat[n] = source.astype(BF16)
        return carry

    lax.fori_loop(0, 24, features, 0)

    def mark(t):
        r, c = t // 4, t % 4
        mark_listed(
            lambda e: far_zero[r, c, e],
            flags,
            t,
            first_row + r // 2 * 2 - 2,
            first_col + c // 2 * 2 - 2,
            grid_cols,
        )

    def make(m, slot=None):
        t = first + m
        r, c = t // 4, t % 4
        moving = slot is not None
        slot = m % 2 * 9 if slot is None else slot
        for k in range(9):
            floors[m * 10 + k] = 1e6
        for e in range(9):
            entry = lists[r, c, e]
            source_row = jnp.maximum(entry, 0) // grid_cols
            source_col = jnp.maximum(entry, 0) - source_row * grid_cols
            k = (source_row - first_row - r + 1) * 3 + source_col - first_col - c + 1
            floors[m * 10 + jnp.where(entry >= 0, k, 9)] = 1e-24
        place = (m // 4 + 1) * 6 + c + 1
        target = target_feat[place].T.astype(BF16)
        for k in range(9):
            square = nn(target, source_feat[place + (k // 3 - 1) * 6 + k % 3 - 1])
            square = jnp.maximum(square, floors[m * 10 + k])
            far = square * lax.rsqrt(square)
            tile = ((far + 1.0) * jnp.exp2(far * -LOG2E)).astype(BF16)
            if moving:
                halo[m * 9 + k] = tile
                made[slot + k] = tile
            elif (t, k) in HALO:
                number = HALO[t, k] % N_HALO
                halo[number] = tile
                out.start(halo.at[number], halo_out.at[number])
            else:
                made[slot + k] = tile

    def use_moving(m, row, slot):
        t = first + m
        c = t % 4
        found = [k for k in range(9) if 0 <= first // 4 + row + k // 3 - 1 < 4]
        lhs = jnp.concatenate([made[slot + k] for k in found], axis=1)
        blocks = []
        for k in found:
            col = c + k % 3 - 1
            place = t + (k // 3 - 1) * 4 + k % 3 - 1
            blocks.append(held[jnp.where((col >= 0) & (col < 4), place, 16)])
        near[m] = nn(lhs, jnp.concatenate(blocks, axis=0))

    def use(m):
        t = first + m
        slot = m % 2 * 9
        found = [k for k in range(9) if (t, k) not in HALO]
        lhs = jnp.concatenate([made[slot + k] for k in found], axis=1)
        blocks = [held[t + (k // 3 - 1) * 4 + k % 3 - 1] for k in found]
        near[m] = nn(lhs, jnp.concatenate(blocks, axis=0))
        sums_out.start(near.at[m], near_out.at[m])

    if not with_far:
        copy.wait()
        held[16] = jnp.zeros((256, 256), BF16)

        def column(c, carry):
            make(c, 0)
            make(4 + c, 9)
            use_moving(c, 0, 0)
            use_moving(4 + c, 1, 9)
            return carry

        lax.fori_loop(0, 4, column, 0)
        for (t, k), number in HALO.items():
            if first <= t < first + 8:
                out.start(halo.at[(t - first) * 9 + k], halo_out.at[number % N_HALO])
        out.wait()
        for m in range(8):
            sums_out.start(near.at[m], near_out.at[m])
        sums_out.wait()
        return

    make(0)
    copy.wait()
    far_in.wait()
    for m in range(1, 8):
        make(m)
        if m % 2 == 1:
            a, b = m // 4, m // 2 % 2
            for p in PARENTS:
                mark(number_of(a, b, p))
            sums = level_zero_sums("inner", a, b, flags, table, far_held, 32)
            for p in PARENTS:
                t = number_of(a, b, p)
                field[t] = sums[p]
                field_copies.start(field.at[t], field_out.at[t])
        use(m - 1)
    use(7)
    out.wait()
    sums_out.wait()
    field_copies.wait()


def near_call(first, grid_rows, grid_cols, lists, far_zero, positions, own, far=()):
    out_shape = [tiles(8, F32), tiles(N_HALO)]
    out_specs = [ANY_SPEC, ANY_SPEC]
    scratch = []
    if far:
        out_shape += [tiles(16, F32), jax.ShapeDtypeStruct((16, 37), jnp.int32)]
        out_specs += [ANY_SPEC, SMEM_SPEC]
        scratch = [
            VMEM((20, 256, 256), BF16),
            VMEM((33, 256, 256), BF16),
            VMEM((16, 256, 256), F32),
            pltpu.SemaphoreType.DMA((5,)),
            pltpu.SemaphoreType.DMA((16,)),
        ]
    return pl.pallas_call(
        functools.partial(near_kernel, first, bool(far), grid_rows, grid_cols),
        out_shape=out_shape,
        in_specs=[SMEM_SPEC, SMEM_SPEC, VMEM_SPEC, ANY_SPEC]
        + ([ANY_SPEC] * 5 if far else []),
        out_specs=out_specs,
        scratch_shapes=scratch
        + [
            VMEM((17, 256, 256), BF16),
            VMEM((24, 32, 256), F32),
            VMEM((24, 32, 256), BF16),
            VMEM((N_HALO if far else 72, 256, 256), BF16),
            VMEM((18, 256, 256), BF16),
            VMEM((8, 256, 256), F32),
            pltpu.SMEM((80,), F32),
            pltpu.SemaphoreType.DMA((1,)),
            pltpu.SemaphoreType.DMA((N_HALO,)),
            pltpu.SemaphoreType.DMA((8,)),
        ],
        compiler_params=params(),
        cost_estimate=cost(600 if far else 12000, 8 << 20),
        name="near_and_inner_far" if far else "near_first",
    )(lists, far_zero, positions, own, *far)


def mark_listed(entries, flags, n, first_row, first_col, grid_cols):
    for w in range(36):
        flags[n, w] = 0
    for e in range(27):
        entry = entries(e)
        row = jnp.maximum(entry, 0) // grid_cols
        col = jnp.maximum(entry, 0) - row * grid_cols
        w = (row - first_row) * 6 + col - first_col
        flags[n, jnp.where(entry >= 0, jnp.clip(w, 0, 35), 36)] = 1


def dot_group(held, couplings, turned, group):
    rows = len(group[0][1])
    lhs = [
        jnp.concatenate([held[places[n]] for _, places in group], axis=1) for n in range(rows)
    ]
    lhs = jnp.concatenate(lhs, axis=0) if rows > 1 else lhs[0]
    if turned:
        return nn(lhs, jnp.concatenate([couplings[k] for k, _ in group], axis=0))
    return nt(lhs, jnp.concatenate([couplings[k] for k, _ in group], axis=1))


def coupled(plan, couplings, held, places):
    total = None
    for turned in (0, 1):
        group = [(k, [places(w)]) for w, k in plan[turned]]
        part = dot_group(held, couplings, turned, group)
        total = part if total is None else total + part
    return total


def upper_kernel(
    grid_cols, n_rows, far_one, far_two, couplings, t_two, upper, above, below, row, row_e, row_d,
    cells, cells_e, quads, quads_e, down, held_one, held_two, field_two, flags, sems,
):
    n_cells = 2 * n_rows
    n_two = 3 * n_cells
    zero_one, zero_two = 36, 2 * n_two
    copies = Copies(sems)
    copies.start(cells, held_two.at[0:n_cells])
    copies.start(quads, held_two.at[n_cells:n_two])
    copies.start(cells_e, held_two.at[n_two : n_two + n_cells])
    copies.start(quads_e, held_two.at[n_two + n_cells : 2 * n_two])
    copies.start(upper.at[0:4], held_one.at[0:4])
    copies.start(row, held_one.at[4:12])
    copies.start(above.at[12:16], held_one.at[12:16])
    copies.start(below.at[12:16], held_one.at[16:20])
    copies.start(row_e, held_one.at[20:28])
    copies.start(row_d, held_one.at[28:36])
    held_one[zero_one] = jnp.zeros((256, 256), BF16)
    held_two[zero_two] = jnp.zeros((256, 256), BF16)
    i = lax.axis_index("qx")
    j = lax.axis_index("qy")
    a = i % 2
    b = j % 2
    for t in range(4):
        mark_listed(
            lambda e: far_one[t // 2, t % 2, e], flags, t, 2 * i - 2, 2 * j - 2, 2 * grid_cols
        )
    mark_listed(
        lambda e: far_two[0, 0, e], flags, 4, i // 2 * 2 - 2, j // 2 * 2 - 2, grid_cols
    )
    core_at = [jnp.where(a == 0, 0, n_two), jnp.where(a == 0, n_two, 0)]
    y_at = [2, 0, 2] if n_rows == 2 else [2, 0, 4]
    pair_tiles = 2 * n_rows
    z_at = [
        jnp.where(b == 0, pair_tiles, 2 * pair_tiles),
        0,
        jnp.where(b == 0, 2 * pair_tiles, pair_tiles),
    ]
    x_at = [b, 1 - b]

    def place_two(w):
        r, c = w // 6, w % 6
        place = core_at[r % 2] + y_at[r // 2] + z_at[c // 2] + x_at[c % 2]
        return jnp.where(flags[4, w] == 1, place, zero_two)

    own_at = [12, 0, 16]
    pair_at = [jnp.where(a == 0, 28, 20), 4, jnp.where(a == 0, 20, 28)]
    col_at = [jnp.where(b == 0, 4, 0), None, jnp.where(b == 0, 0, 4)]

    def place_one(t, w):
        r, c = w // 6, w % 6
        base = own_at[r // 2] if c // 2 == 1 else pair_at[r // 2] + col_at[c // 2]
        place = base + (r % 2) * 2 + c % 2
        return jnp.where(flags[t, w] == 1, place, zero_one)

    for copy in copies.started[:4]:
        copy.wait()
    for u in range(2):
        for v in range(2):

            @pl.when((a == u) & (b == v))
            def _():
                field_two[...] = coupled(
                    class_plan(u, v), couplings.at[1], held_two, place_two
                ).astype(BF16)

    for copy in copies.started[4:]:
        copy.wait()
    for u in range(2):
        for v in range(2):
            t = u * 2 + v
            field = coupled(
                class_plan(u, v), couplings.at[0], held_one, functools.partial(place_one, t)
            )
            down[t] = (field + nt(field_two[...], t_two[u, v])).astype(BF16)


def upper_levels(grid_cols, far_one, far_two, couplings, t_two, *received):
    n_two = 3 * received[6].shape[0]
    return pl.pallas_call(
        functools.partial(upper_kernel, grid_cols, n_two // 6),
        grid=(1,),
        out_shape=tiles(4),
        in_specs=[
            SMEM_SPEC,
            SMEM_SPEC,
            pl.BlockSpec(
                (pl.Element(2), pl.Element(20), pl.Element(256), pl.Element(256)),
                lambda g: (1, 0, 0, 0),
            ),
            pl.BlockSpec((2, 2, 256, 256), lambda g: (0, 0, 0, 0)),
        ]
        + [ANY_SPEC] * 10,
        out_specs=pl.BlockSpec((4, 256, 256), lambda g: (0, 0, 0)),
        scratch_shapes=[
            VMEM((37, 256, 256), BF16),
            VMEM((2 * n_two + 1, 256, 256), BF16),
            VMEM((256, 256), BF16),
            pltpu.SMEM((5, 37), jnp.int32),
            pltpu.SemaphoreType.DMA((10,)),
        ],
        compiler_params=params(),
        cost_estimate=cost(340, 14 << 20),
        name="upper_levels",
    )(far_one, far_two, couplings, t_two, *received)


def source_of(x, y, w):
    r, c = 2 * x + w // 6, 2 * y + w % 6
    if 2 <= c < 6:
        return "inner", r * 4 + c - 2
    side = 0 if c < 2 else 1
    c = c if c < 2 else c - 6
    if 2 <= r < 6:
        return ("left", "right")[side], (r - 2) * 2 + c
    return "corners", (0 if r < 2 else 8) + side * 4 + (r if r < 2 else r - 6) * 2 + c


PARENTS = [(x, y) for x in range(2) for y in range(2)]


def number_of(a, b, parent):
    x, y = parent
    return (2 * x + a) * 4 + 2 * y + b


def level_zero_sums(kind, a, b, flags, couplings, held, zero):
    plan = class_plan(a, b)
    sums = {}
    for turned in (0, 1):
        groups = {}
        for w, k in plan[turned]:
            members = tuple(p for p in PARENTS if source_of(*p, w)[0] == kind)
            if members:
                groups.setdefault(members, []).append((w, k))
        for members, entries in groups.items():
            group = []
            for w, k in entries:
                places = [
                    jnp.where(flags[number_of(a, b, p), w] == 1, source_of(*p, w)[1], zero)
                    for p in members
                ]
                group.append((k, places))
            total = dot_group(held, couplings, turned, group)
            for n, p in enumerate(members):
                part = total[256 * n : 256 * n + 256]
                sums[p] = part if p not in sums else sums[p] + part
    return sums


def grouped(x):
    return x.reshape(2, 2, 2, 2, 256, 256)


CLASS_BLOCK = pl.BlockSpec((2, 1, 2, 1, 256, 256), lambda g: (0, g // 2, 0, g % 2, 0, 0))
COUPLING_BLOCK = pl.BlockSpec((1, 20, 256, 256), lambda g: (0, 0, 0, 0))
GROUPED_F32 = jax.ShapeDtypeStruct((2, 2, 2, 2, 256, 256), F32)


def each_class(step, body):
    for a in range(2):
        for b in range(2):
            pl.when(step == a * 2 + b)(functools.partial(body, a, b))


def near_source(r, c):
    rows_in, cols_in = 1 <= r < 5, 1 <= c < 5
    if rows_in and cols_in:
        return "own", None
    if rows_in:
        return ("left" if c == 0 else "right"), r - 1
    if cols_in:
        return "rows", (0 if r == 0 else 4) + c - 1
    return "corners", (0 if r == 0 else 2) + (0 if c == 0 else 1)


def halo_of(kinds):
    return [
        n for (t, k), n in HALO.items() if near_source(t // 4 + k // 3, t % 4 + k % 3)[0] in kinds
    ]


EARLY_HALO = halo_of(("left", "rows"))
LATE_HALO = halo_of(("right", "corners"))


def near_part(at, t, halo, numbers, held):
    r, c = t // 4, t % 4
    made, blocks = [], []
    for k in range(9):
        found, place = near_source(r + k // 3, c + k % 3)
        if found in at:
            made.append(halo[numbers.index(HALO[t, k])])
            blocks.append(held[at[found] + place])
    if not made:
        return None
    return nn(jnp.concatenate(made, axis=1), jnp.concatenate(blocks, axis=0))


def halo_pairs(numbers, halo_a, halo_b, halo):
    return [
        ((halo_a if n < N_HALO else halo_b).at[n % N_HALO], halo.at[m])
        for m, n in enumerate(numbers)
    ]


def started_first(step, pairs, sems, first):
    def copies():
        return [pltpu.make_async_copy(src, dst, sems.at[n]) for n, (src, dst) in enumerate(pairs)]

    @pl.when(step == 0)
    def _():
        started = copies()
        for copy in started:
            copy.start()
        for copy in started[:first]:
            copy.wait()

    def rest():
        for copy in copies()[first:]:
            copy.wait()

    return rest


def left_kernel(
    flags, couplings, field_in, near_a, near_b, halo_a, halo_b, left, above, below,
    field, near, held, near_held, halo, sems,
):
    step = pl.program_id(0)
    pairs = [(left.at[0:8], held.at[0:8])]
    for n, src in enumerate((left, above, below)):
        pairs.append((src.at[8:12], near_held.at[4 * n : 4 * n + 4]))
    pairs += halo_pairs(EARLY_HALO, halo_a, halo_b, halo)
    held[8] = jnp.zeros((256, 256), BF16)
    wait_rest = started_first(step, pairs, sems, 1)

    def body(a, b):
        sums = level_zero_sums("left", a, b, flags, couplings.at[0], held, 8)
        for x, y in PARENTS:
            value = field_in[x, 0, y, 0]
            field[x, 0, y, 0] = value + sums[x, y] if (x, y) in sums else value
        if a == 0 and b == 0:
            wait_rest()
        for x, y in PARENTS:
            part = near_part(
                {"left": 0, "rows": 4}, number_of(a, b, (x, y)), halo, EARLY_HALO, near_held
            )
            here = (near_b if x else near_a)[0, y, 0]
            near[x, 0, y, 0] = here if part is None else here + part

    each_class(step, body)


HALF_BLOCK = pl.BlockSpec((1, 2, 1, 256, 256), lambda g: (g // 2, 0, g % 2, 0, 0))


def left_level(flags, couplings, field, near_a, near_b, *received):
    half = lambda x: x.reshape(2, 2, 2, 256, 256)
    return pl.pallas_call(
        left_kernel,
        grid=(4,),
        out_shape=(GROUPED_F32, GROUPED_F32),
        in_specs=[SMEM_SPEC, COUPLING_BLOCK, CLASS_BLOCK, HALF_BLOCK, HALF_BLOCK] + [ANY_SPEC] * 5,
        out_specs=[CLASS_BLOCK, CLASS_BLOCK],
        scratch_shapes=[
            VMEM((9, 256, 256), BF16),
            VMEM((12, 256, 256), BF16),
            VMEM((len(EARLY_HALO), 256, 256), BF16),
            pltpu.SemaphoreType.DMA((4 + len(EARLY_HALO),)),
        ],
        compiler_params=params(),
        cost_estimate=cost(300, 30 << 20),
        name="far_left",
    )(flags, couplings, grouped(field), half(near_a), half(near_b), *received)


def right_kernel(flags, couplings, field_in, right, field, held, sems):
    step = pl.program_id(0)
    held[8] = jnp.zeros((256, 256), BF16)
    started_first(step, [(right.at[0:8], held.at[0:8])], sems, 1)

    def body(a, b):
        sums = level_zero_sums("right", a, b, flags, couplings.at[0], held, 8)
        for x, y in PARENTS:
            value = field_in[x, 0, y, 0]
            field[x, 0, y, 0] = value + sums[x, y] if (x, y) in sums else value

    each_class(step, body)


def right_level(flags, couplings, field, right):
    return pl.pallas_call(
        right_kernel,
        grid=(4,),
        out_shape=GROUPED_F32,
        in_specs=[SMEM_SPEC, COUPLING_BLOCK, CLASS_BLOCK, ANY_SPEC],
        out_specs=CLASS_BLOCK,
        scratch_shapes=[VMEM((9, 256, 256), BF16), pltpu.SemaphoreType.DMA((1,))],
        compiler_params=params(),
        cost_estimate=cost(200, 12 << 20),
        name="far_right",
    )(flags, couplings, field, right)


def last_kernel(
    flags, couplings, t_one, basis, down_one, field, near, halo_a, halo_b, right,
    left_above, left_below, right_above, right_below, out, held, near_held, halo, sems,
):
    step = pl.program_id(0)
    corners = (left_above, right_above, left_below, right_below)
    pairs = [(src.at[0:4], held.at[4 * n : 4 * n + 4]) for n, src in enumerate(corners)]
    pairs += [(src.at[4:5], near_held.at[n : n + 1]) for n, src in enumerate(corners)]
    pairs.append((right.at[8:12], near_held.at[4:8]))
    pairs += halo_pairs(LATE_HALO, halo_a, halo_b, halo)
    held[16] = jnp.zeros((256, 256), BF16)
    wait_rest = started_first(step, pairs, sems, 4)

    def body(a, b):
        sums = level_zero_sums("corners", a, b, flags, couplings.at[0], held, 16)
        if a == 0 and b == 0:
            wait_rest()
        for x, y in PARENTS:
            total = field[x, 0, y, 0] + nt(down_one[x * 2 + y], t_one[x, 0, y, 0])
            if (x, y) in sums:
                total = total + sums[x, y]
            far = nt(basis[x, 0, y, 0], total.astype(BF16))
            near_sum = near[x, 0, y, 0]
            part = near_part(
                {"corners": 0, "right": 4}, number_of(a, b, (x, y)), halo, LATE_HALO, near_held
            )
            if part is not None:
                near_sum = near_sum + part
            out[x, 0, y, 0] = (near_sum * TILE_SCALE + far).astype(BF16)

    each_class(step, body)


def last_level(flags, couplings, t_one, basis, *rest):
    return pl.pallas_call(
        last_kernel,
        grid=(4,),
        out_shape=jax.ShapeDtypeStruct((2, 2, 2, 2, 256, 256), BF16),
        in_specs=[
            SMEM_SPEC,
            COUPLING_BLOCK,
            CLASS_BLOCK,
            CLASS_BLOCK,
            pl.BlockSpec((4, 256, 256), lambda g: (0, 0, 0)),
            CLASS_BLOCK,
            CLASS_BLOCK,
        ]
        + [ANY_SPEC] * 7,
        out_specs=CLASS_BLOCK,
        scratch_shapes=[
            VMEM((17, 256, 256), BF16),
            VMEM((8, 256, 256), BF16),
            VMEM((len(LATE_HALO), 256, 256), BF16),
            pltpu.SemaphoreType.DMA((9 + len(LATE_HALO),)),
        ],
        compiler_params=params(),
        cost_estimate=cost(270, 20 << 20),
        name="last_level",
    )(flags, couplings, grouped(t_one), grouped(basis), *rest)


def per_device(
    positions,
    samples,
    leaf_basis,
    transfer_one,
    transfer_two,
    couplings,
    near_lists,
    far_zero,
    far_one,
    far_two,
):
    nx = lax.axis_size("qx")
    ny = lax.axis_size("qy")
    down_x = [(k, k + 1) for k in range(nx - 1)]
    up_x = [(k + 1, k) for k in range(nx - 1)]
    down_y = [(k, k + 1) for k in range(ny - 1)]
    up_y = [(k + 1, k) for k in range(ny - 1)]

    up, down, left, right, upper, cell = coefficients(
        samples, leaf_basis, transfer_one, transfer_two
    )

    swap_y = [(k, k ^ 1) for k in range(ny)]
    swap_x = [(k, k ^ 1) for k in range(nx)]
    cross_x = [(k, k + 1) for k in range(1, nx - 1, 2)] + [(k + 1, k) for k in range(1, nx - 1, 2)]
    pair = lax.ppermute(upper, "qy", swap_y)
    if nx == 4:
        others = [lax.ppermute(cell, "qx", [(k, k ^ 2) for k in range(nx)])]
    else:
        others = [
            lax.ppermute(cell, "qx", [(k, k + 2) for k in range(nx - 2)]),
            lax.ppermute(cell, "qx", [(k + 2, k) for k in range(nx - 2)]),
        ]
    others_pair = [lax.ppermute(x, "qy", swap_y) for x in others]
    above = lax.ppermute(down, "qx", down_x)
    below = lax.ppermute(up, "qx", up_x)
    sites = positions.reshape(-1, 2, 256)
    flat_samples = samples.reshape(16, 256, 256)
    near_a, halo_a = near_call(
        0, 4 * nx, 4 * ny, near_lists, far_zero, sites, flat_samples
    )
    pair, others_pair, near_a = lax.optimization_barrier((pair, others_pair, near_a))
    outward = [(k, k + 2) for k in range(0, ny - 2, 2)] + [(k + 2, k) for k in range(1, ny - 2, 2)]
    inward = [(k + 2, k) for k in range(0, ny - 2, 2)] + [(k, k + 2) for k in range(1, ny - 2, 2)]
    n_others = len(others)
    quad = [(0, 4, 1), (1, 4, 1)]
    for n in range(n_others):
        quad += [(2 + n, 0, 1), (2 + n_others + n, 0, 1)]
    n_quad = len(quad)
    across, cells = assembled(
        "pair_payload",
        (upper, pair, *others, *others_pair),
        [(1, 0, 4)] + quad,
        [(0, 4 + n_quad), (4, 4 + n_quad)],
    )
    across, cells, left, right = lax.optimization_barrier((across, cells, left, right))
    outer = lax.ppermute(across, "qy", outward)
    inner = lax.ppermute(cells, "qy", inward)
    cells_e = lax.ppermute(cells, "qx", swap_x)
    on_left = lax.ppermute(right, "qy", down_y)
    _, above, below = lax.optimization_barrier((across, above, below))
    near_b, halo_b, field, flags = near_call(
        8,
        4 * nx,
        4 * ny,
        near_lists,
        far_zero,
        sites,
        flat_samples,
        (couplings, up, down, above, below),
    )
    inner, outer, near_b = lax.optimization_barrier((inner, outer, near_b))
    row, quads = assembled(
        "row_payload",
        (pair, outer, inner),
        [(0, 0, 4), (1, 0, 4), (1, 4, n_quad), (2, 0, n_quad)],
        [(0, 8), (8, 8 + 2 * n_quad)],
    )
    row_d = lax.ppermute(row, "qx", cross_x)
    row_e = lax.ppermute(row, "qx", swap_x)
    quads_e = lax.ppermute(quads, "qx", swap_x)
    on_left, left, row_e, quads_e, cells_e = lax.optimization_barrier(
        (on_left, left, row_e, quads_e, cells_e)
    )
    on_right = lax.ppermute(left, "qy", up_y)
    down_one = upper_levels(
        ny, far_one, far_two, couplings, transfer_two, upper, above, below, row, row_e, row_d,
        cells, cells_e, quads, quads_e,
    )

    def corners(name, halo):
        to_down, to_up = assembled(
            name, (halo,), [(0, 4, 4), (0, 11, 1), (0, 0, 4), (0, 8, 1)], [(0, 5), (5, 10)]
        )
        return [lax.ppermute(to_down, "qx", down_x), lax.ppermute(to_up, "qx", up_x)]

    left_corners = corners("left_corners", on_left)
    field, near = left_level(
        flags, couplings, field, near_a, near_b, halo_a, halo_b, on_left, above, below
    )
    on_right, down_one, near = lax.optimization_barrier((on_right, down_one, near))
    right_corners = corners("right_corners", on_right)
    field = right_level(flags, couplings, field, on_right)
    result = last_level(
        flags, couplings, transfer_one, leaf_basis, down_one, field, near, halo_a, halo_b,
        on_right, *left_corners, *right_corners,
    )
    return result.reshape(4, 4, 256, 256)


def solution(mesh):
    return jax.shard_map(
        per_device,
        mesh=mesh,
        in_specs=(
            P(),
            P("qx", "qy", None, None),
            P("qx", "qy", None, None),
            P("qx", "qy", None, None),
            P("qx", "qy", None, None),
            P(),
            P("qx", "qy", None),
            P("qx", "qy", None),
            P("qx", "qy", None),
            P("qx", "qy", None),
        ),
        out_specs=P("qx", "qy", None, None),
        check_vma=False,
    )
```

```python
import functools

import jax
import jax.numpy as jnp
import numpy as np
from jax import lax
from jax.experimental import pallas as pl
from jax.experimental.pallas import tpu as pltpu
from jax.sharding import PartitionSpec as P

root_three = 1.7320508075688772
length_scale = 1.0
VMEM = pltpu.VMEM
SMEM = pltpu.SMEM
F32 = jnp.float32
BF16 = jnp.bfloat16
BIG = 64 * 1024 * 1024 - 256 * 1024


def nn(a, b):
    return lax.dot_general(a, b, (((1,), (0,)), ((), ())), preferred_element_type=F32)


def nt(a, b):
    return lax.dot_general(a, b, (((1,), (1,)), ((), ())), preferred_element_type=F32)


def tn(a, b):
    return lax.dot_general(a, b, (((0,), (0,)), ((), ())), preferred_element_type=F32)


def params():
    return pltpu.CompilerParams(vmem_limit_bytes=BIG)


def cost(products, bytes_accessed):
    return pl.CostEstimate(
        flops=products * 2 * 256**3 // 8, bytes_accessed=bytes_accessed // 8, transcendentals=0
    )


def half_offsets():
    kept = []
    for u in range(-3, 4):
        for v in range(-3, 4):
            if max(abs(u), abs(v)) >= 2 and (u > 0 or (u == 0 and v > 0)):
                kept.append((u, v))
    return kept


HALF_OFFSETS = half_offsets()


def class_plan(a, b):
    plain, turned = [], []
    for w in range(36):
        u, v = w // 6 - 2 - a, w % 6 - 2 - b
        if max(abs(u), abs(v)) < 2:
            continue
        if (u, v) in HALF_OFFSETS:
            plain.append((w, HALF_OFFSETS.index((u, v))))
        else:
            turned.append((w, HALF_OFFSETS.index((-u, -v))))
    return plain, turned


LOG2E = 1.4426950408889634
TILE_SCALE = 256 ** -0.5


def tiles(n, dtype=BF16):
    return jax.ShapeDtypeStruct((n, 256, 256), dtype)


ANY_SPEC = pl.BlockSpec(memory_space=pltpu.HBM)
SMEM_SPEC = pl.BlockSpec(memory_space=SMEM)
VMEM_SPEC = pl.BlockSpec(memory_space=VMEM)


def row_number(entry, grid_cols):
    if grid_cols & (grid_cols - 1) == 0:
        return entry >> (grid_cols.bit_length() - 1)
    return lax.div(entry, jnp.int32(grid_cols))


class Copies:
    def __init__(self, sems):
        self.sems = sems
        self.started = []

    def start(self, src, dst):
        copy = pltpu.make_async_copy(src, dst, self.sems.at[len(self.started)])
        copy.start()
        self.started.append(copy)
        return copy

    def wait(self):
        for copy in self.started:
            copy.wait()


def coef_kernel(
    samples, basis, t_one, t_two, up, down, left, right, upper, cell,
    sv, bv, t1v, t2v, cv, uv, in_sems, out_sems,
):
    into = Copies(in_sems)
    out = Copies(out_sems)
    rows = []
    for x in range(4):
        rows.append(
            (
                into.start(samples.at[x], sv.at[x]),
                into.start(basis.at[x], bv.at[x]),
                into.start(t_one.at[x], t1v.at[x]),
            )
        )
    last = into.start(t_two, t2v)
    for x in range(4):
        rows[x][0].wait()
        rows[x][1].wait()
        for y in range(4):
            cv[x * 4 + y] = tn(sv[x, y], bv[x, y]).astype(BF16)
        own = cv.at[4 * x : 4 * x + 4]
        out.start(own, (up if x < 2 else down).at[4 * (x % 2) : 4 * (x % 2) + 4])
        out.start(cv.at[4 * x : 4 * x + 2], left.at[2 * x : 2 * x + 2])
        out.start(cv.at[4 * x + 2 : 4 * x + 4], right.at[2 * x : 2 * x + 2])
        out.start(sv.at[x, 0], left.at[8 + x])
        out.start(sv.at[x, 3], right.at[8 + x])
        if x == 0:
            out.start(sv.at[x], up.at[8:12])
        if x == 3:
            out.start(sv.at[x], down.at[8:12])
        if x % 2 == 1:
            rows[x - 1][2].wait()
            rows[x][2].wait()
            for y in range(2):
                kids = [(x - 1 + a, 2 * y + b) for a in range(2) for b in range(2)]
                lhs = jnp.concatenate([cv[k * 4 + m] for k, m in kids], axis=1)
                rhs = jnp.concatenate([t1v[k] for k in kids], axis=0)
                uv[x // 2 * 2 + y] = nn(lhs, rhs).astype(BF16)
    last.wait()
    lhs = jnp.concatenate([uv[k] for k in range(4)], axis=1)
    rhs = jnp.concatenate([t2v[k // 2, k % 2] for k in range(4)], axis=0)
    uv[4] = nn(lhs, rhs).astype(BF16)
    out.start(uv.at[0:4], up.at[12:16])
    out.start(uv.at[0:4], down.at[12:16])
    out.start(uv, upper)
    out.start(uv.at[4:5], cell)
    out.wait()


def coefficients(samples, basis, t_one, t_two):
    return pl.pallas_call(
        coef_kernel,
        out_shape=[tiles(n) for n in (16, 16, 12, 12, 5, 1)],
        in_specs=[ANY_SPEC] * 4,
        out_specs=[ANY_SPEC] * 6,
        scratch_shapes=[
            VMEM((4, 4, 256, 256), BF16),
            VMEM((4, 4, 256, 256), BF16),
            VMEM((4, 4, 256, 256), BF16),
            VMEM((2, 2, 256, 256), BF16),
            VMEM((16, 256, 256), BF16),
            VMEM((5, 256, 256), BF16),
            pltpu.SemaphoreType.DMA((13,)),
            pltpu.SemaphoreType.DMA((26,)),
        ],
        compiler_params=params(),
        cost_estimate=cost(170, 12 << 20),
        name="coefficients",
    )(samples, basis, t_one, t_two)


def assembled(name, sources, pieces, ranges, stated=35):
    count = sum(n for _, _, n in pieces)

    def kernel(*refs):
        ins, outs = refs[: len(sources)], refs[len(sources) : -3]
        held, in_sems, out_sems = refs[-3:]
        into = Copies(in_sems)
        at = 0
        for source, first, n in pieces:
            into.start(ins[source].at[first : first + n], held.at[at : at + n])
            at += n
        into.wait()
        out = Copies(out_sems)
        for (first, last), ref in zip(ranges, outs):
            out.start(held.at[first:last], ref)
        out.wait()

    return pl.pallas_call(
        kernel,
        out_shape=[tiles(last - first) for first, last in ranges],
        in_specs=[ANY_SPEC] * len(sources),
        out_specs=[ANY_SPEC] * len(ranges),
        scratch_shapes=[
            VMEM((count, 256, 256), BF16),
            pltpu.SemaphoreType.DMA((len(pieces),)),
            pltpu.SemaphoreType.DMA((len(ranges),)),
        ],
        compiler_params=params(),
        cost_estimate=cost(stated, 0),
        name=name,
    )(*sources)


def halo_places():
    numbers = {}
    for r in range(4):
        for c in range(4):
            for k in range(9):
                y, x = r + k // 3 - 1, c + k % 3 - 1
                if not (0 <= y < 4 and 0 <= x < 4):
                    numbers[r * 4 + c, k] = len(numbers)
    return numbers


HALO = halo_places()
N_HALO = len(HALO) // 2


def split3(x):
    first = x.astype(BF16).astype(F32)
    rest = x - first
    second = rest.astype(BF16).astype(F32)
    return first, second, rest - second


def site_features(x, y):
    n = lax.broadcasted_iota(jnp.int32, (8, 256), 0)
    square = x * x + y * y
    target, source = [], []
    for parts in (split3(x), split3(y)):
        first, second, third = parts
        target.append(jnp.where(n < 3, first, jnp.where(n < 5, second, jnp.where(n < 6, third, 0.0))))
        other = jnp.where(
            (n == 0) | (n == 3) | (n == 5),
            first,
            jnp.where((n == 1) | (n == 4), second, jnp.where(n == 2, third, 0.0)),
        )
        source.append(-2.0 * other)
    first, second, third = split3(square)
    low = jnp.where(n == 0, first, jnp.where(n == 1, second, third))
    high = jnp.where(n == 3, first, jnp.where(n == 4, second, third))
    one = jnp.where(n < 6, 1.0, 0.0)
    target.append(jnp.where(n < 3, low, one))
    source.append(jnp.where(n < 3, 1.0, jnp.where(n < 6, high, 0.0)))
    zero = jnp.zeros((8, 256), F32)
    return jnp.concatenate(target + [zero], axis=0), jnp.concatenate(source + [zero], axis=0)


def near_kernel(
    first, with_far, grid_rows, grid_cols, lists, far_zero, positions, own, *rest
):
    if with_far:
        flags, couplings, up, down, above, below, near_out, halo_out, field_out = rest[:9]
        table, far_held, field, far_sems, field_sems = rest[9:14]
        rest = rest[14:]
    else:
        near_out, halo_out, flags = rest[:3]
        rest = rest[3:]
    held, target_feat, source_feat, halo, made, near, floors, sems, halo_sems, near_sems = rest
    copy = pltpu.make_async_copy(own, held, sems.at[0])
    copy.start()
    out = Copies(halo_sems)
    sums_out = Copies(near_sems)
    if with_far:
        far_in = Copies(far_sems)
        far_in.start(couplings.at[0], table)
        for n, src in enumerate((above, up, down, below)):
            far_in.start(src.at[0:8], far_held.at[8 * n : 8 * n + 8])
        far_held[32] = jnp.zeros((256, 256), BF16)
        field_copies = Copies(field_sems)
    first_row = lax.axis_index("qx") * 4
    first_col = lax.axis_index("qy") * 4
    scale = root_three / length_scale
    mid_row = first_row.astype(F32) + 2.0
    mid_col = first_col.astype(F32) + 2.0
    first_place = first // 4 * 6

    def features(n, carry):
        r = jnp.clip(first_row + (first_place + n) // 6 - 1, 0, grid_rows - 1)
        c = jnp.clip(first_col + n % 6 - 1, 0, grid_cols - 1)
        here = positions[r * grid_cols + c]
        target, source = site_features(
            (here[0:1] - mid_row) * scale, (here[1:2] - mid_col) * scale
        )
        target_feat[n] = target
        source_feat[n] = source.astype(BF16)
        return carry

    lax.fori_loop(0, 24, features, 0)

    def mark(t):
        r, c = t // 4, t % 4
        mark_listed(
            lambda e: far_zero[r, c, e],
            flags,
            t,
            first_row + r // 2 * 2 - 2,
            first_col + c // 2 * 2 - 2,
            grid_cols,
        )

    def make(m):
        t = first + m
        r, c = t // 4, t % 4
        slot = m % 2 * 9
        for k in range(9):
            floors[m * 10 + k] = 1e6
        for e in range(9):
            entry = lists[r, c, e]
            source_row = row_number(jnp.maximum(entry, 0), grid_cols)
            source_col = jnp.maximum(entry, 0) - source_row * grid_cols
            k = (source_row - first_row - r + 1) * 3 + source_col - first_col - c + 1
            floors[m * 10 + jnp.where(entry >= 0, k, 9)] = 1e-24
        if not with_far:
            mark(2 * m)
            mark(2 * m + 1)
        place = (m // 4 + 1) * 6 + c + 1
        target = target_feat[place].T.astype(BF16)
        for k in range(9):
            square = nn(target, source_feat[place + (k // 3 - 1) * 6 + k % 3 - 1])
            square = jnp.maximum(square, floors[m * 10 + k])
            far = square * lax.rsqrt(square)
            tile = ((far + 1.0) * jnp.exp2(far * -LOG2E)).astype(BF16)
            if (t, k) in HALO:
                number = HALO[t, k] % N_HALO
                halo[number] = tile
                out.start(halo.at[number], halo_out.at[number])
            else:
                made[slot + k] = tile

    def use(m):
        t = first + m
        slot = m % 2 * 9
        found = [k for k in range(9) if (t, k) not in HALO]
        lhs = jnp.concatenate([made[slot + k] for k in found], axis=1)
        blocks = [held[t + (k // 3 - 1) * 4 + k % 3 - 1] for k in found]
        near[m] = nn(lhs, jnp.concatenate(blocks, axis=0))
        sums_out.start(near.at[m], near_out.at[m])

    make(0)
    copy.wait()
    if with_far:
        far_in.wait()
    for m in range(1, 8):
        make(m)
        if with_far and m % 2 == 1:
            a, b = m // 4, m // 2 % 2
            sums = level_zero_sums("inner", a, b, flags, table, far_held, 32)
            for p in PARENTS:
                t = number_of(a, b, p)
                field[t] = sums[p]
                field_copies.start(field.at[t], field_out.at[t])
        use(m - 1)
    use(7)
    out.wait()
    sums_out.wait()
    if with_far:
        field_copies.wait()


def near_call(first, grid_rows, grid_cols, lists, far_zero, positions, own, far=()):
    out_shape = [tiles(8, F32), tiles(N_HALO)]
    out_specs = [ANY_SPEC, ANY_SPEC]
    scratch = []
    if far:
        out_shape.append(tiles(16, F32))
        out_specs.append(ANY_SPEC)
        scratch = [
            VMEM((20, 256, 256), BF16),
            VMEM((33, 256, 256), BF16),
            VMEM((16, 256, 256), F32),
            pltpu.SemaphoreType.DMA((5,)),
            pltpu.SemaphoreType.DMA((16,)),
        ]
    else:
        out_shape.append(jax.ShapeDtypeStruct((16, 37), jnp.int32))
        out_specs.append(SMEM_SPEC)
    return pl.pallas_call(
        functools.partial(near_kernel, first, bool(far), grid_rows, grid_cols),
        out_shape=out_shape,
        in_specs=[SMEM_SPEC, SMEM_SPEC, VMEM_SPEC, ANY_SPEC]
        + ([SMEM_SPEC] + [ANY_SPEC] * 5 if far else []),
        out_specs=out_specs,
        scratch_shapes=scratch
        + [
            VMEM((16, 256, 256), BF16),
            VMEM((24, 32, 256), F32),
            VMEM((24, 32, 256), BF16),
            VMEM((N_HALO, 256, 256), BF16),
            VMEM((18, 256, 256), BF16),
            VMEM((8, 256, 256), F32),
            pltpu.SMEM((80,), F32),
            pltpu.SemaphoreType.DMA((1,)),
            pltpu.SemaphoreType.DMA((N_HALO,)),
            pltpu.SemaphoreType.DMA((8,)),
        ],
        compiler_params=params(),
        cost_estimate=cost(600 if far else 12000, 8 << 20),
        name="near_and_inner_far" if far else "near_first",
    )(lists, far_zero, positions, own, *far)


def mark_listed(entries, flags, n, first_row, first_col, grid_cols):
    for w in range(36):
        flags[n, w] = 0
    for e in range(27):
        entry = entries(e)
        row = row_number(jnp.maximum(entry, 0), grid_cols)
        col = jnp.maximum(entry, 0) - row * grid_cols
        w = (row - first_row) * 6 + col - first_col
        flags[n, jnp.where(entry >= 0, jnp.clip(w, 0, 35), 36)] = 1


def dot_group(held, couplings, turned, group):
    rows = len(group[0][1])
    lhs = [
        jnp.concatenate([held[places[n]] for _, places in group], axis=1) for n in range(rows)
    ]
    lhs = jnp.concatenate(lhs, axis=0) if rows > 1 else lhs[0]
    if turned:
        return nn(lhs, jnp.concatenate([couplings[k] for k, _ in group], axis=0))
    return nt(lhs, jnp.concatenate([couplings[k] for k, _ in group], axis=1))


def coupled(plan, couplings, held, places):
    total = None
    for turned in (0, 1):
        group = [(k, [places(w)]) for w, k in plan[turned]]
        part = dot_group(held, couplings, turned, group)
        total = part if total is None else total + part
    return total


def upper_kernel(
    grid_cols, n_rows, far_one, far_two, couplings, t_two, upper, above, below, row, row_e, row_d,
    cells, cells_e, quads, quads_e, down, held_one, held_two, field_two, flags, sems,
):
    n_cells = 2 * n_rows
    n_two = 3 * n_cells
    zero_one, zero_two = 36, 2 * n_two
    copies = Copies(sems)
    copies.start(cells, held_two.at[0:n_cells])
    copies.start(quads, held_two.at[n_cells:n_two])
    copies.start(cells_e, held_two.at[n_two : n_two + n_cells])
    copies.start(quads_e, held_two.at[n_two + n_cells : 2 * n_two])
    copies.start(upper.at[0:4], held_one.at[0:4])
    copies.start(row, held_one.at[4:12])
    copies.start(above.at[12:16], held_one.at[12:16])
    copies.start(below.at[12:16], held_one.at[16:20])
    copies.start(row_e, held_one.at[20:28])
    copies.start(row_d, held_one.at[28:36])
    held_one[zero_one] = jnp.zeros((256, 256), BF16)
    held_two[zero_two] = jnp.zeros((256, 256), BF16)
    i = lax.axis_index("qx")
    j = lax.axis_index("qy")
    a = i % 2
    b = j % 2
    for t in range(4):
        mark_listed(
            lambda e: far_one[t // 2, t % 2, e], flags, t, 2 * i - 2, 2 * j - 2, 2 * grid_cols
        )
    mark_listed(
        lambda e: far_two[0, 0, e], flags, 4, i // 2 * 2 - 2, j // 2 * 2 - 2, grid_cols
    )
    core_at = [jnp.where(a == 0, 0, n_two), jnp.where(a == 0, n_two, 0)]
    y_at = [2, 0, 2] if n_rows == 2 else [2, 0, 4]
    pair_tiles = 2 * n_rows
    z_at = [
        jnp.where(b == 0, pair_tiles, 2 * pair_tiles),
        0,
        jnp.where(b == 0, 2 * pair_tiles, pair_tiles),
    ]
    x_at = [b, 1 - b]

    def place_two(w):
        r, c = w // 6, w % 6
        place = core_at[r % 2] + y_at[r // 2] + z_at[c // 2] + x_at[c % 2]
        return jnp.where(flags[4, w] == 1, place, zero_two)

    own_at = [12, 0, 16]
    pair_at = [jnp.where(a == 0, 28, 20), 4, jnp.where(a == 0, 20, 28)]
    col_at = [jnp.where(b == 0, 4, 0), None, jnp.where(b == 0, 0, 4)]

    def place_one(t, w):
        r, c = w // 6, w % 6
        base = own_at[r // 2] if c // 2 == 1 else pair_at[r // 2] + col_at[c // 2]
        place = base + (r % 2) * 2 + c % 2
        return jnp.where(flags[t, w] == 1, place, zero_one)

    for copy in copies.started[:4]:
        copy.wait()
    for u in range(2):
        for v in range(2):

            @pl.when((a == u) & (b == v))
            def _():
                field_two[...] = coupled(
                    class_plan(u, v), couplings.at[1], held_two, place_two
                ).astype(BF16)

    for copy in copies.started[4:]:
        copy.wait()
    for u in range(2):
        for v in range(2):
            t = u * 2 + v
            field = coupled(
                class_plan(u, v), couplings.at[0], held_one, functools.partial(place_one, t)
            )
            down[t] = (field + nt(field_two[...], t_two[u, v])).astype(BF16)


def upper_levels(grid_cols, far_one, far_two, couplings, t_two, *received):
    n_two = 3 * received[6].shape[0]
    return pl.pallas_call(
        functools.partial(upper_kernel, grid_cols, n_two // 6),
        grid=(1,),
        out_shape=tiles(4),
        in_specs=[
            SMEM_SPEC,
            SMEM_SPEC,
            pl.BlockSpec(
                (pl.Element(2), pl.Element(20), pl.Element(256), pl.Element(256)),
                lambda g: (1, 0, 0, 0),
            ),
            pl.BlockSpec((2, 2, 256, 256), lambda g: (0, 0, 0, 0)),
        ]
        + [ANY_SPEC] * 10,
        out_specs=pl.BlockSpec((4, 256, 256), lambda g: (0, 0, 0)),
        scratch_shapes=[
            VMEM((37, 256, 256), BF16),
            VMEM((2 * n_two + 1, 256, 256), BF16),
            VMEM((256, 256), BF16),
            pltpu.SMEM((5, 37), jnp.int32),
            pltpu.SemaphoreType.DMA((10,)),
        ],
        compiler_params=params(),
        cost_estimate=cost(340, 14 << 20),
        name="upper_levels",
    )(far_one, far_two, couplings, t_two, *received)


def source_of(x, y, w):
    r, c = 2 * x + w // 6, 2 * y + w % 6
    if 2 <= c < 6:
        return "inner", r * 4 + c - 2
    side = 0 if c < 2 else 1
    c = c if c < 2 else c - 6
    if 2 <= r < 6:
        return "sides", side * 8 + (r - 2) * 2 + c
    return "corners", (0 if r < 2 else 8) + side * 4 + (r if r < 2 else r - 6) * 2 + c


PARENTS = [(x, y) for x in range(2) for y in range(2)]


def number_of(a, b, parent):
    x, y = parent
    return (2 * x + a) * 4 + 2 * y + b


def level_zero_sums(kind, a, b, flags, couplings, held, zero):
    plan = class_plan(a, b)
    sums = {}
    for turned in (0, 1):
        groups = {}
        for w, k in plan[turned]:
            members = tuple(p for p in PARENTS if source_of(*p, w)[0] == kind)
            if members:
                groups.setdefault(members, []).append((w, k))
        for members, entries in groups.items():
            group = []
            for w, k in entries:
                places = [
                    jnp.where(flags[number_of(a, b, p), w] == 1, source_of(*p, w)[1], zero)
                    for p in members
                ]
                group.append((k, places))
            total = dot_group(held, couplings, turned, group)
            for n, p in enumerate(members):
                part = total[256 * n : 256 * n + 256]
                sums[p] = part if p not in sums else sums[p] + part
    return sums


def grouped(x):
    return x.reshape(2, 2, 2, 2, 256, 256)


CLASS_BLOCK = pl.BlockSpec((2, 1, 2, 1, 256, 256), lambda g: (0, g // 2, 0, g % 2, 0, 0))
COUPLING_BLOCK = pl.BlockSpec((1, 20, 256, 256), lambda g: (0, 0, 0, 0))
GROUPED_F32 = jax.ShapeDtypeStruct((2, 2, 2, 2, 256, 256), F32)


def each_class(step, body):
    for a in range(2):
        for b in range(2):
            pl.when(step == a * 2 + b)(functools.partial(body, a, b))


def near_source(r, c):
    rows_in, cols_in = 1 <= r < 5, 1 <= c < 5
    if rows_in and cols_in:
        return "own", None
    if rows_in:
        return "sides", (0 if c == 0 else 4) + r - 1
    if cols_in:
        return "sides", (8 if r == 0 else 12) + c - 1
    return "corners", (0 if r == 0 else 2) + (0 if c == 0 else 1)


CORNER_HALO = [
    n for (t, k), n in HALO.items() if near_source(t // 4 + k // 3, t % 4 + k % 3)[0] == "corners"
]


def near_part(kind, t, tile_of, held):
    r, c = t // 4, t % 4
    made, blocks = [], []
    for k in range(9):
        found, place = near_source(r + k // 3, c + k % 3)
        if found == kind:
            made.append(tile_of(HALO[t, k]))
            blocks.append(held[place])
    if not made:
        return None
    return nn(jnp.concatenate(made, axis=1), jnp.concatenate(blocks, axis=0))


def sides_kernel(
    flags, couplings, field_in, near_a, near_b, halo_a, halo_b, left, right, above, below,
    field, near, held, near_held, halo, sems,
):
    step = pl.program_id(0)

    def copies():
        pairs = [(left.at[0:8], held.at[0:8]), (right.at[0:8], held.at[8:16])]
        for n, src in enumerate((left, right, above, below)):
            pairs.append((src.at[8:12], near_held.at[4 * n : 4 * n + 4]))
        pairs.append((halo_a, halo.at[0:N_HALO]))
        pairs.append((halo_b, halo.at[N_HALO : 2 * N_HALO]))
        return [pltpu.make_async_copy(src, dst, sems.at[n]) for n, (src, dst) in enumerate(pairs)]

    @pl.when(step == 0)
    def _():
        started = copies()
        for copy in started:
            copy.start()
        held[16] = jnp.zeros((256, 256), BF16)
        for copy in started[:2]:
            copy.wait()

    def body(a, b):
        sums = level_zero_sums("sides", a, b, flags, couplings.at[0], held, 16)
        for x, y in PARENTS:
            field[x, 0, y, 0] = field_in[x, 0, y, 0] + sums[x, y]
        if a == 0 and b == 0:
            for copy in copies()[2:]:
                copy.wait()
        for x, y in PARENTS:
            part = near_part("sides", number_of(a, b, (x, y)), lambda n: halo[n], near_held)
            here = (near_b if x else near_a)[0, y, 0]
            near[x, 0, y, 0] = here if part is None else here + part

    each_class(step, body)


HALF_BLOCK = pl.BlockSpec((1, 2, 1, 256, 256), lambda g: (g // 2, 0, g % 2, 0, 0))


def sides_level(flags, couplings, field, near_a, near_b, *received):
    half = lambda x: x.reshape(2, 2, 2, 256, 256)
    return pl.pallas_call(
        sides_kernel,
        grid=(4,),
        out_shape=(GROUPED_F32, GROUPED_F32),
        in_specs=[SMEM_SPEC, COUPLING_BLOCK, CLASS_BLOCK, HALF_BLOCK, HALF_BLOCK] + [ANY_SPEC] * 6,
        out_specs=[CLASS_BLOCK, CLASS_BLOCK],
        scratch_shapes=[
            VMEM((17, 256, 256), BF16),
            VMEM((16, 256, 256), BF16),
            VMEM((2 * N_HALO, 256, 256), BF16),
            pltpu.SemaphoreType.DMA((8,)),
        ],
        compiler_params=params(),
        cost_estimate=cost(300, 30 << 20),
        name="far_sides",
    )(flags, couplings, field, half(near_a), half(near_b), *received)


def last_kernel(
    flags, couplings, t_one, basis, down_one, field, near, halo_a, halo_b, above, below, out,
    held, near_held, halo, sems,
):
    step = pl.program_id(0)

    @pl.when(step == 0)
    def _():
        copies = Copies(sems)
        copies.start(above.at[0:8], held.at[0:8])
        copies.start(below.at[0:8], held.at[8:16])
        copies.start(above.at[8:10], near_held.at[0:2])
        copies.start(below.at[8:10], near_held.at[2:4])
        for m, n in enumerate(CORNER_HALO):
            copies.start((halo_a if n < N_HALO else halo_b).at[n % N_HALO], halo.at[m])
        held[16] = jnp.zeros((256, 256), BF16)
        copies.wait()

    def body(a, b):
        sums = level_zero_sums("corners", a, b, flags, couplings.at[0], held, 16)
        for x, y in PARENTS:
            total = field[x, 0, y, 0] + nt(down_one[x * 2 + y], t_one[x, 0, y, 0])
            if (x, y) in sums:
                total = total + sums[x, y]
            far = nt(basis[x, 0, y, 0], total.astype(BF16))
            near_sum = near[x, 0, y, 0]
            part = near_part(
                "corners",
                number_of(a, b, (x, y)),
                lambda n: halo[CORNER_HALO.index(n)],
                near_held,
            )
            if part is not None:
                near_sum = near_sum + part
            out[x, 0, y, 0] = (near_sum * TILE_SCALE + far).astype(BF16)

    each_class(step, body)


def last_level(flags, couplings, t_one, basis, *rest):
    return pl.pallas_call(
        last_kernel,
        grid=(4,),
        out_shape=jax.ShapeDtypeStruct((2, 2, 2, 2, 256, 256), BF16),
        in_specs=[
            SMEM_SPEC,
            COUPLING_BLOCK,
            CLASS_BLOCK,
            CLASS_BLOCK,
            pl.BlockSpec((4, 256, 256), lambda g: (0, 0, 0)),
            CLASS_BLOCK,
            CLASS_BLOCK,
        ]
        + [ANY_SPEC] * 4,
        out_specs=CLASS_BLOCK,
        scratch_shapes=[
            VMEM((17, 256, 256), BF16),
            VMEM((4, 256, 256), BF16),
            VMEM((len(CORNER_HALO), 256, 256), BF16),
            pltpu.SemaphoreType.DMA((4 + len(CORNER_HALO),)),
        ],
        compiler_params=params(),
        cost_estimate=cost(270, 20 << 20),
        name="last_level",
    )(flags, couplings, grouped(t_one), grouped(basis), *rest)


def per_device(
    positions,
    samples,
    leaf_basis,
    transfer_one,
    transfer_two,
    couplings,
    near_lists,
    far_zero,
    far_one,
    far_two,
):
    nx = lax.axis_size("qx")
    ny = lax.axis_size("qy")
    down_x = [(k, k + 1) for k in range(nx - 1)]
    up_x = [(k + 1, k) for k in range(nx - 1)]
    down_y = [(k, k + 1) for k in range(ny - 1)]
    up_y = [(k + 1, k) for k in range(ny - 1)]

    up, down, left, right, upper, cell = coefficients(
        samples, leaf_basis, transfer_one, transfer_two
    )

    swap_y = [(k, k ^ 1) for k in range(ny)]
    swap_x = [(k, k ^ 1) for k in range(nx)]
    cross_x = [(k, k + 1) for k in range(1, nx - 1, 2)] + [(k + 1, k) for k in range(1, nx - 1, 2)]
    pair = lax.ppermute(upper, "qy", swap_y)
    if nx == 4:
        others = [lax.ppermute(cell, "qx", [(k, k ^ 2) for k in range(nx)])]
    else:
        others = [
            lax.ppermute(cell, "qx", [(k, k + 2) for k in range(nx - 2)]),
            lax.ppermute(cell, "qx", [(k + 2, k) for k in range(nx - 2)]),
        ]
    others_pair = [lax.ppermute(x, "qy", swap_y) for x in others]
    above = lax.ppermute(down, "qx", down_x)
    below = lax.ppermute(up, "qx", up_x)
    sites = positions.reshape(-1, 2, 256)
    flat_samples = samples.reshape(16, 256, 256)
    near_a, halo_a, flags = near_call(
        0, 4 * nx, 4 * ny, near_lists, far_zero, sites, flat_samples
    )
    pair, others_pair, near_a = lax.optimization_barrier((pair, others_pair, near_a))
    outward = [(k, k + 2) for k in range(0, ny - 2, 2)] + [(k + 2, k) for k in range(1, ny - 2, 2)]
    inward = [(k + 2, k) for k in range(0, ny - 2, 2)] + [(k, k + 2) for k in range(1, ny - 2, 2)]
    n_others = len(others)
    quad = [(0, 4, 1), (1, 4, 1)]
    for n in range(n_others):
        quad += [(2 + n, 0, 1), (2 + n_others + n, 0, 1)]
    n_quad = len(quad)
    across, cells = assembled(
        "pair_payload",
        (upper, pair, *others, *others_pair),
        [(1, 0, 4)] + quad,
        [(0, 4 + n_quad), (4, 4 + n_quad)],
    )
    across, cells, left, right = lax.optimization_barrier((across, cells, left, right))
    outer = lax.ppermute(across, "qy", outward)
    inner = lax.ppermute(cells, "qy", inward)
    cells_e = lax.ppermute(cells, "qx", swap_x)
    on_left = lax.ppermute(right, "qy", down_y)
    on_right = lax.ppermute(left, "qy", up_y)
    near_b, halo_b, field = near_call(
        8,
        4 * nx,
        4 * ny,
        near_lists,
        far_zero,
        sites,
        flat_samples,
        (flags, couplings, up, down, above, below),
    )
    inner, outer, near_b = lax.optimization_barrier((inner, outer, near_b))
    row, quads = assembled(
        "row_payload",
        (pair, outer, inner),
        [(0, 0, 4), (1, 0, 4), (1, 4, n_quad), (2, 0, n_quad)],
        [(0, 8), (8, 8 + 2 * n_quad)],
    )
    row_d = lax.ppermute(row, "qx", cross_x)
    row_e = lax.ppermute(row, "qx", swap_x)
    quads_e = lax.ppermute(quads, "qx", swap_x)
    down_one = upper_levels(
        ny, far_one, far_two, couplings, transfer_two, upper, above, below, row, row_e, row_d,
        cells, cells_e, quads, quads_e,
    )

    on_left, on_right, down_one = lax.optimization_barrier((on_left, on_right, down_one))
    corner_down, corner_up = assembled(
        "corner_payload",
        (on_left, on_right),
        [(0, 4, 4), (1, 4, 4), (0, 11, 1), (1, 11, 1)]
        + [(0, 0, 4), (1, 0, 4), (0, 8, 1), (1, 8, 1)],
        [(0, 10), (10, 20)],
        stated=35,
    )
    corner_above = lax.ppermute(corner_down, "qx", down_x)
    corner_below = lax.ppermute(corner_up, "qx", up_x)
    field, near = sides_level(
        flags, couplings, grouped(field), near_a, near_b, halo_a, halo_b,
        on_left, on_right, above, below,
    )
    result = last_level(
        flags, couplings, transfer_one, leaf_basis, down_one, field, near, halo_a, halo_b,
        corner_above, corner_below,
    )
    return result.reshape(4, 4, 256, 256)


def solution(mesh):
    return jax.shard_map(
        per_device,
        mesh=mesh,
        in_specs=(
            P(),
            P("qx", "qy", None, None),
            P("qx", "qy", None, None),
            P("qx", "qy", None, None),
            P("qx", "qy", None, None),
            P(),
            P("qx", "qy", None),
            P("qx", "qy", None),
            P("qx", "qy", None),
            P("qx", "qy", None),
        ),
        out_specs=P("qx", "qy", None, None),
        check_vma=False,
    )
```
